32 devices in a mesh: wide: 8 (over y, x, core), narrow: 4 (over z).
Axes of the slice: x: 2, y: 2, z: 4, core: 2. Of those that a mesh axis runs over, the one named last changes fastest.
Arguments:
- density: float32 [256, 256, 256], P('wide', 'narrow'), may hold values from -48 to 48
Outputs:
- recon_real: float32 [256, 256, 256], P('narrow', 'wide')
- recon_imag: float32 [256, 256, 256], P('narrow', 'wide')
The draws below stay inside these ranges and needn't reach their ends.
All inputs are finite; a program needn't handle non-finite values.
Results may differ from the reference program's by a relative error of at most 0.0003.
Values sent between devices are 32-bit elements; how exact they have to be, the bound alone decides.
No kernel may reach another device: no remote copies, remote signals or barrier semaphores. Data moves between devices by JAX's collectives and lax.ppermute only.
A program may use at most 192 MiB of HBM per device.

```python
import math
import jax
import jax.numpy as jnp

GRID = 256


def block_scale(rng, shape, split, smallest, high):
    loudness, own = 1.0, jax.random.fold_in(rng, 6)
    for position, shards_of in split:
        steps = jnp.exp(jax.random.uniform(jax.random.fold_in(own, position), (shards_of,), jnp.float32, smallest / len(split), high / len(split)))
        loudness = loudness * jnp.repeat(steps, shape[position] // shards_of).reshape([-1 if axis == position else 1 for axis in range(len(shape))])
    return loudness


def normal_values(own_key, shape, deviation, reach, cuts=(), kind=jnp.bfloat16):
    drawn = deviation * jax.random.normal(own_key, shape, jnp.float32)
    if cuts:
        drawn = drawn * block_scale(own_key, shape, cuts, -0.22, 0.18)
    return jnp.clip(drawn, -reach, reach).astype(kind)


def setup_inputs(seed: int = 0) -> dict:
    splits = jax.random.split(jax.random.key(seed), 2)
    density = normal_values(splits[0], (GRID, GRID, GRID), 8.0, 48.0, ((0, 8), (1, 4)), jnp.float32)
    return {"density": density}


def wavenumbers():
    indices = jnp.arange(GRID, dtype=jnp.int32)
    signed = jnp.where(indices < GRID // 2, indices, indices - GRID)
    return signed.astype(jnp.float32) * (2.0 * math.pi / GRID), indices != GRID // 2


def reference(density):
    spectrum = jnp.fft.fftn(density)
    wave, usable = wavenumbers()
    wave_x = wave[:, None, None]
    wave_y = wave[None, :, None]
    wave_z = wave[None, None, :]
    squared = wave_x * wave_x + wave_y * wave_y + wave_z * wave_z
    keep = usable[:, None, None] & usable[None, :, None] & usable[None, None, :] & (squared > 0)
    squared_safe = jnp.where(squared > 0, squared, jnp.ones_like(squared))
    smooth_kernel = jnp.where(keep, jnp.exp(-0.5 * squared) / squared_safe, jnp.zeros_like(squared))
    waves = [wave_x, wave_y, wave_z]
    pairs = [(0, 0), (1, 1), (2, 2), (0, 1), (0, 2), (1, 2)]
    shear = jnp.zeros(density.shape, jnp.float32)
    for number, (first, second) in enumerate(pairs):
        kernel = smooth_kernel * waves[first] * waves[second]
        tidal = jnp.real(jnp.fft.ifftn(spectrum * kernel))
        weight = 1.0 if number < 3 else 2.0
        shear = shear + weight * tidal * tidal
    recon = jnp.fft.fftn(shear) / (float(GRID) ** 1.5)
    recon = recon.at[0, 0, 0].set(0.0)
    recon_real = jnp.transpose(jnp.real(recon), (2, 1, 0)).astype(jnp.float32)
    recon_imag = jnp.transpose(jnp.imag(recon), (2, 1, 0)).astype(jnp.float32)
    return recon_real, recon_imag
```

```python
import math

import jax
import jax.numpy as jnp
import ml_dtypes
import numpy as np
from jax import lax
from jax.experimental import pallas as pl
from jax.experimental.pallas import tpu as pltpu
from jax.sharding import PartitionSpec as P

AXES = ("wide", "narrow")
TILE = 128
LIMIT = 56 * 1024 * 1024


def angles(rows, columns, length):
    return (2.0 * math.pi / length) * (np.outer(rows, columns) % length)


def split_table(table):
    table = np.asarray(table, np.float64)
    high = table.astype(ml_dtypes.bfloat16)
    low = (table - high.astype(np.float64)).astype(ml_dtypes.bfloat16)
    return np.stack([high, low])


def split(value):
    high = value.astype(jnp.bfloat16)
    low = (value - high.astype(jnp.float32)).astype(jnp.bfloat16)
    return high, low


def product(left, right, contract=((1,), (0,))):
    def dot(a, b):
        return lax.dot_general(a, b, (contract, ((), ())), preferred_element_type=jnp.float32)

    return dot(left[0], right[0]) + (dot(left[0], right[1]) + dot(left[1], right[0]))


def pair(ref):
    return ref[0], ref[1]


def signed_wave(index, length):
    index = np.asarray(index)
    return np.where(index < length // 2, index, index - length) * (2.0 * math.pi / length)


def params(steps):
    return pltpu.CompilerParams(
        vmem_limit_bytes=LIMIT, dimension_semantics=("arbitrary",) * steps
    )


def whole(shape):
    return pl.BlockSpec(shape, lambda *_: (0,) * len(shape))


def cost(macs, moved):
    return pl.CostEstimate(flops=6 * macs, bytes_accessed=moved, transcendentals=0)


def third_kernel(table_ref, density_ref, out_ref):
    rows_x, rows_y, length = density_ref.shape
    half = out_ref.shape[0]
    flat = out_ref.reshape(half * rows_x, 2 * rows_y)
    table = pair(table_ref)
    left_half = lax.broadcasted_iota(jnp.int32, (half, 2 * rows_y), 1) < rows_y
    group = 4
    for first in range(0, rows_x, group):
        block = density_ref[first : first + group].reshape(group * rows_y, length)
        result = product(table, split(block), ((1,), (1,)))
        for inner in range(0, group, 2):
            lanes = slice(inner * rows_y, (inner + 2) * rows_y)
            real = result[:half, lanes]
            imag = result[half:, lanes]
            even = jnp.where(left_half, real, pltpu.roll(imag, rows_y, 1))
            odd = jnp.where(left_half, pltpu.roll(real, rows_y, 1), imag)
            flat[pl.ds(first + inner, half, stride=rows_x), :] = even
            flat[pl.ds(first + inner + 1, half, stride=rows_x), :] = odd


def third_pass(density):
    rows_x, rows_y, length = density.shape
    half = length // 2
    angle = angles(np.arange(half), np.arange(length), length)
    table = split_table(np.concatenate([np.cos(angle), -np.sin(angle)]))
    step = min(8, rows_x)
    return pl.pallas_call(
        third_kernel,
        grid=(rows_x // step,),
        in_specs=[
            whole(table.shape),
            pl.BlockSpec((step, rows_y, length), lambda i: (i, 0, 0)),
        ],
        out_specs=pl.BlockSpec((half, step, 2 * rows_y), lambda i: (0, i, 0)),
        out_shape=jax.ShapeDtypeStruct((half, rows_x, 2 * rows_y), jnp.float32),
        compiler_params=params(1),
        cost_estimate=cost(density.size * length, 8 * density.size),
    )(table, density)


def spectrum_kernel(
    fields, per_c, groups, pairs_x, wave_c_ref, wave_ref, row_ref, second_ref, first_ref, back_ref, in_ref, *outs
):
    wide, narrow, _, rows_x, lanes = in_ref.shape
    length = wide * rows_x
    plane = jnp.concatenate(
        [in_ref[:, n, 0].reshape(length, lanes) for n in range(narrow)], axis=1
    )
    plane = product(split(plane), pair(second_ref))
    both = product(pair(first_ref), split(plane))
    real = both[:length, :length] + both[length:, length:]
    imag = both[:length, length:] - both[length:, :length]
    wave_a = wave_ref[...]
    wave_b = row_ref[...]
    wave_c = wave_c_ref[pl.program_id(0)]
    squared = wave_a * wave_a + (wave_b * wave_b + wave_c * wave_c)
    spot_a = lax.broadcasted_iota(jnp.int32, (length, length), 0)
    spot_b = lax.broadcasted_iota(jnp.int32, (length, length), 1)
    keep = (spot_a != length // 2) & (spot_b != length // 2) & (squared > 0)
    safe = jnp.where(squared > 0, squared, 1.0)
    smooth = jnp.where(keep, jnp.exp(-0.5 * squared) / safe, 0.0) * (1.0 / float(length) ** 3)
    field = jnp.concatenate([real * smooth, imag * smooth], axis=1)
    tiles, message, tile = outs[0].shape[1:]
    devices = length // (groups * pairs_x)
    flats = [ref.reshape(devices * tiles * message, tile) for ref in outs]
    for number in range(fields):
        both = product(pair(back_ref), split(field))
        real = both[:length, :length] - both[length:, length:]
        imag = both[:length, length:] + both[length:, :length]
        value = jnp.concatenate([real, imag], axis=1)
        count = tiles // fields
        for group in range(groups):
            for x in range(pairs_x):
                start = (group * pairs_x + x) * devices
                for spot in range(count):
                    at = (number * count + spot) * message + x * per_c + pl.program_id(0)
                    flats[group][pl.ds(at, devices, stride=tiles * message), :] = value[
                        start : start + devices, spot * tile : (spot + 1) * tile
                    ]
        if number + 1 < fields:
            field = field * wave_a


def spectrum_pass(received, waves_c, devices, pairs_x):
    wide, narrow, per_c, rows_x, lanes = received.shape
    length = wide * rows_x
    rows_y = lanes // 2
    index = np.arange(length)
    angle = angles(index, index, length)
    cosine, sine = np.cos(angle), np.sin(angle)
    second = np.zeros((narrow, 2, rows_y, 2 * length))
    for n in range(narrow):
        spots = slice(n * rows_y, (n + 1) * rows_y)
        second[n, 0] = np.concatenate([cosine[spots], -sine[spots]], axis=1)
        second[n, 1] = np.concatenate([sine[spots], cosine[spots]], axis=1)
    second = split_table(second.reshape(2 * length, 2 * length))
    first = split_table(np.concatenate([cosine, sine]))
    slab = length // devices
    groups = slab // pairs_x
    order = index.reshape(devices, groups, pairs_x).transpose(1, 2, 0).reshape(-1)
    back = split_table(np.concatenate([cosine[order], sine[order]]))
    wave = signed_wave(index, length).astype(np.float32)
    fields = 3
    out_shape = (devices, fields * 2 * length // TILE, pairs_x * per_c, TILE)

    def body(*refs):
        spectrum_kernel(fields, per_c, groups, pairs_x, *refs)

    return pl.pallas_call(
        body,
        grid=(per_c,),
        in_specs=[
            pl.BlockSpec(memory_space=pltpu.SMEM),
            whole((length, 1)),
            whole((1, length)),
            whole(second.shape),
            whole(first.shape),
            whole(back.shape),
            pl.BlockSpec((wide, narrow, 1, rows_x, lanes), lambda i: (0, 0, i, 0, 0)),
        ],
        out_specs=[whole(out_shape)] * groups,
        out_shape=[jax.ShapeDtypeStruct(out_shape, jnp.float32)] * groups,
        compiler_params=params(1),
        cost_estimate=cost(per_c * 20 * length**3, 20 * per_c * length**2 * 2),
    )(waves_c, wave[:, None], wave[None, :], second, first, back, received)


def shear_kernel(
    pairs_x, row_ref, lane_ref, second_ref, third_ref, ahead_ref, last_ref, in_ref, out_ref, shear_ref
):
    step = pl.program_id(0)
    length = shear_ref.shape[1]

    @pl.when(step == 0)
    def _():
        shear_ref[...] = jnp.zeros_like(shear_ref)

    devices, tiles, message, tile = in_ref.shape
    field = jnp.concatenate(
        [in_ref[:, spot].reshape(devices * message, tile) for spot in range(tiles)], axis=1
    )
    field = field * row_ref[0] * lane_ref[0]
    field = product(split(field), pair(second_ref))
    field = jnp.concatenate([field[:, :length], field[:, length:]], axis=0)
    field = product(pair(third_ref), split(field))
    shear_ref[...] += field * field

    @pl.when(step == 5)
    def _():
        wide, narrow, _, rows_b, lanes = out_ref.shape
        ahead = product(pair(ahead_ref), split(shear_ref[...]), ((1,), (1,)))
        for spot in range(pairs_x):
            part = slice(spot * length, (spot + 1) * length)
            value = jnp.concatenate([ahead[:length, part], ahead[length:, part]], axis=1)
            value = product(split(value), pair(last_ref))
            for w in range(wide):
                for n in range(narrow):
                    out_ref[w, n, spot] = value[
                        w * rows_b : (w + 1) * rows_b, n * lanes : (n + 1) * lanes
                    ]


def shear_pass(received, wide, narrow, pairs_x, per_c):
    devices, tiles, message, tile = received.shape
    rows = devices * message
    length = tiles * tile // 6
    index = np.arange(length)
    angle = angles(index, index, length)
    cosine, sine = np.cos(angle), np.sin(angle)
    second = np.block([[cosine, sine], [-sine, cosine]])
    spots = np.arange(rows).reshape(devices, pairs_x, per_c)
    row_c = (np.arange(devices)[:, None, None] * per_c + np.arange(per_c)[None, None, :]) + 0 * spots
    row_c = row_c.reshape(-1)
    row_x = (np.arange(pairs_x)[None, :, None] + 0 * spots).reshape(-1)
    weight = np.where(row_c == 0, 1.0, 2.0)
    angle = angles(index, row_c, length)
    third = np.concatenate(
        [
            np.concatenate(
                [(row_x == x) * weight * np.cos(angle), (row_x == x) * weight * -np.sin(angle)], axis=1
            )
            for x in range(pairs_x)
        ]
    )
    ahead = np.concatenate([cosine, -sine])
    cos_z = cosine.reshape(length, narrow, 1, length // narrow)
    sin_z = sine.reshape(length, narrow, 1, length // narrow)
    last = np.concatenate(
        [
            np.concatenate([cos_z, -sin_z], axis=2).reshape(length, 2 * length),
            np.concatenate([sin_z, cos_z], axis=2).reshape(length, 2 * length),
        ]
    )
    wave = signed_wave(index, length)
    wave_rows = wave[row_c]
    wave_lanes = np.concatenate([wave, wave])
    twice = math.sqrt(2.0)
    one_row, one_lane = np.ones_like(wave_rows), np.ones_like(wave_lanes)
    row_factor = np.stack(
        [one_row, twice * one_row, twice * wave_rows, one_row, twice * wave_rows, wave_rows**2]
    ).astype(np.float32)[:, :, None]
    lane_factor = np.stack(
        [one_lane, wave_lanes, one_lane, wave_lanes**2, wave_lanes, one_lane]
    ).astype(np.float32)[:, None, :]
    tables = [split_table(table) for table in (second, third, ahead, last)]
    out_shape = (wide, narrow, pairs_x, length // wide, 2 * length // narrow)

    def body(*refs):
        shear_kernel(pairs_x, *refs)

    def which(i):
        return (0, 2 - (i >= 1).astype(jnp.int32) - (i >= 3).astype(jnp.int32), 0, 0)

    return pl.pallas_call(
        body,
        grid=(6,),
        in_specs=[
            pl.BlockSpec((1, rows, 1), lambda i: (i, 0, 0)),
            pl.BlockSpec((1, 1, 2 * length), lambda i: (i, 0, 0)),
            *[whole(table.shape) for table in tables],
            pl.BlockSpec((devices, tiles // 3, message, tile), which),
        ],
        out_specs=whole(out_shape),
        out_shape=jax.ShapeDtypeStruct(out_shape, jnp.float32),
        scratch_shapes=[pltpu.VMEM((pairs_x * length, length), jnp.float32)],
        compiler_params=params(1),
        cost_estimate=cost(60 * length**3, 4 * received.size + 4 * 2**20),
    )(row_factor, lane_factor, *tables, received)


def first_kernel(scale, anchor_ref, table_ref, *refs):
    ins, (real_ref, imag_ref, real_tile_ref, imag_tile_ref) = refs[:-4], refs[-4:]
    devices, pairs_x, rows_b, lanes = ins[0].shape
    half, length = lanes // 2, real_ref.shape[2]
    table = pair(table_ref)
    flats = [ref.reshape(devices * pairs_x * rows_b, lanes) for ref in ins]
    tile = real_tile_ref.shape[2]
    spot_c = lax.broadcasted_iota(jnp.int32, (half, length), 0)
    spot_a = lax.broadcasted_iota(jnp.int32, (half, length), 1)
    is_anchor = (anchor_ref[0] == 1) & (pl.program_id(0) == 0)
    anchor = (spot_c == 0) & (spot_a == 0) & is_anchor
    group = min(4, rows_b)
    for first in range(0, rows_b, group):
        columns = []
        for b in range(first, first + group):
            column = jnp.concatenate(
                [flat[pl.ds(b, devices * pairs_x, stride=rows_b), :] for flat in flats], axis=0
            )
            columns.append(column.T)
        result = product(split(jnp.concatenate(columns, axis=0)), table)
        for number in range(group):
            b = first + number
            here = result[number * lanes : (number + 1) * lanes]
            real = (here[:half, :length] + here[half:, length:]) * scale
            imag = (here[half:, :length] - here[:half, length:]) * scale
            if b == 0:
                real = jnp.where(anchor, 0.0, real)
                imag = jnp.where(anchor, 0.0, imag)
            for spot in range(length // tile):
                part = slice(spot * tile, (spot + 1) * tile)
                real_tile_ref[spot, pl.ds(b, half, stride=rows_b), :] = real[:, part]
                imag_tile_ref[spot, pl.ds(b, half, stride=rows_b), :] = imag[:, part]
    for spot in range(length // tile):
        part = slice(spot * tile, (spot + 1) * tile)
        real_ref[:, :, part] = real_tile_ref[spot].reshape(half, rows_b, tile)
        imag_ref[:, :, part] = imag_tile_ref[spot].reshape(half, rows_b, tile)


def first_pass(parts, is_anchor, length):
    devices, pairs_x, rows_b, lanes = parts[0].shape
    groups = len(parts)
    index = np.arange(length)
    order = index.reshape(devices, groups, pairs_x).transpose(1, 0, 2).reshape(-1)
    angle = angles(order, index, length)
    table = split_table(np.concatenate([np.cos(angle), np.sin(angle)], axis=1))
    step = min(8, rows_b)
    scale = 1.0 / float(length) ** 1.5

    def body(*refs):
        first_kernel(scale, *refs)

    out_shape = jax.ShapeDtypeStruct((lanes // 2, rows_b, length), jnp.float32)
    return pl.pallas_call(
        body,
        grid=(rows_b // step,),
        in_specs=[
            pl.BlockSpec(memory_space=pltpu.SMEM),
            whole(table.shape),
            *[pl.BlockSpec((devices, pairs_x, step, lanes), lambda i: (0, 0, i, 0))] * groups,
        ],
        out_specs=[pl.BlockSpec((lanes // 2, step, length), lambda i: (0, i, 0))] * 2,
        out_shape=[out_shape] * 2,
        scratch_shapes=[pltpu.VMEM((length // TILE, lanes // 2 * step, TILE), jnp.float32)] * 2,
        compiler_params=params(1),
        cost_estimate=cost(rows_b * lanes * length * 2 * length, 8 * rows_b * lanes * length),
    )(is_anchor, table, *parts)


def transpose(value):
    return lax.all_to_all(value, AXES, split_axis=0, concat_axis=0, tiled=True)


def solution(mesh):
    wide, narrow = mesh.shape["wide"], mesh.shape["narrow"]
    devices = wide * narrow

    def per_device(density):
        rows_x, rows_y, length = density.shape
        per_c = length // 2 // devices
        pairs_x = 2
        spot_wide, spot_narrow = lax.axis_index("wide"), lax.axis_index("narrow")
        here = spot_wide * narrow + spot_narrow
        planes = third_pass(density).reshape(devices, per_c, rows_x, 2 * rows_y)
        planes = transpose(planes).reshape(wide, narrow, per_c, rows_x, 2 * rows_y)
        waves_c = (here * per_c + jnp.arange(per_c, dtype=jnp.int32)).astype(jnp.float32)
        waves_c = waves_c * (2.0 * math.pi / length)
        chunks = spectrum_pass(planes, waves_c, devices, pairs_x)
        is_anchor = (here == 0).astype(jnp.int32).reshape(1)
        parts = []
        for chunk in chunks:
            part = shear_pass(transpose(chunk), wide, narrow, pairs_x, per_c)
            part = part.reshape((devices,) + part.shape[2:])
            parts.append(transpose(part))
        return tuple(first_pass(parts, is_anchor, length))

    return jax.shard_map(
        per_device,
        mesh=mesh,
        in_specs=(P("wide", "narrow", None),),
        out_specs=(P("narrow", "wide", None), P("narrow", "wide", None)),
        check_vma=False,
    )
```

```python
import math

import jax
import jax.numpy as jnp
import ml_dtypes
import numpy as np
from jax import lax
from jax.experimental import pallas as pl
from jax.experimental.pallas import tpu as pltpu
from jax.sharding import PartitionSpec as P

AXES = ("wide", "narrow")
TILE = 128
LIMIT = 56 * 1024 * 1024


def angles(rows, columns, length):
    return (2.0 * math.pi / length) * (np.outer(rows, columns) % length)


def split_table(table):
    table = np.asarray(table, np.float64)
    high = table.astype(ml_dtypes.bfloat16)
    low = (table - high.astype(np.float64)).astype(ml_dtypes.bfloat16)
    return np.stack([high, low])


def split(value):
    high = value.astype(jnp.bfloat16)
    low = (value - high.astype(jnp.float32)).astype(jnp.bfloat16)
    return high, low


def product(left, right, contract=((1,), (0,))):
    (left_axis,), (right_axis,) = contract
    left = jnp.concatenate([left[0], left[0], left[1]], axis=left_axis)
    right = jnp.concatenate([right[0], right[1], right[0]], axis=right_axis)
    return lax.dot_general(
        left, right, (contract, ((), ())), preferred_element_type=jnp.float32
    )


def pair(ref):
    return ref[0], ref[1]


def signed_wave(index, length):
    index = np.asarray(index)
    return np.where(index < length // 2, index, index - length) * (2.0 * math.pi / length)


def params(steps):
    return pltpu.CompilerParams(
        vmem_limit_bytes=LIMIT, dimension_semantics=("arbitrary",) * steps
    )


def whole(shape):
    return pl.BlockSpec(shape, lambda *_: (0,) * len(shape))


def cost(macs, moved):
    return pl.CostEstimate(flops=6 * macs, bytes_accessed=moved, transcendentals=0)


def third_kernel(table_ref, density_ref, out_ref):
    rows_x, rows_y, length = density_ref.shape
    half = out_ref.shape[0]
    flat = out_ref.reshape(half * rows_x, 2 * rows_y)
    table = pair(table_ref)
    left_half = lax.broadcasted_iota(jnp.int32, (half, 2 * rows_y), 1) < rows_y
    group = 4
    for first in range(0, rows_x, group):
        block = density_ref[first : first + group].reshape(group * rows_y, length)
        result = product(table, split(block), ((1,), (1,)))
        for inner in range(0, group, 2):
            lanes = slice(inner * rows_y, (inner + 2) * rows_y)
            real = result[:half, lanes]
            imag = result[half:, lanes]
            even = jnp.where(left_half, real, pltpu.roll(imag, rows_y, 1))
            odd = jnp.where(left_half, pltpu.roll(real, rows_y, 1), imag)
            flat[pl.ds(first + inner, half, stride=rows_x), :] = even
            flat[pl.ds(first + inner + 1, half, stride=rows_x), :] = odd


def third_pass(density):
    rows_x, rows_y, length = density.shape
    half = length // 2
    angle = angles(np.arange(half), np.arange(length), length)
    table = split_table(np.concatenate([np.cos(angle), -np.sin(angle)]))
    step = min(8, rows_x)
    return pl.pallas_call(
        third_kernel,
        grid=(rows_x // step,),
        in_specs=[
            whole(table.shape),
            pl.BlockSpec((step, rows_y, length), lambda i: (i, 0, 0)),
        ],
        out_specs=pl.BlockSpec((half, step, 2 * rows_y), lambda i: (0, i, 0)),
        out_shape=jax.ShapeDtypeStruct((half, rows_x, 2 * rows_y), jnp.float32),
        compiler_params=params(1),
        cost_estimate=cost(density.size * length, 8 * density.size),
    )(table, density)


def turn(angle):
    cosine, sine = np.cos(angle), np.sin(angle)
    return np.block([[cosine, -sine], [sine, cosine]])


def spectrum_kernel(per_c, slab, wave_c_ref, a_ref, b_ref, second_ref, first_ref, back_ref, in_ref, *outs):
    wide, narrow, _, rows_x, lanes = in_ref.shape
    length = wide * rows_x
    half = length // 2

    def column(n):
        return in_ref[:, n, 0].reshape(length, lanes)

    low = jnp.concatenate([column(n) for n in range(narrow // 2)], axis=1)
    high = jnp.concatenate([column(n) for n in range(narrow // 2, narrow)], axis=1)
    planes = [
        product(split(low + high), pair(second_ref.at[0])),
        product(split(low - high), pair(second_ref.at[1])),
    ]

    def stacked(sign):
        return jnp.concatenate(
            [
                jnp.concatenate(
                    [
                        plane[:half, part * half : (part + 1) * half]
                        + sign * plane[half:, part * half : (part + 1) * half]
                        for plane in planes
                    ],
                    axis=1,
                )
                for part in range(2)
            ],
            axis=0,
        )

    wave_b = b_ref[0]
    wave_c = wave_c_ref[pl.program_id(0)]
    field = []
    for parity, sign in ((0, 1.0), (1, -1.0)):
        value = product(pair(first_ref.at[parity]), split(stacked(sign)))
        wave_a = a_ref[0, parity]
        squared = wave_a * wave_a + (wave_b * wave_b + wave_c * wave_c)
        safe = jnp.where(squared > 0, squared, 1.0)
        usable = a_ref[1, parity] * b_ref[1] * (1.0 / float(length) ** 3)
        smooth = jnp.where(squared > 0, jnp.exp(-0.5 * squared) / safe, 0.0) * usable
        field.append(value * jnp.concatenate([smooth, smooth], axis=0))
    tiles, message, tile = outs[0].shape[1:]
    devices = outs[0].shape[0]
    near = devices // 2
    count = slab // len(outs)
    flats = [ref.reshape(devices * tiles * message, tile) for ref in outs]
    for number in range(3):
        even = product(pair(back_ref.at[0]), split(field[0]))
        odd = product(pair(back_ref.at[1]), split(field[1]))
        for side, value in enumerate((even + odd, even - odd)):
            for group in range(len(outs)):
                for x in range(count):
                    for spot in range(tiles // 3):
                        parity, part = divmod(spot, 2)
                        start = part * half + (group * count + x) * near
                        at = (
                            (side * near * tiles + number * (tiles // 3) + spot) * message
                            + x * per_c
                            + pl.program_id(0)
                        )
                        flats[group][pl.ds(at, near, stride=tiles * message), :] = value[
                            start : start + near, parity * tile : (parity + 1) * tile
                        ]
        if number < 2:
            for parity in range(2):
                wave_a = a_ref[0, parity]
                field[parity] = field[parity] * jnp.concatenate([wave_a, wave_a], axis=0)


def halves(length):
    return np.arange(length).reshape(length // 2, 2).T


def spectrum_pass(received, waves_c, devices, chunks):
    wide, narrow, per_c, rows_x, lanes = received.shape
    length = wide * rows_x
    rows_y = lanes // 2
    half = length // 2
    near = np.arange(half)
    split_index = halves(length)
    slab = length // devices
    second, first, back = [], [], []
    order = near.reshape(devices // 2, slab).T.reshape(-1)
    for index in split_index:
        table = turn(-angles(index, near, length)).reshape(2, half, 2, narrow // 2, rows_y)
        second.append(table.transpose(3, 2, 4, 0, 1).reshape(length, length))
        first.append(turn(-angles(index, near, length)))
        back.append(turn(angles(order, index, length)))
    tables = [np.stack([split_table(table) for table in each]) for each in (second, first, back)]
    wave = signed_wave(split_index, length)
    a_table = np.stack([wave, split_index != half]).astype(np.float32)[..., None]
    b_table = a_table.reshape(2, 1, length)
    out_shape = (devices, 3 * 2 * length // TILE, slab // chunks * per_c, TILE)

    def body(*refs):
        spectrum_kernel(per_c, slab, *refs)

    return pl.pallas_call(
        body,
        grid=(per_c,),
        in_specs=[
            pl.BlockSpec(memory_space=pltpu.SMEM),
            whole(a_table.shape),
            whole(b_table.shape),
            *[whole(table.shape) for table in tables],
            pl.BlockSpec((wide, narrow, 1, rows_x, lanes), lambda i: (0, 0, i, 0, 0)),
        ],
        out_specs=[whole(out_shape)] * chunks,
        out_shape=[jax.ShapeDtypeStruct(out_shape, jnp.float32)] * chunks,
        compiler_params=params(1),
        cost_estimate=cost(per_c * 10 * length**3, 20 * per_c * length**2 * 2),
    )(waves_c, a_table, b_table, *tables, received)


def shear_kernel(
    pairs_x, row_ref, lane_ref, second_ref, third_ref, ahead_ref, last_ref, in_ref, out_ref, shear_ref
):
    step = pl.program_id(1)
    length = shear_ref.shape[1]
    half = length // 2

    @pl.when(step == 0)
    def _():
        shear_ref[...] = jnp.zeros_like(shear_ref)

    devices, tiles, message, tile = in_ref.shape
    field = jnp.concatenate(
        [in_ref[:, spot].reshape(devices * message, tile) for spot in range(tiles)], axis=1
    )
    field = field * row_ref[0] * lane_ref[0]
    even = product(split(field[:, :length]), pair(second_ref.at[0]))
    odd = product(split(field[:, length:]), pair(second_ref.at[1]))
    near, far = even + odd, even - odd
    field = jnp.concatenate(
        [
            jnp.concatenate([near[:, :half], far[:, :half]], axis=1),
            jnp.concatenate([near[:, half:], far[:, half:]], axis=1),
        ],
        axis=0,
    )
    field = product(pair(third_ref), split(field))
    shear_ref[...] += field * field

    @pl.when(step == 5)
    def _():
        wide, narrow, _, rows_b, lanes = out_ref.shape
        ahead = product(pair(ahead_ref), split(shear_ref[...]), ((1,), (1,)))
        for spot in range(pairs_x):
            part = slice(spot * length, (spot + 1) * length)
            value = jnp.concatenate([ahead[:length, part], ahead[length:, part]], axis=1)
            value = product(split(value), pair(last_ref))
            for w in range(wide):
                for n in range(narrow):
                    out_ref[w, n, spot] = value[
                        w * rows_b : (w + 1) * rows_b, n * lanes : (n + 1) * lanes
                    ]


def shear_pass(received, wide, narrow, pairs_x, per_c):
    devices, tiles, message, tile = received.shape
    pairs = message // (pairs_x * per_c)
    rows = devices * pairs_x * per_c
    length = tiles * tile // 6
    half = length // 2
    index = np.arange(length)
    angle = angles(index, index, length)
    cosine, sine = np.cos(angle), np.sin(angle)
    split_index = halves(length)
    second = np.stack(
        [split_table(turn(angles(np.arange(half), b, length)).T) for b in split_index]
    )
    spots = np.arange(rows).reshape(devices, pairs_x, per_c)
    row_c = (np.arange(devices)[:, None, None] * per_c + np.arange(per_c)[None, None, :]) + 0 * spots
    row_c = row_c.reshape(-1)
    row_x = (np.arange(pairs_x)[None, :, None] + 0 * spots).reshape(-1)
    weight = np.where(row_c == 0, 1.0, 2.0)
    angle = angles(index, row_c, length)
    third = np.concatenate(
        [
            np.concatenate(
                [(row_x == x) * weight * np.cos(angle), (row_x == x) * weight * -np.sin(angle)], axis=1
            )
            for x in range(pairs_x)
        ]
    )
    ahead = np.concatenate([cosine, -sine])
    cos_z = cosine.reshape(length, narrow, 1, length // narrow)
    sin_z = sine.reshape(length, narrow, 1, length // narrow)
    last = np.concatenate(
        [
            np.concatenate([cos_z, -sin_z], axis=2).reshape(length, 2 * length),
            np.concatenate([sin_z, cos_z], axis=2).reshape(length, 2 * length),
        ]
    )
    wave = signed_wave(index, length)
    wave_rows = wave[row_c]
    wave_lanes = np.stack([wave[split_index]] * 2, axis=1).reshape(-1)
    twice = math.sqrt(2.0)
    one_row, one_lane = np.ones_like(wave_rows), np.ones_like(wave_lanes)
    row_factor = np.stack(
        [one_row, twice * one_row, twice * wave_rows, one_row, twice * wave_rows, wave_rows**2]
    ).astype(np.float32)[:, :, None]
    lane_factor = np.stack(
        [one_lane, wave_lanes, one_lane, wave_lanes**2, wave_lanes, one_lane]
    ).astype(np.float32)[:, None, :]
    tables = [second] + [split_table(table) for table in (third, ahead, last)]
    block = (wide, narrow, pairs_x, length // wide, 2 * length // narrow)
    out_shape = (wide, narrow, pairs * pairs_x, length // wide, 2 * length // narrow)

    def body(*refs):
        shear_kernel(pairs_x, *refs)

    def which(p, i):
        return (0, 2 - (i >= 1).astype(jnp.int32) - (i >= 3).astype(jnp.int32), p, 0)

    return pl.pallas_call(
        body,
        grid=(pairs, 6),
        in_specs=[
            pl.BlockSpec((1, rows, 1), lambda p, i: (i, 0, 0)),
            pl.BlockSpec((1, 1, 2 * length), lambda p, i: (i, 0, 0)),
            *[whole(table.shape) for table in tables],
            pl.BlockSpec((devices, tiles // 3, pairs_x * per_c, tile), which),
        ],
        out_specs=pl.BlockSpec(block, lambda p, i: (0, 0, p, 0, 0)),
        out_shape=jax.ShapeDtypeStruct(out_shape, jnp.float32),
        scratch_shapes=[pltpu.VMEM((pairs_x * length, length), jnp.float32)],
        compiler_params=params(2),
        cost_estimate=cost(pairs * 48 * length**3, 4 * received.size + 4 * 2**20),
    )(row_factor, lane_factor, *tables, received)


def first_kernel(scale, anchor_ref, table_ref, *refs):
    ins, (real_ref, imag_ref, real_tile_ref, imag_tile_ref) = refs[:-4], refs[-4:]
    devices, count, rows_b, lanes = ins[0].shape
    half_c, length = lanes // 2, real_ref.shape[2]
    half = length // 2
    tables = [pair(table_ref.at[0]), pair(table_ref.at[1])]
    flats = [ref.reshape(devices * count * rows_b, lanes) for ref in ins]
    tile = real_tile_ref.shape[2]
    spot_c = lax.broadcasted_iota(jnp.int32, (half_c, half), 0)
    spot_a = lax.broadcasted_iota(jnp.int32, (half_c, half), 1)
    is_anchor = (anchor_ref[0] == 1) & (pl.program_id(0) == 0)
    anchor = (spot_c == 0) & (spot_a == 0) & is_anchor
    group = min(8, rows_b)
    spots = devices * count // 2
    for first in range(0, rows_b, group):
        sums = []
        for parity in range(2):
            columns = []
            for b in range(first, first + group):
                start = parity * rows_b + b
                column = jnp.concatenate(
                    [flat[pl.ds(start, spots, stride=2 * rows_b), :] for flat in flats], axis=0
                ).T
                columns.append(jnp.concatenate([column[:half_c], column[half_c:]], axis=1))
            sums.append(product(split(jnp.concatenate(columns, axis=0)), tables[parity]))
        even, odd = sums
        for side, value in enumerate((even + odd, even - odd)):
            value = value * scale
            for number in range(group):
                b = first + number
                rows = slice(number * half_c, (number + 1) * half_c)
                real, imag = value[rows, :half], value[rows, half:]
                if b == 0 and side == 0:
                    real = jnp.where(anchor, 0.0, real)
                    imag = jnp.where(anchor, 0.0, imag)
                for spot in range(half // tile):
                    part = slice(spot * tile, (spot + 1) * tile)
                    at = side * (half // tile) + spot
                    real_tile_ref[at, pl.ds(b, half_c, stride=rows_b), :] = real[:, part]
                    imag_tile_ref[at, pl.ds(b, half_c, stride=rows_b), :] = imag[:, part]
    for spot in range(length // tile):
        part = slice(spot * tile, (spot + 1) * tile)
        real_ref[:, :, part] = real_tile_ref[spot].reshape(half_c, rows_b, tile)
        imag_ref[:, :, part] = imag_tile_ref[spot].reshape(half_c, rows_b, tile)


def first_pass(parts, is_anchor, length):
    devices, count, rows_b, lanes = parts[0].shape
    groups = len(parts)
    index = np.arange(length).reshape(devices, groups, count // 2, 2)
    index = index.transpose(3, 1, 0, 2).reshape(2, -1)
    table = np.stack(
        [split_table(turn(-angles(np.arange(length // 2), x, length)).T) for x in index]
    )
    step = min(8, rows_b)
    scale = 1.0 / float(length) ** 1.5

    def body(*refs):
        first_kernel(scale, *refs)

    out_shape = jax.ShapeDtypeStruct((lanes // 2, rows_b, length), jnp.float32)
    return pl.pallas_call(
        body,
        grid=(rows_b // step,),
        in_specs=[
            pl.BlockSpec(memory_space=pltpu.SMEM),
            whole(table.shape),
            *[pl.BlockSpec((devices, count, step, lanes), lambda i: (0, 0, i, 0))] * groups,
        ],
        out_specs=[pl.BlockSpec((lanes // 2, step, length), lambda i: (0, i, 0))] * 2,
        out_shape=[out_shape] * 2,
        scratch_shapes=[pltpu.VMEM((length // TILE, lanes // 2 * step, TILE), jnp.float32)] * 2,
        compiler_params=params(1),
        cost_estimate=cost(rows_b * lanes * length * length, 8 * rows_b * lanes * length),
    )(is_anchor, table, *parts)


def transpose(value):
    return lax.all_to_all(value, AXES, split_axis=0, concat_axis=0, tiled=True)


def solution(mesh):
    wide, narrow = mesh.shape["wide"], mesh.shape["narrow"]
    devices = wide * narrow

    def per_device(density):
        rows_x, rows_y, length = density.shape
        per_c = length // 2 // devices
        pairs_x = 2
        spot_wide, spot_narrow = lax.axis_index("wide"), lax.axis_index("narrow")
        here = spot_wide * narrow + spot_narrow
        planes = third_pass(density).reshape(devices, per_c, rows_x, 2 * rows_y)
        planes = transpose(planes).reshape(wide, narrow, per_c, rows_x, 2 * rows_y)
        waves_c = (here * per_c + jnp.arange(per_c, dtype=jnp.int32)).astype(jnp.float32)
        waves_c = waves_c * (2.0 * math.pi / length)
        chunks = spectrum_pass(planes, waves_c, devices, min(2, length // devices // pairs_x))
        is_anchor = (here == 0).astype(jnp.int32).reshape(1)
        parts = []
        for chunk in chunks:
            part = shear_pass(transpose(chunk), wide, narrow, pairs_x, per_c)
            part = part.reshape((devices,) + part.shape[2:])
            parts.append(transpose(part))
        return tuple(first_pass(parts, is_anchor, length))

    return jax.shard_map(
        per_device,
        mesh=mesh,
        in_specs=(P("wide", "narrow", None),),
        out_specs=(P("narrow", "wide", None), P("narrow", "wide", None)),
        check_vma=False,
    )
```

```python
import math

import jax
import jax.numpy as jnp
import ml_dtypes
import numpy as np
from jax import lax
from jax.experimental import pallas as pl
from jax.experimental.pallas import tpu as pltpu
from jax.sharding import PartitionSpec as P

AXES = ("wide", "narrow")
TILE = 128
LIMIT = 56 * 1024 * 1024


def angles(rows, columns, length):
    return (2.0 * math.pi / length) * (np.outer(rows, columns) % length)


def split_table(table):
    table = np.asarray(table, np.float64)
    high = table.astype(ml_dtypes.bfloat16)
    low = (table - high.astype(np.float64)).astype(ml_dtypes.bfloat16)
    return np.stack([high, low])


def split(value):
    high = value.astype(jnp.bfloat16)
    low = (value - high.astype(jnp.float32)).astype(jnp.bfloat16)
    return high, low


def product(left, right, contract=((1,), (0,))):
    (left_axis,), (right_axis,) = contract
    left = jnp.concatenate([left[0], left[0], left[1]], axis=left_axis)
    right = jnp.concatenate([right[0], right[1], right[0]], axis=right_axis)
    return lax.dot_general(
        left, right, (contract, ((), ())), preferred_element_type=jnp.float32
    )


def pair(ref):
    return ref[0], ref[1]


def signed_wave(index, length):
    index = np.asarray(index)
    return np.where(index < length // 2, index, index - length) * (2.0 * math.pi / length)


def params(steps):
    return pltpu.CompilerParams(
        vmem_limit_bytes=LIMIT, dimension_semantics=("arbitrary",) * steps
    )


def whole(shape):
    return pl.BlockSpec(shape, lambda *_: (0,) * len(shape))


def cost(macs, moved):
    return pl.CostEstimate(flops=6 * macs, bytes_accessed=moved, transcendentals=0)


def third_kernel(counts, table_ref, density_ref, *outs):
    rows_x, rows_y, length = density_ref.shape
    wide, sides, ranks = outs[0].shape[:3]
    half = length // 2
    flats = [ref.reshape(math.prod(ref.shape[:5]), 2 * rows_y) for ref in outs]
    table = pair(table_ref)
    left_half = lax.broadcasted_iota(jnp.int32, (half, 2 * rows_y), 1) < rows_y
    group = 4
    for first in range(0, rows_x, group):
        block = density_ref[first : first + group].reshape(group * rows_y, length)
        result = product(table, split(block), ((1,), (1,)))
        for inner in range(0, group, 2):
            lanes = slice(inner * rows_y, (inner + 2) * rows_y)
            real = result[:half, lanes]
            imag = result[half:, lanes]
            even = jnp.where(left_half, real, pltpu.roll(imag, rows_y, 1))
            odd = jnp.where(left_half, pltpu.roll(real, rows_y, 1), imag)
            for x, value in ((first + inner, even), (first + inner + 1, odd)):
                start = 0
                for flat, count in zip(flats, counts):
                    for c in range(count):
                        for rank in range(ranks):
                            for side in range(sides):
                                at = ((side * ranks + rank) * count + c) * rows_x + x
                                stride = sides * ranks * count * rows_x
                                flat[pl.ds(at, wide, stride=stride), :] = value[start : start + wide]
                            start += wide


def third_pass(density, wide, sides, ranks, counts):
    rows_x, rows_y, length = density.shape
    half = length // 2
    per_c = sum(counts)
    order = np.arange(half).reshape(wide, ranks, per_c).transpose(2, 1, 0).reshape(-1)
    angle = angles(order, np.arange(length), length)
    table = split_table(np.concatenate([np.cos(angle), -np.sin(angle)]))
    step = min(8, rows_x)

    def body(*refs):
        third_kernel(counts, *refs)

    return pl.pallas_call(
        body,
        grid=(rows_x // step,),
        in_specs=[
            whole(table.shape),
            pl.BlockSpec((step, rows_y, length), lambda i: (i, 0, 0)),
        ],
        out_specs=[
            pl.BlockSpec(
                (wide, sides, ranks, count, step, 2 * rows_y), lambda i: (0, 0, 0, 0, i, 0)
            )
            for count in counts
        ],
        out_shape=[
            jax.ShapeDtypeStruct((wide, sides, ranks, count, rows_x, 2 * rows_y), jnp.float32)
            for count in counts
        ],
        compiler_params=params(1),
        cost_estimate=cost(density.size * length, 12 * density.size),
    )(table, density)


PAIR = 2


def turn(angle):
    cosine, sine = np.cos(angle), np.sin(angle)
    return np.block([[cosine, -sine], [sine, cosine]])


def spectrum_kernel(
    slab, groups, side_ref, wave_c_ref, a_ref, b_ref, second_ref, first_ref, back_ref, in_ref, *refs
):
    outs = refs[-groups:]
    wide, narrow, _, rows_x, lanes = in_ref.shape
    length = wide * rows_x
    half = length // 2
    quarter = half // 2
    devices, tiles, message, tile = outs[0].shape
    count = slab // groups
    flats = [ref.reshape(devices * tiles * message, tile) for ref in outs]
    side = side_ref[0]
    sign_back = 1.0 - 2.0 * side.astype(jnp.float32)
    wave_b = b_ref[0]
    for c in range(PAIR):

        def column(n):
            return in_ref[:, n, c].reshape(length, lanes)

        low = jnp.concatenate([column(n) for n in range(narrow // 2)], axis=1)
        high = jnp.concatenate([column(n) for n in range(narrow // 2, narrow)], axis=1)
        planes = [
            product(split(low + high), pair(second_ref.at[0])),
            product(split(low - high), pair(second_ref.at[1])),
        ]

        def stacked(sign):
            return jnp.concatenate(
                [
                    jnp.concatenate(
                        [
                            plane[:half, part * half : (part + 1) * half]
                            + sign * plane[half:, part * half : (part + 1) * half]
                            for plane in planes
                        ],
                        axis=1,
                    )
                    for part in range(2)
                ],
                axis=0,
            )

        wave_c = wave_c_ref[pl.program_id(0) * PAIR + c]
        field = []
        for parity, sign in ((0, 1.0), (1, -1.0)):
            value = product(pair(first_ref.at[parity]), split(stacked(sign)))
            wave_a = a_ref[0, parity]
            squared = wave_a * wave_a + (wave_b * wave_b + wave_c * wave_c)
            safe = jnp.where(squared > 0, squared, 1.0)
            usable = a_ref[1, parity] * b_ref[1] * (1.0 / float(length) ** 3)
            smooth = jnp.where(squared > 0, jnp.exp(-0.5 * squared) / safe, 0.0) * usable
            field.append(value * jnp.concatenate([smooth, smooth], axis=0))
        for number in range(3):
            folded = jnp.concatenate(
                [
                    field[parity][part * half : part * half + quarter]
                    + sign_back * field[parity][part * half + quarter : (part + 1) * half]
                    for part in range(2)
                    for parity in range(2)
                ],
                axis=0,
            )
            value = product(pair(back_ref.at[side]), split(folded))
            for x in range(slab):
                group, within = divmod(x, count)
                for spot in range(tiles // 3):
                    parity, part = divmod(spot, 2)
                    start = part * half + x * devices
                    at = (number * (tiles // 3) + spot) * message + c * count + within
                    flats[group][pl.ds(at, devices, stride=tiles * message), :] = value[
                        start : start + devices, parity * tile : (parity + 1) * tile
                    ]
            if number < 2:
                for parity in range(2):
                    wave_a = a_ref[0, parity]
                    field[parity] = field[parity] * jnp.concatenate([wave_a, wave_a], axis=0)


def halves(length):
    return np.arange(length).reshape(length // 2, 2).T


def spectrum_pass(received, side, waves_c, devices, groups, steps, first_step, filled):
    wide, narrow, per_c, rows_x, lanes = received.shape
    length = wide * rows_x
    rows_y = lanes // 2
    half = length // 2
    near = np.arange(half)
    split_index = halves(length)
    slab = half // devices
    second, first, back = [], [], []
    order = near.reshape(devices, slab).T.reshape(-1)
    for parity, index in enumerate(split_index):
        table = turn(-angles(index, near, length)).reshape(2, half, 2, narrow // 2, rows_y)
        second.append(table.transpose(3, 2, 4, 0, 1).reshape(length, length))
        first.append(turn(-angles(index, near, length)))
        back.append(turn(angles(2 * order + parity, split_index[:, : half // 2].reshape(-1), length)))
    tables = [np.stack([split_table(table) for table in each]) for each in (second, first, back)]
    wave = signed_wave(split_index, length)
    a_table = np.stack([wave, split_index != half]).astype(np.float32)[..., None]
    b_table = a_table.reshape(2, 1, length)
    message = PAIR * slab // groups
    out_shape = (devices, 3 * 2 * length // TILE, steps * message, TILE)
    block = out_shape[:2] + (message, TILE)

    def body(*refs):
        spectrum_kernel(slab, groups, *refs)

    return pl.pallas_call(
        body,
        grid=(per_c // PAIR,),
        in_specs=[
            pl.BlockSpec(memory_space=pltpu.SMEM),
            pl.BlockSpec(memory_space=pltpu.SMEM),
            whole(a_table.shape),
            whole(b_table.shape),
            *[whole(table.shape) for table in tables],
            pl.BlockSpec((wide, narrow, PAIR, rows_x, lanes), lambda i: (0, 0, i, 0, 0)),
            *[pl.BlockSpec(memory_space=pl.ANY)] * len(filled),
        ],
        out_specs=[pl.BlockSpec(block, lambda i: (0, 0, first_step + i, 0))] * groups,
        out_shape=[jax.ShapeDtypeStruct(out_shape, jnp.float32)] * groups,
        input_output_aliases={8 + spot: spot for spot in range(len(filled))},
        compiler_params=params(1),
        cost_estimate=cost(per_c * 7 * length**3, 20 * per_c * length**2 * 2),
    )(side, waves_c, a_table, b_table, *tables, received, *filled)


def shear_kernel(
    per_c, row_ref, lane_ref, second_ref, third_ref, ahead_ref, last_ref, in_ref, out_ref, shear_ref
):
    step = pl.program_id(0)
    length = shear_ref.shape[0]
    half = length // 2
    devices, tiles, message, tile = in_ref.shape
    count = message // per_c
    flat = in_ref.reshape(devices * tiles * message, tile)

    @pl.when(step == 0)
    def _():
        shear_ref[...] = jnp.zeros_like(shear_ref)

    field = jnp.concatenate(
        [
            jnp.concatenate(
                [
                    flat[pl.ds((source * tiles + spot) * message + x, per_c, stride=count), :]
                    for x in range(count)
                    for source in range(devices)
                ],
                axis=0,
            )
            for spot in range(tiles)
        ],
        axis=1,
    )
    field = field * row_ref[0] * lane_ref[0]
    even = product(split(field[:, :length]), pair(second_ref.at[0]))
    odd = product(split(field[:, length:]), pair(second_ref.at[1]))
    near, far = even + odd, even - odd
    field = jnp.concatenate(
        [
            jnp.concatenate(
                [
                    value[x * half : (x + 1) * half, part * half : (part + 1) * half]
                    for x in range(count)
                    for value in (near, far)
                ],
                axis=1,
            )
            for part in range(2)
        ],
        axis=0,
    )
    field = product(pair(third_ref), split(field))
    shear_ref[...] += field * field

    @pl.when(step == 5)
    def _():
        wide, narrow, _, rows_b, lanes = out_ref.shape
        for x in range(count):
            shear = shear_ref[:, x * length : (x + 1) * length]
            ahead = product(pair(ahead_ref), split(shear), ((1,), (1,)))
            value = jnp.concatenate([ahead[:length], ahead[length:]], axis=1)
            value = product(split(value), pair(last_ref))
            for w in range(wide):
                for n in range(narrow):
                    out_ref[w, n, x] = value[
                        w * rows_b : (w + 1) * rows_b, n * lanes : (n + 1) * lanes
                    ]


def shear_pass(received, wide, narrow, per_c):
    devices, tiles, message, tile = received.shape
    count = message // per_c
    length = tiles * tile // 6
    half = length // 2
    index = np.arange(length)
    angle = angles(index, index, length)
    cosine, sine = np.cos(angle), np.sin(angle)
    split_index = halves(length)
    second = np.stack(
        [split_table(turn(angles(np.arange(half), b, length)).T) for b in split_index]
    )
    row_c = np.arange(half)
    weight = np.where(row_c == 0, 1.0, 2.0)
    angle = angles(index, row_c, length)
    third = np.concatenate([weight * np.cos(angle), -weight * np.sin(angle)], axis=1)
    ahead = np.concatenate([cosine, -sine])
    cos_z = cosine.reshape(length, narrow, 1, length // narrow)
    sin_z = sine.reshape(length, narrow, 1, length // narrow)
    last = np.concatenate(
        [
            np.concatenate([cos_z, -sin_z], axis=2).reshape(length, 2 * length),
            np.concatenate([sin_z, cos_z], axis=2).reshape(length, 2 * length),
        ]
    )
    wave = signed_wave(index, length)
    wave_rows = np.tile(wave[row_c], count)
    wave_lanes = np.stack([wave[split_index]] * 2, axis=1).reshape(-1)
    twice = math.sqrt(2.0)
    one_row, one_lane = np.ones_like(wave_rows), np.ones_like(wave_lanes)
    row_factor = np.stack(
        [one_row, twice * one_row, twice * wave_rows, one_row, twice * wave_rows, wave_rows**2]
    ).astype(np.float32)[:, :, None]
    lane_factor = np.stack(
        [one_lane, wave_lanes, one_lane, wave_lanes**2, wave_lanes, one_lane]
    ).astype(np.float32)[:, None, :]
    tables = [second] + [split_table(table) for table in (third, ahead, last)]
    out_shape = (wide, narrow, count, length // wide, 2 * length // narrow)

    def body(*refs):
        shear_kernel(per_c, *refs)

    def which(i):
        return (0, 2 - (i >= 1).astype(jnp.int32) - (i >= 3).astype(jnp.int32), 0, 0)

    return pl.pallas_call(
        body,
        grid=(6,),
        in_specs=[
            pl.BlockSpec((1, count * half, 1), lambda i: (i, 0, 0)),
            pl.BlockSpec((1, 1, 2 * length), lambda i: (i, 0, 0)),
            *[whole(table.shape) for table in tables],
            pl.BlockSpec((devices, tiles // 3, message, tile), which),
        ],
        out_specs=whole(out_shape),
        out_shape=jax.ShapeDtypeStruct(out_shape, jnp.float32),
        scratch_shapes=[pltpu.VMEM((length, count * length), jnp.float32)],
        compiler_params=params(1),
        cost_estimate=cost(count * 18 * length**3, 4 * received.size + 4 * 2**20),
    )(row_factor, lane_factor, *tables, received)


def first_kernel(scale, wide, sides, anchor_ref, table_ref, *refs):
    ins, (real_ref, imag_ref, real_tile_ref, imag_tile_ref) = refs[:-4], refs[-4:]
    devices, count, rows_b, lanes = ins[0].shape
    half_c, length = lanes // 2, real_ref.shape[2]
    half = length // 2
    tables = [pair(table_ref.at[0]), pair(table_ref.at[1])]
    flats = [ref.reshape(devices * count * rows_b, lanes) for ref in ins]
    tile = real_tile_ref.shape[2]
    spot_c = lax.broadcasted_iota(jnp.int32, (half_c, half), 0)
    spot_a = lax.broadcasted_iota(jnp.int32, (half_c, half), 1)
    is_anchor = (anchor_ref[0] == 1) & (pl.program_id(0) == 0)
    anchor = (spot_c == 0) & (spot_a == 0) & is_anchor
    group = min(8, rows_b)
    run = devices // wide // sides * count
    for first in range(0, rows_b, group):
        sums = []
        for parity in range(2):
            columns = []
            for b in range(first, first + group):
                column = jnp.concatenate(
                    [
                        flat[pl.ds((w * sides + parity) * run * rows_b + b, run, stride=rows_b), :]
                        for flat in flats
                        for w in range(wide)
                    ],
                    axis=0,
                ).T
                columns.append(jnp.concatenate([column[:half_c], column[half_c:]], axis=1))
            sums.append(product(split(jnp.concatenate(columns, axis=0)), tables[parity]))
        even, odd = sums
        for side, value in enumerate((even + odd, even - odd)):
            value = value * scale
            for number in range(group):
                b = first + number
                rows = slice(number * half_c, (number + 1) * half_c)
                real, imag = value[rows, :half], value[rows, half:]
                if b == 0 and side == 0:
                    real = jnp.where(anchor, 0.0, real)
                    imag = jnp.where(anchor, 0.0, imag)
                for spot in range(half // tile):
                    part = slice(spot * tile, (spot + 1) * tile)
                    at = side * (half // tile) + spot
                    real_tile_ref[at, pl.ds(b, half_c, stride=rows_b), :] = real[:, part]
                    imag_tile_ref[at, pl.ds(b, half_c, stride=rows_b), :] = imag[:, part]
    for spot in range(length // tile):
        part = slice(spot * tile, (spot + 1) * tile)
        real_ref[:, :, part] = real_tile_ref[spot].reshape(half_c, rows_b, tile)
        imag_ref[:, :, part] = imag_tile_ref[spot].reshape(half_c, rows_b, tile)


def first_pass(parts, is_anchor, length, wide, sides):
    devices, count, rows_b, lanes = parts[0].shape
    groups = len(parts)
    ranks = devices // wide // sides
    index = np.arange(length).reshape(wide, ranks, groups, count, sides)
    index = index.transpose(4, 2, 0, 1, 3).reshape(2, -1)
    table = np.stack(
        [split_table(turn(-angles(np.arange(length // 2), x, length)).T) for x in index]
    )
    step = min(8, rows_b)
    scale = 1.0 / float(length) ** 1.5

    def body(*refs):
        first_kernel(scale, wide, sides, *refs)

    out_shape = jax.ShapeDtypeStruct((lanes // 2, rows_b, length), jnp.float32)
    return pl.pallas_call(
        body,
        grid=(rows_b // step,),
        in_specs=[
            pl.BlockSpec(memory_space=pltpu.SMEM),
            whole(table.shape),
            *[pl.BlockSpec((devices, count, step, lanes), lambda i: (0, 0, i, 0))] * groups,
        ],
        out_specs=[pl.BlockSpec((lanes // 2, step, length), lambda i: (0, i, 0))] * 2,
        out_shape=[out_shape] * 2,
        scratch_shapes=[pltpu.VMEM((length // TILE, lanes // 2 * step, TILE), jnp.float32)] * 2,
        compiler_params=params(1),
        cost_estimate=cost(rows_b * lanes * length * length, 8 * rows_b * lanes * length),
    )(is_anchor, table, *parts)


def transpose(value, members=None):
    return lax.all_to_all(
        value, AXES, split_axis=0, concat_axis=0, tiled=True, axis_index_groups=members
    )


def solution(mesh):
    wide, narrow = mesh.shape["wide"], mesh.shape["narrow"]
    sides = 2
    ranks = narrow // sides
    devices = wide * ranks
    members = [
        [w * narrow + side * ranks + rank for w in range(wide) for rank in range(ranks)]
        for side in range(sides)
    ]

    def per_device(density):
        rows_x, rows_y, length = density.shape
        half = length // 2
        per_c = half // devices
        slab = half // devices
        steps = per_c // PAIR
        counts = [per_c - PAIR, PAIR] if steps > 1 else [per_c]
        groups = 2 if slab > 2 else 1
        spot_wide, spot_narrow = lax.axis_index("wide"), lax.axis_index("narrow")
        side = (spot_narrow // ranks).astype(jnp.int32).reshape(1)
        rank = spot_wide * ranks + spot_narrow % ranks
        waves_c = (rank * per_c + jnp.arange(per_c, dtype=jnp.int32)).astype(jnp.float32)
        waves_c = waves_c * (2.0 * math.pi / length)
        chunks, start = [], 0
        for planes, count in zip(third_pass(density, wide, sides, ranks, counts), counts):
            planes = transpose(planes.reshape(wide * narrow, count, rows_x, 2 * rows_y))
            planes = planes.reshape(wide, narrow, count, rows_x, 2 * rows_y)
            chunks = spectrum_pass(
                planes, side, waves_c[start : start + count], devices, groups, steps, start // PAIR, chunks
            )
            start += count
        is_anchor = ((spot_wide == 0) & (spot_narrow == 0)).astype(jnp.int32).reshape(1)
        parts = []
        for chunk in chunks:
            part = shear_pass(transpose(chunk, members), wide, narrow, per_c)
            parts.append(transpose(part.reshape((wide * narrow,) + part.shape[2:])))
        return tuple(first_pass(parts, is_anchor, length, wide, sides))

    return jax.shard_map(
        per_device,
        mesh=mesh,
        in_specs=(P("wide", "narrow", None),),
        out_specs=(P("narrow", "wide", None), P("narrow", "wide", None)),
        check_vma=False,
    )
```

```python
import math

import jax
import jax.numpy as jnp
import ml_dtypes
import numpy as np
from jax import lax
from jax.experimental import pallas as pl
from jax.experimental.pallas import tpu as pltpu
from jax.sharding import PartitionSpec as P

AXES = ("wide", "narrow")
TILE = 128
LIMIT = 16 * 1024 * 1024


def angles(rows, columns, length):
    return (2.0 * math.pi / length) * (np.outer(rows, columns) % length)


def split_table(table):
    table = np.asarray(table, np.float64)
    high = table.astype(ml_dtypes.bfloat16)
    low = (table - high.astype(np.float64)).astype(ml_dtypes.bfloat16)
    return np.stack([high, low])


def split(value):
    high = value.astype(jnp.bfloat16)
    low = (value - high.astype(jnp.float32)).astype(jnp.bfloat16)
    return high, low


def product(left, right, contract=((1,), (0,))):
    (left_axis,), (right_axis,) = contract
    left = jnp.concatenate([left[0], left[0], left[1]], axis=left_axis)
    right = jnp.concatenate([right[0], right[1], right[0]], axis=right_axis)
    return lax.dot_general(
        left, right, (contract, ((), ())), preferred_element_type=jnp.float32
    )


def pair(ref):
    return ref[0], ref[1]


def signed_wave(index, length):
    index = np.asarray(index)
    return np.where(index < length // 2, index, index - length) * (2.0 * math.pi / length)


def params(steps):
    return pltpu.CompilerParams(
        vmem_limit_bytes=LIMIT, dimension_semantics=("arbitrary",) * steps
    )


def whole(shape):
    return pl.BlockSpec(shape, lambda *_: (0,) * len(shape))


def cost(macs, moved):
    return pl.CostEstimate(flops=6 * macs, bytes_accessed=moved, transcendentals=0)


def third_kernel(counts, table_ref, density_ref, *outs):
    rows_x, rows_y, length = density_ref.shape
    wide, sides, ranks = outs[0].shape[:3]
    half = length // 2
    flats = [ref.reshape(math.prod(ref.shape[:5]), 2 * rows_y) for ref in outs]
    table = pair(table_ref)
    left_half = lax.broadcasted_iota(jnp.int32, (half, 2 * rows_y), 1) < rows_y
    group = 4
    for first in range(0, rows_x, group):
        block = density_ref[first : first + group].reshape(group * rows_y, length)
        result = product(table, split(block), ((1,), (1,)))
        for inner in range(0, group, 2):
            lanes = slice(inner * rows_y, (inner + 2) * rows_y)
            real = result[:half, lanes]
            imag = result[half:, lanes]
            even = jnp.where(left_half, real, pltpu.roll(imag, rows_y, 1))
            odd = jnp.where(left_half, pltpu.roll(real, rows_y, 1), imag)
            for x, value in ((first + inner, even), (first + inner + 1, odd)):
                start = 0
                for flat, count in zip(flats, counts):
                    for c in range(count):
                        for rank in range(ranks):
                            for side in range(sides):
                                at = ((side * ranks + rank) * count + c) * rows_x + x
                                stride = sides * ranks * count * rows_x
                                flat[pl.ds(at, wide, stride=stride), :] = value[start : start + wide]
                            start += wide


def third_pass(density, wide, sides, ranks, counts):
    rows_x, rows_y, length = density.shape
    half = length // 2
    per_c = sum(counts)
    order = np.arange(half).reshape(wide, ranks, per_c).transpose(2, 1, 0).reshape(-1)
    angle = angles(order, np.arange(length), length)
    table = split_table(np.concatenate([np.cos(angle), -np.sin(angle)]))
    step = min(8, rows_x)

    def body(*refs):
        third_kernel(counts, *refs)

    return pl.pallas_call(
        body,
        grid=(rows_x // step,),
        in_specs=[
            whole(table.shape),
            pl.BlockSpec((step, rows_y, length), lambda i: (i, 0, 0)),
        ],
        out_specs=[
            pl.BlockSpec(
                (wide, sides, ranks, count, step, 2 * rows_y), lambda i: (0, 0, 0, 0, i, 0)
            )
            for count in counts
        ],
        out_shape=[
            jax.ShapeDtypeStruct((wide, sides, ranks, count, rows_x, 2 * rows_y), jnp.float32)
            for count in counts
        ],
        compiler_params=params(1),
        cost_estimate=cost(density.size * length, 12 * density.size),
    )(table, density)


PAIR = 2


def turn(angle):
    cosine, sine = np.cos(angle), np.sin(angle)
    return np.block([[cosine, -sine], [sine, cosine]])


def spectrum_kernel(
    slab, groups, side_ref, wave_c_ref, a_ref, b_ref, second_ref, first_ref, back_ref, in_ref, *refs
):
    outs = refs[-groups:]
    wide, narrow, _, rows_x, lanes = in_ref.shape
    length = wide * rows_x
    half = length // 2
    quarter = half // 2
    devices, tiles, message, tile = outs[0].shape
    count = slab // groups
    flats = [ref.reshape(devices * tiles * message, tile) for ref in outs]
    side = side_ref[0]
    sign_back = 1.0 - 2.0 * side.astype(jnp.float32)
    wave_b = b_ref[0]
    for c in range(PAIR):

        def column(n):
            return in_ref[:, n, c].reshape(length, lanes)

        low = jnp.concatenate([column(n) for n in range(narrow // 2)], axis=1)
        high = jnp.concatenate([column(n) for n in range(narrow // 2, narrow)], axis=1)
        planes = [
            product(split(low + high), pair(second_ref.at[0])),
            product(split(low - high), pair(second_ref.at[1])),
        ]

        def stacked(sign):
            return jnp.concatenate(
                [
                    jnp.concatenate(
                        [
                            plane[:half, part * half : (part + 1) * half]
                            + sign * plane[half:, part * half : (part + 1) * half]
                            for plane in planes
                        ],
                        axis=1,
                    )
                    for part in range(2)
                ],
                axis=0,
            )

        wave_c = wave_c_ref[pl.program_id(0) * PAIR + c]
        field = []
        for parity, sign in ((0, 1.0), (1, -1.0)):
            value = product(pair(first_ref.at[parity]), split(stacked(sign)))
            wave_a = a_ref[0, parity]
            squared = wave_a * wave_a + (wave_b * wave_b + wave_c * wave_c)
            safe = jnp.where(squared > 0, squared, 1.0)
            usable = a_ref[1, parity] * b_ref[1] * (1.0 / float(length) ** 3)
            smooth = jnp.where(squared > 0, jnp.exp(-0.5 * squared) / safe, 0.0) * usable
            field.append(value * jnp.concatenate([smooth, smooth], axis=0))
        for number in range(3):
            folded = jnp.concatenate(
                [
                    field[parity][part * half : part * half + quarter]
                    + sign_back * field[parity][part * half + quarter : (part + 1) * half]
                    for part in range(2)
                    for parity in range(2)
                ],
                axis=0,
            )
            value = product(pair(back_ref.at[side]), split(folded))
            for x in range(slab):
                group, within = divmod(x, count)
                for spot in range(tiles // 3):
                    parity, part = divmod(spot, 2)
                    start = part * half + x * devices
                    at = (number * (tiles // 3) + spot) * message + c * count + within
                    flats[group][pl.ds(at, devices, stride=tiles * message), :] = value[
                        start : start + devices, parity * tile : (parity + 1) * tile
                    ]
            if number < 2:
                for parity in range(2):
                    wave_a = a_ref[0, parity]
                    field[parity] = field[parity] * jnp.concatenate([wave_a, wave_a], axis=0)


def halves(length):
    return np.arange(length).reshape(length // 2, 2).T


def spectrum_pass(received, side, waves_c, devices, groups, steps, first_step, filled):
    wide, narrow, per_c, rows_x, lanes = received.shape
    length = wide * rows_x
    rows_y = lanes // 2
    half = length // 2
    near = np.arange(half)
    split_index = halves(length)
    slab = half // devices
    second, first, back = [], [], []
    order = near.reshape(devices, slab).T.reshape(-1)
    for parity, index in enumerate(split_index):
        table = turn(-angles(index, near, length)).reshape(2, half, 2, narrow // 2, rows_y)
        second.append(table.transpose(3, 2, 4, 0, 1).reshape(length, length))
        first.append(turn(-angles(index, near, length)))
        back.append(turn(angles(2 * order + parity, split_index[:, : half // 2].reshape(-1), length)))
    tables = [np.stack([split_table(table) for table in each]) for each in (second, first, back)]
    wave = signed_wave(split_index, length)
    a_table = np.stack([wave, split_index != half]).astype(np.float32)[..., None]
    b_table = a_table.reshape(2, 1, length)
    message = PAIR * slab // groups
    out_shape = (devices, 3 * 2 * length // TILE, steps * message, TILE)
    block = out_shape[:2] + (message, TILE)

    def body(*refs):
        spectrum_kernel(slab, groups, *refs)

    return pl.pallas_call(
        body,
        grid=(per_c // PAIR,),
        in_specs=[
            pl.BlockSpec(memory_space=pltpu.SMEM),
            pl.BlockSpec(memory_space=pltpu.SMEM),
            whole(a_table.shape),
            whole(b_table.shape),
            *[whole(table.shape) for table in tables],
            pl.BlockSpec((wide, narrow, PAIR, rows_x, lanes), lambda i: (0, 0, i, 0, 0)),
            *[pl.BlockSpec(memory_space=pl.ANY)] * len(filled),
        ],
        out_specs=[pl.BlockSpec(block, lambda i: (0, 0, first_step + i, 0))] * groups,
        out_shape=[jax.ShapeDtypeStruct(out_shape, jnp.float32)] * groups,
        input_output_aliases={8 + spot: spot for spot in range(len(filled))},
        compiler_params=params(1),
        cost_estimate=cost(per_c * 7 * length**3, 20 * per_c * length**2 * 2),
    )(side, waves_c, a_table, b_table, *tables, received, *filled)


def shear_kernel(
    per_c, row_ref, lane_ref, second_ref, third_ref, ahead_ref, last_ref, in_ref, out_ref, shear_ref
):
    step = pl.program_id(0)
    length = shear_ref.shape[0]
    half = length // 2
    devices, tiles, message, tile = in_ref.shape
    count = message // per_c
    flat = in_ref.reshape(devices * tiles * message, tile)

    @pl.when(step == 0)
    def _():
        shear_ref[...] = jnp.zeros_like(shear_ref)

    field = jnp.concatenate(
        [
            jnp.concatenate(
                [
                    flat[pl.ds((source * tiles + spot) * message + x, per_c, stride=count), :]
                    for x in range(count)
                    for source in range(devices)
                ],
                axis=0,
            )
            for spot in range(tiles)
        ],
        axis=1,
    )
    field = field * row_ref[0] * lane_ref[0]
    even = product(split(field[:, :length]), pair(second_ref.at[0]))
    odd = product(split(field[:, length:]), pair(second_ref.at[1]))
    near, far = even + odd, even - odd
    field = jnp.concatenate(
        [
            jnp.concatenate(
                [
                    value[x * half : (x + 1) * half, part * half : (part + 1) * half]
                    for x in range(count)
                    for value in (near, far)
                ],
                axis=1,
            )
            for part in range(2)
        ],
        axis=0,
    )
    field = product(pair(third_ref), split(field))
    shear_ref[...] += field * field

    @pl.when(step == 5)
    def _():
        wide, narrow, _, rows_b, lanes = out_ref.shape
        for x in range(count):
            shear = shear_ref[:, x * length : (x + 1) * length]
            ahead = product(pair(ahead_ref), split(shear), ((1,), (1,)))
            value = jnp.concatenate([ahead[:length], ahead[length:]], axis=1)
            value = product(split(value), pair(last_ref))
            for w in range(wide):
                for n in range(narrow):
                    out_ref[w, n, x] = value[
                        w * rows_b : (w + 1) * rows_b, n * lanes : (n + 1) * lanes
                    ]


def shear_pass(received, wide, narrow, per_c):
    devices, tiles, message, tile = received.shape
    count = message // per_c
    length = tiles * tile // 6
    half = length // 2
    index = np.arange(length)
    angle = angles(index, index, length)
    cosine, sine = np.cos(angle), np.sin(angle)
    split_index = halves(length)
    second = np.stack(
        [split_table(turn(angles(np.arange(half), b, length)).T) for b in split_index]
    )
    row_c = np.arange(half)
    weight = np.where(row_c == 0, 1.0, 2.0)
    angle = angles(index, row_c, length)
    third = np.concatenate([weight * np.cos(angle), -weight * np.sin(angle)], axis=1)
    ahead = np.concatenate([cosine, -sine])
    cos_z = cosine.reshape(length, narrow, 1, length // narrow)
    sin_z = sine.reshape(length, narrow, 1, length // narrow)
    last = np.concatenate(
        [
            np.concatenate([cos_z, -sin_z], axis=2).reshape(length, 2 * length),
            np.concatenate([sin_z, cos_z], axis=2).reshape(length, 2 * length),
        ]
    )
    wave = signed_wave(index, length)
    wave_rows = np.tile(wave[row_c], count)
    wave_lanes = np.stack([wave[split_index]] * 2, axis=1).reshape(-1)
    twice = math.sqrt(2.0)
    one_row, one_lane = np.ones_like(wave_rows), np.ones_like(wave_lanes)
    row_factor = np.stack(
        [one_row, twice * one_row, twice * wave_rows, one_row, twice * wave_rows, wave_rows**2]
    ).astype(np.float32)[:, :, None]
    lane_factor = np.stack(
        [one_lane, wave_lanes, one_lane, wave_lanes**2, wave_lanes, one_lane]
    ).astype(np.float32)[:, None, :]
    tables = [second] + [split_table(table) for table in (third, ahead, last)]
    out_shape = (wide, narrow, count, length // wide, 2 * length // narrow)

    def body(*refs):
        shear_kernel(per_c, *refs)

    def which(i):
        return (0, 2 - (i >= 1).astype(jnp.int32) - (i >= 3).astype(jnp.int32), 0, 0)

    return pl.pallas_call(
        body,
        grid=(6,),
        in_specs=[
            pl.BlockSpec((1, count * half, 1), lambda i: (i, 0, 0)),
            pl.BlockSpec((1, 1, 2 * length), lambda i: (i, 0, 0)),
            *[whole(table.shape) for table in tables],
            pl.BlockSpec((devices, tiles // 3, message, tile), which),
        ],
        out_specs=whole(out_shape),
        out_shape=jax.ShapeDtypeStruct(out_shape, jnp.float32),
        scratch_shapes=[pltpu.VMEM((length, count * length), jnp.float32)],
        compiler_params=params(1),
        cost_estimate=cost(count * 18 * length**3, 4 * received.size + 4 * 2**20),
    )(row_factor, lane_factor, *tables, received)


def first_kernel(scale, wide, sides, anchor_ref, table_ref, *refs):
    ins, (real_ref, imag_ref, real_tile_ref, imag_tile_ref) = refs[:-4], refs[-4:]
    devices, count, rows_b, lanes = ins[0].shape
    half_c, length = lanes // 2, real_ref.shape[2]
    half = length // 2
    tables = [pair(table_ref.at[0]), pair(table_ref.at[1])]
    flats = [ref.reshape(devices * count * rows_b, lanes) for ref in ins]
    tile = real_tile_ref.shape[2]
    spot_c = lax.broadcasted_iota(jnp.int32, (half_c, half), 0)
    spot_a = lax.broadcasted_iota(jnp.int32, (half_c, half), 1)
    is_anchor = (anchor_ref[0] == 1) & (pl.program_id(0) == 0)
    anchor = (spot_c == 0) & (spot_a == 0) & is_anchor
    group = min(8, rows_b)
    run = devices // wide // sides * count
    for first in range(0, rows_b, group):
        sums = []
        for parity in range(2):
            columns = []
            for b in range(first, first + group):
                column = jnp.concatenate(
                    [
                        flat[pl.ds((w * sides + parity) * run * rows_b + b, run, stride=rows_b), :]
                        for flat in flats
                        for w in range(wide)
                    ],
                    axis=0,
                ).T
                columns.append(jnp.concatenate([column[:half_c], column[half_c:]], axis=1))
            sums.append(product(split(jnp.concatenate(columns, axis=0)), tables[parity]))
        even, odd = sums
        for side, value in enumerate((even + odd, even - odd)):
            value = value * scale
            for number in range(group):
                b = first + number
                rows = slice(number * half_c, (number + 1) * half_c)
                real, imag = value[rows, :half], value[rows, half:]
                if b == 0 and side == 0:
                    real = jnp.where(anchor, 0.0, real)
                    imag = jnp.where(anchor, 0.0, imag)
                for spot in range(half // tile):
                    part = slice(spot * tile, (spot + 1) * tile)
                    at = side * (half // tile) + spot
                    real_tile_ref[at, pl.ds(b, half_c, stride=rows_b), :] = real[:, part]
                    imag_tile_ref[at, pl.ds(b, half_c, stride=rows_b), :] = imag[:, part]
    for spot in range(length // tile):
        part = slice(spot * tile, (spot + 1) * tile)
        real_ref[:, :, part] = real_tile_ref[spot].reshape(half_c, rows_b, tile)
        imag_ref[:, :, part] = imag_tile_ref[spot].reshape(half_c, rows_b, tile)


def first_pass(parts, is_anchor, length, wide, sides):
    devices, count, rows_b, lanes = parts[0].shape
    groups = len(parts)
    ranks = devices // wide // sides
    index = np.arange(length).reshape(wide, ranks, groups, count, sides)
    index = index.transpose(4, 2, 0, 1, 3).reshape(2, -1)
    table = np.stack(
        [split_table(turn(-angles(np.arange(length // 2), x, length)).T) for x in index]
    )
    step = min(8, rows_b)
    scale = 1.0 / float(length) ** 1.5

    def body(*refs):
        first_kernel(scale, wide, sides, *refs)

    out_shape = jax.ShapeDtypeStruct((lanes // 2, rows_b, length), jnp.float32)
    return pl.pallas_call(
        body,
        grid=(rows_b // step,),
        in_specs=[
            pl.BlockSpec(memory_space=pltpu.SMEM),
            whole(table.shape),
            *[pl.BlockSpec((devices, count, step, lanes), lambda i: (0, 0, i, 0))] * groups,
        ],
        out_specs=[pl.BlockSpec((lanes // 2, step, length), lambda i: (0, i, 0))] * 2,
        out_shape=[out_shape] * 2,
        scratch_shapes=[pltpu.VMEM((length // TILE, lanes // 2 * step, TILE), jnp.float32)] * 2,
        compiler_params=params(1),
        cost_estimate=cost(rows_b * lanes * length * length, 8 * rows_b * lanes * length),
    )(is_anchor, table, *parts)


def transpose(value, members=None):
    return lax.all_to_all(
        value, AXES, split_axis=0, concat_axis=0, tiled=True, axis_index_groups=members
    )


def solution(mesh):
    wide, narrow = mesh.shape["wide"], mesh.shape["narrow"]
    sides = 2
    ranks = narrow // sides
    devices = wide * ranks
    members = [
        [w * narrow + side * ranks + rank for w in range(wide) for rank in range(ranks)]
        for side in range(sides)
    ]

    def per_device(density):
        rows_x, rows_y, length = density.shape
        half = length // 2
        per_c = half // devices
        slab = half // devices
        steps = per_c // PAIR
        counts = [per_c - PAIR, PAIR] if steps > 1 else [per_c]
        groups = 2 if slab > 2 else 1
        spot_wide, spot_narrow = lax.axis_index("wide"), lax.axis_index("narrow")
        side = (spot_narrow // ranks).astype(jnp.int32).reshape(1)
        rank = spot_wide * ranks + spot_narrow % ranks
        waves_c = (rank * per_c + jnp.arange(per_c, dtype=jnp.int32)).astype(jnp.float32)
        waves_c = waves_c * (2.0 * math.pi / length)
        chunks, start = [], 0
        for planes, count in zip(third_pass(density, wide, sides, ranks, counts), counts):
            planes = transpose(planes.reshape(wide * narrow, count, rows_x, 2 * rows_y))
            planes = planes.reshape(wide, narrow, count, rows_x, 2 * rows_y)
            chunks = spectrum_pass(
                planes, side, waves_c[start : start + count], devices, groups, steps, start // PAIR, chunks
            )
            start += count
        is_anchor = ((spot_wide == 0) & (spot_narrow == 0)).astype(jnp.int32).reshape(1)
        parts = []
        for chunk in chunks:
            part = shear_pass(transpose(chunk, members), wide, narrow, per_c)
            parts.append(transpose(part.reshape((wide * narrow,) + part.shape[2:])))
        return tuple(first_pass(parts, is_anchor, length, wide, sides))

    return jax.shard_map(
        per_device,
        mesh=mesh,
        in_specs=(P("wide", "narrow", None),),
        out_specs=(P("narrow", "wide", None), P("narrow", "wide", None)),
        check_vma=False,
    )
```

```python
import math

import jax
import jax.numpy as jnp
import ml_dtypes
import numpy as np
from jax import lax
from jax.experimental import pallas as pl
from jax.experimental.pallas import tpu as pltpu
from jax.sharding import PartitionSpec as P

AXES = ("wide", "narrow")
TILE = 128
LIMIT = 16 * 1024 * 1024


def angles(rows, columns, length):
    return (2.0 * math.pi / length) * (np.outer(rows, columns) % length)


def split_table(table):
    table = np.asarray(table, np.float64)
    high = table.astype(ml_dtypes.bfloat16)
    low = (table - high.astype(np.float64)).astype(ml_dtypes.bfloat16)
    return np.stack([high, low])


def split(value):
    high = value.astype(jnp.bfloat16)
    low = (value - high.astype(jnp.float32)).astype(jnp.bfloat16)
    return high, low


def product(left, right, contract=((1,), (0,))):
    (left_axis,), (right_axis,) = contract
    left = jnp.concatenate([left[0], left[0], left[1]], axis=left_axis)
    right = jnp.concatenate([right[0], right[1], right[0]], axis=right_axis)
    return lax.dot_general(
        left, right, (contract, ((), ())), preferred_element_type=jnp.float32
    )


def pair(ref):
    return ref[0], ref[1]


def signed_wave(index, length):
    index = np.asarray(index)
    return np.where(index < length // 2, index, index - length) * (2.0 * math.pi / length)


def params(steps):
    return pltpu.CompilerParams(
        vmem_limit_bytes=LIMIT, dimension_semantics=("arbitrary",) * steps
    )


def whole(shape):
    return pl.BlockSpec(shape, lambda *_: (0,) * len(shape))


def in_hbm(value):
    return pltpu.with_memory_space_constraint(jnp.asarray(value), pltpu.HBM)


def cost(macs, moved):
    return pl.CostEstimate(flops=6 * macs, bytes_accessed=moved, transcendentals=0)


def third_kernel(counts, table_ref, density_ref, *outs):
    rows_x, rows_y, length = density_ref.shape
    wide, sides, ranks = outs[0].shape[:3]
    half = length // 2
    flats = [ref.reshape(math.prod(ref.shape[:5]), 2 * rows_y) for ref in outs]
    table = pair(table_ref)
    left_half = lax.broadcasted_iota(jnp.int32, (half, 2 * rows_y), 1) < rows_y
    group = 4
    for first in range(0, rows_x, group):
        block = density_ref[first : first + group].reshape(group * rows_y, length)
        result = product(table, split(block), ((1,), (1,)))
        for inner in range(0, group, 2):
            lanes = slice(inner * rows_y, (inner + 2) * rows_y)
            real = result[:half, lanes]
            imag = result[half:, lanes]
            even = jnp.where(left_half, real, pltpu.roll(imag, rows_y, 1))
            odd = jnp.where(left_half, pltpu.roll(real, rows_y, 1), imag)
            for x, value in ((first + inner, even), (first + inner + 1, odd)):
                start = 0
                for flat, count in zip(flats, counts):
                    for c in range(count):
                        for rank in range(ranks):
                            at = (rank * count + c) * rows_x + x
                            stride = sides * ranks * count * rows_x
                            flat[pl.ds(at, wide, stride=stride), :] = value[start : start + wide]
                            start += wide
    for ref in outs:
        for side in range(1, sides):
            ref[:, side] = ref[:, 0]


def third_pass(density, wide, sides, ranks, counts):
    rows_x, rows_y, length = density.shape
    half = length // 2
    per_c = sum(counts)
    order = np.arange(half).reshape(wide, ranks, per_c).transpose(2, 1, 0).reshape(-1)
    angle = angles(order, np.arange(length), length)
    table = split_table(np.concatenate([np.cos(angle), -np.sin(angle)]))
    step = min(8, rows_x)

    def body(*refs):
        third_kernel(counts, *refs)

    return pl.pallas_call(
        body,
        grid=(rows_x // step,),
        in_specs=[
            whole(table.shape),
            pl.BlockSpec((step, rows_y, length), lambda i: (i, 0, 0)),
        ],
        out_specs=[
            pl.BlockSpec(
                (wide, sides, ranks, count, step, 2 * rows_y), lambda i: (0, 0, 0, 0, i, 0)
            )
            for count in counts
        ],
        out_shape=[
            jax.ShapeDtypeStruct((wide, sides, ranks, count, rows_x, 2 * rows_y), jnp.float32)
            for count in counts
        ],
        compiler_params=params(1),
        cost_estimate=cost(density.size * length, 12 * density.size),
    )(in_hbm(table), in_hbm(density))


PAIR = 2


def turn(angle):
    cosine, sine = np.cos(angle), np.sin(angle)
    return np.block([[cosine, -sine], [sine, cosine]])


def spectrum_kernel(slab, groups, side_ref, wave_c_ref, a_ref, b_ref, second_ref, first_ref, back_ref, in_ref, *refs):
    outs = refs[-groups:]
    wide, narrow, _, rows_x, lanes = in_ref.shape
    length = wide * rows_x
    half = length // 2
    quarter = half // 2
    devices, tiles, message, tile = outs[0].shape
    count = slab // groups
    sign_back = 1.0 - 2.0 * side_ref[0].astype(jnp.float32)

    def column(c, n):
        return in_ref[:, n, c].reshape(length, lanes)

    def columns(numbers):
        return jnp.concatenate(
            [
                jnp.concatenate([column(c, n) for n in numbers], axis=1)
                for c in range(PAIR)
            ],
            axis=0,
        )

    low, high = columns(range(narrow // 2)), columns(range(narrow // 2, narrow))
    planes = [
        product(split(low + high), pair(second_ref.at[0])),
        product(split(low - high), pair(second_ref.at[1])),
    ]

    def stacked(sign):
        return jnp.concatenate(
            [
                jnp.concatenate(
                    [
                        plane[c * length : c * length + half, part * half : (part + 1) * half]
                        + sign
                        * plane[c * length + half : (c + 1) * length, part * half : (part + 1) * half]
                        for c in range(PAIR)
                        for plane in planes
                    ],
                    axis=1,
                )
                for part in range(2)
            ],
            axis=0,
        )

    squared_b, scale_b = b_ref[0], b_ref[1]
    field = []
    for parity, sign in ((0, 1.0), (1, -1.0)):
        value = product(pair(first_ref.at[parity]), split(stacked(sign)))
        smooth = []
        for c in range(PAIR):
            wave_c = wave_c_ref[pl.program_id(0) * PAIR + c]
            scale_c = wave_c_ref[wave_c_ref.shape[0] // 2 + pl.program_id(0) * PAIR + c]
            squared = a_ref[1, parity] + (squared_b + wave_c * wave_c)
            inverse = scale_c / jnp.where(squared > 0, squared, 1.0)
            smooth.append(jnp.where(squared > 0, inverse * scale_b, 0.0) * a_ref[2, parity])
        smooth = jnp.concatenate(smooth, axis=1)
        field.append(value * jnp.concatenate([smooth, smooth], axis=0))
    upper = lax.broadcasted_iota(jnp.int32, (devices, message, tile), 1) < count
    for number in range(3):
        folded = jnp.concatenate(
            [
                field[parity][part * half : part * half + quarter]
                + sign_back * field[parity][part * half + quarter : (part + 1) * half]
                for part in range(2)
                for parity in range(2)
            ],
            axis=0,
        )
        values = [
            product(
                pair(back_ref.at[0, c % back_ref.shape[1]]),
                split(folded[:, c * length : (c + 1) * length]),
            )
            for c in range(PAIR)
        ]
        for spot in range(tiles // 3):
            parity, part = divmod(spot, 2)
            at = number * (tiles // 3) + spot
            here = [
                value[part * half : (part + 1) * half, parity * tile : (parity + 1) * tile]
                for value in values
            ]
            if groups == 2:
                even, odd = [value.reshape(devices, message, tile) for value in here]
                outs[0][:, at] = jnp.where(upper, even, odd)
                outs[1][:, at] = jnp.where(upper, odd, even)
            else:
                flat = outs[0].reshape(devices * tiles * message, tile)
                for c in range(PAIR):
                    for x in range(slab):
                        start = at * message + c * count + x
                        flat[pl.ds(start, devices, stride=tiles * message), :] = here[c][
                            x * devices : (x + 1) * devices
                        ]
        if number < 2:
            for parity in range(2):
                wave_a = a_ref[0, parity]
                field[parity] = field[parity] * jnp.concatenate([wave_a, wave_a], axis=0)


def halves(length):
    return np.arange(length).reshape(length // 2, 2).T


def spectrum_pass(received, side, waves_c, devices, groups, steps, first_step, filled):
    wide, narrow, per_c, rows_x, lanes = received.shape
    length = wide * rows_x
    rows_y = lanes // 2
    half = length // 2
    near = np.arange(half)
    split_index = halves(length)
    slab = half // devices
    second, first, back = [], [], []
    if groups == 2:
        orders = [
            near.reshape(devices, 2, slab // 2)[:, ::step].reshape(-1) for step in (1, -1)
        ]
    else:
        orders = [near.reshape(devices, slab).T.reshape(-1)]
    for parity, index in enumerate(split_index):
        table = turn(-angles(index, near, length)).reshape(2, half, 2, narrow // 2, rows_y)
        second.append(split_table(table.transpose(3, 2, 4, 0, 1).reshape(length, length)))
        first.append(split_table(turn(-angles(index, near, length))))
        columns = split_index[:, : half // 2].reshape(-1)
        back.append(
            [split_table(turn(angles(2 * order + parity, columns, length))) for order in orders]
        )
    tables = [np.stack(second), np.stack(first), np.stack([np.stack(each) for each in back])]
    wave = signed_wave(split_index, length)
    scale = np.where(split_index == half, 0.0, np.exp(-0.5 * wave**2))
    a_table = np.stack([wave, wave**2, scale]).astype(np.float32)[..., None]
    b_table = np.stack([wave**2, scale]).astype(np.float32).reshape(2, 1, length)
    message = PAIR * slab // groups
    out_shape = (devices, 3 * 2 * length // TILE, steps * message, TILE)
    block = out_shape[:2] + (message, TILE)

    def body(*refs):
        spectrum_kernel(slab, groups, *refs)

    def fixed(shape):
        return pl.BlockSpec(shape, lambda *_: (0,) * len(shape))

    return pl.pallas_call(
        body,
        grid_spec=pltpu.PrefetchScalarGridSpec(
            num_scalar_prefetch=2,
            grid=(per_c // PAIR,),
            in_specs=[
                fixed(a_table.shape),
                fixed(b_table.shape),
                fixed(tables[0].shape),
                fixed(tables[1].shape),
                pl.BlockSpec((1,) + tables[2].shape[1:], lambda i, s, _: (s[0], 0, 0, 0, 0)),
                pl.BlockSpec((wide, narrow, PAIR, rows_x, lanes), lambda i, *_: (0, 0, i, 0, 0)),
                *[pl.BlockSpec(memory_space=pl.ANY)] * len(filled),
            ],
            out_specs=[pl.BlockSpec(block, lambda i, *_: (0, 0, first_step + i, 0))] * groups,
        ),
        out_shape=[pltpu.HBM(out_shape, jnp.float32)] * groups,
        input_output_aliases={8 + spot: spot for spot in range(len(filled))},
        compiler_params=params(1),
        cost_estimate=cost(per_c * 7 * length**3, 20 * per_c * length**2 * 2),
    )(
        side,
        waves_c,
        *[in_hbm(table) for table in (a_table, b_table, *tables)],
        in_hbm(received),
        *[in_hbm(each) for each in filled],
    )


def shear_kernel(
    per_c, group, joined, row_ref, lane_ref, second_ref, third_ref, ahead_ref, last_ref, in_ref, out_ref, shear_ref
):
    step = pl.program_id(0)
    length = shear_ref.shape[0]
    half = length // 2
    devices, tiles, message, tile = in_ref.shape
    count = message // per_c
    flat = in_ref.reshape(devices * tiles * message, tile)

    @pl.when(step == 0)
    def _():
        shear_ref[...] = jnp.zeros_like(shear_ref)

    field = jnp.concatenate(
        [
            jnp.concatenate(
                [
                    flat[pl.ds((source * tiles + spot) * message + x, per_c, stride=count), :]
                    for x in range(count)
                    for source in range(devices)
                ],
                axis=0,
            )
            for spot in range(tiles)
        ],
        axis=1,
    )
    field = field * row_ref[0] * lane_ref[0]
    even = product(split(field[:, :length]), pair(second_ref.at[0]))
    odd = product(split(field[:, length:]), pair(second_ref.at[1]))
    near, far = even + odd, even - odd
    field = jnp.concatenate(
        [
            jnp.concatenate(
                [
                    value[x * half : (x + 1) * half, part * half : (part + 1) * half]
                    for x in range(count)
                    for value in (near, far)
                ],
                axis=1,
            )
            for part in range(2)
        ],
        axis=0,
    )
    field = product(pair(third_ref), split(field))
    shear_ref[...] += field * field

    @pl.when(step == 5)
    def _():
        ahead = jnp.concatenate(
            [shear_ref[:, x * length : (x + 1) * length] for x in range(count)], axis=0
        )
        ahead = product(split(ahead), pair(ahead_ref))
        ahead = jnp.concatenate(
            [
                jnp.concatenate(
                    [
                        ahead[x * length : (x + 1) * length, part * length : (part + 1) * length]
                        for x in range(count)
                    ],
                    axis=1,
                )
                for part in range(2)
            ],
            axis=0,
        )
        value = product(pair(last_ref), split(ahead))
        wide, narrow, message_out, _ = out_ref.shape
        rows_b = length // wide
        slots = tile // rows_b
        rows = 2 * length // slots
        run = rows // (2 * narrow * joined)
        out = out_ref.reshape(wide * narrow * message_out, tile)
        lane = lax.broadcasted_iota(jnp.int32, (rows, tile), 1) // rows_b
        for x in range(count):
            for w in range(wide):
                block, place = divmod(w, slots)
                lanes = slice(x * length + block * tile, x * length + (block + 1) * tile)
                moved = None
                for slot in range(slots):
                    piece = value[slot * rows : (slot + 1) * rows, lanes]
                    if slot != place:
                        piece = pltpu.roll(piece, (slot - place) * rows_b % tile, 1)
                    moved = piece if moved is None else jnp.where(lane == slot, piece, moved)
                for n in range(narrow):
                    for part in range(2):
                        for join in range(joined):
                            start = ((n * 2 + part) * joined + join) * run
                            piece = moved[start : start + run]
                            at = (w * narrow + n) * message_out
                            if joined == 2:
                                at += part * 2 * count + (join ^ group) * count + x
                                out[pl.ds(at, run, stride=4 * count), :] = piece
                            else:
                                at += (x * 2 + part) * run
                                out[pl.ds(at, run), :] = piece


def shear_pass(received, wide, narrow, per_c, group, joined):
    devices, tiles, message, tile = received.shape
    count = message // per_c
    length = tiles * tile // 6
    half = length // 2
    index = np.arange(length)
    angle = angles(index, index, length)
    cosine, sine = np.cos(angle), np.sin(angle)
    split_index = halves(length)
    second = np.stack(
        [split_table(turn(angles(np.arange(half), b, length)).T) for b in split_index]
    )
    row_c = np.arange(half) ^ group
    weight = np.where(row_c == 0, 1.0, 2.0)
    angle = angles(index, row_c, length)
    third = np.concatenate([weight * np.cos(angle), -weight * np.sin(angle)], axis=1)
    ahead = np.concatenate([cosine, -sine], axis=1)
    slots = TILE * wide // length
    order = index.reshape(narrow, -1, joined, slots).transpose(3, 0, 2, 1)
    angle = angles(order.reshape(-1), index, length)
    last = np.stack(
        [
            np.concatenate([np.cos(angle), np.sin(angle)], axis=1),
            np.concatenate([-np.sin(angle), np.cos(angle)], axis=1),
        ]
    )
    last = last.reshape(2, slots, narrow, -1, 2 * length).transpose(1, 2, 0, 3, 4)
    last = last.reshape(2 * length, 2 * length)
    wave = signed_wave(index, length)
    wave_rows = np.tile(wave[row_c], count)
    wave_lanes = np.stack([wave[split_index]] * 2, axis=1).reshape(-1)
    twice = math.sqrt(2.0)
    one_row, one_lane = np.ones_like(wave_rows), np.ones_like(wave_lanes)
    row_factor = np.stack(
        [one_row, twice * one_row, twice * wave_rows, one_row, twice * wave_rows, wave_rows**2]
    ).astype(np.float32)[:, :, None]
    lane_factor = np.stack(
        [one_lane, wave_lanes, one_lane, wave_lanes**2, wave_lanes, one_lane]
    ).astype(np.float32)[:, None, :]
    tables = [second] + [split_table(table) for table in (third, ahead, last)]
    out_shape = (wide, narrow, count * 2 * length // (narrow * slots), TILE)

    def body(*refs):
        shear_kernel(per_c, group, joined, *refs)

    def which(i):
        return (0, 2 - (i >= 1).astype(jnp.int32) - (i >= 3).astype(jnp.int32), 0, 0)

    return pl.pallas_call(
        body,
        grid=(6,),
        in_specs=[
            pl.BlockSpec((1, count * half, 1), lambda i: (i, 0, 0)),
            pl.BlockSpec((1, 1, 2 * length), lambda i: (i, 0, 0)),
            *[whole(table.shape) for table in tables],
            pl.BlockSpec((devices, tiles // 3, message, tile), which),
        ],
        out_specs=whole(out_shape),
        out_shape=pltpu.HBM(out_shape, jnp.float32),
        scratch_shapes=[pltpu.VMEM((length, count * length), jnp.float32)],
        compiler_params=params(1),
        cost_estimate=cost(count * 18 * length**3, 4 * received.size + 4 * 2**20),
    )(*[in_hbm(value) for value in (row_factor, lane_factor, *tables, received)])


def first_kernel(count, rows_b, anchor_ref, table_ref, *refs):
    ins, (real_ref, imag_ref) = refs[:-2], refs[-2:]
    wide, sides, ranks, rows, lanes = ins[0].shape
    length = real_ref.shape[2]
    half = length // 2
    slots = lanes // rows_b
    joined = len(ins)
    steps = real_ref.shape[0] // (slots * joined)
    spot_row = lax.broadcasted_iota(jnp.int32, (lanes, half), 0)
    spot_a = lax.broadcasted_iota(jnp.int32, (lanes, half), 1)
    is_anchor = (anchor_ref[0] == 1) & (pl.program_id(0) == 0)
    anchor = (spot_row == 0) & (spot_a == 0) & is_anchor
    upper = lax.broadcasted_iota(jnp.int32, (wide * ranks, joined * count, lanes), 1) < count

    def gathered(side, step, join, part):
        if joined == 2:
            at = pl.ds((step * 2 + part) * 2 * count, 2 * count)
            own, other = [
                ref[:, side, :, at].reshape(wide * ranks, 2 * count, lanes)
                for ref in (ins if join == 0 else ins[::-1])
            ]
            return jnp.where(upper, own, other).reshape(half, lanes)
        flat = ins[0].reshape(wide * sides * ranks * rows, lanes)
        run = rows // count
        return jnp.concatenate(
            [
                flat[
                    pl.ds((w * sides + side) * ranks * rows + part * steps + step, ranks * count, stride=run),
                    :,
                ]
                for w in range(wide)
            ],
            axis=0,
        )

    for join in range(joined):
        sums = []
        for side in range(sides):
            left = jnp.concatenate(
                [
                    jnp.concatenate([gathered(side, step, join, part).T for part in range(2)], axis=1)
                    for step in range(steps)
                ],
                axis=0,
            )
            sums.append(product(split(left), pair(table_ref.at[join, side])))
        even, odd = sums
        for far, value in enumerate((even + odd, even - odd)):
            for step in range(steps):
                at = (step * joined + join) * slots
                columns = slice(far * half, (far + 1) * half)
                for part, ref in enumerate((real_ref, imag_ref)):
                    here = value[step * lanes : (step + 1) * lanes, part * half : (part + 1) * half]
                    if at == 0 and far == 0:
                        here = jnp.where(anchor, 0.0, here)
                    ref[at : at + slots, :, columns] = here.reshape(slots, rows_b, half)


def first_pass(parts, is_anchor, length, wide, sides, count):
    devices, rows, lanes = parts[0].shape
    joined = len(parts)
    ranks = devices // wide // sides
    rows_b = length // wide
    slots = lanes // rows_b
    scale = 1.0 / float(length) ** 1.5
    index = np.arange(length).reshape(wide * ranks, joined, count, sides)
    tables = []
    for join in range(joined):
        order = index[:, :: 1 - 2 * join].transpose(3, 0, 1, 2).reshape(sides, -1)
        tables.append(
            [split_table(scale * turn(-angles(np.arange(length // 2), x, length)).T) for x in order]
        )
    table = np.stack([np.stack(each) for each in tables])
    total = rows // (2 * joined * count) if joined == 2 else rows // (2 * count)
    grid = 4 if joined == 2 and total % 4 == 0 else 1
    parts = [part.reshape(wide, sides, ranks, rows, lanes) for part in parts]

    def body(*refs):
        first_kernel(count, rows_b, *refs)

    rows_c = total * joined * slots
    out_shape = jax.ShapeDtypeStruct((rows_c, rows_b, length), jnp.float32)
    return pl.pallas_call(
        body,
        grid=(grid,),
        in_specs=[
            pl.BlockSpec(memory_space=pltpu.SMEM),
            whole(table.shape),
            *[pl.BlockSpec((wide, sides, ranks, rows // grid, lanes), lambda i: (0, 0, 0, i, 0))]
            * joined,
        ],
        out_specs=[pl.BlockSpec((rows_c // grid, rows_b, length), lambda i: (i, 0, 0))] * 2,
        out_shape=[out_shape] * 2,
        compiler_params=params(1),
        cost_estimate=cost(rows_c * 2 * rows_b * length * length, 16 * rows_c * rows_b * length),
    )(is_anchor, table, *parts)


def transpose(value, members=None):
    return lax.all_to_all(
        value, AXES, split_axis=0, concat_axis=0, tiled=True, axis_index_groups=members
    )


def solution(mesh):
    wide, narrow = mesh.shape["wide"], mesh.shape["narrow"]
    sides = 2
    ranks = narrow // sides
    devices = wide * ranks
    members = [
        [w * narrow + side * ranks + rank for w in range(wide) for rank in range(ranks)]
        for side in range(sides)
    ]

    def per_device(density):
        rows_x, rows_y, length = density.shape
        half = length // 2
        per_c = half // devices
        slab = half // devices
        steps = per_c // PAIR
        counts = [per_c - PAIR, PAIR] if steps > 1 else [per_c]
        groups = 2 if slab > 2 else 1
        spot_wide, spot_narrow = lax.axis_index("wide"), lax.axis_index("narrow")
        side = (spot_narrow // ranks).astype(jnp.int32).reshape(1)
        rank = spot_wide * ranks + spot_narrow % ranks
        waves_c = (rank * per_c + jnp.arange(per_c, dtype=jnp.int32)).astype(jnp.float32)
        waves_c = waves_c * (2.0 * math.pi / length)
        scales_c = jnp.exp(-0.5 * waves_c * waves_c) * (1.0 / float(length) ** 3)
        chunks, start = [], 0
        for planes, count in zip(third_pass(density, wide, sides, ranks, counts), counts):
            planes = transpose(planes.reshape(wide * narrow, count, rows_x, 2 * rows_y))
            planes = planes.reshape(wide, narrow, count, rows_x, 2 * rows_y)
            spots = slice(start, start + count)
            both_c = jnp.concatenate([waves_c[spots], scales_c[spots]])
            chunks = spectrum_pass(
                planes, side, both_c, devices, groups, steps, start // PAIR, chunks
            )
            start += count
        is_anchor = ((spot_wide == 0) & (spot_narrow == 0)).astype(jnp.int32).reshape(1)
        parts = []
        for group, chunk in enumerate(chunks):
            part = shear_pass(transpose(chunk, members), wide, narrow, per_c, group, groups)
            parts.append(transpose(part.reshape((wide * narrow,) + part.shape[2:])))
        return tuple(first_pass(parts, is_anchor, length, wide, sides, slab // groups))

    return jax.shard_map(
        per_device,
        mesh=mesh,
        in_specs=(P("wide", "narrow", None),),
        out_specs=(P("narrow", "wide", None), P("narrow", "wide", None)),
        check_vma=False,
    )
```

```python
import math

import jax
import jax.numpy as jnp
import ml_dtypes
import numpy as np
from jax import lax
from jax.experimental import pallas as pl
from jax.experimental.pallas import tpu as pltpu
from jax.sharding import PartitionSpec as P

AXES = ("wide", "narrow")
TILE = 128
LIMIT = 16 * 1024 * 1024


def angles(rows, columns, length):
    return (2.0 * math.pi / length) * (np.outer(rows, columns) % length)


def split_table(table):
    table = np.asarray(table, np.float64)
    high = table.astype(ml_dtypes.bfloat16)
    low = (table - high.astype(np.float64)).astype(ml_dtypes.bfloat16)
    return np.stack([high, low])


def split(value):
    high = value.astype(jnp.bfloat16)
    low = (value - high.astype(jnp.float32)).astype(jnp.bfloat16)
    return high, low


def product(left, right, contract=((1,), (0,))):
    (left_axis,), (right_axis,) = contract
    left = jnp.concatenate([left[0], left[0], left[1]], axis=left_axis)
    right = jnp.concatenate([right[0], right[1], right[0]], axis=right_axis)
    return lax.dot_general(
        left, right, (contract, ((), ())), preferred_element_type=jnp.float32
    )


def pair(ref):
    return ref[0], ref[1]


def signed_wave(index, length):
    index = np.asarray(index)
    return np.where(index < length // 2, index, index - length) * (2.0 * math.pi / length)


def params(steps):
    return pltpu.CompilerParams(
        vmem_limit_bytes=LIMIT, dimension_semantics=("arbitrary",) * steps
    )


def whole(shape):
    return pl.BlockSpec(shape, lambda *_: (0,) * len(shape))


def keep(value, near):
    return pltpu.with_memory_space_constraint(jnp.asarray(value), pltpu.VMEM if near else pltpu.HBM)


def in_hbm(value):
    return keep(value, False)


def cost(macs, moved):
    return pl.CostEstimate(flops=6 * macs, bytes_accessed=moved, transcendentals=0)


def third_kernel(counts, table_ref, density_ref, *outs):
    rows_x, rows_y, length = density_ref.shape
    wide, sides, ranks = outs[0].shape[:3]
    half = length // 2
    flats = [ref.reshape(math.prod(ref.shape[:5]), 2 * rows_y) for ref in outs]
    table = pair(table_ref)
    left_half = lax.broadcasted_iota(jnp.int32, (half, 2 * rows_y), 1) < rows_y
    group = 4
    for first in range(0, rows_x, group):
        block = density_ref[first : first + group].reshape(group * rows_y, length)
        result = product(table, split(block), ((1,), (1,)))
        for inner in range(0, group, 2):
            lanes = slice(inner * rows_y, (inner + 2) * rows_y)
            real = result[:half, lanes]
            imag = result[half:, lanes]
            even = jnp.where(left_half, real, pltpu.roll(imag, rows_y, 1))
            odd = jnp.where(left_half, pltpu.roll(real, rows_y, 1), imag)
            for x, value in ((first + inner, even), (first + inner + 1, odd)):
                start = 0
                for flat, count in zip(flats, counts):
                    for c in range(count):
                        for rank in range(ranks):
                            at = (rank * count + c) * rows_x + x
                            stride = sides * ranks * count * rows_x
                            flat[pl.ds(at, wide, stride=stride), :] = value[start : start + wide]
                            start += wide
    for ref in outs:
        for side in range(1, sides):
            ref[:, side] = ref[:, 0]


def third_pass(density, wide, sides, ranks, counts):
    rows_x, rows_y, length = density.shape
    half = length // 2
    per_c = sum(counts)
    order = np.arange(half).reshape(wide, ranks, per_c).transpose(2, 1, 0).reshape(-1)
    angle = angles(order, np.arange(length), length)
    table = split_table(np.concatenate([np.cos(angle), -np.sin(angle)]))
    step = min(8, rows_x)

    def body(*refs):
        third_kernel(counts, *refs)

    return pl.pallas_call(
        body,
        grid=(rows_x // step,),
        in_specs=[
            whole(table.shape),
            pl.BlockSpec((step, rows_y, length), lambda i: (i, 0, 0)),
        ],
        out_specs=[
            pl.BlockSpec(
                (wide, sides, ranks, count, step, 2 * rows_y), lambda i: (0, 0, 0, 0, i, 0)
            )
            for count in counts
        ],
        out_shape=[
            jax.ShapeDtypeStruct((wide, sides, ranks, count, rows_x, 2 * rows_y), jnp.float32)
            for count in counts
        ],
        compiler_params=params(1),
        cost_estimate=cost(density.size * length, 12 * density.size),
    )(in_hbm(table), in_hbm(density))


PAIR = 2


def turn(angle):
    cosine, sine = np.cos(angle), np.sin(angle)
    return np.block([[cosine, -sine], [sine, cosine]])


def spectrum_kernel(slab, groups, side_ref, wave_c_ref, a_ref, b_ref, second_ref, first_ref, back_ref, in_ref, *refs):
    outs = refs[-groups:]
    wide, narrow, _, rows_x, lanes = in_ref.shape
    length = wide * rows_x
    half = length // 2
    quarter = half // 2
    devices, tiles, message, tile = outs[0].shape
    count = slab // groups
    sign_back = 1.0 - 2.0 * side_ref[0].astype(jnp.float32)

    def column(c, n):
        return in_ref[:, n, c].reshape(length, lanes)

    def columns(numbers):
        return jnp.concatenate(
            [
                jnp.concatenate([column(c, n) for n in numbers], axis=1)
                for c in range(PAIR)
            ],
            axis=0,
        )

    low, high = columns(range(narrow // 2)), columns(range(narrow // 2, narrow))
    planes = [
        product(split(low + high), pair(second_ref.at[0])),
        product(split(low - high), pair(second_ref.at[1])),
    ]

    def stacked(sign):
        return jnp.concatenate(
            [
                jnp.concatenate(
                    [
                        plane[c * length : c * length + half, part * half : (part + 1) * half]
                        + sign
                        * plane[c * length + half : (c + 1) * length, part * half : (part + 1) * half]
                        for c in range(PAIR)
                        for plane in planes
                    ],
                    axis=1,
                )
                for part in range(2)
            ],
            axis=0,
        )

    squared_b, scale_b = b_ref[0], b_ref[1]
    field = []
    for parity, sign in ((0, 1.0), (1, -1.0)):
        value = product(pair(first_ref.at[parity]), split(stacked(sign)))
        smooth = []
        for c in range(PAIR):
            wave_c = wave_c_ref[pl.program_id(0) * PAIR + c]
            scale_c = wave_c_ref[wave_c_ref.shape[0] // 2 + pl.program_id(0) * PAIR + c]
            squared = a_ref[1, parity] + (squared_b + wave_c * wave_c)
            inverse = scale_c / jnp.where(squared > 0, squared, 1.0)
            smooth.append(jnp.where(squared > 0, inverse * scale_b, 0.0) * a_ref[2, parity])
        smooth = jnp.concatenate(smooth, axis=1)
        field.append(value * jnp.concatenate([smooth, smooth], axis=0))
    upper = lax.broadcasted_iota(jnp.int32, (devices, message, tile), 1) < count
    for number in range(3):
        folded = jnp.concatenate(
            [
                field[parity][part * half : part * half + quarter]
                + sign_back * field[parity][part * half + quarter : (part + 1) * half]
                for part in range(2)
                for parity in range(2)
            ],
            axis=0,
        )
        values = [
            product(
                pair(back_ref.at[0, c % back_ref.shape[1]]),
                split(folded[:, c * length : (c + 1) * length]),
            )
            for c in range(PAIR)
        ]
        for spot in range(tiles // 3):
            parity, part = divmod(spot, 2)
            at = number * (tiles // 3) + spot
            here = [
                value[part * half : (part + 1) * half, parity * tile : (parity + 1) * tile]
                for value in values
            ]
            if groups == 2:
                even, odd = [value.reshape(devices, message, tile) for value in here]
                outs[0][:, at] = jnp.where(upper, even, odd)
                outs[1][:, at] = jnp.where(upper, odd, even)
            else:
                flat = outs[0].reshape(devices * tiles * message, tile)
                for c in range(PAIR):
                    for x in range(slab):
                        start = at * message + c * count + x
                        flat[pl.ds(start, devices, stride=tiles * message), :] = here[c][
                            x * devices : (x + 1) * devices
                        ]
        if number < 2:
            for parity in range(2):
                wave_a = a_ref[0, parity]
                field[parity] = field[parity] * jnp.concatenate([wave_a, wave_a], axis=0)


def halves(length):
    return np.arange(length).reshape(length // 2, 2).T


def spectrum_pass(received, side, waves_c, devices, groups, steps, first_step, filled):
    wide, narrow, per_c, rows_x, lanes = received.shape
    length = wide * rows_x
    rows_y = lanes // 2
    half = length // 2
    near = np.arange(half)
    split_index = halves(length)
    slab = half // devices
    second, first, back = [], [], []
    if groups == 2:
        orders = [
            near.reshape(devices, 2, slab // 2)[:, ::step].reshape(-1) for step in (1, -1)
        ]
    else:
        orders = [near.reshape(devices, slab).T.reshape(-1)]
    for parity, index in enumerate(split_index):
        table = turn(-angles(index, near, length)).reshape(2, half, 2, narrow // 2, rows_y)
        second.append(split_table(table.transpose(3, 2, 4, 0, 1).reshape(length, length)))
        first.append(split_table(turn(-angles(index, near, length))))
        columns = split_index[:, : half // 2].reshape(-1)
        back.append(
            [split_table(turn(angles(2 * order + parity, columns, length))) for order in orders]
        )
    tables = [np.stack(second), np.stack(first), np.stack([np.stack(each) for each in back])]
    wave = signed_wave(split_index, length)
    scale = np.where(split_index == half, 0.0, np.exp(-0.5 * wave**2))
    a_table = np.stack([wave, wave**2, scale]).astype(np.float32)[..., None]
    b_table = np.stack([wave**2, scale]).astype(np.float32).reshape(2, 1, length)
    message = PAIR * slab // groups
    out_shape = (devices, 3 * 2 * length // TILE, steps * message, TILE)
    block = out_shape[:2] + (message, TILE)

    def body(*refs):
        spectrum_kernel(slab, groups, *refs)

    def fixed(shape):
        return pl.BlockSpec(shape, lambda *_: (0,) * len(shape))

    return pl.pallas_call(
        body,
        grid_spec=pltpu.PrefetchScalarGridSpec(
            num_scalar_prefetch=2,
            grid=(per_c // PAIR,),
            in_specs=[
                fixed(a_table.shape),
                fixed(b_table.shape),
                fixed(tables[0].shape),
                fixed(tables[1].shape),
                pl.BlockSpec((1,) + tables[2].shape[1:], lambda i, s, _: (s[0], 0, 0, 0, 0)),
                pl.BlockSpec((wide, narrow, PAIR, rows_x, lanes), lambda i, *_: (0, 0, i, 0, 0)),
                *[pl.BlockSpec(memory_space=pl.ANY)] * len(filled),
            ],
            out_specs=[pl.BlockSpec(block, lambda i, *_: (0, 0, first_step + i, 0))] * groups,
        ),
        out_shape=[pltpu.HBM(out_shape, jnp.float32)] * groups,
        input_output_aliases={8 + spot: spot for spot in range(len(filled))},
        compiler_params=params(1),
        cost_estimate=cost(per_c * 7 * length**3, 20 * per_c * length**2 * 2),
    )(
        side,
        waves_c,
        *[in_hbm(table) for table in (a_table, b_table, *tables)],
        received,
        *[in_hbm(each) for each in filled],
    )


def shear_kernel(
    per_c,
    group,
    joined,
    _,
    row_ref,
    lane_ref,
    second_ref,
    third_ref,
    ahead_ref,
    last_ref,
    in_ref,
    own_ref,
    other_ref,
    shear_ref,
):
    step = pl.program_id(0)
    length = shear_ref.shape[0]
    half = length // 2
    devices, tiles, message, tile = in_ref.shape
    count = message // per_c
    flat = in_ref.reshape(devices * tiles * message, tile)

    @pl.when(step == 0)
    def _():
        shear_ref[...] = jnp.zeros_like(shear_ref)

    field = jnp.concatenate(
        [
            jnp.concatenate(
                [
                    flat[pl.ds((source * tiles + spot) * message + x, per_c, stride=count), :]
                    for x in range(count)
                    for source in range(devices)
                ],
                axis=0,
            )
            for spot in range(tiles)
        ],
        axis=1,
    )
    field = field * row_ref[0] * lane_ref[0]
    even = product(split(field[:, :length]), pair(second_ref.at[0]))
    odd = product(split(field[:, length:]), pair(second_ref.at[1]))
    near, far = even + odd, even - odd
    field = jnp.concatenate(
        [
            jnp.concatenate(
                [
                    value[x * half : (x + 1) * half, part * half : (part + 1) * half]
                    for x in range(count)
                    for value in (near, far)
                ],
                axis=1,
            )
            for part in range(2)
        ],
        axis=0,
    )
    field = product(pair(third_ref), split(field))
    shear_ref[...] += field * field

    @pl.when(step == 5)
    def _():
        ahead = jnp.concatenate(
            [shear_ref[:, x * length : (x + 1) * length] for x in range(count)], axis=0
        )
        ahead = product(split(ahead), pair(ahead_ref))
        ahead = jnp.concatenate(
            [
                jnp.concatenate(
                    [
                        ahead[x * length : (x + 1) * length, part * length : (part + 1) * length]
                        for x in range(count)
                    ],
                    axis=1,
                )
                for part in range(2)
            ],
            axis=0,
        )
        value = product(pair(last_ref.at[0]), split(ahead))
        wide, ranks, message_out, _ = own_ref.shape
        narrow = 2 * ranks
        rows_b = length // wide
        slots = tile // rows_b
        rows = 2 * length // slots
        run = rows // (2 * narrow * joined)
        outs = [ref.reshape(wide * ranks * message_out, tile) for ref in (own_ref, other_ref)]
        lane = lax.broadcasted_iota(jnp.int32, (rows, tile), 1) // rows_b
        for x in range(count):
            for w in range(wide):
                block, place = divmod(w, slots)
                lanes = slice(x * length + block * tile, x * length + (block + 1) * tile)
                moved = None
                for slot in range(slots):
                    piece = value[slot * rows : (slot + 1) * rows, lanes]
                    if slot != place:
                        piece = pltpu.roll(piece, (slot - place) * rows_b % tile, 1)
                    moved = piece if moved is None else jnp.where(lane == slot, piece, moved)
                for n in range(narrow):
                    out = outs[n // ranks]
                    for part in range(2):
                        for join in range(joined):
                            start = ((n * 2 + part) * joined + join) * run
                            piece = moved[start : start + run]
                            at = (w * ranks + n % ranks) * message_out
                            if joined == 2:
                                at += part * 2 * count + (join ^ group) * count + x
                                out[pl.ds(at, run, stride=4 * count), :] = piece
                            else:
                                at += (x * 2 + part) * run
                                out[pl.ds(at, run), :] = piece


def shear_pass(received, side, wide, narrow, per_c, group, joined):
    devices, tiles, message, tile = received.shape
    count = message // per_c
    length = tiles * tile // 6
    half = length // 2
    index = np.arange(length)
    angle = angles(index, index, length)
    cosine, sine = np.cos(angle), np.sin(angle)
    split_index = halves(length)
    second = np.stack(
        [split_table(turn(angles(np.arange(half), b, length)).T) for b in split_index]
    )
    row_c = np.arange(half) ^ group
    weight = np.where(row_c == 0, 1.0, 2.0)
    angle = angles(index, row_c, length)
    third = np.concatenate([weight * np.cos(angle), -weight * np.sin(angle)], axis=1)
    ahead = np.concatenate([cosine, -sine], axis=1)
    slots = TILE * wide // length
    order = index.reshape(narrow, -1, joined, slots).transpose(3, 0, 2, 1)
    angle = angles(order.reshape(-1), index, length)
    last = np.stack(
        [
            np.concatenate([np.cos(angle), np.sin(angle)], axis=1),
            np.concatenate([-np.sin(angle), np.cos(angle)], axis=1),
        ]
    )
    last = last.reshape(2, slots, narrow, -1, 2 * length).transpose(1, 2, 0, 3, 4)
    last = np.stack(
        [
            split_table(np.roll(last, -own, axis=1).reshape(2 * length, 2 * length))
            for own in (0, narrow // 2)
        ]
    )
    wave = signed_wave(index, length)
    wave_rows = np.tile(wave[row_c], count)
    wave_lanes = np.stack([wave[split_index]] * 2, axis=1).reshape(-1)
    twice = math.sqrt(2.0)
    one_row, one_lane = np.ones_like(wave_rows), np.ones_like(wave_lanes)
    row_factor = np.stack(
        [one_row, twice * one_row, twice * wave_rows, one_row, twice * wave_rows, wave_rows**2]
    ).astype(np.float32)[:, :, None]
    lane_factor = np.stack(
        [one_lane, wave_lanes, one_lane, wave_lanes**2, wave_lanes, one_lane]
    ).astype(np.float32)[:, None, :]
    tables = [second, split_table(third), split_table(ahead)]
    out_shape = (wide, narrow // 2, count * 2 * length // (narrow * slots), TILE)

    def body(*refs):
        shear_kernel(per_c, group, joined, *refs)

    def which(i, _):
        return (0, 2 - (i >= 1).astype(jnp.int32) - (i >= 3).astype(jnp.int32), 0, 0)

    return pl.pallas_call(
        body,
        grid_spec=pltpu.PrefetchScalarGridSpec(
            num_scalar_prefetch=1,
            grid=(6,),
            in_specs=[
                pl.BlockSpec((1, count * half, 1), lambda i, _: (i, 0, 0)),
                pl.BlockSpec((1, 1, 2 * length), lambda i, _: (i, 0, 0)),
                *[whole(table.shape) for table in tables],
                pl.BlockSpec((1,) + last.shape[1:], lambda i, s: (s[0], 0, 0, 0)),
                pl.BlockSpec((devices, tiles // 3, message, tile), which),
            ],
            out_specs=[whole(out_shape)] * 2,
            scratch_shapes=[pltpu.VMEM((length, count * length), jnp.float32)],
        ),
        out_shape=[pltpu.HBM(out_shape, jnp.float32)] * 2,
        compiler_params=params(1),
        cost_estimate=cost(count * 18 * length**3, 4 * received.size + 4 * 2**20),
    )(side, *[in_hbm(value) for value in (row_factor, lane_factor, *tables, last)], received)


def first_kernel(count, rows_b, side_ref, anchor_ref, table_ref, *refs):
    ins, (real_ref, imag_ref) = refs[:-2], refs[-2:]
    wide, ranks, rows, lanes = ins[0].shape
    length = real_ref.shape[2]
    half = length // 2
    slots = lanes // rows_b
    joined = len(ins) // 2
    sources = ins[:joined], ins[joined:]
    side = side_ref[0]
    sign = 1.0 - 2.0 * side.astype(jnp.float32)
    steps = real_ref.shape[0] // (slots * joined)
    spot_row = lax.broadcasted_iota(jnp.int32, (lanes, half), 0)
    spot_a = lax.broadcasted_iota(jnp.int32, (lanes, half), 1)
    is_anchor = (anchor_ref[0] == 1) & (pl.program_id(0) == 0)
    anchor = (spot_row == 0) & (spot_a == 0) & is_anchor
    upper = lax.broadcasted_iota(jnp.int32, (wide * ranks, joined * count, lanes), 1) < count

    def gathered(source, step, join, part):
        if joined == 2:
            at = pl.ds((step * 2 + part) * 2 * count, 2 * count)
            own, other = [
                ref[:, :, at].reshape(wide * ranks, 2 * count, lanes)
                for ref in (source if join == 0 else source[::-1])
            ]
            return jnp.where(upper, own, other).reshape(half, lanes)
        flat = source[0].reshape(wide * ranks * rows, lanes)
        return flat[pl.ds(part * steps + step, half, stride=rows // count), :]

    for join in range(joined):
        sums = []
        for parity, source in ((side, sources[0]), (1 - side, sources[1])):
            left = jnp.concatenate(
                [
                    jnp.concatenate([gathered(source, step, join, part).T for part in range(2)], axis=1)
                    for step in range(steps)
                ],
                axis=0,
            )
            sums.append(product(split(left), pair(table_ref.at[join, parity])))
        own, other = sums
        for far, value in enumerate((own + other, (own - other) * sign)):
            for step in range(steps):
                at = (step * joined + join) * slots
                columns = slice(far * half, (far + 1) * half)
                for part, ref in enumerate((real_ref, imag_ref)):
                    here = value[step * lanes : (step + 1) * lanes, part * half : (part + 1) * half]
                    if at == 0 and far == 0:
                        here = jnp.where(anchor, 0.0, here)
                    ref[at : at + slots, :, columns] = here.reshape(slots, rows_b, half)


def first_pass(parts, side, is_anchor, length, wide, sides, count):
    devices, rows, lanes = parts[0].shape
    joined = len(parts) // 2
    ranks = devices // wide
    rows_b = length // wide
    slots = lanes // rows_b
    scale = 1.0 / float(length) ** 1.5
    index = np.arange(length).reshape(wide * ranks, joined, count, sides)
    tables = []
    for join in range(joined):
        order = index[:, :: 1 - 2 * join].transpose(3, 0, 1, 2).reshape(sides, -1)
        tables.append(
            [split_table(scale * turn(-angles(np.arange(length // 2), x, length)).T) for x in order]
        )
    table = np.stack([np.stack(each) for each in tables])
    total = rows // (2 * joined * count) if joined == 2 else rows // (2 * count)
    grid = 4 if joined == 2 and total % 4 == 0 else 1
    parts = [part.reshape(wide, ranks, rows, lanes) for part in parts]

    def body(*refs):
        first_kernel(count, rows_b, *refs)

    rows_c = total * joined * slots
    out_shape = jax.ShapeDtypeStruct((rows_c, rows_b, length), jnp.float32)
    return pl.pallas_call(
        body,
        grid=(grid,),
        in_specs=[
            pl.BlockSpec(memory_space=pltpu.SMEM),
            pl.BlockSpec(memory_space=pltpu.SMEM),
            whole(table.shape),
            *[pl.BlockSpec((wide, ranks, rows // grid, lanes), lambda i: (0, 0, i, 0))]
            * (2 * joined),
        ],
        out_specs=[pl.BlockSpec((rows_c // grid, rows_b, length), lambda i: (i, 0, 0))] * 2,
        out_shape=[out_shape] * 2,
        compiler_params=params(1),
        cost_estimate=cost(rows_c * 2 * rows_b * length * length, 16 * rows_c * rows_b * length),
    )(side, is_anchor, table, *parts)


def transpose(value, members=None):
    return lax.all_to_all(
        value, AXES, split_axis=0, concat_axis=0, tiled=True, axis_index_groups=members
    )


def solution(mesh):
    wide, narrow = mesh.shape["wide"], mesh.shape["narrow"]
    sides = 2
    ranks = narrow // sides
    devices = wide * ranks
    members = [
        [w * narrow + side * ranks + rank for w in range(wide) for rank in range(ranks)]
        for side in range(sides)
    ]

    def per_device(density):
        rows_x, rows_y, length = density.shape
        half = length // 2
        per_c = half // devices
        slab = half // devices
        steps = per_c // PAIR
        counts = [per_c - PAIR, PAIR] if steps > 1 else [per_c]
        groups = 2 if slab > 2 else 1
        spot_wide, spot_narrow = lax.axis_index("wide"), lax.axis_index("narrow")
        side = (spot_narrow // ranks).astype(jnp.int32).reshape(1)
        rank = spot_wide * ranks + spot_narrow % ranks
        waves_c = (rank * per_c + jnp.arange(per_c, dtype=jnp.int32)).astype(jnp.float32)
        waves_c = waves_c * (2.0 * math.pi / length)
        scales_c = jnp.exp(-0.5 * waves_c * waves_c) * (1.0 / float(length) ** 3)
        chunks, start = [], 0
        for planes, count in zip(third_pass(density, wide, sides, ranks, counts), counts):
            planes = transpose(planes.reshape(wide * narrow, count, rows_x, 2 * rows_y))
            planes = planes.reshape(wide, narrow, count, rows_x, 2 * rows_y)
            spots = slice(start, start + count)
            both_c = jnp.concatenate([waves_c[spots], scales_c[spots]])
            chunks = spectrum_pass(
                keep(planes, start > 0), side, both_c, devices, groups, steps, start // PAIR, chunks
            )
            start += count
        is_anchor = ((spot_wide == 0) & (spot_narrow == 0)).astype(jnp.int32).reshape(1)
        across = [(n, (n + ranks) % narrow) for n in range(narrow)]
        owns, others = [], []
        for group, chunk in enumerate(chunks):
            received = keep(transpose(chunk, members), group > 0)
            own, other = shear_pass(received, side, wide, narrow, per_c, group, groups)
            other = lax.ppermute(other, "narrow", across)
            owns.append(transpose(own.reshape((devices,) + own.shape[2:]), members))
            others.append(transpose(other.reshape((devices,) + other.shape[2:]), members))
        return tuple(first_pass(owns + others, side, is_anchor, length, wide, sides, slab // groups))

    return jax.shard_map(
        per_device,
        mesh=mesh,
        in_specs=(P("wide", "narrow", None),),
        out_specs=(P("narrow", "wide", None), P("narrow", "wide", None)),
        check_vma=False,
    )
```

```python
import math

import jax
import jax.numpy as jnp
import ml_dtypes
import numpy as np
from jax import lax
from jax.experimental import pallas as pl
from jax.experimental.pallas import tpu as pltpu
from jax.sharding import PartitionSpec as P

AXES = ("wide", "narrow")
TILE = 128
LIMIT = 16 * 1024 * 1024


def angles(rows, columns, length):
    return (2.0 * math.pi / length) * (np.outer(rows, columns) % length)


def split_table(table):
    table = np.asarray(table, np.float64)
    high = table.astype(ml_dtypes.bfloat16)
    low = (table - high.astype(np.float64)).astype(ml_dtypes.bfloat16)
    return np.stack([high, low])


def split(value):
    high = value.astype(jnp.bfloat16)
    low = (value - high.astype(jnp.float32)).astype(jnp.bfloat16)
    return high, low


def product(left, right, contract=((1,), (0,))):
    (left_axis,), (right_axis,) = contract
    left = jnp.concatenate([left[0], left[0], left[1]], axis=left_axis)
    right = jnp.concatenate([right[0], right[1], right[0]], axis=right_axis)
    return lax.dot_general(
        left, right, (contract, ((), ())), preferred_element_type=jnp.float32
    )


def pair(ref):
    return ref[0], ref[1]


def signed_wave(index, length):
    index = np.asarray(index)
    return np.where(index < length // 2, index, index - length) * (2.0 * math.pi / length)


def params(steps):
    return pltpu.CompilerParams(
        vmem_limit_bytes=LIMIT, dimension_semantics=("arbitrary",) * steps
    )


def whole(shape):
    return pl.BlockSpec(shape, lambda *_: (0,) * len(shape))


def keep(value, space):
    return pltpu.with_memory_space_constraint(jnp.asarray(value), space)


def in_hbm(value):
    return keep(value, pltpu.HBM)


def cost(macs, moved):
    return pl.CostEstimate(flops=6 * macs, bytes_accessed=moved, transcendentals=0)


def third_kernel(counts, table_ref, density_ref, *outs):
    rows_x, rows_y, length = density_ref.shape
    wide, sides, ranks = outs[0].shape[:3]
    half = length // 2
    flats = [ref.reshape(math.prod(ref.shape[:5]), 2 * rows_y) for ref in outs]
    table = pair(table_ref)
    left_half = lax.broadcasted_iota(jnp.int32, (half, 2 * rows_y), 1) < rows_y
    group = 4
    for first in range(0, rows_x, group):
        block = density_ref[first : first + group].reshape(group * rows_y, length)
        result = product(table, split(block), ((1,), (1,)))
        for inner in range(0, group, 2):
            lanes = slice(inner * rows_y, (inner + 2) * rows_y)
            real = result[:half, lanes]
            imag = result[half:, lanes]
            even = jnp.where(left_half, real, pltpu.roll(imag, rows_y, 1))
            odd = jnp.where(left_half, pltpu.roll(real, rows_y, 1), imag)
            for x, value in ((first + inner, even), (first + inner + 1, odd)):
                start = 0
                for flat, count in zip(flats, counts):
                    for c in range(count):
                        for rank in range(ranks):
                            at = (rank * count + c) * rows_x + x
                            stride = sides * ranks * count * rows_x
                            flat[pl.ds(at, wide, stride=stride), :] = value[start : start + wide]
                            start += wide
    for ref in outs:
        for side in range(1, sides):
            ref[:, side] = ref[:, 0]


def third_pass(density, wide, sides, ranks, counts):
    rows_x, rows_y, length = density.shape
    half = length // 2
    per_c = sum(counts)
    order = np.arange(half).reshape(wide, ranks, per_c).transpose(2, 1, 0).reshape(-1)
    angle = angles(order, np.arange(length), length)
    table = split_table(np.concatenate([np.cos(angle), -np.sin(angle)]))
    step = min(8, rows_x)

    def body(*refs):
        third_kernel(counts, *refs)

    return pl.pallas_call(
        body,
        grid=(rows_x // step,),
        in_specs=[
            whole(table.shape),
            pl.BlockSpec((step, rows_y, length), lambda i: (i, 0, 0)),
        ],
        out_specs=[
            pl.BlockSpec(
                (wide, sides, ranks, count, step, 2 * rows_y), lambda i: (0, 0, 0, 0, i, 0)
            )
            for count in counts
        ],
        out_shape=[
            pltpu.VMEM((wide, sides, ranks, count, rows_x, 2 * rows_y), jnp.float32)
            for count in counts
        ],
        compiler_params=params(1),
        cost_estimate=cost(density.size * length, 12 * density.size),
    )(in_hbm(table), in_hbm(density))


PAIR = 2


def turn(angle):
    cosine, sine = np.cos(angle), np.sin(angle)
    return np.block([[cosine, -sine], [sine, cosine]])


def spectrum_kernel(slab, groups, side_ref, wave_c_ref, a_ref, b_ref, second_ref, first_ref, back_ref, in_ref, *refs):
    outs = refs[-groups:]
    wide, narrow, _, rows_x, lanes = in_ref.shape
    length = wide * rows_x
    half = length // 2
    quarter = half // 2
    devices, tiles, message, tile = outs[0].shape
    count = slab // groups
    sign_back = 1.0 - 2.0 * side_ref[0].astype(jnp.float32)

    def column(c, n):
        return in_ref[:, n, c].reshape(length, lanes)

    def columns(numbers):
        return jnp.concatenate(
            [
                jnp.concatenate([column(c, n) for n in numbers], axis=1)
                for c in range(PAIR)
            ],
            axis=0,
        )

    low, high = columns(range(narrow // 2)), columns(range(narrow // 2, narrow))
    planes = [
        product(split(low + high), pair(second_ref.at[0])),
        product(split(low - high), pair(second_ref.at[1])),
    ]

    def stacked(sign):
        return jnp.concatenate(
            [
                jnp.concatenate(
                    [
                        plane[c * length : c * length + half, part * half : (part + 1) * half]
                        + sign
                        * plane[c * length + half : (c + 1) * length, part * half : (part + 1) * half]
                        for c in range(PAIR)
                        for plane in planes
                    ],
                    axis=1,
                )
                for part in range(2)
            ],
            axis=0,
        )

    squared_b, scale_b = b_ref[0], b_ref[1]
    field = []
    for parity, sign in ((0, 1.0), (1, -1.0)):
        value = product(pair(first_ref.at[parity]), split(stacked(sign)))
        smooth = []
        for c in range(PAIR):
            wave_c = wave_c_ref[pl.program_id(0) * PAIR + c]
            scale_c = wave_c_ref[wave_c_ref.shape[0] // 2 + pl.program_id(0) * PAIR + c]
            squared = a_ref[1, parity] + (squared_b + wave_c * wave_c)
            inverse = scale_c / jnp.where(squared > 0, squared, 1.0)
            smooth.append(jnp.where(squared > 0, inverse * scale_b, 0.0) * a_ref[2, parity])
        smooth = jnp.concatenate(smooth, axis=1)
        field.append(value * jnp.concatenate([smooth, smooth], axis=0))
    upper = lax.broadcasted_iota(jnp.int32, (devices, message, tile), 1) < count
    for number in range(3):
        folded = jnp.concatenate(
            [
                field[parity][part * half : part * half + quarter]
                + sign_back * field[parity][part * half + quarter : (part + 1) * half]
                for part in range(2)
                for parity in range(2)
            ],
            axis=0,
        )
        values = [
            product(
                pair(back_ref.at[0, c % back_ref.shape[1]]),
                split(folded[:, c * length : (c + 1) * length]),
            )
            for c in range(PAIR)
        ]
        for spot in range(tiles // 3):
            parity, part = divmod(spot, 2)
            at = number * (tiles // 3) + spot
            here = [
                value[part * half : (part + 1) * half, parity * tile : (parity + 1) * tile]
                for value in values
            ]
            if groups == 2:
                even, odd = [value.reshape(devices, message, tile) for value in here]
                outs[0][:, at] = jnp.where(upper, even, odd)
                outs[1][:, at] = jnp.where(upper, odd, even)
            else:
                flat = outs[0].reshape(devices * tiles * message, tile)
                for c in range(PAIR):
                    for x in range(slab):
                        start = at * message + c * count + x
                        flat[pl.ds(start, devices, stride=tiles * message), :] = here[c][
                            x * devices : (x + 1) * devices
                        ]
        if number < 2:
            for parity in range(2):
                wave_a = a_ref[0, parity]
                field[parity] = field[parity] * jnp.concatenate([wave_a, wave_a], axis=0)


def halves(length):
    return np.arange(length).reshape(length // 2, 2).T


def spectrum_pass(received, side, waves_c, devices, groups, steps, first_step, filled):
    wide, narrow, per_c, rows_x, lanes = received.shape
    length = wide * rows_x
    rows_y = lanes // 2
    half = length // 2
    near = np.arange(half)
    split_index = halves(length)
    slab = half // devices
    second, first, back = [], [], []
    if groups == 2:
        orders = [
            near.reshape(devices, 2, slab // 2)[:, ::step].reshape(-1) for step in (1, -1)
        ]
    else:
        orders = [near.reshape(devices, slab).T.reshape(-1)]
    for parity, index in enumerate(split_index):
        table = turn(-angles(index, near, length)).reshape(2, half, 2, narrow // 2, rows_y)
        second.append(split_table(table.transpose(3, 2, 4, 0, 1).reshape(length, length)))
        first.append(split_table(turn(-angles(index, near, length))))
        columns = split_index[:, : half // 2].reshape(-1)
        back.append(
            [split_table(turn(angles(2 * order + parity, columns, length))) for order in orders]
        )
    tables = [np.stack(second), np.stack(first), np.stack([np.stack(each) for each in back])]
    wave = signed_wave(split_index, length)
    scale = np.where(split_index == half, 0.0, np.exp(-0.5 * wave**2))
    a_table = np.stack([wave, wave**2, scale]).astype(np.float32)[..., None]
    b_table = np.stack([wave**2, scale]).astype(np.float32).reshape(2, 1, length)
    message = PAIR * slab // groups
    out_shape = (devices, 3 * 2 * length // TILE, steps * message, TILE)
    block = out_shape[:2] + (message, TILE)

    def body(*refs):
        spectrum_kernel(slab, groups, *refs)

    def fixed(shape):
        return pl.BlockSpec(shape, lambda *_: (0,) * len(shape))

    return pl.pallas_call(
        body,
        grid_spec=pltpu.PrefetchScalarGridSpec(
            num_scalar_prefetch=2,
            grid=(per_c // PAIR,),
            in_specs=[
                fixed(a_table.shape),
                fixed(b_table.shape),
                fixed(tables[0].shape),
                fixed(tables[1].shape),
                pl.BlockSpec((1,) + tables[2].shape[1:], lambda i, s, _: (s[0], 0, 0, 0, 0)),
                pl.BlockSpec((wide, narrow, PAIR, rows_x, lanes), lambda i, *_: (0, 0, i, 0, 0)),
                *[pl.BlockSpec(memory_space=pl.ANY)] * len(filled),
            ],
            out_specs=[pl.BlockSpec(block, lambda i, *_: (0, 0, first_step + i, 0))] * groups,
        ),
        out_shape=[pltpu.VMEM(out_shape, jnp.float32)] * groups,
        input_output_aliases={8 + spot: spot for spot in range(len(filled))},
        compiler_params=params(1),
        cost_estimate=cost(per_c * 7 * length**3, 20 * per_c * length**2 * 2),
    )(
        side,
        waves_c,
        *[in_hbm(table) for table in (a_table, b_table, *tables)],
        received,
        *[keep(each, pltpu.VMEM) for each in filled],
    )


def shear_kernel(
    per_c, group, joined, row_ref, lane_ref, second_ref, third_ref, ahead_ref, last_ref, in_ref, out_ref, shear_ref
):
    step = pl.program_id(0)
    length = shear_ref.shape[0]
    half = length // 2
    devices, tiles, message, tile = in_ref.shape
    count = message // per_c
    flat = in_ref.reshape(devices * tiles * message, tile)

    @pl.when(step == 0)
    def _():
        shear_ref[...] = jnp.zeros_like(shear_ref)

    field = jnp.concatenate(
        [
            jnp.concatenate(
                [
                    flat[pl.ds((source * tiles + spot) * message + x, per_c, stride=count), :]
                    for x in range(count)
                    for source in range(devices)
                ],
                axis=0,
            )
            for spot in range(tiles)
        ],
        axis=1,
    )
    field = field * row_ref[0] * lane_ref[0]
    even = product(split(field[:, :length]), pair(second_ref.at[0]))
    odd = product(split(field[:, length:]), pair(second_ref.at[1]))
    near, far = even + odd, even - odd
    field = jnp.concatenate(
        [
            jnp.concatenate(
                [
                    value[x * half : (x + 1) * half, part * half : (part + 1) * half]
                    for x in range(count)
                    for value in (near, far)
                ],
                axis=1,
            )
            for part in range(2)
        ],
        axis=0,
    )
    field = product(pair(third_ref), split(field))
    shear_ref[...] += field * field

    @pl.when(step == 5)
    def _():
        ahead = jnp.concatenate(
            [shear_ref[:, x * length : (x + 1) * length] for x in range(count)], axis=0
        )
        ahead = product(split(ahead), pair(ahead_ref))
        ahead = jnp.concatenate(
            [
                jnp.concatenate(
                    [
                        ahead[x * length : (x + 1) * length, part * length : (part + 1) * length]
                        for x in range(count)
                    ],
                    axis=1,
                )
                for part in range(2)
            ],
            axis=0,
        )
        value = product(pair(last_ref), split(ahead))
        wide, narrow, message_out, _ = out_ref.shape
        rows_b = length // wide
        slots = tile // rows_b
        rows = 2 * length // slots
        run = rows // (2 * narrow * joined)
        out = out_ref.reshape(wide * narrow * message_out, tile)
        lane = lax.broadcasted_iota(jnp.int32, (rows, tile), 1) // rows_b
        for x in range(count):
            for w in range(wide):
                block, place = divmod(w, slots)
                lanes = slice(x * length + block * tile, x * length + (block + 1) * tile)
                moved = None
                for slot in range(slots):
                    piece = value[slot * rows : (slot + 1) * rows, lanes]
                    if slot != place:
                        piece = pltpu.roll(piece, (slot - place) * rows_b % tile, 1)
                    moved = piece if moved is None else jnp.where(lane == slot, piece, moved)
                for n in range(narrow):
                    for part in range(2):
                        for join in range(joined):
                            start = ((n * 2 + part) * joined + join) * run
                            piece = moved[start : start + run]
                            at = (w * narrow + n) * message_out
                            if joined == 2:
                                at += part * 2 * count + (join ^ group) * count + x
                                out[pl.ds(at, run, stride=4 * count), :] = piece
                            else:
                                at += (x * 2 + part) * run
                                out[pl.ds(at, run), :] = piece


def shear_pass(received, wide, narrow, per_c, group, joined):
    devices, tiles, message, tile = received.shape
    count = message // per_c
    length = tiles * tile // 6
    half = length // 2
    index = np.arange(length)
    angle = angles(index, index, length)
    cosine, sine = np.cos(angle), np.sin(angle)
    split_index = halves(length)
    second = np.stack(
        [split_table(turn(angles(np.arange(half), b, length)).T) for b in split_index]
    )
    row_c = np.arange(half) ^ group
    weight = np.where(row_c == 0, 1.0, 2.0)
    angle = angles(index, row_c, length)
    third = np.concatenate([weight * np.cos(angle), -weight * np.sin(angle)], axis=1)
    ahead = np.concatenate([cosine, -sine], axis=1)
    slots = TILE * wide // length
    order = index.reshape(narrow, -1, joined, slots).transpose(3, 0, 2, 1)
    angle = angles(order.reshape(-1), index, length)
    last = np.stack(
        [
            np.concatenate([np.cos(angle), np.sin(angle)], axis=1),
            np.concatenate([-np.sin(angle), np.cos(angle)], axis=1),
        ]
    )
    last = last.reshape(2, slots, narrow, -1, 2 * length).transpose(1, 2, 0, 3, 4)
    last = last.reshape(2 * length, 2 * length)
    wave = signed_wave(index, length)
    wave_rows = np.tile(wave[row_c], count)
    wave_lanes = np.stack([wave[split_index]] * 2, axis=1).reshape(-1)
    twice = math.sqrt(2.0)
    one_row, one_lane = np.ones_like(wave_rows), np.ones_like(wave_lanes)
    row_factor = np.stack(
        [one_row, twice * one_row, twice * wave_rows, one_row, twice * wave_rows, wave_rows**2]
    ).astype(np.float32)[:, :, None]
    lane_factor = np.stack(
        [one_lane, wave_lanes, one_lane, wave_lanes**2, wave_lanes, one_lane]
    ).astype(np.float32)[:, None, :]
    tables = [second] + [split_table(table) for table in (third, ahead, last)]
    out_shape = (wide, narrow, count * 2 * length // (narrow * slots), TILE)

    def body(*refs):
        shear_kernel(per_c, group, joined, *refs)

    def which(i):
        return (0, 2 - (i >= 1).astype(jnp.int32) - (i >= 3).astype(jnp.int32), 0, 0)

    return pl.pallas_call(
        body,
        grid=(6,),
        in_specs=[
            pl.BlockSpec((1, count * half, 1), lambda i: (i, 0, 0)),
            pl.BlockSpec((1, 1, 2 * length), lambda i: (i, 0, 0)),
            *[whole(table.shape) for table in tables],
            pl.BlockSpec((devices, tiles // 3, message, tile), which),
        ],
        out_specs=whole(out_shape),
        out_shape=pltpu.VMEM(out_shape, jnp.float32),
        scratch_shapes=[pltpu.VMEM((length, count * length), jnp.float32)],
        compiler_params=params(1),
        cost_estimate=cost(count * 18 * length**3, 4 * received.size + 4 * 2**20),
    )(*[in_hbm(value) for value in (row_factor, lane_factor, *tables)], received)


def first_kernel(count, rows_b, anchor_ref, table_ref, *refs):
    ins, (real_ref, imag_ref) = refs[:-2], refs[-2:]
    wide, sides, ranks, rows, lanes = ins[0].shape
    length = real_ref.shape[2]
    half = length // 2
    slots = lanes // rows_b
    joined = len(ins)
    steps = real_ref.shape[0] // (slots * joined)
    spot_row = lax.broadcasted_iota(jnp.int32, (lanes, half), 0)
    spot_a = lax.broadcasted_iota(jnp.int32, (lanes, half), 1)
    is_anchor = (anchor_ref[0] == 1) & (pl.program_id(0) == 0)
    anchor = (spot_row == 0) & (spot_a == 0) & is_anchor
    upper = lax.broadcasted_iota(jnp.int32, (wide * ranks, joined * count, lanes), 1) < count

    def gathered(side, step, join, part):
        if joined == 2:
            at = pl.ds((step * 2 + part) * 2 * count, 2 * count)
            own, other = [
                ref[:, side, :, at].reshape(wide * ranks, 2 * count, lanes)
                for ref in (ins if join == 0 else ins[::-1])
            ]
            return jnp.where(upper, own, other).reshape(half, lanes)
        flat = ins[0].reshape(wide * sides * ranks * rows, lanes)
        run = rows // count
        return jnp.concatenate(
            [
                flat[
                    pl.ds((w * sides + side) * ranks * rows + part * steps + step, ranks * count, stride=run),
                    :,
                ]
                for w in range(wide)
            ],
            axis=0,
        )

    for join in range(joined):
        sums = []
        for side in range(sides):
            left = jnp.concatenate(
                [
                    jnp.concatenate([gathered(side, step, join, part).T for part in range(2)], axis=1)
                    for step in range(steps)
                ],
                axis=0,
            )
            sums.append(product(split(left), pair(table_ref.at[join, side])))
        even, odd = sums
        for far, value in enumerate((even + odd, even - odd)):
            for step in range(steps):
                at = (step * joined + join) * slots
                columns = slice(far * half, (far + 1) * half)
                for part, ref in enumerate((real_ref, imag_ref)):
                    here = value[step * lanes : (step + 1) * lanes, part * half : (part + 1) * half]
                    if at == 0 and far == 0:
                        here = jnp.where(anchor, 0.0, here)
                    ref[at : at + slots, :, columns] = here.reshape(slots, rows_b, half)


def first_pass(parts, is_anchor, length, wide, sides, count):
    devices, rows, lanes = parts[0].shape
    joined = len(parts)
    ranks = devices // wide // sides
    rows_b = length // wide
    slots = lanes // rows_b
    scale = 1.0 / float(length) ** 1.5
    index = np.arange(length).reshape(wide * ranks, joined, count, sides)
    tables = []
    for join in range(joined):
        order = index[:, :: 1 - 2 * join].transpose(3, 0, 1, 2).reshape(sides, -1)
        tables.append(
            [split_table(scale * turn(-angles(np.arange(length // 2), x, length)).T) for x in order]
        )
    table = np.stack([np.stack(each) for each in tables])
    total = rows // (2 * joined * count) if joined == 2 else rows // (2 * count)
    grid = 4 if joined == 2 and total % 4 == 0 else 1
    parts = [part.reshape(wide, sides, ranks, rows, lanes) for part in parts]

    def body(*refs):
        first_kernel(count, rows_b, *refs)

    rows_c = total * joined * slots
    out_shape = jax.ShapeDtypeStruct((rows_c, rows_b, length), jnp.float32)
    return pl.pallas_call(
        body,
        grid=(grid,),
        in_specs=[
            pl.BlockSpec(memory_space=pltpu.SMEM),
            whole(table.shape),
            *[pl.BlockSpec((wide, sides, ranks, rows // grid, lanes), lambda i: (0, 0, 0, i, 0))]
            * joined,
        ],
        out_specs=[pl.BlockSpec((rows_c // grid, rows_b, length), lambda i: (i, 0, 0))] * 2,
        out_shape=[out_shape] * 2,
        compiler_params=params(1),
        cost_estimate=cost(rows_c * 2 * rows_b * length * length, 16 * rows_c * rows_b * length),
    )(is_anchor, table, *[keep(part, pltpu.VMEM) for part in parts])


def transpose(value, members=None):
    return lax.all_to_all(
        value, AXES, split_axis=0, concat_axis=0, tiled=True, axis_index_groups=members
    )


def solution(mesh):
    wide, narrow = mesh.shape["wide"], mesh.shape["narrow"]
    sides = 2
    ranks = narrow // sides
    devices = wide * ranks
    members = [
        [w * narrow + side * ranks + rank for w in range(wide) for rank in range(ranks)]
        for side in range(sides)
    ]

    def per_device(density):
        rows_x, rows_y, length = density.shape
        half = length // 2
        per_c = half // devices
        slab = half // devices
        steps = per_c // PAIR
        counts = [per_c - PAIR, PAIR] if steps > 1 else [per_c]
        groups = 2 if slab > 2 else 1
        spot_wide, spot_narrow = lax.axis_index("wide"), lax.axis_index("narrow")
        side = (spot_narrow // ranks).astype(jnp.int32).reshape(1)
        rank = spot_wide * ranks + spot_narrow % ranks
        waves_c = (rank * per_c + jnp.arange(per_c, dtype=jnp.int32)).astype(jnp.float32)
        waves_c = waves_c * (2.0 * math.pi / length)
        scales_c = jnp.exp(-0.5 * waves_c * waves_c) * (1.0 / float(length) ** 3)
        chunks, start = [], 0
        for planes, count in zip(third_pass(density, wide, sides, ranks, counts), counts):
            planes = transpose(planes.reshape(wide * narrow, count, rows_x, 2 * rows_y))
            planes = planes.reshape(wide, narrow, count, rows_x, 2 * rows_y)
            spots = slice(start, start + count)
            both_c = jnp.concatenate([waves_c[spots], scales_c[spots]])
            planes = keep(planes, pltpu.VMEM if start else pltpu.HBM)
            chunks = spectrum_pass(
                planes, side, both_c, devices, groups, steps, start // PAIR, chunks
            )
            start += count
        is_anchor = ((spot_wide == 0) & (spot_narrow == 0)).astype(jnp.int32).reshape(1)
        parts = []
        for group, chunk in enumerate(chunks):
            received = keep(transpose(chunk, members), pltpu.VMEM if group else pltpu.HBM)
            part = shear_pass(received, wide, narrow, per_c, group, groups)
            parts.append(transpose(part.reshape((wide * narrow,) + part.shape[2:])))
        return tuple(first_pass(parts, is_anchor, length, wide, sides, slab // groups))

    return jax.shard_map(
        per_device,
        mesh=mesh,
        in_specs=(P("wide", "narrow", None),),
        out_specs=(P("narrow", "wide", None), P("narrow", "wide", None)),
        check_vma=False,
    )
```

```python
import math

import jax
import jax.numpy as jnp
import ml_dtypes
import numpy as np
from jax import lax
from jax.experimental import pallas as pl
from jax.experimental.pallas import tpu as pltpu
from jax.sharding import PartitionSpec as P

AXES = ("wide", "narrow")
TILE = 128
LIMIT = 16 * 1024 * 1024


def angles(rows, columns, length):
    return (2.0 * math.pi / length) * (np.outer(rows, columns) % length)


def split_table(table):
    table = np.asarray(table, np.float64)
    high = table.astype(ml_dtypes.bfloat16)
    low = (table - high.astype(np.float64)).astype(ml_dtypes.bfloat16)
    return np.stack([high, low])


def split(value):
    high = value.astype(jnp.bfloat16)
    low = (value - high.astype(jnp.float32)).astype(jnp.bfloat16)
    return high, low


def product(left, right, contract=((1,), (0,))):
    (left_axis,), (right_axis,) = contract
    left = jnp.concatenate([left[0], left[0], left[1]], axis=left_axis)
    right = jnp.concatenate([right[0], right[1], right[0]], axis=right_axis)
    return lax.dot_general(
        left, right, (contract, ((), ())), preferred_element_type=jnp.float32
    )


def pair(ref):
    return ref[0], ref[1]


def signed_wave(index, length):
    index = np.asarray(index)
    return np.where(index < length // 2, index, index - length) * (2.0 * math.pi / length)


def params(steps):
    return pltpu.CompilerParams(
        vmem_limit_bytes=LIMIT, dimension_semantics=("arbitrary",) * steps
    )


def whole(shape):
    return pl.BlockSpec(shape, lambda *_: (0,) * len(shape))


def keep(value, space):
    return pltpu.with_memory_space_constraint(jnp.asarray(value), space)


def in_hbm(value):
    return keep(value, pltpu.HBM)


def cost(macs, moved):
    return pl.CostEstimate(flops=6 * macs, bytes_accessed=moved, transcendentals=0)


def third_kernel(counts, table_ref, density_ref, *outs):
    rows_x, rows_y, length = density_ref.shape
    wide, sides, ranks = outs[0].shape[:3]
    half = length // 2
    flats = [ref.reshape(math.prod(ref.shape[:5]), 2 * rows_y) for ref in outs]
    table = pair(table_ref)
    left_half = lax.broadcasted_iota(jnp.int32, (half, 2 * rows_y), 1) < rows_y
    group = 4
    for first in range(0, rows_x, group):
        block = density_ref[first : first + group].reshape(group * rows_y, length)
        result = product(table, split(block), ((1,), (1,)))
        for inner in range(0, group, 2):
            lanes = slice(inner * rows_y, (inner + 2) * rows_y)
            real = result[:half, lanes]
            imag = result[half:, lanes]
            even = jnp.where(left_half, real, pltpu.roll(imag, rows_y, 1))
            odd = jnp.where(left_half, pltpu.roll(real, rows_y, 1), imag)
            for x, value in ((first + inner, even), (first + inner + 1, odd)):
                start = 0
                for flat, count in zip(flats, counts):
                    for c in range(count):
                        for rank in range(ranks):
                            at = (rank * count + c) * rows_x + x
                            stride = sides * ranks * count * rows_x
                            flat[pl.ds(at, wide, stride=stride), :] = value[start : start + wide]
                            start += wide
    for ref in outs:
        for side in range(1, sides):
            ref[:, side] = ref[:, 0]


def third_pass(density, wide, sides, ranks, counts):
    rows_x, rows_y, length = density.shape
    half = length // 2
    per_c = sum(counts)
    order = np.arange(half).reshape(wide, ranks, per_c).transpose(2, 1, 0).reshape(-1)
    angle = angles(order, np.arange(length), length)
    table = split_table(np.concatenate([np.cos(angle), -np.sin(angle)]))
    step = min(8, rows_x)

    def body(*refs):
        third_kernel(counts, *refs)

    return pl.pallas_call(
        body,
        grid=(rows_x // step,),
        in_specs=[
            whole(table.shape),
            pl.BlockSpec((step, rows_y, length), lambda i: (i, 0, 0)),
        ],
        out_specs=[
            pl.BlockSpec(
                (wide, sides, ranks, count, step, 2 * rows_y), lambda i: (0, 0, 0, 0, i, 0)
            )
            for count in counts
        ],
        out_shape=[
            pltpu.VMEM((wide, sides, ranks, count, rows_x, 2 * rows_y), jnp.float32)
            for count in counts
        ],
        compiler_params=params(1),
        cost_estimate=cost(density.size * length, 12 * density.size),
    )(in_hbm(table), in_hbm(density))


PAIR = 2


def turn(angle):
    cosine, sine = np.cos(angle), np.sin(angle)
    return np.block([[cosine, -sine], [sine, cosine]])


def spectrum_kernel(slab, groups, first_c, side_ref, start_ref, a_ref, b_ref, second_ref, first_ref, back_ref, in_ref, *refs):
    outs = refs[-groups:]
    wide, narrow, _, rows_x, lanes = in_ref.shape
    length = wide * rows_x
    half = length // 2
    quarter = half // 2
    devices, tiles, message, tile = outs[0].shape
    count = slab // groups
    sign_back = 1.0 - 2.0 * side_ref[0].astype(jnp.float32)

    def column(c, n):
        return in_ref[:, n, c].reshape(length, lanes)

    def columns(numbers):
        return jnp.concatenate(
            [
                jnp.concatenate([column(c, n) for n in numbers], axis=1)
                for c in range(PAIR)
            ],
            axis=0,
        )

    low, high = columns(range(narrow // 2)), columns(range(narrow // 2, narrow))
    planes = [
        product(split(low + high), pair(second_ref.at[0])),
        product(split(low - high), pair(second_ref.at[1])),
    ]

    def stacked(sign):
        return jnp.concatenate(
            [
                jnp.concatenate(
                    [
                        plane[c * length : c * length + half, part * half : (part + 1) * half]
                        + sign
                        * plane[c * length + half : (c + 1) * length, part * half : (part + 1) * half]
                        for c in range(PAIR)
                        for plane in planes
                    ],
                    axis=1,
                )
                for part in range(2)
            ],
            axis=0,
        )

    squared_b, scale_b = b_ref[0], b_ref[1]
    field = []
    for parity, sign in ((0, 1.0), (1, -1.0)):
        value = product(pair(first_ref.at[parity]), split(stacked(sign)))
        smooth = []
        for c in range(PAIR):
            spot_c = start_ref[0] + (first_c + pl.program_id(0) * PAIR + c)
            wave_c = jnp.full_like(squared_b, spot_c.astype(jnp.float32)) * (2.0 * math.pi / length)
            scale_c = jnp.exp(-0.5 * wave_c * wave_c) * (1.0 / float(length) ** 3)
            squared = a_ref[1, parity] + (squared_b + wave_c * wave_c)
            inverse = scale_c / jnp.where(squared > 0, squared, 1.0)
            smooth.append(jnp.where(squared > 0, inverse * scale_b, 0.0) * a_ref[2, parity])
        smooth = jnp.concatenate(smooth, axis=1)
        field.append(value * jnp.concatenate([smooth, smooth], axis=0))
    upper = lax.broadcasted_iota(jnp.int32, (devices, message, tile), 1) < count
    for number in range(3):
        folded = jnp.concatenate(
            [
                field[parity][part * half : part * half + quarter]
                + sign_back * field[parity][part * half + quarter : (part + 1) * half]
                for part in range(2)
                for parity in range(2)
            ],
            axis=0,
        )
        values = [
            product(
                pair(back_ref.at[0, c % back_ref.shape[1]]),
                split(folded[:, c * length : (c + 1) * length]),
            )
            for c in range(PAIR)
        ]
        for spot in range(tiles // 3):
            parity, part = divmod(spot, 2)
            at = number * (tiles // 3) + spot
            here = [
                value[part * half : (part + 1) * half, parity * tile : (parity + 1) * tile]
                for value in values
            ]
            if groups == 2:
                even, odd = [value.reshape(devices, message, tile) for value in here]
                outs[0][:, at] = jnp.where(upper, even, odd)
                outs[1][:, at] = jnp.where(upper, odd, even)
            else:
                flat = outs[0].reshape(devices * tiles * message, tile)
                for c in range(PAIR):
                    for x in range(slab):
                        start = at * message + c * count + x
                        flat[pl.ds(start, devices, stride=tiles * message), :] = here[c][
                            x * devices : (x + 1) * devices
                        ]
        if number < 2:
            for parity in range(2):
                wave_a = a_ref[0, parity]
                field[parity] = field[parity] * jnp.concatenate([wave_a, wave_a], axis=0)


def halves(length):
    return np.arange(length).reshape(length // 2, 2).T


def spectrum_pass(received, side, start_c, devices, groups, steps, first_step, filled):
    wide, narrow, per_c, rows_x, lanes = received.shape
    length = wide * rows_x
    rows_y = lanes // 2
    half = length // 2
    near = np.arange(half)
    split_index = halves(length)
    slab = half // devices
    second, first, back = [], [], []
    if groups == 2:
        orders = [
            near.reshape(devices, 2, slab // 2)[:, ::step].reshape(-1) for step in (1, -1)
        ]
    else:
        orders = [near.reshape(devices, slab).T.reshape(-1)]
    for parity, index in enumerate(split_index):
        table = turn(-angles(index, near, length)).reshape(2, half, 2, narrow // 2, rows_y)
        second.append(split_table(table.transpose(3, 2, 4, 0, 1).reshape(length, length)))
        first.append(split_table(turn(-angles(index, near, length))))
        columns = split_index[:, : half // 2].reshape(-1)
        back.append(
            [split_table(turn(angles(2 * order + parity, columns, length))) for order in orders]
        )
    tables = [np.stack(second), np.stack(first), np.stack([np.stack(each) for each in back])]
    wave = signed_wave(split_index, length)
    scale = np.where(split_index == half, 0.0, np.exp(-0.5 * wave**2))
    a_table = np.stack([wave, wave**2, scale]).astype(np.float32)[..., None]
    b_table = np.stack([wave**2, scale]).astype(np.float32).reshape(2, 1, length)
    message = PAIR * slab // groups
    out_shape = (devices, 3 * 2 * length // TILE, steps * message, TILE)
    block = out_shape[:2] + (message, TILE)

    def body(*refs):
        spectrum_kernel(slab, groups, first_step * PAIR, *refs)

    def fixed(shape):
        return pl.BlockSpec(shape, lambda *_: (0,) * len(shape))

    return pl.pallas_call(
        body,
        grid_spec=pltpu.PrefetchScalarGridSpec(
            num_scalar_prefetch=2,
            grid=(per_c // PAIR,),
            in_specs=[
                fixed(a_table.shape),
                fixed(b_table.shape),
                fixed(tables[0].shape),
                fixed(tables[1].shape),
                pl.BlockSpec((1,) + tables[2].shape[1:], lambda i, s, _: (s[0], 0, 0, 0, 0)),
                pl.BlockSpec((wide, narrow, PAIR, rows_x, lanes), lambda i, *_: (0, 0, i, 0, 0)),
                *[pl.BlockSpec(memory_space=pl.ANY)] * len(filled),
            ],
            out_specs=[pl.BlockSpec(block, lambda i, *_: (0, 0, first_step + i, 0))] * groups,
        ),
        out_shape=[pltpu.VMEM(out_shape, jnp.float32)] * groups,
        input_output_aliases={8 + spot: spot for spot in range(len(filled))},
        compiler_params=params(1),
        cost_estimate=cost(per_c * 7 * length**3, 20 * per_c * length**2 * 2),
    )(
        side,
        start_c,
        *[in_hbm(table) for table in (a_table, b_table, *tables)],
        received,
        *[keep(each, pltpu.VMEM) for each in filled],
    )


def shear_kernel(
    per_c, group, joined, row_ref, lane_ref, second_ref, third_ref, ahead_ref, last_ref, in_ref, out_ref, shear_ref
):
    step = pl.program_id(0)
    length = shear_ref.shape[0]
    half = length // 2
    devices, tiles, message, tile = in_ref.shape
    count = message // per_c
    flat = in_ref.reshape(devices * tiles * message, tile)

    @pl.when(step == 0)
    def _():
        shear_ref[...] = jnp.zeros_like(shear_ref)

    field = jnp.concatenate(
        [
            jnp.concatenate(
                [
                    flat[pl.ds((source * tiles + spot) * message + x, per_c, stride=count), :]
                    for x in range(count)
                    for source in range(devices)
                ],
                axis=0,
            )
            for spot in range(tiles)
        ],
        axis=1,
    )
    field = field * row_ref[0] * lane_ref[0]
    even = product(split(field[:, :length]), pair(second_ref.at[0]))
    odd = product(split(field[:, length:]), pair(second_ref.at[1]))
    near, far = even + odd, even - odd
    field = jnp.concatenate(
        [
            jnp.concatenate(
                [
                    value[x * half : (x + 1) * half, part * half : (part + 1) * half]
                    for x in range(count)
                    for value in (near, far)
                ],
                axis=1,
            )
            for part in range(2)
        ],
        axis=0,
    )
    field = product(pair(third_ref), split(field))
    shear_ref[...] += field * field

    @pl.when(step == 5)
    def _():
        ahead = jnp.concatenate(
            [shear_ref[:, x * length : (x + 1) * length] for x in range(count)], axis=0
        )
        ahead = product(split(ahead), pair(ahead_ref))
        ahead = jnp.concatenate(
            [
                jnp.concatenate(
                    [
                        ahead[x * length : (x + 1) * length, part * length : (part + 1) * length]
                        for x in range(count)
                    ],
                    axis=1,
                )
                for part in range(2)
            ],
            axis=0,
        )
        value = product(pair(last_ref), split(ahead))
        wide, narrow, message_out, _ = out_ref.shape
        rows_b = length // wide
        slots = tile // rows_b
        rows = 2 * length // slots
        run = rows // (2 * narrow * joined)
        out = out_ref.reshape(wide * narrow * message_out, tile)
        lane = lax.broadcasted_iota(jnp.int32, (rows, tile), 1) // rows_b
        for x in range(count):
            for w in range(wide):
                block, place = divmod(w, slots)
                lanes = slice(x * length + block * tile, x * length + (block + 1) * tile)
                moved = None
                for slot in range(slots):
                    piece = value[slot * rows : (slot + 1) * rows, lanes]
                    if slot != place:
                        piece = pltpu.roll(piece, (slot - place) * rows_b % tile, 1)
                    moved = piece if moved is None else jnp.where(lane == slot, piece, moved)
                for n in range(narrow):
                    for part in range(2):
                        for join in range(joined):
                            start = ((n * 2 + part) * joined + join) * run
                            piece = moved[start : start + run]
                            at = (w * narrow + n) * message_out
                            if joined == 2:
                                at += part * 2 * count + (join ^ group) * count + x
                                out[pl.ds(at, run, stride=4 * count), :] = piece
                            else:
                                at += (x * 2 + part) * run
                                out[pl.ds(at, run), :] = piece


def shear_pass(received, wide, narrow, per_c, group, joined):
    devices, tiles, message, tile = received.shape
    count = message // per_c
    length = tiles * tile // 6
    half = length // 2
    index = np.arange(length)
    angle = angles(index, index, length)
    cosine, sine = np.cos(angle), np.sin(angle)
    split_index = halves(length)
    second = np.stack(
        [split_table(turn(angles(np.arange(half), b, length)).T) for b in split_index]
    )
    row_c = np.arange(half) ^ group
    weight = np.where(row_c == 0, 1.0, 2.0)
    angle = angles(index, row_c, length)
    third = np.concatenate([weight * np.cos(angle), -weight * np.sin(angle)], axis=1)
    ahead = np.concatenate([cosine, -sine], axis=1)
    slots = TILE * wide // length
    order = index.reshape(narrow, -1, joined, slots).transpose(3, 0, 2, 1)
    angle = angles(order.reshape(-1), index, length)
    last = np.stack(
        [
            np.concatenate([np.cos(angle), np.sin(angle)], axis=1),
            np.concatenate([-np.sin(angle), np.cos(angle)], axis=1),
        ]
    )
    last = last.reshape(2, slots, narrow, -1, 2 * length).transpose(1, 2, 0, 3, 4)
    last = last.reshape(2 * length, 2 * length)
    wave = signed_wave(index, length)
    wave_rows = np.tile(wave[row_c], count)
    wave_lanes = np.stack([wave[split_index]] * 2, axis=1).reshape(-1)
    twice = math.sqrt(2.0)
    one_row, one_lane = np.ones_like(wave_rows), np.ones_like(wave_lanes)
    row_factor = np.stack(
        [one_row, twice * one_row, twice * wave_rows, one_row, twice * wave_rows, wave_rows**2]
    ).astype(np.float32)[:, :, None]
    lane_factor = np.stack(
        [one_lane, wave_lanes, one_lane, wave_lanes**2, wave_lanes, one_lane]
    ).astype(np.float32)[:, None, :]
    tables = [second] + [split_table(table) for table in (third, ahead, last)]
    out_shape = (wide, narrow, count * 2 * length // (narrow * slots), TILE)

    def body(*refs):
        shear_kernel(per_c, group, joined, *refs)

    def which(i):
        return (0, 2 - (i >= 1).astype(jnp.int32) - (i >= 3).astype(jnp.int32), 0, 0)

    return pl.pallas_call(
        body,
        grid=(6,),
        in_specs=[
            pl.BlockSpec((1, count * half, 1), lambda i: (i, 0, 0)),
            pl.BlockSpec((1, 1, 2 * length), lambda i: (i, 0, 0)),
            *[whole(table.shape) for table in tables],
            pl.BlockSpec((devices, tiles // 3, message, tile), which),
        ],
        out_specs=whole(out_shape),
        out_shape=pltpu.VMEM(out_shape, jnp.float32),
        scratch_shapes=[pltpu.VMEM((length, count * length), jnp.float32)],
        compiler_params=params(1),
        cost_estimate=cost(count * 18 * length**3, 4 * received.size + 4 * 2**20),
    )(*[in_hbm(value) for value in (row_factor, lane_factor, *tables)], received)


def first_kernel(count, rows_b, anchor_ref, table_ref, *refs):
    ins, (real_ref, imag_ref) = refs[:-2], refs[-2:]
    wide, sides, ranks, rows, lanes = ins[0].shape
    length = real_ref.shape[2]
    half = length // 2
    slots = lanes // rows_b
    joined = len(ins)
    steps = real_ref.shape[0] // (slots * joined)
    spot_row = lax.broadcasted_iota(jnp.int32, (lanes, half), 0)
    spot_a = lax.broadcasted_iota(jnp.int32, (lanes, half), 1)
    is_anchor = (anchor_ref[0] == 1) & (pl.program_id(0) == 0)
    anchor = (spot_row == 0) & (spot_a == 0) & is_anchor
    upper = lax.broadcasted_iota(jnp.int32, (wide * ranks, joined * count, lanes), 1) < count

    def gathered(side, step, join, part):
        if joined == 2:
            at = pl.ds((step * 2 + part) * 2 * count, 2 * count)
            own, other = [
                ref[:, side, :, at].reshape(wide * ranks, 2 * count, lanes)
                for ref in (ins if join == 0 else ins[::-1])
            ]
            return jnp.where(upper, own, other).reshape(half, lanes)
        flat = ins[0].reshape(wide * sides * ranks * rows, lanes)
        run = rows // count
        return jnp.concatenate(
            [
                flat[
                    pl.ds((w * sides + side) * ranks * rows + part * steps + step, ranks * count, stride=run),
                    :,
                ]
                for w in range(wide)
            ],
            axis=0,
        )

    for join in range(joined):
        sums = []
        for side in range(sides):
            left = jnp.concatenate(
                [
                    jnp.concatenate([gathered(side, step, join, part).T for part in range(2)], axis=1)
                    for step in range(steps)
                ],
                axis=0,
            )
            sums.append(product(split(left), pair(table_ref.at[join, side])))
        even, odd = sums
        for far, value in enumerate((even + odd, even - odd)):
            for step in range(steps):
                at = (step * joined + join) * slots
                columns = slice(far * half, (far + 1) * half)
                for part, ref in enumerate((real_ref, imag_ref)):
                    here = value[step * lanes : (step + 1) * lanes, part * half : (part + 1) * half]
                    if at == 0 and far == 0:
                        here = jnp.where(anchor, 0.0, here)
                    ref[at : at + slots, :, columns] = here.reshape(slots, rows_b, half)


def first_pass(parts, is_anchor, length, wide, sides, count):
    devices, rows, lanes = parts[0].shape
    joined = len(parts)
    ranks = devices // wide // sides
    rows_b = length // wide
    slots = lanes // rows_b
    scale = 1.0 / float(length) ** 1.5
    index = np.arange(length).reshape(wide * ranks, joined, count, sides)
    tables = []
    for join in range(joined):
        order = index[:, :: 1 - 2 * join].transpose(3, 0, 1, 2).reshape(sides, -1)
        tables.append(
            [split_table(scale * turn(-angles(np.arange(length // 2), x, length)).T) for x in order]
        )
    table = np.stack([np.stack(each) for each in tables])
    total = rows // (2 * joined * count) if joined == 2 else rows // (2 * count)
    grid = 4 if joined == 2 and total % 4 == 0 else 1
    parts = [part.reshape(wide, sides, ranks, rows, lanes) for part in parts]

    def body(*refs):
        first_kernel(count, rows_b, *refs)

    rows_c = total * joined * slots
    out_shape = jax.ShapeDtypeStruct((rows_c, rows_b, length), jnp.float32)
    return pl.pallas_call(
        body,
        grid=(grid,),
        in_specs=[
            pl.BlockSpec(memory_space=pltpu.SMEM),
            whole(table.shape),
            *[pl.BlockSpec((wide, sides, ranks, rows // grid, lanes), lambda i: (0, 0, 0, i, 0))]
            * joined,
        ],
        out_specs=[pl.BlockSpec((rows_c // grid, rows_b, length), lambda i: (i, 0, 0))] * 2,
        out_shape=[out_shape] * 2,
        compiler_params=params(1),
        cost_estimate=cost(rows_c * 2 * rows_b * length * length, 16 * rows_c * rows_b * length),
    )(is_anchor, table, *[keep(part, pltpu.VMEM) for part in parts])


def transpose(value, members=None):
    return lax.all_to_all(
        value, AXES, split_axis=0, concat_axis=0, tiled=True, axis_index_groups=members
    )


def solution(mesh):
    wide, narrow = mesh.shape["wide"], mesh.shape["narrow"]
    sides = 2
    ranks = narrow // sides
    devices = wide * ranks
    members = [
        [w * narrow + side * ranks + rank for w in range(wide) for rank in range(ranks)]
        for side in range(sides)
    ]

    def per_device(density):
        rows_x, rows_y, length = density.shape
        half = length // 2
        per_c = half // devices
        slab = half // devices
        steps = per_c // PAIR
        counts = [per_c - PAIR, PAIR] if steps > 1 else [per_c]
        groups = 2 if slab > 2 else 1
        spot_wide, spot_narrow = lax.axis_index("wide"), lax.axis_index("narrow")
        side = (spot_narrow // ranks).astype(jnp.int32).reshape(1)
        rank = spot_wide * ranks + spot_narrow % ranks
        start_c = (rank * per_c).astype(jnp.int32).reshape(1)
        chunks, start = [], 0
        for planes, count in zip(third_pass(density, wide, sides, ranks, counts), counts):
            planes = transpose(planes.reshape(wide * narrow, count, rows_x, 2 * rows_y))
            planes = planes.reshape(wide, narrow, count, rows_x, 2 * rows_y)
            planes = keep(planes, pltpu.VMEM)
            chunks = spectrum_pass(
                planes, side, start_c, devices, groups, steps, start // PAIR, chunks
            )
            start += count
        is_anchor = ((spot_wide == 0) & (spot_narrow == 0)).astype(jnp.int32).reshape(1)
        parts = []
        for group, chunk in enumerate(chunks):
            received = keep(transpose(chunk, members), pltpu.VMEM)
            part = shear_pass(received, wide, narrow, per_c, group, groups)
            parts.append(transpose(part.reshape((wide * narrow,) + part.shape[2:])))
        return tuple(first_pass(parts, is_anchor, length, wide, sides, slab // groups))

    return jax.shard_map(
        per_device,
        mesh=mesh,
        in_specs=(P("wide", "narrow", None),),
        out_specs=(P("narrow", "wide", None), P("narrow", "wide", None)),
        check_vma=False,
    )
```

```python
import math

import jax
import jax.numpy as jnp
import ml_dtypes
import numpy as np
from jax import lax
from jax.experimental import pallas as pl
from jax.experimental.pallas import tpu as pltpu
from jax.sharding import PartitionSpec as P

AXES = ("wide", "narrow")
TILE = 128
LIMIT = 16 * 1024 * 1024


def angles(rows, columns, length):
    return (2.0 * math.pi / length) * (np.outer(rows, columns) % length)


def split_table(table):
    table = np.asarray(table, np.float64)
    high = table.astype(ml_dtypes.bfloat16)
    low = (table - high.astype(np.float64)).astype(ml_dtypes.bfloat16)
    return np.stack([high, low])


def split(value):
    high = value.astype(jnp.bfloat16)
    low = (value - high.astype(jnp.float32)).astype(jnp.bfloat16)
    return high, low


def product(left, right, contract=((1,), (0,))):
    (left_axis,), (right_axis,) = contract
    left = jnp.concatenate([left[0], left[0], left[1]], axis=left_axis)
    right = jnp.concatenate([right[0], right[1], right[0]], axis=right_axis)
    return lax.dot_general(
        left, right, (contract, ((), ())), preferred_element_type=jnp.float32
    )


def pair(ref):
    return ref[0], ref[1]


def signed_wave(index, length):
    index = np.asarray(index)
    return np.where(index < length // 2, index, index - length) * (2.0 * math.pi / length)


def params(steps):
    return pltpu.CompilerParams(
        vmem_limit_bytes=LIMIT, dimension_semantics=("arbitrary",) * steps
    )


def whole(shape):
    return pl.BlockSpec(shape, lambda *_: (0,) * len(shape))


def keep(value, space):
    return pltpu.with_memory_space_constraint(jnp.asarray(value), space)


def in_hbm(value):
    return keep(value, pltpu.HBM)


def cost(macs, moved):
    return pl.CostEstimate(flops=6 * macs, bytes_accessed=moved, transcendentals=0)


def third_kernel(counts, table_ref, density_ref, *outs):
    step_x, rows_y, length = density_ref.shape
    wide, sides, ranks, _, rows_x, _ = outs[0].shape
    half = length // 2
    flats = [ref.reshape(math.prod(ref.shape[:5]), 2 * rows_y) for ref in outs]
    table = pair(table_ref)
    left_half = lax.broadcasted_iota(jnp.int32, (half, 2 * rows_y), 1) < rows_y
    group = 4
    start_x = pl.program_id(0) * step_x
    for first in range(0, step_x, group):
        block = density_ref[first : first + group].reshape(group * rows_y, length)
        result = product(table, split(block), ((1,), (1,)))
        for inner in range(0, group, 2):
            lanes = slice(inner * rows_y, (inner + 2) * rows_y)
            real = result[:half, lanes]
            imag = result[half:, lanes]
            even = jnp.where(left_half, real, pltpu.roll(imag, rows_y, 1))
            odd = jnp.where(left_half, pltpu.roll(real, rows_y, 1), imag)
            for x, value in ((first + inner, even), (first + inner + 1, odd)):
                start = 0
                for flat, count in zip(flats, counts):
                    for c in range(count):
                        for rank in range(ranks):
                            at = (rank * count + c) * rows_x + x + start_x
                            stride = sides * ranks * count * rows_x
                            flat[pl.ds(at, wide, stride=stride), :] = value[start : start + wide]
                            start += wide
    for ref in outs:
        rows = pl.ds(pl.multiple_of(start_x, step_x), step_x)
        for side in range(1, sides):
            ref[:, side, :, :, rows] = ref[:, 0, :, :, rows]


def third_pass(density, wide, sides, ranks, counts):
    rows_x, rows_y, length = density.shape
    half = length // 2
    per_c = sum(counts)
    order = np.arange(half).reshape(wide, ranks, per_c).transpose(2, 1, 0).reshape(-1)
    angle = angles(order, np.arange(length), length)
    table = split_table(np.concatenate([np.cos(angle), -np.sin(angle)]))
    step = min(8, rows_x)

    def body(*refs):
        third_kernel(counts, *refs)

    return pl.pallas_call(
        body,
        grid=(rows_x // step,),
        in_specs=[
            whole(table.shape),
            pl.BlockSpec((step, rows_y, length), lambda i: (i, 0, 0)),
        ],
        out_specs=[
            whole((wide, sides, ranks, count, rows_x, 2 * rows_y)) for count in counts
        ],
        out_shape=[
            pltpu.VMEM((wide, sides, ranks, count, rows_x, 2 * rows_y), jnp.float32)
            for count in counts
        ],
        compiler_params=params(1),
        cost_estimate=cost(density.size * length, 12 * density.size),
    )(in_hbm(table), in_hbm(density))


PAIR = 2


def turn(angle):
    cosine, sine = np.cos(angle), np.sin(angle)
    return np.block([[cosine, -sine], [sine, cosine]])


def spectrum_kernel(slab, groups, first_c, side_ref, start_ref, a_ref, b_ref, second_ref, first_ref, back_ref, in_ref, *refs):
    outs = refs[-groups:]
    wide, narrow, _, rows_x, lanes = in_ref.shape
    length = wide * rows_x
    half = length // 2
    quarter = half // 2
    devices, tiles, message, tile = outs[0].shape
    count = slab // groups
    sign_back = 1.0 - 2.0 * side_ref[0].astype(jnp.float32)

    def column(c, n):
        return in_ref[:, n, c].reshape(length, lanes)

    def columns(numbers):
        return jnp.concatenate(
            [
                jnp.concatenate([column(c, n) for n in numbers], axis=1)
                for c in range(PAIR)
            ],
            axis=0,
        )

    low, high = columns(range(narrow // 2)), columns(range(narrow // 2, narrow))
    planes = [
        product(split(low + high), pair(second_ref.at[0])),
        product(split(low - high), pair(second_ref.at[1])),
    ]

    def stacked(sign):
        return jnp.concatenate(
            [
                jnp.concatenate(
                    [
                        plane[c * length : c * length + half, part * half : (part + 1) * half]
                        + sign
                        * plane[c * length + half : (c + 1) * length, part * half : (part + 1) * half]
                        for c in range(PAIR)
                        for plane in planes
                    ],
                    axis=1,
                )
                for part in range(2)
            ],
            axis=0,
        )

    squared_b, scale_b = b_ref[0], b_ref[1]
    field = []
    for parity, sign in ((0, 1.0), (1, -1.0)):
        value = product(pair(first_ref.at[parity]), split(stacked(sign)))
        smooth = []
        for c in range(PAIR):
            spot_c = start_ref[0] + (first_c + pl.program_id(0) * PAIR + c)
            wave_c = jnp.full_like(squared_b, spot_c.astype(jnp.float32)) * (2.0 * math.pi / length)
            scale_c = jnp.exp(-0.5 * wave_c * wave_c) * (1.0 / float(length) ** 3)
            squared = a_ref[1, parity] + (squared_b + wave_c * wave_c)
            inverse = scale_c / jnp.where(squared > 0, squared, 1.0)
            smooth.append(jnp.where(squared > 0, inverse * scale_b, 0.0) * a_ref[2, parity])
        smooth = jnp.concatenate(smooth, axis=1)
        field.append(value * jnp.concatenate([smooth, smooth], axis=0))
    upper = lax.broadcasted_iota(jnp.int32, (devices, message, tile), 1) < count
    for number in range(3):
        folded = jnp.concatenate(
            [
                field[parity][part * half : part * half + quarter]
                + sign_back * field[parity][part * half + quarter : (part + 1) * half]
                for part in range(2)
                for parity in range(2)
            ],
            axis=0,
        )
        values = [
            product(
                pair(back_ref.at[0, c % back_ref.shape[1]]),
                split(folded[:, c * length : (c + 1) * length]),
            )
            for c in range(PAIR)
        ]
        for spot in range(tiles // 3):
            parity, part = divmod(spot, 2)
            at = number * (tiles // 3) + spot
            here = [
                value[part * half : (part + 1) * half, parity * tile : (parity + 1) * tile]
                for value in values
            ]
            if groups == 2:
                even, odd = [value.reshape(devices, message, tile) for value in here]
                outs[0][:, at] = jnp.where(upper, even, odd)
                outs[1][:, at] = jnp.where(upper, odd, even)
            else:
                flat = outs[0].reshape(devices * tiles * message, tile)
                for c in range(PAIR):
                    for x in range(slab):
                        start = at * message + c * count + x
                        flat[pl.ds(start, devices, stride=tiles * message), :] = here[c][
                            x * devices : (x + 1) * devices
                        ]
        if number < 2:
            for parity in range(2):
                wave_a = a_ref[0, parity]
                field[parity] = field[parity] * jnp.concatenate([wave_a, wave_a], axis=0)


def halves(length):
    return np.arange(length).reshape(length // 2, 2).T


def spectrum_pass(received, side, start_c, devices, groups, steps, first_step, filled):
    wide, narrow, per_c, rows_x, lanes = received.shape
    length = wide * rows_x
    rows_y = lanes // 2
    half = length // 2
    near = np.arange(half)
    split_index = halves(length)
    slab = half // devices
    second, first, back = [], [], []
    if groups == 2:
        orders = [
            near.reshape(devices, 2, slab // 2)[:, ::step].reshape(-1) for step in (1, -1)
        ]
    else:
        orders = [near.reshape(devices, slab).T.reshape(-1)]
    for parity, index in enumerate(split_index):
        table = turn(-angles(index, near, length)).reshape(2, half, 2, narrow // 2, rows_y)
        second.append(split_table(table.transpose(3, 2, 4, 0, 1).reshape(length, length)))
        first.append(split_table(turn(-angles(index, near, length))))
        columns = split_index[:, : half // 2].reshape(-1)
        back.append(
            [split_table(turn(angles(2 * order + parity, columns, length))) for order in orders]
        )
    tables = [np.stack(second), np.stack(first), np.stack([np.stack(each) for each in back])]
    wave = signed_wave(split_index, length)
    scale = np.where(split_index == half, 0.0, np.exp(-0.5 * wave**2))
    a_table = np.stack([wave, wave**2, scale]).astype(np.float32)[..., None]
    b_table = np.stack([wave**2, scale]).astype(np.float32).reshape(2, 1, length)
    message = PAIR * slab // groups
    spaces = [pltpu.VMEM, pltpu.HBM][:groups]
    out_shape = (devices, 3 * 2 * length // TILE, steps * message, TILE)
    block = out_shape[:2] + (message, TILE)

    def body(*refs):
        spectrum_kernel(slab, groups, first_step * PAIR, *refs)

    def fixed(shape):
        return pl.BlockSpec(shape, lambda *_: (0,) * len(shape))

    return pl.pallas_call(
        body,
        grid_spec=pltpu.PrefetchScalarGridSpec(
            num_scalar_prefetch=2,
            grid=(per_c // PAIR,),
            in_specs=[
                fixed(a_table.shape),
                fixed(b_table.shape),
                fixed(tables[0].shape),
                fixed(tables[1].shape),
                pl.BlockSpec((1,) + tables[2].shape[1:], lambda i, s, _: (s[0], 0, 0, 0, 0)),
                pl.BlockSpec((wide, narrow, PAIR, rows_x, lanes), lambda i, *_: (0, 0, i, 0, 0)),
                *[pl.BlockSpec(memory_space=pl.ANY)] * len(filled),
            ],
            out_specs=[pl.BlockSpec(block, lambda i, *_: (0, 0, first_step + i, 0))] * groups,
        ),
        out_shape=[space(out_shape, jnp.float32) for space in spaces],
        input_output_aliases={8 + spot: spot for spot in range(len(filled))},
        compiler_params=params(1),
        cost_estimate=cost(per_c * 7 * length**3, 20 * per_c * length**2 * 2),
    )(
        side,
        start_c,
        *[in_hbm(table) for table in (a_table, b_table, *tables)],
        received,
        *[keep(each, space) for each, space in zip(filled, spaces)],
    )


def shear_kernel(
    per_c, group, joined, row_ref, lane_ref, second_ref, third_ref, ahead_ref, last_ref, in_ref, out_ref, shear_ref
):
    step = pl.program_id(0)
    length = shear_ref.shape[0]
    half = length // 2
    devices, tiles, message, tile = in_ref.shape
    count = message // per_c
    flat = in_ref.reshape(devices * tiles * message, tile)

    @pl.when(step == 0)
    def _():
        shear_ref[...] = jnp.zeros_like(shear_ref)

    field = jnp.concatenate(
        [
            jnp.concatenate(
                [
                    flat[pl.ds((source * tiles + spot) * message + x, per_c, stride=count), :]
                    for x in range(count)
                    for source in range(devices)
                ],
                axis=0,
            )
            for spot in range(tiles)
        ],
        axis=1,
    )
    field = field * row_ref[0] * lane_ref[0]
    even = product(split(field[:, :length]), pair(second_ref.at[0]))
    odd = product(split(field[:, length:]), pair(second_ref.at[1]))
    near, far = even + odd, even - odd
    field = jnp.concatenate(
        [
            jnp.concatenate(
                [
                    value[x * half : (x + 1) * half, part * half : (part + 1) * half]
                    for x in range(count)
                    for value in (near, far)
                ],
                axis=1,
            )
            for part in range(2)
        ],
        axis=0,
    )
    field = product(pair(third_ref), split(field))
    shear_ref[...] += field * field

    @pl.when(step == 5)
    def _():
        ahead = jnp.concatenate(
            [shear_ref[:, x * length : (x + 1) * length] for x in range(count)], axis=0
        )
        ahead = product(split(ahead), pair(ahead_ref))
        ahead = jnp.concatenate(
            [
                jnp.concatenate(
                    [
                        ahead[x * length : (x + 1) * length, part * length : (part + 1) * length]
                        for x in range(count)
                    ],
                    axis=1,
                )
                for part in range(2)
            ],
            axis=0,
        )
        value = product(pair(last_ref), split(ahead))
        wide, narrow, message_out, _ = out_ref.shape
        rows_b = length // wide
        slots = tile // rows_b
        rows = 2 * length // slots
        run = rows // (2 * narrow * joined)
        out = out_ref.reshape(wide * narrow * message_out, tile)
        lane = lax.broadcasted_iota(jnp.int32, (rows, tile), 1) // rows_b
        for x in range(count):
            for w in range(wide):
                block, place = divmod(w, slots)
                lanes = slice(x * length + block * tile, x * length + (block + 1) * tile)
                moved = None
                for slot in range(slots):
                    piece = value[slot * rows : (slot + 1) * rows, lanes]
                    if slot != place:
                        piece = pltpu.roll(piece, (slot - place) * rows_b % tile, 1)
                    moved = piece if moved is None else jnp.where(lane == slot, piece, moved)
                for n in range(narrow):
                    for part in range(2):
                        for join in range(joined):
                            start = ((n * 2 + part) * joined + join) * run
                            piece = moved[start : start + run]
                            at = (w * narrow + n) * message_out
                            if joined == 2:
                                at += part * 2 * count + (join ^ group) * count + x
                                out[pl.ds(at, run, stride=4 * count), :] = piece
                            else:
                                at += (x * 2 + part) * run
                                out[pl.ds(at, run), :] = piece


def shear_pass(received, wide, narrow, per_c, group, joined):
    devices, tiles, message, tile = received.shape
    count = message // per_c
    length = tiles * tile // 6
    half = length // 2
    index = np.arange(length)
    angle = angles(index, index, length)
    cosine, sine = np.cos(angle), np.sin(angle)
    split_index = halves(length)
    second = np.stack(
        [split_table(turn(angles(np.arange(half), b, length)).T) for b in split_index]
    )
    row_c = np.arange(half) ^ group
    weight = np.where(row_c == 0, 1.0, 2.0)
    angle = angles(index, row_c, length)
    third = np.concatenate([weight * np.cos(angle), -weight * np.sin(angle)], axis=1)
    ahead = np.concatenate([cosine, -sine], axis=1)
    slots = TILE * wide // length
    order = index.reshape(narrow, -1, joined, slots).transpose(3, 0, 2, 1)
    angle = angles(order.reshape(-1), index, length)
    last = np.stack(
        [
            np.concatenate([np.cos(angle), np.sin(angle)], axis=1),
            np.concatenate([-np.sin(angle), np.cos(angle)], axis=1),
        ]
    )
    last = last.reshape(2, slots, narrow, -1, 2 * length).transpose(1, 2, 0, 3, 4)
    last = last.reshape(2 * length, 2 * length)
    wave = signed_wave(index, length)
    wave_rows = np.tile(wave[row_c], count)
    wave_lanes = np.stack([wave[split_index]] * 2, axis=1).reshape(-1)
    twice = math.sqrt(2.0)
    one_row, one_lane = np.ones_like(wave_rows), np.ones_like(wave_lanes)
    row_factor = np.stack(
        [one_row, twice * one_row, twice * wave_rows, one_row, twice * wave_rows, wave_rows**2]
    ).astype(np.float32)[:, :, None]
    lane_factor = np.stack(
        [one_lane, wave_lanes, one_lane, wave_lanes**2, wave_lanes, one_lane]
    ).astype(np.float32)[:, None, :]
    tables = [second] + [split_table(table) for table in (third, ahead, last)]
    out_shape = (wide, narrow, count * 2 * length // (narrow * slots), TILE)

    def body(*refs):
        shear_kernel(per_c, group, joined, *refs)

    def which(i):
        return (0, 2 - (i >= 1).astype(jnp.int32) - (i >= 3).astype(jnp.int32), 0, 0)

    return pl.pallas_call(
        body,
        grid=(6,),
        in_specs=[
            pl.BlockSpec((1, count * half, 1), lambda i: (i, 0, 0)),
            pl.BlockSpec((1, 1, 2 * length), lambda i: (i, 0, 0)),
            *[whole(table.shape) for table in tables],
            pl.BlockSpec((devices, tiles // 3, message, tile), which),
        ],
        out_specs=whole(out_shape),
        out_shape=pltpu.HBM(out_shape, jnp.float32),
        scratch_shapes=[pltpu.VMEM((length, count * length), jnp.float32)],
        compiler_params=params(1),
        cost_estimate=cost(count * 18 * length**3, 4 * received.size + 4 * 2**20),
    )(*[in_hbm(value) for value in (row_factor, lane_factor, *tables)], received)


def first_kernel(count, rows_b, anchor_ref, table_ref, *refs):
    ins, (real_ref, imag_ref) = refs[:-2], refs[-2:]
    wide, sides, ranks, rows, lanes = ins[0].shape
    length = real_ref.shape[2]
    half = length // 2
    slots = lanes // rows_b
    joined = len(ins)
    steps = real_ref.shape[0] // (slots * joined)
    spot_row = lax.broadcasted_iota(jnp.int32, (lanes, half), 0)
    spot_a = lax.broadcasted_iota(jnp.int32, (lanes, half), 1)
    is_anchor = (anchor_ref[0] == 1) & (pl.program_id(0) == 0)
    start = pl.program_id(0) * steps
    anchor = (spot_row == 0) & (spot_a == 0) & is_anchor
    upper = lax.broadcasted_iota(jnp.int32, (wide * ranks, joined * count, lanes), 1) < count

    def gathered(side, step, join, part):
        if joined == 2:
            at = ((start + step) * 2 + part) * 2 * count
            at = pl.ds(pl.multiple_of(at, 2 * count), 2 * count)
            own, other = [
                ref[:, side, :, at].reshape(wide * ranks, 2 * count, lanes)
                for ref in (ins if join == 0 else ins[::-1])
            ]
            return jnp.where(upper, own, other).reshape(half, lanes)
        flat = ins[0].reshape(wide * sides * ranks * rows, lanes)
        run = rows // count
        return jnp.concatenate(
            [
                flat[
                    pl.ds((w * sides + side) * ranks * rows + part * steps + step, ranks * count, stride=run),
                    :,
                ]
                for w in range(wide)
            ],
            axis=0,
        )

    for join in range(joined):
        sums = []
        for side in range(sides):
            left = jnp.concatenate(
                [
                    jnp.concatenate([gathered(side, step, join, part).T for part in range(2)], axis=1)
                    for step in range(steps)
                ],
                axis=0,
            )
            sums.append(product(split(left), pair(table_ref.at[join, side])))
        even, odd = sums
        for far, value in enumerate((even + odd, even - odd)):
            for step in range(steps):
                at = (step * joined + join) * slots
                columns = slice(far * half, (far + 1) * half)
                for part, ref in enumerate((real_ref, imag_ref)):
                    here = value[step * lanes : (step + 1) * lanes, part * half : (part + 1) * half]
                    if at == 0 and far == 0:
                        here = jnp.where(anchor, 0.0, here)
                    ref[at : at + slots, :, columns] = here.reshape(slots, rows_b, half)


def first_pass(parts, is_anchor, length, wide, sides, count):
    devices, rows, lanes = parts[0].shape
    joined = len(parts)
    ranks = devices // wide // sides
    rows_b = length // wide
    slots = lanes // rows_b
    scale = 1.0 / float(length) ** 1.5
    index = np.arange(length).reshape(wide * ranks, joined, count, sides)
    tables = []
    for join in range(joined):
        order = index[:, :: 1 - 2 * join].transpose(3, 0, 1, 2).reshape(sides, -1)
        tables.append(
            [split_table(scale * turn(-angles(np.arange(length // 2), x, length)).T) for x in order]
        )
    table = np.stack([np.stack(each) for each in tables])
    total = rows // (2 * joined * count) if joined == 2 else rows // (2 * count)
    grid = 4 if joined == 2 and total % 4 == 0 else 1
    parts = [part.reshape(wide, sides, ranks, rows, lanes) for part in parts]

    def body(*refs):
        first_kernel(count, rows_b, *refs)

    rows_c = total * joined * slots
    out_shape = jax.ShapeDtypeStruct((rows_c, rows_b, length), jnp.float32)
    return pl.pallas_call(
        body,
        grid=(grid,),
        in_specs=[
            pl.BlockSpec(memory_space=pltpu.SMEM),
            whole(table.shape),
            *[whole((wide, sides, ranks, rows, lanes))] * joined,
        ],
        out_specs=[pl.BlockSpec((rows_c // grid, rows_b, length), lambda i: (i, 0, 0))] * 2,
        out_shape=[out_shape] * 2,
        compiler_params=params(1),
        cost_estimate=cost(rows_c * 2 * rows_b * length * length, 16 * rows_c * rows_b * length),
    )(is_anchor, table, *[keep(part, pltpu.VMEM) for part in parts])


def transpose(value, members=None):
    return lax.all_to_all(
        value, AXES, split_axis=0, concat_axis=0, tiled=True, axis_index_groups=members
    )


def solution(mesh):
    wide, narrow = mesh.shape["wide"], mesh.shape["narrow"]
    sides = 2
    ranks = narrow // sides
    devices = wide * ranks
    members = [
        [w * narrow + side * ranks + rank for w in range(wide) for rank in range(ranks)]
        for side in range(sides)
    ]

    def per_device(density):
        rows_x, rows_y, length = density.shape
        half = length // 2
        per_c = half // devices
        slab = half // devices
        steps = per_c // PAIR
        counts = [per_c - PAIR, PAIR] if steps > 1 else [per_c]
        groups = 2 if slab > 2 else 1
        spot_wide, spot_narrow = lax.axis_index("wide"), lax.axis_index("narrow")
        side = (spot_narrow // ranks).astype(jnp.int32).reshape(1)
        rank = spot_wide * ranks + spot_narrow % ranks
        start_c = (rank * per_c).astype(jnp.int32).reshape(1)
        chunks, start = [], 0
        for planes, count in zip(third_pass(density, wide, sides, ranks, counts), counts):
            planes = transpose(planes.reshape(wide * narrow, count, rows_x, 2 * rows_y))
            planes = planes.reshape(wide, narrow, count, rows_x, 2 * rows_y)
            planes = keep(planes, pltpu.VMEM if start else pltpu.HBM)
            chunks = spectrum_pass(
                planes, side, start_c, devices, groups, steps, start // PAIR, chunks
            )
            start += count
        is_anchor = ((spot_wide == 0) & (spot_narrow == 0)).astype(jnp.int32).reshape(1)
        parts = []
        for group, chunk in enumerate(chunks):
            received = keep(transpose(chunk, members), pltpu.VMEM if group else pltpu.HBM)
            part = shear_pass(received, wide, narrow, per_c, group, groups)
            parts.append(transpose(part.reshape((wide * narrow,) + part.shape[2:])))
        return tuple(first_pass(parts, is_anchor, length, wide, sides, slab // groups))

    return jax.shard_map(
        per_device,
        mesh=mesh,
        in_specs=(P("wide", "narrow", None),),
        out_specs=(P("narrow", "wide", None), P("narrow", "wide", None)),
        check_vma=False,
    )
```

```python
import math

import jax
import jax.numpy as jnp
import ml_dtypes
import numpy as np
from jax import lax
from jax.experimental import pallas as pl
from jax.experimental.pallas import tpu as pltpu
from jax.sharding import PartitionSpec as P

AXES = ("wide", "narrow")
TILE = 128
LIMIT = 16 * 1024 * 1024


def angles(rows, columns, length):
    return (2.0 * math.pi / length) * (np.outer(rows, columns) % length)


def split_table(table):
    table = np.asarray(table, np.float64)
    high = table.astype(ml_dtypes.bfloat16)
    low = (table - high.astype(np.float64)).astype(ml_dtypes.bfloat16)
    return np.stack([high, low])


def split(value):
    high = value.astype(jnp.bfloat16)
    low = (value - high.astype(jnp.float32)).astype(jnp.bfloat16)
    return high, low


def product(left, right, contract=((1,), (0,))):
    (left_axis,), (right_axis,) = contract
    left = jnp.concatenate([left[0], left[0], left[1]], axis=left_axis)
    right = jnp.concatenate([right[0], right[1], right[0]], axis=right_axis)
    return lax.dot_general(
        left, right, (contract, ((), ())), preferred_element_type=jnp.float32
    )


def pair(ref):
    return ref[0], ref[1]


def signed_wave(index, length):
    index = np.asarray(index)
    return np.where(index < length // 2, index, index - length) * (2.0 * math.pi / length)


def params(steps):
    return pltpu.CompilerParams(
        vmem_limit_bytes=LIMIT, dimension_semantics=("arbitrary",) * steps
    )


def whole(shape):
    return pl.BlockSpec(shape, lambda *_: (0,) * len(shape))


def keep(value, space):
    return pltpu.with_memory_space_constraint(jnp.asarray(value), space)


def in_hbm(value):
    return keep(value, pltpu.HBM)


def cost(macs, moved):
    return pl.CostEstimate(flops=6 * macs, bytes_accessed=moved, transcendentals=0)


def third_kernel(counts, table_ref, density_ref, *outs):
    step_x, rows_y, length = density_ref.shape
    wide, sides, ranks, _, rows_x, _ = outs[0].shape
    half = length // 2
    flats = [ref.reshape(math.prod(ref.shape[:5]), 2 * rows_y) for ref in outs]
    table = pair(table_ref)
    group = 4
    start_x = pl.program_id(0) * step_x
    for first in range(0, step_x, group):
        block = density_ref[first : first + group].reshape(group * rows_y, length)
        result = product(split(block), table)
        for inner in range(group):
            rows = slice(inner * rows_y, (inner + 1) * rows_y)
            value = jnp.concatenate([result[rows, :half], result[rows, half:]], axis=0).T
            start = 0
            for flat, count in zip(flats, counts):
                for c in range(count):
                    for rank in range(ranks):
                        at = (rank * count + c) * rows_x + first + inner + start_x
                        stride = sides * ranks * count * rows_x
                        flat[pl.ds(at, wide, stride=stride), :] = value[start : start + wide]
                        start += wide
    for ref in outs:
        rows = pl.ds(pl.multiple_of(start_x, step_x), step_x)
        for side in range(1, sides):
            ref[:, side, :, :, rows] = ref[:, 0, :, :, rows]


def third_pass(density, wide, sides, ranks, counts):
    rows_x, rows_y, length = density.shape
    half = length // 2
    per_c = sum(counts)
    order = np.arange(half).reshape(wide, ranks, per_c).transpose(2, 1, 0).reshape(-1)
    angle = angles(np.arange(length), order, length)
    table = split_table(np.concatenate([np.cos(angle), -np.sin(angle)], axis=1))
    step = min(8, rows_x)

    def body(*refs):
        third_kernel(counts, *refs)

    return pl.pallas_call(
        body,
        grid=(rows_x // step,),
        in_specs=[
            whole(table.shape),
            pl.BlockSpec((step, rows_y, length), lambda i: (i, 0, 0)),
        ],
        out_specs=[
            whole((wide, sides, ranks, count, rows_x, 2 * rows_y)) for count in counts
        ],
        out_shape=[
            pltpu.VMEM((wide, sides, ranks, count, rows_x, 2 * rows_y), jnp.float32)
            for count in counts
        ],
        compiler_params=params(1),
        cost_estimate=cost(density.size * length, 12 * density.size),
    )(in_hbm(table), in_hbm(density))


PAIR = 2


def turn(angle):
    cosine, sine = np.cos(angle), np.sin(angle)
    return np.block([[cosine, -sine], [sine, cosine]])


def spectrum_kernel(slab, groups, first_c, side_ref, start_ref, a_ref, b_ref, second_ref, first_ref, back_ref, in_ref, *refs):
    outs = refs[-groups:]
    wide, narrow, _, rows_x, lanes = in_ref.shape
    length = wide * rows_x
    half = length // 2
    quarter = half // 2
    devices, tiles, message, tile = outs[0].shape
    count = slab // groups
    sign_back = 1.0 - 2.0 * side_ref[0].astype(jnp.float32)

    def column(c, n):
        return in_ref[:, n, c].reshape(length, lanes)

    def columns(numbers):
        return jnp.concatenate(
            [
                jnp.concatenate([column(c, n) for n in numbers], axis=1)
                for c in range(PAIR)
            ],
            axis=0,
        )

    low, high = columns(range(narrow // 2)), columns(range(narrow // 2, narrow))
    planes = [
        product(split(low + high), pair(second_ref.at[0])),
        product(split(low - high), pair(second_ref.at[1])),
    ]

    def stacked(sign):
        return jnp.concatenate(
            [
                jnp.concatenate(
                    [
                        plane[c * length : c * length + half, part * half : (part + 1) * half]
                        + sign
                        * plane[c * length + half : (c + 1) * length, part * half : (part + 1) * half]
                        for c in range(PAIR)
                        for plane in planes
                    ],
                    axis=1,
                )
                for part in range(2)
            ],
            axis=0,
        )

    squared_b, scale_b = b_ref[0], b_ref[1]
    field = []
    for parity, sign in ((0, 1.0), (1, -1.0)):
        value = product(pair(first_ref.at[parity]), split(stacked(sign)))
        smooth = []
        for c in range(PAIR):
            spot_c = start_ref[0] + (first_c + pl.program_id(0) * PAIR + c)
            wave_c = jnp.full_like(squared_b, spot_c.astype(jnp.float32)) * (2.0 * math.pi / length)
            scale_c = jnp.exp(-0.5 * wave_c * wave_c) * (1.0 / float(length) ** 3)
            squared = a_ref[1, parity] + (squared_b + wave_c * wave_c)
            inverse = scale_c / jnp.where(squared > 0, squared, 1.0)
            smooth.append(jnp.where(squared > 0, inverse * scale_b, 0.0) * a_ref[2, parity])
        smooth = jnp.concatenate(smooth, axis=1)
        field.append(value * jnp.concatenate([smooth, smooth], axis=0))
    upper = lax.broadcasted_iota(jnp.int32, (devices, message, tile), 1) < count
    for number in range(3):
        folded = jnp.concatenate(
            [
                field[parity][part * half : part * half + quarter]
                + sign_back * field[parity][part * half + quarter : (part + 1) * half]
                for part in range(2)
                for parity in range(2)
            ],
            axis=0,
        )
        values = [
            product(
                pair(back_ref.at[0, c % back_ref.shape[1]]),
                split(folded[:, c * length : (c + 1) * length]),
            )
            for c in range(PAIR)
        ]
        for spot in range(tiles // 3):
            parity, part = divmod(spot, 2)
            at = number * (tiles // 3) + spot
            here = [
                value[part * half : (part + 1) * half, parity * tile : (parity + 1) * tile]
                for value in values
            ]
            if groups == 2:
                even, odd = [value.reshape(devices, message, tile) for value in here]
                outs[0][:, at] = jnp.where(upper, even, odd)
                outs[1][:, at] = jnp.where(upper, odd, even)
            else:
                flat = outs[0].reshape(devices * tiles * message, tile)
                for c in range(PAIR):
                    for x in range(slab):
                        start = at * message + c * count + x
                        flat[pl.ds(start, devices, stride=tiles * message), :] = here[c][
                            x * devices : (x + 1) * devices
                        ]
        if number < 2:
            for parity in range(2):
                wave_a = a_ref[0, parity]
                field[parity] = field[parity] * jnp.concatenate([wave_a, wave_a], axis=0)


def halves(length):
    return np.arange(length).reshape(length // 2, 2).T


def spectrum_pass(received, side, start_c, devices, groups, steps, first_step, filled):
    wide, narrow, per_c, rows_x, lanes = received.shape
    length = wide * rows_x
    rows_y = lanes // 2
    half = length // 2
    near = np.arange(half)
    split_index = halves(length)
    slab = half // devices
    second, first, back = [], [], []
    if groups == 2:
        orders = [
            near.reshape(devices, 2, slab // 2)[:, ::step].reshape(-1) for step in (1, -1)
        ]
    else:
        orders = [near.reshape(devices, slab).T.reshape(-1)]
    for parity, index in enumerate(split_index):
        table = turn(-angles(index, near, length)).reshape(2, half, 2, narrow // 2, rows_y)
        second.append(split_table(table.transpose(3, 2, 4, 0, 1).reshape(length, length)))
        first.append(split_table(turn(-angles(index, near, length))))
        columns = split_index[:, : half // 2].reshape(-1)
        back.append(
            [split_table(turn(angles(2 * order + parity, columns, length))) for order in orders]
        )
    tables = [np.stack(second), np.stack(first), np.stack([np.stack(each) for each in back])]
    wave = signed_wave(split_index, length)
    scale = np.where(split_index == half, 0.0, np.exp(-0.5 * wave**2))
    a_table = np.stack([wave, wave**2, scale]).astype(np.float32)[..., None]
    b_table = np.stack([wave**2, scale]).astype(np.float32).reshape(2, 1, length)
    message = PAIR * slab // groups
    spaces = [pltpu.VMEM, pltpu.HBM][:groups]
    out_shape = (devices, 3 * 2 * length // TILE, steps * message, TILE)
    block = out_shape[:2] + (message, TILE)

    def body(*refs):
        spectrum_kernel(slab, groups, first_step * PAIR, *refs)

    def fixed(shape):
        return pl.BlockSpec(shape, lambda *_: (0,) * len(shape))

    return pl.pallas_call(
        body,
        grid_spec=pltpu.PrefetchScalarGridSpec(
            num_scalar_prefetch=2,
            grid=(per_c // PAIR,),
            in_specs=[
                fixed(a_table.shape),
                fixed(b_table.shape),
                fixed(tables[0].shape),
                fixed(tables[1].shape),
                pl.BlockSpec((1,) + tables[2].shape[1:], lambda i, s, _: (s[0], 0, 0, 0, 0)),
                pl.BlockSpec((wide, narrow, PAIR, rows_x, lanes), lambda i, *_: (0, 0, i, 0, 0)),
                *[pl.BlockSpec(memory_space=pl.ANY)] * len(filled),
            ],
            out_specs=[pl.BlockSpec(block, lambda i, *_: (0, 0, first_step + i, 0))] * groups,
        ),
        out_shape=[space(out_shape, jnp.float32) for space in spaces],
        input_output_aliases={8 + spot: spot for spot in range(len(filled))},
        compiler_params=params(1),
        cost_estimate=cost(per_c * 7 * length**3, 20 * per_c * length**2 * 2),
    )(
        side,
        start_c,
        *[in_hbm(table) for table in (a_table, b_table, *tables)],
        received,
        *[keep(each, space) for each, space in zip(filled, spaces)],
    )


def shear_kernel(
    per_c, group, joined, row_ref, lane_ref, second_ref, third_ref, ahead_ref, last_ref, in_ref, out_ref, shear_ref
):
    step = pl.program_id(0)
    length = shear_ref.shape[0]
    half = length // 2
    devices, tiles, message, tile = in_ref.shape
    count = message // per_c
    flat = in_ref.reshape(devices * tiles * message, tile)

    @pl.when(step == 0)
    def _():
        shear_ref[...] = jnp.zeros_like(shear_ref)

    field = jnp.concatenate(
        [
            jnp.concatenate(
                [
                    flat[pl.ds((source * tiles + spot) * message + x, per_c, stride=count), :]
                    for x in range(count)
                    for source in range(devices)
                ],
                axis=0,
            )
            for spot in range(tiles)
        ],
        axis=1,
    )
    field = field * row_ref[0] * lane_ref[0]
    even = product(split(field[:, :length]), pair(second_ref.at[0]))
    odd = product(split(field[:, length:]), pair(second_ref.at[1]))
    near, far = even + odd, even - odd
    field = jnp.concatenate(
        [
            jnp.concatenate(
                [
                    value[x * half : (x + 1) * half, part * half : (part + 1) * half]
                    for x in range(count)
                    for value in (near, far)
                ],
                axis=1,
            )
            for part in range(2)
        ],
        axis=0,
    )
    field = product(pair(third_ref), split(field))
    shear_ref[...] += field * field

    @pl.when(step == 5)
    def _():
        ahead = jnp.concatenate(
            [shear_ref[:, x * length : (x + 1) * length] for x in range(count)], axis=0
        )
        ahead = product(split(ahead), pair(ahead_ref))
        ahead = jnp.concatenate(
            [
                jnp.concatenate(
                    [
                        ahead[x * length : (x + 1) * length, part * length : (part + 1) * length]
                        for x in range(count)
                    ],
                    axis=1,
                )
                for part in range(2)
            ],
            axis=0,
        )
        value = product(pair(last_ref), split(ahead))
        wide, narrow, message_out, _ = out_ref.shape
        rows_b = length // wide
        slots = tile // rows_b
        rows = 2 * length // slots
        run = rows // (2 * narrow * joined)
        out = out_ref.reshape(wide * narrow * message_out, tile)
        lane = lax.broadcasted_iota(jnp.int32, (rows, tile), 1) // rows_b
        for x in range(count):
            for w in range(wide):
                block, place = divmod(w, slots)
                lanes = slice(x * length + block * tile, x * length + (block + 1) * tile)
                moved = None
                for slot in range(slots):
                    piece = value[slot * rows : (slot + 1) * rows, lanes]
                    if slot != place:
                        piece = pltpu.roll(piece, (slot - place) * rows_b % tile, 1)
                    moved = piece if moved is None else jnp.where(lane == slot, piece, moved)
                for n in range(narrow):
                    for part in range(2):
                        for join in range(joined):
                            start = ((n * 2 + part) * joined + join) * run
                            piece = moved[start : start + run]
                            at = (w * narrow + n) * message_out
                            if joined == 2:
                                at += part * 2 * count + (join ^ group) * count + x
                                out[pl.ds(at, run, stride=4 * count), :] = piece
                            else:
                                at += (x * 2 + part) * run
                                out[pl.ds(at, run), :] = piece


def shear_pass(received, wide, narrow, per_c, group, joined):
    devices, tiles, message, tile = received.shape
    count = message // per_c
    length = tiles * tile // 6
    half = length // 2
    index = np.arange(length)
    angle = angles(index, index, length)
    cosine, sine = np.cos(angle), np.sin(angle)
    split_index = halves(length)
    second = np.stack(
        [split_table(turn(angles(np.arange(half), b, length)).T) for b in split_index]
    )
    row_c = np.arange(half) ^ group
    weight = np.where(row_c == 0, 1.0, 2.0)
    angle = angles(index, row_c, length)
    third = np.concatenate([weight * np.cos(angle), -weight * np.sin(angle)], axis=1)
    ahead = np.concatenate([cosine, -sine], axis=1)
    slots = TILE * wide // length
    order = index.reshape(narrow, -1, joined, slots).transpose(3, 0, 2, 1)
    angle = angles(order.reshape(-1), index, length)
    last = np.stack(
        [
            np.concatenate([np.cos(angle), np.sin(angle)], axis=1),
            np.concatenate([-np.sin(angle), np.cos(angle)], axis=1),
        ]
    )
    last = last.reshape(2, slots, narrow, -1, 2 * length).transpose(1, 2, 0, 3, 4)
    last = last.reshape(2 * length, 2 * length)
    wave = signed_wave(index, length)
    wave_rows = np.tile(wave[row_c], count)
    wave_lanes = np.stack([wave[split_index]] * 2, axis=1).reshape(-1)
    twice = math.sqrt(2.0)
    one_row, one_lane = np.ones_like(wave_rows), np.ones_like(wave_lanes)
    row_factor = np.stack(
        [one_row, twice * one_row, twice * wave_rows, one_row, twice * wave_rows, wave_rows**2]
    ).astype(np.float32)[:, :, None]
    lane_factor = np.stack(
        [one_lane, wave_lanes, one_lane, wave_lanes**2, wave_lanes, one_lane]
    ).astype(np.float32)[:, None, :]
    tables = [second] + [split_table(table) for table in (third, ahead, last)]
    out_shape = (wide, narrow, count * 2 * length // (narrow * slots), TILE)

    def body(*refs):
        shear_kernel(per_c, group, joined, *refs)

    def which(i):
        return (0, 2 - (i >= 1).astype(jnp.int32) - (i >= 3).astype(jnp.int32), 0, 0)

    return pl.pallas_call(
        body,
        grid=(6,),
        in_specs=[
            pl.BlockSpec((1, count * half, 1), lambda i: (i, 0, 0)),
            pl.BlockSpec((1, 1, 2 * length), lambda i: (i, 0, 0)),
            *[whole(table.shape) for table in tables],
            pl.BlockSpec((devices, tiles // 3, message, tile), which),
        ],
        out_specs=whole(out_shape),
        out_shape=pltpu.HBM(out_shape, jnp.float32),
        scratch_shapes=[pltpu.VMEM((length, count * length), jnp.float32)],
        compiler_params=params(1),
        cost_estimate=cost(count * 18 * length**3, 4 * received.size + 4 * 2**20),
    )(*[in_hbm(value) for value in (row_factor, lane_factor, *tables)], received)


def first_kernel(count, rows_b, anchor_ref, table_ref, *refs):
    ins, (real_ref, imag_ref) = refs[:-2], refs[-2:]
    wide, sides, ranks, rows, lanes = ins[0].shape
    length = real_ref.shape[2]
    half = length // 2
    slots = lanes // rows_b
    joined = len(ins)
    steps = real_ref.shape[0] // (slots * joined)
    spot_row = lax.broadcasted_iota(jnp.int32, (lanes, half), 0)
    spot_a = lax.broadcasted_iota(jnp.int32, (lanes, half), 1)
    is_anchor = (anchor_ref[0] == 1) & (pl.program_id(0) == 0)
    start = pl.program_id(0) * steps
    anchor = (spot_row == 0) & (spot_a == 0) & is_anchor
    upper = lax.broadcasted_iota(jnp.int32, (wide * ranks, joined * count, lanes), 1) < count

    def gathered(side, step, part):
        if joined == 2:
            at = ((start + step) * 2 + part) * 2 * count
            at = pl.ds(pl.multiple_of(at, 2 * count), 2 * count)
            own, other = [
                ref[:, side, :, at].reshape(wide * ranks, 2 * count, lanes) for ref in ins
            ]
            both = [jnp.where(upper, own, other), jnp.where(upper, other, own)]
            return [value.reshape(half, lanes).T for value in both]
        flat = ins[0].reshape(wide * sides * ranks * rows, lanes)
        run = rows // count
        value = jnp.concatenate(
            [
                flat[
                    pl.ds((w * sides + side) * ranks * rows + part * steps + step, ranks * count, stride=run),
                    :,
                ]
                for w in range(wide)
            ],
            axis=0,
        )
        return [value.T]

    lefts = []
    for side in range(sides):
        tiles = [[gathered(side, step, part) for part in range(2)] for step in range(steps)]
        lefts.append(
            [
                jnp.concatenate(
                    [jnp.concatenate([part[join] for part in parts], axis=1) for parts in tiles], axis=0
                )
                for join in range(joined)
            ]
        )
    for join in range(joined):
        sums = [
            product(split(lefts[side][join]), pair(table_ref.at[join, side])) for side in range(sides)
        ]
        even, odd = sums
        for far, value in enumerate((even + odd, even - odd)):
            for step in range(steps):
                at = (step * joined + join) * slots
                columns = slice(far * half, (far + 1) * half)
                for part, ref in enumerate((real_ref, imag_ref)):
                    here = value[step * lanes : (step + 1) * lanes, part * half : (part + 1) * half]
                    if at == 0 and far == 0:
                        here = jnp.where(anchor, 0.0, here)
                    ref[at : at + slots, :, columns] = here.reshape(slots, rows_b, half)


def first_pass(parts, is_anchor, length, wide, sides, count):
    devices, rows, lanes = parts[0].shape
    joined = len(parts)
    ranks = devices // wide // sides
    rows_b = length // wide
    slots = lanes // rows_b
    scale = 1.0 / float(length) ** 1.5
    index = np.arange(length).reshape(wide * ranks, joined, count, sides)
    tables = []
    for join in range(joined):
        order = index[:, :: 1 - 2 * join].transpose(3, 0, 1, 2).reshape(sides, -1)
        tables.append(
            [split_table(scale * turn(-angles(np.arange(length // 2), x, length)).T) for x in order]
        )
    table = np.stack([np.stack(each) for each in tables])
    total = rows // (2 * joined * count) if joined == 2 else rows // (2 * count)
    grid = 4 if joined == 2 and total % 4 == 0 else 1
    parts = [part.reshape(wide, sides, ranks, rows, lanes) for part in parts]

    def body(*refs):
        first_kernel(count, rows_b, *refs)

    rows_c = total * joined * slots
    out_shape = jax.ShapeDtypeStruct((rows_c, rows_b, length), jnp.float32)
    return pl.pallas_call(
        body,
        grid=(grid,),
        in_specs=[
            pl.BlockSpec(memory_space=pltpu.SMEM),
            whole(table.shape),
            *[whole((wide, sides, ranks, rows, lanes))] * joined,
        ],
        out_specs=[pl.BlockSpec((rows_c // grid, rows_b, length), lambda i: (i, 0, 0))] * 2,
        out_shape=[out_shape] * 2,
        compiler_params=params(1),
        cost_estimate=cost(rows_c * 2 * rows_b * length * length, 16 * rows_c * rows_b * length),
    )(is_anchor, table, *[keep(part, pltpu.VMEM) for part in parts])


def transpose(value, members=None):
    return lax.all_to_all(
        value, AXES, split_axis=0, concat_axis=0, tiled=True, axis_index_groups=members
    )


def solution(mesh):
    wide, narrow = mesh.shape["wide"], mesh.shape["narrow"]
    sides = 2
    ranks = narrow // sides
    devices = wide * ranks
    members = [
        [w * narrow + side * ranks + rank for w in range(wide) for rank in range(ranks)]
        for side in range(sides)
    ]

    def per_device(density):
        rows_x, rows_y, length = density.shape
        half = length // 2
        per_c = half // devices
        slab = half // devices
        steps = per_c // PAIR
        counts = [per_c - PAIR, PAIR] if steps > 1 else [per_c]
        groups = 2 if slab > 2 else 1
        spot_wide, spot_narrow = lax.axis_index("wide"), lax.axis_index("narrow")
        side = (spot_narrow // ranks).astype(jnp.int32).reshape(1)
        rank = spot_wide * ranks + spot_narrow % ranks
        start_c = (rank * per_c).astype(jnp.int32).reshape(1)
        chunks, start = [], 0
        for planes, count in zip(third_pass(density, wide, sides, ranks, counts), counts):
            planes = transpose(planes.reshape(wide * narrow, count, rows_x, 2 * rows_y))
            planes = planes.reshape(wide, narrow, count, rows_x, 2 * rows_y)
            planes = keep(planes, pltpu.VMEM if start else pltpu.HBM)
            chunks = spectrum_pass(
                planes, side, start_c, devices, groups, steps, start // PAIR, chunks
            )
            start += count
        is_anchor = ((spot_wide == 0) & (spot_narrow == 0)).astype(jnp.int32).reshape(1)
        parts = []
        for group, chunk in enumerate(chunks):
            received = keep(transpose(chunk, members), pltpu.VMEM if group else pltpu.HBM)
            part = shear_pass(received, wide, narrow, per_c, group, groups)
            parts.append(transpose(part.reshape((wide * narrow,) + part.shape[2:])))
        return tuple(first_pass(parts, is_anchor, length, wide, sides, slab // groups))

    return jax.shard_map(
        per_device,
        mesh=mesh,
        in_specs=(P("wide", "narrow", None),),
        out_specs=(P("narrow", "wide", None), P("narrow", "wide", None)),
        check_vma=False,
    )
```

```python
import math

import jax
import jax.numpy as jnp
import ml_dtypes
import numpy as np
from jax import lax
from jax.experimental import pallas as pl
from jax.experimental.pallas import tpu as pltpu
from jax.sharding import PartitionSpec as P

AXES = ("wide", "narrow")
TILE = 128
LIMIT = 16 * 1024 * 1024


def angles(rows, columns, length):
    return (2.0 * math.pi / length) * (np.outer(rows, columns) % length)


def split_table(table):
    table = np.asarray(table, np.float64)
    high = table.astype(ml_dtypes.bfloat16)
    low = (table - high.astype(np.float64)).astype(ml_dtypes.bfloat16)
    return np.stack([high, low])


def split(value):
    high = value.astype(jnp.bfloat16)
    low = (value - high.astype(jnp.float32)).astype(jnp.bfloat16)
    return high, low


def product(left, right, contract=((1,), (0,))):
    (left_axis,), (right_axis,) = contract
    left = jnp.concatenate([left[0], left[0], left[1]], axis=left_axis)
    right = jnp.concatenate([right[0], right[1], right[0]], axis=right_axis)
    return lax.dot_general(
        left, right, (contract, ((), ())), preferred_element_type=jnp.float32
    )


def pair(ref):
    return ref[0], ref[1]


def signed_wave(index, length):
    index = np.asarray(index)
    return np.where(index < length // 2, index, index - length) * (2.0 * math.pi / length)


def params(steps):
    return pltpu.CompilerParams(
        vmem_limit_bytes=LIMIT, dimension_semantics=("arbitrary",) * steps
    )


def whole(shape):
    return pl.BlockSpec(shape, lambda *_: (0,) * len(shape))


def keep(value, space):
    return pltpu.with_memory_space_constraint(jnp.asarray(value), space)


def in_hbm(value):
    return keep(value, pltpu.HBM)


def cost(macs, moved):
    return pl.CostEstimate(flops=6 * macs, bytes_accessed=moved, transcendentals=0)


def third_kernel(counts, table_ref, density_ref, *outs):
    step_x, rows_y, length = density_ref.shape
    wide, sides, ranks, _, rows_x, _ = outs[0].shape
    half = length // 2
    flats = [ref.reshape(math.prod(ref.shape[:5]), 2 * rows_y) for ref in outs]
    table = pair(table_ref)
    group = 4
    start_x = pl.program_id(0) * step_x
    for first in range(0, step_x, group):
        block = density_ref[first : first + group].reshape(group * rows_y, length)
        result = product(split(block), table)
        for inner in range(group):
            rows = slice(inner * rows_y, (inner + 1) * rows_y)
            value = jnp.concatenate([result[rows, :half], result[rows, half:]], axis=0).T
            start = 0
            for flat, count in zip(flats, counts):
                for c in range(count):
                    for rank in range(ranks):
                        at = (rank * count + c) * rows_x + first + inner + start_x
                        stride = sides * ranks * count * rows_x
                        flat[pl.ds(at, wide, stride=stride), :] = value[start : start + wide]
                        start += wide
    for ref in outs:
        rows = pl.ds(pl.multiple_of(start_x, step_x), step_x)
        for side in range(1, sides):
            ref[:, side, :, :, rows] = ref[:, 0, :, :, rows]


def third_pass(density, wide, sides, ranks, counts):
    rows_x, rows_y, length = density.shape
    half = length // 2
    per_c = sum(counts)
    order = np.arange(half).reshape(wide, ranks, per_c).transpose(2, 1, 0).reshape(-1)
    angle = angles(np.arange(length), order, length)
    table = split_table(np.concatenate([np.cos(angle), -np.sin(angle)], axis=1))
    step = max(rows_x // 2, min(8, rows_x))

    def body(*refs):
        third_kernel(counts, *refs)

    return pl.pallas_call(
        body,
        grid=(rows_x // step,),
        in_specs=[
            whole(table.shape),
            pl.BlockSpec((step, rows_y, length), lambda i: (i, 0, 0)),
        ],
        out_specs=[
            whole((wide, sides, ranks, count, rows_x, 2 * rows_y)) for count in counts
        ],
        out_shape=[
            pltpu.VMEM((wide, sides, ranks, count, rows_x, 2 * rows_y), jnp.float32)
            for count in counts
        ],
        compiler_params=params(1),
        cost_estimate=cost(density.size * length, 12 * density.size),
    )(in_hbm(table), in_hbm(density))


PAIR = 2


def turn(angle):
    cosine, sine = np.cos(angle), np.sin(angle)
    return np.block([[cosine, -sine], [sine, cosine]])


def hand_on(sources, targets):
    @pl.when(pl.program_id(0) == 0)
    def _():
        for source, target in zip(sources, targets):
            target[...] = source[...]


def spectrum_kernel(slab, groups, first_c, filled, side_ref, start_ref, *refs):
    tables, in_ref, outs = refs[:5], refs[5], refs[6 + filled :]
    a_ref, b_ref, second_ref, first_ref, back_ref = tables
    hand_on(tables, outs[groups:])
    outs = outs[:groups]
    wide, narrow, _, rows_x, lanes = in_ref.shape
    length = wide * rows_x
    half = length // 2
    quarter = half // 2
    devices, tiles, message, tile = outs[0].shape
    count = slab // groups
    sign_back = 1.0 - 2.0 * side_ref[0].astype(jnp.float32)

    def column(c, n):
        return in_ref[:, n, c].reshape(length, lanes)

    def columns(numbers):
        return jnp.concatenate(
            [
                jnp.concatenate([column(c, n) for n in numbers], axis=1)
                for c in range(PAIR)
            ],
            axis=0,
        )

    low, high = columns(range(narrow // 2)), columns(range(narrow // 2, narrow))
    planes = [
        product(split(low + high), pair(second_ref.at[0])),
        product(split(low - high), pair(second_ref.at[1])),
    ]

    def stacked(sign):
        return jnp.concatenate(
            [
                jnp.concatenate(
                    [
                        plane[c * length : c * length + half, part * half : (part + 1) * half]
                        + sign
                        * plane[c * length + half : (c + 1) * length, part * half : (part + 1) * half]
                        for c in range(PAIR)
                        for plane in planes
                    ],
                    axis=1,
                )
                for part in range(2)
            ],
            axis=0,
        )

    squared_b, scale_b = b_ref[0], b_ref[1]
    field = []
    for parity, sign in ((0, 1.0), (1, -1.0)):
        value = product(pair(first_ref.at[parity]), split(stacked(sign)))
        smooth = []
        for c in range(PAIR):
            spot_c = start_ref[0] + (first_c + pl.program_id(0) * PAIR + c)
            wave_c = jnp.full_like(squared_b, spot_c.astype(jnp.float32)) * (2.0 * math.pi / length)
            scale_c = jnp.exp(-0.5 * wave_c * wave_c) * (1.0 / float(length) ** 3)
            squared = a_ref[1, parity] + (squared_b + wave_c * wave_c)
            inverse = scale_c / jnp.where(squared > 0, squared, 1.0)
            smooth.append(jnp.where(squared > 0, inverse * scale_b, 0.0) * a_ref[2, parity])
        smooth = jnp.concatenate(smooth, axis=1)
        field.append(value * jnp.concatenate([smooth, smooth], axis=0))
    upper = lax.broadcasted_iota(jnp.int32, (devices, message, tile), 1) < count
    for number in range(3):
        folded = jnp.concatenate(
            [
                field[parity][part * half : part * half + quarter]
                + sign_back * field[parity][part * half + quarter : (part + 1) * half]
                for part in range(2)
                for parity in range(2)
            ],
            axis=0,
        )
        values = [
            product(
                pair(back_ref.at[0, c % back_ref.shape[1]]),
                split(folded[:, c * length : (c + 1) * length]),
            )
            for c in range(PAIR)
        ]
        for spot in range(tiles // 3):
            parity, part = divmod(spot, 2)
            at = number * (tiles // 3) + spot
            here = [
                value[part * half : (part + 1) * half, parity * tile : (parity + 1) * tile]
                for value in values
            ]
            if groups == 2:
                even, odd = [value.reshape(devices, message, tile) for value in here]
                outs[0][:, at] = jnp.where(upper, even, odd)
                outs[1][:, at] = jnp.where(upper, odd, even)
            else:
                flat = outs[0].reshape(devices * tiles * message, tile)
                for c in range(PAIR):
                    for x in range(slab):
                        start = at * message + c * count + x
                        flat[pl.ds(start, devices, stride=tiles * message), :] = here[c][
                            x * devices : (x + 1) * devices
                        ]
        if number < 2:
            for parity in range(2):
                wave_a = a_ref[0, parity]
                field[parity] = field[parity] * jnp.concatenate([wave_a, wave_a], axis=0)


def halves(length):
    return np.arange(length).reshape(length // 2, 2).T


def spectrum_pass(received, side, start_c, devices, groups, steps, first_step, filled, carried):
    wide, narrow, per_c, rows_x, lanes = received.shape
    length = wide * rows_x
    rows_y = lanes // 2
    half = length // 2
    near = np.arange(half)
    split_index = halves(length)
    slab = half // devices
    second, first, back = [], [], []
    if groups == 2:
        orders = [
            near.reshape(devices, 2, slab // 2)[:, ::step].reshape(-1) for step in (1, -1)
        ]
    else:
        orders = [near.reshape(devices, slab).T.reshape(-1)]
    for parity, index in enumerate(split_index):
        table = turn(-angles(index, near, length)).reshape(2, half, 2, narrow // 2, rows_y)
        second.append(split_table(table.transpose(3, 2, 4, 0, 1).reshape(length, length)))
        first.append(split_table(turn(-angles(index, near, length))))
        columns = split_index[:, : half // 2].reshape(-1)
        back.append(
            [split_table(turn(angles(2 * order + parity, columns, length))) for order in orders]
        )
    tables = [np.stack(second), np.stack(first), np.stack([np.stack(each) for each in back])]
    wave = signed_wave(split_index, length)
    scale = np.where(split_index == half, 0.0, np.exp(-0.5 * wave**2))
    a_table = np.stack([wave, wave**2, scale]).astype(np.float32)[..., None]
    b_table = np.stack([wave**2, scale]).astype(np.float32).reshape(2, 1, length)
    message = PAIR * slab // groups
    spaces = [pltpu.VMEM, pltpu.HBM][:groups]
    out_shape = (devices, 3 * 2 * length // TILE, steps * message, TILE)
    block = out_shape[:2] + (message, TILE)

    def body(*refs):
        spectrum_kernel(slab, groups, first_step * PAIR, len(filled), *refs)

    def fixed(shape):
        return pl.BlockSpec(shape, lambda *_: (0,) * len(shape))

    tables = [a_table, b_table, *tables]
    table_specs = [fixed(table.shape) for table in tables[:4]]
    carry = [pltpu.VMEM(table.shape, table.dtype) for table in tables[:4]]
    carry.append(pltpu.VMEM((1,) + tables[4].shape[1:], tables[4].dtype))
    if carried:
        tables, last_spec = [keep(table, pltpu.VMEM) for table in carried], fixed(carry[4].shape)
    else:
        tables = [in_hbm(table) for table in tables]
        last_spec = pl.BlockSpec(carry[4].shape, lambda i, s, _: (s[0], 0, 0, 0, 0))
    if first_step + per_c // PAIR == steps:
        carry = []
    result = pl.pallas_call(
        body,
        grid_spec=pltpu.PrefetchScalarGridSpec(
            num_scalar_prefetch=2,
            grid=(per_c // PAIR,),
            in_specs=[
                *table_specs,
                last_spec,
                pl.BlockSpec((wide, narrow, PAIR, rows_x, lanes), lambda i, *_: (0, 0, i, 0, 0)),
                *[pl.BlockSpec(memory_space=pl.ANY)] * len(filled),
            ],
            out_specs=[pl.BlockSpec(block, lambda i, *_: (0, 0, first_step + i, 0))] * groups
            + [fixed(each.shape) for each in carry],
        ),
        out_shape=[space(out_shape, jnp.float32) for space in spaces] + carry,
        input_output_aliases={8 + spot: spot for spot in range(len(filled))},
        compiler_params=params(1),
        cost_estimate=cost(per_c * 7 * length**3, 20 * per_c * length**2 * 2),
    )(
        side,
        start_c,
        *tables,
        received,
        *[keep(each, space) for each, space in zip(filled, spaces)],
    )
    return result[:groups], result[groups:]


def shear_kernel(
    per_c, group, joined, row_ref, lane_ref, second_ref, third_ref, ahead_ref, last_ref, in_ref, *refs
):
    shear_ref = refs[-1]
    out_ref, carry_refs = refs[len(refs) // 2 - 1], refs[: len(refs) // 2 - 1]
    hand_on(carry_refs, refs[len(refs) // 2 : -1])
    step = pl.program_id(0)
    length = shear_ref.shape[0]
    half = length // 2
    devices, tiles, message, tile = in_ref.shape
    count = message // per_c
    flat = in_ref.reshape(devices * tiles * message, tile)

    @pl.when(step == 0)
    def _():
        shear_ref[...] = jnp.zeros_like(shear_ref)

    field = jnp.concatenate(
        [
            jnp.concatenate(
                [
                    flat[pl.ds((source * tiles + spot) * message + x, per_c, stride=count), :]
                    for x in range(count)
                    for source in range(devices)
                ],
                axis=0,
            )
            for spot in range(tiles)
        ],
        axis=1,
    )
    field = field * row_ref[0] * lane_ref[0]
    even = product(split(field[:, :length]), pair(second_ref.at[0]))
    odd = product(split(field[:, length:]), pair(second_ref.at[1]))
    near, far = even + odd, even - odd
    field = jnp.concatenate(
        [
            jnp.concatenate(
                [
                    value[x * half : (x + 1) * half, part * half : (part + 1) * half]
                    for x in range(count)
                    for value in (near, far)
                ],
                axis=1,
            )
            for part in range(2)
        ],
        axis=0,
    )
    field = product(pair(third_ref), split(field))
    shear_ref[...] += field * field

    @pl.when(step == 5)
    def _():
        ahead = jnp.concatenate(
            [shear_ref[:, x * length : (x + 1) * length] for x in range(count)], axis=0
        )
        ahead = product(split(ahead), pair(ahead_ref))
        ahead = jnp.concatenate(
            [
                jnp.concatenate(
                    [
                        ahead[x * length : (x + 1) * length, part * length : (part + 1) * length]
                        for x in range(count)
                    ],
                    axis=1,
                )
                for part in range(2)
            ],
            axis=0,
        )
        value = product(pair(last_ref), split(ahead))
        wide, narrow, message_out, _ = out_ref.shape
        rows_b = length // wide
        slots = tile // rows_b
        rows = 2 * length // slots
        run = rows // (2 * narrow * joined)
        out = out_ref.reshape(wide * narrow * message_out, tile)
        lane = lax.broadcasted_iota(jnp.int32, (rows, tile), 1) // rows_b
        for x in range(count):
            for w in range(wide):
                block, place = divmod(w, slots)
                lanes = slice(x * length + block * tile, x * length + (block + 1) * tile)
                moved = None
                for slot in range(slots):
                    piece = value[slot * rows : (slot + 1) * rows, lanes]
                    if slot != place:
                        piece = pltpu.roll(piece, (slot - place) * rows_b % tile, 1)
                    moved = piece if moved is None else jnp.where(lane == slot, piece, moved)
                for n in range(narrow):
                    for part in range(2):
                        for join in range(joined):
                            start = ((n * 2 + part) * joined + join) * run
                            piece = moved[start : start + run]
                            at = (w * narrow + n) * message_out
                            if joined == 2:
                                at += part * 2 * count + (join ^ group) * count + x
                                out[pl.ds(at, run, stride=4 * count), :] = piece
                            else:
                                at += (x * 2 + part) * run
                                out[pl.ds(at, run), :] = piece


def shear_pass(received, wide, narrow, per_c, group, joined, carry):
    devices, tiles, message, tile = received.shape
    count = message // per_c
    length = tiles * tile // 6
    half = length // 2
    index = np.arange(length)
    angle = angles(index, index, length)
    cosine, sine = np.cos(angle), np.sin(angle)
    split_index = halves(length)
    second = np.stack(
        [split_table(turn(angles(np.arange(half), b, length)).T) for b in split_index]
    )
    row_c = np.arange(half) ^ group
    weight = np.where(row_c == 0, 1.0, 2.0)
    angle = angles(index, row_c, length)
    third = np.concatenate([weight * np.cos(angle), -weight * np.sin(angle)], axis=1)
    ahead = np.concatenate([cosine, -sine], axis=1)
    slots = TILE * wide // length
    order = index.reshape(narrow, -1, joined, slots).transpose(3, 0, 2, 1)
    angle = angles(order.reshape(-1), index, length)
    last = np.stack(
        [
            np.concatenate([np.cos(angle), np.sin(angle)], axis=1),
            np.concatenate([-np.sin(angle), np.cos(angle)], axis=1),
        ]
    )
    last = last.reshape(2, slots, narrow, -1, 2 * length).transpose(1, 2, 0, 3, 4)
    last = last.reshape(2 * length, 2 * length)
    wave = signed_wave(index, length)
    wave_rows = np.tile(wave[row_c], count)
    wave_lanes = np.stack([wave[split_index]] * 2, axis=1).reshape(-1)
    twice = math.sqrt(2.0)
    one_row, one_lane = np.ones_like(wave_rows), np.ones_like(wave_lanes)
    row_factor = np.stack(
        [one_row, twice * one_row, twice * wave_rows, one_row, twice * wave_rows, wave_rows**2]
    ).astype(np.float32)[:, :, None]
    lane_factor = np.stack(
        [one_lane, wave_lanes, one_lane, wave_lanes**2, wave_lanes, one_lane]
    ).astype(np.float32)[:, None, :]
    tables = [second] + [split_table(table) for table in (third, ahead, last)]
    out_shape = (wide, narrow, count * 2 * length // (narrow * slots), TILE)

    def body(*refs):
        shear_kernel(per_c, group, joined, *refs)

    def which(i):
        return (0, 2 - (i >= 1).astype(jnp.int32) - (i >= 3).astype(jnp.int32), 0, 0)

    return pl.pallas_call(
        body,
        grid=(6,),
        in_specs=[
            pl.BlockSpec((1, count * half, 1), lambda i: (i, 0, 0)),
            pl.BlockSpec((1, 1, 2 * length), lambda i: (i, 0, 0)),
            *[whole(table.shape) for table in tables],
            pl.BlockSpec((devices, tiles // 3, message, tile), which),
            *[whole(each.shape) for each in carry],
        ],
        out_specs=[whole(out_shape)] + [whole(each.shape) for each in carry],
        out_shape=[pltpu.HBM(out_shape, jnp.float32)]
        + [pltpu.VMEM(each.shape, each.dtype) for each in carry],
        scratch_shapes=[pltpu.VMEM((length, count * length), jnp.float32)],
        compiler_params=params(1),
        cost_estimate=cost(count * 18 * length**3, 4 * received.size + 4 * 2**20),
    )(
        *[in_hbm(value) for value in (row_factor, lane_factor, *tables)],
        received,
        *[in_hbm(each) for each in carry],
    )


def first_kernel(count, rows_b, anchor_ref, table_ref, *refs):
    ins, (real_ref, imag_ref) = refs[:-2], refs[-2:]
    wide, sides, ranks, rows, lanes = ins[0].shape
    length = real_ref.shape[2]
    half = length // 2
    slots = lanes // rows_b
    joined = len(ins)
    steps = real_ref.shape[0] // (slots * joined)
    spot_row = lax.broadcasted_iota(jnp.int32, (lanes, half), 0)
    spot_a = lax.broadcasted_iota(jnp.int32, (lanes, half), 1)
    is_anchor = (anchor_ref[0] == 1) & (pl.program_id(0) == 0)
    start = pl.program_id(0) * steps
    anchor = (spot_row == 0) & (spot_a == 0) & is_anchor
    upper = lax.broadcasted_iota(jnp.int32, (wide * ranks, joined * count, lanes), 1) < count

    def gathered(side, step, part):
        if joined == 2:
            at = ((start + step) * 2 + part) * 2 * count
            at = pl.ds(pl.multiple_of(at, 2 * count), 2 * count)
            own, other = [
                ref[:, side, :, at].reshape(wide * ranks, 2 * count, lanes) for ref in ins
            ]
            both = [jnp.where(upper, own, other), jnp.where(upper, other, own)]
            return [value.reshape(half, lanes).T for value in both]
        flat = ins[0].reshape(wide * sides * ranks * rows, lanes)
        run = rows // count
        value = jnp.concatenate(
            [
                flat[
                    pl.ds((w * sides + side) * ranks * rows + part * steps + step, ranks * count, stride=run),
                    :,
                ]
                for w in range(wide)
            ],
            axis=0,
        )
        return [value.T]

    lefts = []
    for side in range(sides):
        tiles = [[gathered(side, step, part) for part in range(2)] for step in range(steps)]
        lefts.append(
            [
                jnp.concatenate(
                    [jnp.concatenate([part[join] for part in parts], axis=1) for parts in tiles], axis=0
                )
                for join in range(joined)
            ]
        )
    for join in range(joined):
        sums = [
            product(split(lefts[side][join]), pair(table_ref.at[join, side])) for side in range(sides)
        ]
        even, odd = sums
        for far, value in enumerate((even + odd, even - odd)):
            for step in range(steps):
                at = (step * joined + join) * slots
                columns = slice(far * half, (far + 1) * half)
                for part, ref in enumerate((real_ref, imag_ref)):
                    here = value[step * lanes : (step + 1) * lanes, part * half : (part + 1) * half]
                    if at == 0 and far == 0:
                        here = jnp.where(anchor, 0.0, here)
                    ref[at : at + slots, :, columns] = here.reshape(slots, rows_b, half)


def first_table(length, devices, joined, count, sides):
    scale = 1.0 / float(length) ** 1.5
    index = np.arange(length).reshape(devices, joined, count, sides)
    tables = []
    for join in range(joined):
        order = index[:, :: 1 - 2 * join].transpose(3, 0, 1, 2).reshape(sides, -1)
        tables.append(
            [split_table(scale * turn(-angles(np.arange(length // 2), x, length)).T) for x in order]
        )
    return np.stack([np.stack(each) for each in tables])


def first_pass(parts, table, is_anchor, length, wide, sides, count):
    devices, rows, lanes = parts[0].shape
    joined = len(parts)
    ranks = devices // wide // sides
    rows_b = length // wide
    slots = lanes // rows_b
    total = rows // (2 * joined * count) if joined == 2 else rows // (2 * count)
    grid = 4 if joined == 2 and total % 4 == 0 else 1
    parts = [part.reshape(wide, sides, ranks, rows, lanes) for part in parts]

    def body(*refs):
        first_kernel(count, rows_b, *refs)

    rows_c = total * joined * slots
    out_shape = jax.ShapeDtypeStruct((rows_c, rows_b, length), jnp.float32)
    return pl.pallas_call(
        body,
        grid=(grid,),
        in_specs=[
            pl.BlockSpec(memory_space=pltpu.SMEM),
            whole(table.shape),
            *[whole((wide, sides, ranks, rows, lanes))] * joined,
        ],
        out_specs=[pl.BlockSpec((rows_c // grid, rows_b, length), lambda i: (i, 0, 0))] * 2,
        out_shape=[out_shape] * 2,
        compiler_params=params(1),
        cost_estimate=cost(rows_c * 2 * rows_b * length * length, 16 * rows_c * rows_b * length),
    )(is_anchor, keep(table, pltpu.VMEM), *[keep(part, pltpu.VMEM) for part in parts])


def transpose(value, members=None):
    return lax.all_to_all(
        value, AXES, split_axis=0, concat_axis=0, tiled=True, axis_index_groups=members
    )


def solution(mesh):
    wide, narrow = mesh.shape["wide"], mesh.shape["narrow"]
    sides = 2
    ranks = narrow // sides
    devices = wide * ranks
    members = [
        [w * narrow + side * ranks + rank for w in range(wide) for rank in range(ranks)]
        for side in range(sides)
    ]

    def per_device(density):
        rows_x, rows_y, length = density.shape
        half = length // 2
        per_c = half // devices
        slab = half // devices
        steps = per_c // PAIR
        counts = [per_c - PAIR, PAIR] if steps > 1 else [per_c]
        groups = 2 if slab > 2 else 1
        spot_wide, spot_narrow = lax.axis_index("wide"), lax.axis_index("narrow")
        side = (spot_narrow // ranks).astype(jnp.int32).reshape(1)
        rank = spot_wide * ranks + spot_narrow % ranks
        start_c = (rank * per_c).astype(jnp.int32).reshape(1)
        chunks, carried, start = [], [], 0
        for planes, count in zip(third_pass(density, wide, sides, ranks, counts), counts):
            planes = transpose(planes.reshape(wide * narrow, count, rows_x, 2 * rows_y))
            planes = planes.reshape(wide, narrow, count, rows_x, 2 * rows_y)
            planes = keep(planes, pltpu.VMEM if start else pltpu.HBM)
            chunks, carried = spectrum_pass(
                planes, side, start_c, devices, groups, steps, start // PAIR, chunks, carried
            )
            start += count
        is_anchor = ((spot_wide == 0) & (spot_narrow == 0)).astype(jnp.int32).reshape(1)
        parts = []
        table = first_table(length, devices, groups, slab // groups, sides)
        for group, chunk in enumerate(chunks):
            carry = [table] if group == groups - 1 else []
            received = keep(transpose(chunk, members), pltpu.VMEM if group else pltpu.HBM)
            part, *carry = shear_pass(received, wide, narrow, per_c, group, groups, carry)
            parts.append(transpose(part.reshape((wide * narrow,) + part.shape[2:])))
        return tuple(first_pass(parts, *carry, is_anchor, length, wide, sides, slab // groups))

    return jax.shard_map(
        per_device,
        mesh=mesh,
        in_specs=(P("wide", "narrow", None),),
        out_specs=(P("narrow", "wide", None), P("narrow", "wide", None)),
        check_vma=False,
    )
```

```python
import math

import jax
import jax.numpy as jnp
import ml_dtypes
import numpy as np
from jax import lax
from jax.experimental import pallas as pl
from jax.experimental.pallas import tpu as pltpu
from jax.sharding import PartitionSpec as P

AXES = ("wide", "narrow")
TILE = 128
LIMIT = 16 * 1024 * 1024


def angles(rows, columns, length):
    return (2.0 * math.pi / length) * (np.outer(rows, columns) % length)


def split_table(table):
    table = np.asarray(table, np.float64)
    high = table.astype(ml_dtypes.bfloat16)
    low = (table - high.astype(np.float64)).astype(ml_dtypes.bfloat16)
    return np.stack([high, low])


def split(value):
    high = value.astype(jnp.bfloat16)
    low = (value - high.astype(jnp.float32)).astype(jnp.bfloat16)
    return high, low


def product(left, right, contract=((1,), (0,))):
    (left_axis,), (right_axis,) = contract
    left = jnp.concatenate([left[0], left[0], left[1]], axis=left_axis)
    right = jnp.concatenate([right[0], right[1], right[0]], axis=right_axis)
    return lax.dot_general(
        left, right, (contract, ((), ())), preferred_element_type=jnp.float32
    )


def pair(ref):
    return ref[0], ref[1]


def signed_wave(index, length):
    index = np.asarray(index)
    return np.where(index < length // 2, index, index - length) * (2.0 * math.pi / length)


def params(steps):
    return pltpu.CompilerParams(
        vmem_limit_bytes=LIMIT, dimension_semantics=("arbitrary",) * steps
    )


def whole(shape):
    return pl.BlockSpec(shape, lambda *_: (0,) * len(shape))


def keep(value, space):
    return pltpu.with_memory_space_constraint(jnp.asarray(value), space)


def in_hbm(value):
    return keep(value, pltpu.HBM)


def cost(macs, moved):
    return pl.CostEstimate(flops=6 * macs, bytes_accessed=moved, transcendentals=0)


def third_kernel(counts, table_ref, density_ref, *outs):
    step_x, rows_y, length = density_ref.shape
    wide, sides, ranks, _, rows_x, _ = outs[0].shape
    half = length // 2
    flats = [ref.reshape(math.prod(ref.shape[:5]), 2 * rows_y) for ref in outs]
    table = pair(table_ref)
    group = 4
    start_x = pl.program_id(0) * step_x
    for first in range(0, step_x, group):
        block = density_ref[first : first + group].reshape(group * rows_y, length)
        result = product(split(block), table)
        for inner in range(group):
            rows = slice(inner * rows_y, (inner + 1) * rows_y)
            value = jnp.concatenate([result[rows, :half], result[rows, half:]], axis=0).T
            start = 0
            for flat, count in zip(flats, counts):
                for c in range(count):
                    for rank in range(ranks):
                        at = (rank * count + c) * rows_x + first + inner + start_x
                        stride = sides * ranks * count * rows_x
                        flat[pl.ds(at, wide, stride=stride), :] = value[start : start + wide]
                        start += wide
    for ref in outs:
        rows = pl.ds(pl.multiple_of(start_x, step_x), step_x)
        for side in range(1, sides):
            ref[:, side, :, :, rows] = ref[:, 0, :, :, rows]


def third_pass(density, wide, sides, ranks, counts):
    rows_x, rows_y, length = density.shape
    half = length // 2
    per_c = sum(counts)
    order = np.arange(half).reshape(wide, ranks, per_c).transpose(2, 1, 0).reshape(-1)
    angle = angles(np.arange(length), order, length)
    table = split_table(np.concatenate([np.cos(angle), -np.sin(angle)], axis=1))
    step = max(rows_x // 2, min(8, rows_x))

    def body(*refs):
        third_kernel(counts, *refs)

    return pl.pallas_call(
        body,
        grid=(rows_x // step,),
        in_specs=[
            whole(table.shape),
            pl.BlockSpec((step, rows_y, length), lambda i: (i, 0, 0)),
        ],
        out_specs=[
            whole((wide, sides, ranks, count, rows_x, 2 * rows_y)) for count in counts
        ],
        out_shape=[
            pltpu.VMEM((wide, sides, ranks, count, rows_x, 2 * rows_y), jnp.float32)
            for count in counts
        ],
        compiler_params=params(1),
        cost_estimate=cost(density.size * length, 12 * density.size),
    )(in_hbm(table), in_hbm(density))


PAIR = 2


def turn(angle):
    cosine, sine = np.cos(angle), np.sin(angle)
    return np.block([[cosine, -sine], [sine, cosine]])


def hand_on(sources, targets):
    @pl.when(pl.program_id(0) == 0)
    def _():
        for source, target in zip(sources, targets):
            target[...] = source[...]


def spectrum_kernel(slab, groups, first_c, filled, side_ref, start_ref, *refs):
    tables, in_ref, outs = refs[:5], refs[5], refs[6 + filled :]
    a_ref, b_ref, second_ref, first_ref, back_ref = tables
    hand_on(tables, outs[groups:])
    outs = outs[:groups]
    wide, narrow, _, rows_x, lanes = in_ref.shape
    length = wide * rows_x
    half = length // 2
    quarter = half // 2
    devices, tiles, message, tile = outs[0].shape
    count = slab // groups
    sign_back = 1.0 - 2.0 * side_ref[0].astype(jnp.float32)

    def column(c, n):
        return in_ref[:, n, c].reshape(length, lanes)

    def columns(numbers):
        return jnp.concatenate(
            [
                jnp.concatenate([column(c, n) for n in numbers], axis=1)
                for c in range(PAIR)
            ],
            axis=0,
        )

    low, high = columns(range(narrow // 2)), columns(range(narrow // 2, narrow))
    planes = [
        product(split(low + high), pair(second_ref.at[0])),
        product(split(low - high), pair(second_ref.at[1])),
    ]

    def stacked(sign):
        return jnp.concatenate(
            [
                jnp.concatenate(
                    [
                        plane[c * length : c * length + half, part * half : (part + 1) * half]
                        + sign
                        * plane[c * length + half : (c + 1) * length, part * half : (part + 1) * half]
                        for c in range(PAIR)
                        for plane in planes
                    ],
                    axis=1,
                )
                for part in range(2)
            ],
            axis=0,
        )

    squared_b, scale_b = b_ref[0], b_ref[1]
    field = []
    for parity, sign in ((0, 1.0), (1, -1.0)):
        value = product(pair(first_ref.at[parity]), split(stacked(sign)))
        smooth = []
        for c in range(PAIR):
            spot_c = start_ref[0] + (first_c + pl.program_id(0) * PAIR + c)
            wave_c = jnp.full_like(squared_b, spot_c.astype(jnp.float32)) * (2.0 * math.pi / length)
            scale_c = jnp.exp(-0.5 * wave_c * wave_c) * (1.0 / float(length) ** 3)
            squared = a_ref[1, parity] + (squared_b + wave_c * wave_c)
            inverse = scale_c / jnp.where(squared > 0, squared, 1.0)
            smooth.append(jnp.where(squared > 0, inverse * scale_b, 0.0) * a_ref[2, parity])
        smooth = jnp.concatenate(smooth, axis=1)
        field.append(value * jnp.concatenate([smooth, smooth], axis=0))
    upper = lax.broadcasted_iota(jnp.int32, (devices, message, tile), 1) < count
    for number in range(3):
        folded = jnp.concatenate(
            [
                field[parity][part * half : part * half + quarter]
                + sign_back * field[parity][part * half + quarter : (part + 1) * half]
                for part in range(2)
                for parity in range(2)
            ],
            axis=0,
        )
        values = [
            product(
                pair(back_ref.at[0, c % back_ref.shape[1]]),
                split(folded[:, c * length : (c + 1) * length]),
            )
            for c in range(PAIR)
        ]
        for spot in range(tiles // 3):
            parity, part = divmod(spot, 2)
            at = number * (tiles // 3) + spot
            here = [
                value[part * half : (part + 1) * half, parity * tile : (parity + 1) * tile]
                for value in values
            ]
            if groups == 2:
                even, odd = [value.reshape(devices, message, tile) for value in here]
                outs[0][:, at] = jnp.where(upper, even, odd)
                outs[1][:, at] = jnp.where(upper, odd, even)
            else:
                flat = outs[0].reshape(devices * tiles * message, tile)
                for c in range(PAIR):
                    for x in range(slab):
                        start = at * message + c * count + x
                        flat[pl.ds(start, devices, stride=tiles * message), :] = here[c][
                            x * devices : (x + 1) * devices
                        ]
        if number < 2:
            for parity in range(2):
                wave_a = a_ref[0, parity]
                field[parity] = field[parity] * jnp.concatenate([wave_a, wave_a], axis=0)


def halves(length):
    return np.arange(length).reshape(length // 2, 2).T


def spectrum_pass(received, side, start_c, devices, groups, steps, first_step, filled, carried):
    wide, narrow, per_c, rows_x, lanes = received.shape
    length = wide * rows_x
    rows_y = lanes // 2
    half = length // 2
    near = np.arange(half)
    split_index = halves(length)
    slab = half // devices
    second, first, back = [], [], []
    if groups == 2:
        orders = [
            near.reshape(devices, 2, slab // 2)[:, ::step].reshape(-1) for step in (1, -1)
        ]
    else:
        orders = [near.reshape(devices, slab).T.reshape(-1)]
    for parity, index in enumerate(split_index):
        table = turn(-angles(index, near, length)).reshape(2, half, 2, narrow // 2, rows_y)
        second.append(split_table(table.transpose(3, 2, 4, 0, 1).reshape(length, length)))
        first.append(split_table(turn(-angles(index, near, length))))
        columns = split_index[:, : half // 2].reshape(-1)
        back.append(
            [split_table(turn(angles(2 * order + parity, columns, length))) for order in orders]
        )
    tables = [np.stack(second), np.stack(first), np.stack([np.stack(each) for each in back])]
    wave = signed_wave(split_index, length)
    scale = np.where(split_index == half, 0.0, np.exp(-0.5 * wave**2))
    a_table = np.stack([wave, wave**2, scale]).astype(np.float32)[..., None]
    b_table = np.stack([wave**2, scale]).astype(np.float32).reshape(2, 1, length)
    message = PAIR * slab // groups
    spaces = [pltpu.VMEM, pltpu.HBM][:groups]
    out_shape = (devices, 3 * 2 * length // TILE, steps * message, TILE)
    block = out_shape[:2] + (message, TILE)

    def body(*refs):
        spectrum_kernel(slab, groups, first_step * PAIR, len(filled), *refs)

    def fixed(shape):
        return pl.BlockSpec(shape, lambda *_: (0,) * len(shape))

    tables = [a_table, b_table, *tables]
    table_specs = [fixed(table.shape) for table in tables[:4]]
    carry = [pltpu.VMEM(table.shape, table.dtype) for table in tables[:4]]
    carry.append(pltpu.VMEM((1,) + tables[4].shape[1:], tables[4].dtype))
    if carried:
        tables, last_spec = [keep(table, pltpu.VMEM) for table in carried], fixed(carry[4].shape)
    else:
        tables = [in_hbm(table) for table in tables]
        last_spec = pl.BlockSpec(carry[4].shape, lambda i, s, _: (s[0], 0, 0, 0, 0))
    if first_step + per_c // PAIR == steps:
        carry = []
    result = pl.pallas_call(
        body,
        grid_spec=pltpu.PrefetchScalarGridSpec(
            num_scalar_prefetch=2,
            grid=(per_c // PAIR,),
            in_specs=[
                *table_specs,
                last_spec,
                pl.BlockSpec((wide, narrow, PAIR, rows_x, lanes), lambda i, *_: (0, 0, i, 0, 0)),
                *[pl.BlockSpec(memory_space=pl.ANY)] * len(filled),
            ],
            out_specs=[pl.BlockSpec(block, lambda i, *_: (0, 0, first_step + i, 0))] * groups
            + [fixed(each.shape) for each in carry],
        ),
        out_shape=[space(out_shape, jnp.float32) for space in spaces] + carry,
        input_output_aliases={8 + spot: spot for spot in range(len(filled))},
        compiler_params=params(1),
        cost_estimate=cost(per_c * 7 * length**3, 20 * per_c * length**2 * 2),
    )(
        side,
        start_c,
        *tables,
        received,
        *[keep(each, space) for each, space in zip(filled, spaces)],
    )
    return result[:groups], result[groups:]


def shear_kernel(
    per_c, group, joined, row_ref, lane_ref, second_ref, third_ref, ahead_ref, last_ref, in_ref, *refs
):
    shear_ref = refs[-1]
    out_ref, carry_refs = refs[len(refs) // 2 - 1], refs[: len(refs) // 2 - 1]
    hand_on(carry_refs, refs[len(refs) // 2 : -1])
    step = pl.program_id(0)
    length = shear_ref.shape[0]
    half = length // 2
    devices, tiles, message, tile = in_ref.shape
    count = message // per_c
    flat = in_ref.reshape(devices * tiles * message, tile)

    @pl.when(step == 0)
    def _():
        shear_ref[...] = jnp.zeros_like(shear_ref)

    field = jnp.concatenate(
        [
            jnp.concatenate(
                [
                    flat[pl.ds((source * tiles + spot) * message + x, per_c, stride=count), :]
                    for x in range(count)
                    for source in range(devices)
                ],
                axis=0,
            )
            for spot in range(tiles)
        ],
        axis=1,
    )
    field = field * row_ref[0] * lane_ref[0]
    even = product(split(field[:, :length]), pair(second_ref.at[0]))
    odd = product(split(field[:, length:]), pair(second_ref.at[1]))
    near, far = even + odd, even - odd
    field = jnp.concatenate(
        [
            jnp.concatenate(
                [
                    value[x * half : (x + 1) * half, part * half : (part + 1) * half]
                    for x in range(count)
                    for value in (near, far)
                ],
                axis=1,
            )
            for part in range(2)
        ],
        axis=0,
    )
    field = product(pair(third_ref), split(field))
    shear_ref[...] += field * field

    @pl.when(step == 5)
    def _():
        ahead = jnp.concatenate(
            [shear_ref[:, x * length : (x + 1) * length] for x in range(count)], axis=0
        )
        ahead = product(split(ahead), pair(ahead_ref))
        ahead = jnp.concatenate(
            [
                jnp.concatenate(
                    [
                        ahead[x * length : (x + 1) * length, part * length : (part + 1) * length]
                        for x in range(count)
                    ],
                    axis=1,
                )
                for part in range(2)
            ],
            axis=0,
        )
        value = product(pair(last_ref), split(ahead))
        wide, narrow, message_out, _ = out_ref.shape
        rows_b = length // wide
        slots = tile // rows_b
        rows = 2 * length // slots
        run = rows // (2 * narrow * joined)
        out = out_ref.reshape(wide * narrow * message_out, tile)
        lane = lax.broadcasted_iota(jnp.int32, (rows, tile), 1) // rows_b
        for x in range(count):
            for w in range(wide):
                block, place = divmod(w, slots)
                lanes = slice(x * length + block * tile, x * length + (block + 1) * tile)
                moved = None
                for slot in range(slots):
                    piece = value[slot * rows : (slot + 1) * rows, lanes]
                    if slot != place:
                        piece = pltpu.roll(piece, (slot - place) * rows_b % tile, 1)
                    moved = piece if moved is None else jnp.where(lane == slot, piece, moved)
                for n in range(narrow):
                    for part in range(2):
                        for join in range(joined):
                            start = ((n * 2 + part) * joined + join) * run
                            piece = moved[start : start + run]
                            at = (w * narrow + n) * message_out
                            if joined == 2:
                                at += part * 2 * count + (join ^ group) * count + x
                                out[pl.ds(at, run, stride=4 * count), :] = piece
                            else:
                                at += (x * 2 + part) * run
                                out[pl.ds(at, run), :] = piece


def shear_pass(received, wide, narrow, per_c, group, joined, carry):
    devices, tiles, message, tile = received.shape
    count = message // per_c
    length = tiles * tile // 6
    half = length // 2
    index = np.arange(length)
    angle = angles(index, index, length)
    cosine, sine = np.cos(angle), np.sin(angle)
    split_index = halves(length)
    second = np.stack(
        [split_table(turn(angles(np.arange(half), b, length)).T) for b in split_index]
    )
    row_c = np.arange(half) ^ group
    weight = np.where(row_c == 0, 1.0, 2.0)
    angle = angles(index, row_c, length)
    third = np.concatenate([weight * np.cos(angle), -weight * np.sin(angle)], axis=1)
    ahead = np.concatenate([cosine, -sine], axis=1)
    slots = TILE * wide // length
    order = index.reshape(narrow, -1, joined, slots).transpose(3, 0, 2, 1)
    angle = angles(order.reshape(-1), index, length)
    last = np.stack(
        [
            np.concatenate([np.cos(angle), np.sin(angle)], axis=1),
            np.concatenate([-np.sin(angle), np.cos(angle)], axis=1),
        ]
    )
    last = last.reshape(2, slots, narrow, -1, 2 * length).transpose(1, 2, 0, 3, 4)
    last = last.reshape(2 * length, 2 * length)
    wave = signed_wave(index, length)
    wave_rows = np.tile(wave[row_c], count)
    wave_lanes = np.stack([wave[split_index]] * 2, axis=1).reshape(-1)
    twice = math.sqrt(2.0)
    one_row, one_lane = np.ones_like(wave_rows), np.ones_like(wave_lanes)
    row_factor = np.stack(
        [one_row, twice * one_row, twice * wave_rows, one_row, twice * wave_rows, wave_rows**2]
    ).astype(np.float32)[:, :, None]
    lane_factor = np.stack(
        [one_lane, wave_lanes, one_lane, wave_lanes**2, wave_lanes, one_lane]
    ).astype(np.float32)[:, None, :]
    tables = [second] + [split_table(table) for table in (third, ahead, last)]
    out_shape = (wide, narrow, count * 2 * length // (narrow * slots), TILE)

    def body(*refs):
        shear_kernel(per_c, group, joined, *refs)

    def which(i):
        return (0, 2 - (i >= 1).astype(jnp.int32) - (i >= 3).astype(jnp.int32), 0, 0)

    return pl.pallas_call(
        body,
        grid=(6,),
        in_specs=[
            pl.BlockSpec((1, count * half, 1), lambda i: (i, 0, 0)),
            pl.BlockSpec((1, 1, 2 * length), lambda i: (i, 0, 0)),
            *[whole(table.shape) for table in tables],
            pl.BlockSpec((devices, tiles // 3, message, tile), which),
            *[whole(each.shape) for each in carry],
        ],
        out_specs=[whole(out_shape)] + [whole(each.shape) for each in carry],
        out_shape=[pltpu.HBM(out_shape, jnp.float32)]
        + [pltpu.VMEM(each.shape, each.dtype) for each in carry],
        scratch_shapes=[pltpu.VMEM((length, count * length), jnp.float32)],
        compiler_params=params(1),
        cost_estimate=cost(count * 18 * length**3, 4 * received.size + 4 * 2**20),
    )(
        *[in_hbm(value) for value in (row_factor, lane_factor, *tables)],
        received,
        *[in_hbm(each) for each in carry],
    )


def turned_tile(ref, side, at):
    wide, _, ranks, _, lanes = ref.shape
    return ref[:, side, :, at].reshape(wide * ranks * at.size, lanes).T


def turned_kernel(in_ref, out_ref):
    sides, tiles, size, _ = out_ref.shape
    message = in_ref.shape[3] // tiles
    for side in range(sides):
        for tile in range(tiles):
            out_ref[side, tile] = turned_tile(in_ref, side, pl.ds(tile * message, message))


def turned_pass(part, wide, sides, message):
    devices, rows, lanes = part.shape
    part = part.reshape(wide, sides, devices // wide // sides, rows, lanes)
    out_shape = (sides, rows // message, lanes, devices // sides * message)
    return pl.pallas_call(
        turned_kernel,
        grid=(1,),
        in_specs=[whole(part.shape)],
        out_specs=whole(out_shape),
        out_shape=pltpu.VMEM(out_shape, jnp.float32),
        compiler_params=params(1),
        cost_estimate=cost(0, 8 * part.size),
    )(keep(part, pltpu.VMEM))


def first_kernel(count, rows_b, joined, anchor_ref, table_ref, *refs):
    ins, (real_ref, imag_ref) = refs[:-2], refs[-2:]
    wide, sides, ranks, rows, lanes = ins[-1].shape
    length = real_ref.shape[2]
    half = length // 2
    slots = lanes // rows_b
    steps = real_ref.shape[0] // (slots * joined)
    spot_row = lax.broadcasted_iota(jnp.int32, (lanes, half), 0)
    spot_a = lax.broadcasted_iota(jnp.int32, (lanes, half), 1)
    is_anchor = (anchor_ref[0] == 1) & (pl.program_id(0) == 0)
    start = pl.program_id(0) * steps
    anchor = (spot_row == 0) & (spot_a == 0) & is_anchor
    upper = lax.broadcasted_iota(jnp.int32, (lanes, half), 1) % (2 * count) < count

    def gathered(side, step, part):
        if joined == 2:
            tile = (start + step) * 2 + part
            at = pl.ds(pl.multiple_of(tile * 2 * count, 2 * count), 2 * count)
            own, other = ins[0][side, tile], turned_tile(ins[1], side, at)
            return [jnp.where(upper, own, other), jnp.where(upper, other, own)]
        flat = ins[0].reshape(wide * sides * ranks * rows, lanes)
        run = rows // count
        value = jnp.concatenate(
            [
                flat[
                    pl.ds((w * sides + side) * ranks * rows + part * steps + step, ranks * count, stride=run),
                    :,
                ]
                for w in range(wide)
            ],
            axis=0,
        )
        return [value.T]

    lefts = []
    for side in range(sides):
        tiles = [[gathered(side, step, part) for part in range(2)] for step in range(steps)]
        lefts.append(
            [
                jnp.concatenate(
                    [jnp.concatenate([part[join] for part in parts], axis=1) for parts in tiles], axis=0
                )
                for join in range(joined)
            ]
        )
    for join in range(joined):
        sums = [
            product(split(lefts[side][join]), pair(table_ref.at[join, side])) for side in range(sides)
        ]
        even, odd = sums
        for far, value in enumerate((even + odd, even - odd)):
            for step in range(steps):
                at = (step * joined + join) * slots
                columns = slice(far * half, (far + 1) * half)
                for part, ref in enumerate((real_ref, imag_ref)):
                    here = value[step * lanes : (step + 1) * lanes, part * half : (part + 1) * half]
                    if at == 0 and far == 0:
                        here = jnp.where(anchor, 0.0, here)
                    ref[at : at + slots, :, columns] = here.reshape(slots, rows_b, half)


def first_table(length, devices, joined, count, sides):
    scale = 1.0 / float(length) ** 1.5
    index = np.arange(length).reshape(devices, joined, count, sides)
    tables = []
    for join in range(joined):
        order = index[:, :: 1 - 2 * join].transpose(3, 0, 1, 2).reshape(sides, -1)
        tables.append(
            [split_table(scale * turn(-angles(np.arange(length // 2), x, length)).T) for x in order]
        )
    return np.stack([np.stack(each) for each in tables])


def first_pass(parts, table, is_anchor, length, wide, sides, count):
    devices, rows, lanes = parts[0].shape
    joined = len(parts)
    ranks = devices // wide // sides
    rows_b = length // wide
    slots = lanes // rows_b
    turned = [turned_pass(parts[0], wide, sides, 2 * count)] if joined == 2 else []
    total = rows // (2 * joined * count) if joined == 2 else rows // (2 * count)
    grid = 4 if joined == 2 and total % 4 == 0 else 1
    parts = turned + [parts[-1].reshape(wide, sides, ranks, rows, lanes)]

    def body(*refs):
        first_kernel(count, rows_b, joined, *refs)

    rows_c = total * joined * slots
    out_shape = jax.ShapeDtypeStruct((rows_c, rows_b, length), jnp.float32)
    return pl.pallas_call(
        body,
        grid=(grid,),
        in_specs=[
            pl.BlockSpec(memory_space=pltpu.SMEM),
            whole(table.shape),
            *[whole(part.shape) for part in parts],
        ],
        out_specs=[pl.BlockSpec((rows_c // grid, rows_b, length), lambda i: (i, 0, 0))] * 2,
        out_shape=[out_shape] * 2,
        compiler_params=params(1),
        cost_estimate=cost(rows_c * 2 * rows_b * length * length, 16 * rows_c * rows_b * length),
    )(is_anchor, keep(table, pltpu.VMEM), *[keep(part, pltpu.VMEM) for part in parts])


def transpose(value, members=None):
    return lax.all_to_all(
        value, AXES, split_axis=0, concat_axis=0, tiled=True, axis_index_groups=members
    )


def solution(mesh):
    wide, narrow = mesh.shape["wide"], mesh.shape["narrow"]
    sides = 2
    ranks = narrow // sides
    devices = wide * ranks
    members = [
        [w * narrow + side * ranks + rank for w in range(wide) for rank in range(ranks)]
        for side in range(sides)
    ]

    def per_device(density):
        rows_x, rows_y, length = density.shape
        half = length // 2
        per_c = half // devices
        slab = half // devices
        steps = per_c // PAIR
        counts = [per_c - PAIR, PAIR] if steps > 1 else [per_c]
        groups = 2 if slab > 2 else 1
        spot_wide, spot_narrow = lax.axis_index("wide"), lax.axis_index("narrow")
        side = (spot_narrow // ranks).astype(jnp.int32).reshape(1)
        rank = spot_wide * ranks + spot_narrow % ranks
        start_c = (rank * per_c).astype(jnp.int32).reshape(1)
        chunks, carried, start = [], [], 0
        for planes, count in zip(third_pass(density, wide, sides, ranks, counts), counts):
            planes = transpose(planes.reshape(wide * narrow, count, rows_x, 2 * rows_y))
            planes = planes.reshape(wide, narrow, count, rows_x, 2 * rows_y)
            planes = keep(planes, pltpu.VMEM if start else pltpu.HBM)
            chunks, carried = spectrum_pass(
                planes, side, start_c, devices, groups, steps, start // PAIR, chunks, carried
            )
            start += count
        is_anchor = ((spot_wide == 0) & (spot_narrow == 0)).astype(jnp.int32).reshape(1)
        parts = []
        table = first_table(length, devices, groups, slab // groups, sides)
        for group, chunk in enumerate(chunks):
            carry = [table] if group == groups - 1 else []
            received = keep(transpose(chunk, members), pltpu.VMEM if group else pltpu.HBM)
            part, *carry = shear_pass(received, wide, narrow, per_c, group, groups, carry)
            parts.append(transpose(part.reshape((wide * narrow,) + part.shape[2:])))
        return tuple(first_pass(parts, *carry, is_anchor, length, wide, sides, slab // groups))

    return jax.shard_map(
        per_device,
        mesh=mesh,
        in_specs=(P("wide", "narrow", None),),
        out_specs=(P("narrow", "wide", None), P("narrow", "wide", None)),
        check_vma=False,
    )
```

```python
import math

import jax
import jax.numpy as jnp
import ml_dtypes
import numpy as np
from jax import lax
from jax.experimental import pallas as pl
from jax.experimental.pallas import tpu as pltpu
from jax.sharding import PartitionSpec as P

AXES = ("wide", "narrow")
TILE = 128
LIMIT = 16 * 1024 * 1024


def angles(rows, columns, length):
    return (2.0 * math.pi / length) * (np.outer(rows, columns) % length)


def split_table(table):
    table = np.asarray(table, np.float64)
    high = table.astype(ml_dtypes.bfloat16)
    low = (table - high.astype(np.float64)).astype(ml_dtypes.bfloat16)
    return np.stack([high, low])


def split(value):
    high = value.astype(jnp.bfloat16)
    low = (value - high.astype(jnp.float32)).astype(jnp.bfloat16)
    return high, low


def product(left, right, contract=((1,), (0,))):
    (left_axis,), (right_axis,) = contract
    left = jnp.concatenate([left[0], left[0], left[1]], axis=left_axis)
    right = jnp.concatenate([right[0], right[1], right[0]], axis=right_axis)
    return lax.dot_general(
        left, right, (contract, ((), ())), preferred_element_type=jnp.float32
    )


def pair(ref):
    return ref[0], ref[1]


def signed_wave(index, length):
    index = np.asarray(index)
    return np.where(index < length // 2, index, index - length) * (2.0 * math.pi / length)


def params(steps):
    return pltpu.CompilerParams(
        vmem_limit_bytes=LIMIT, dimension_semantics=("arbitrary",) * steps
    )


def whole(shape):
    return pl.BlockSpec(shape, lambda *_: (0,) * len(shape))


def keep(value, space):
    return pltpu.with_memory_space_constraint(jnp.asarray(value), space)


def in_hbm(value):
    return keep(value, pltpu.HBM)


def cost(macs, moved):
    return pl.CostEstimate(flops=6 * macs, bytes_accessed=moved, transcendentals=0)


def third_kernel(counts, table_ref, density_ref, *outs):
    step_x, rows_y, length = density_ref.shape
    wide, sides, ranks, _, rows_x, _ = outs[0].shape
    half = length // 2
    flats = [ref.reshape(math.prod(ref.shape[:5]), 2 * rows_y) for ref in outs]
    table = pair(table_ref)
    group = 4
    start_x = pl.program_id(0) * step_x
    for first in range(0, step_x, group):
        block = density_ref[first : first + group].reshape(group * rows_y, length)
        result = product(split(block), table)
        for inner in range(group):
            rows = slice(inner * rows_y, (inner + 1) * rows_y)
            value = jnp.concatenate([result[rows, :half], result[rows, half:]], axis=0).T
            start = 0
            for flat, count in zip(flats, counts):
                for c in range(count):
                    for rank in range(ranks):
                        at = (rank * count + c) * rows_x + first + inner + start_x
                        stride = sides * ranks * count * rows_x
                        flat[pl.ds(at, wide, stride=stride), :] = value[start : start + wide]
                        start += wide
    for ref in outs:
        rows = pl.ds(pl.multiple_of(start_x, step_x), step_x)
        for side in range(1, sides):
            ref[:, side, :, :, rows] = ref[:, 0, :, :, rows]


def third_pass(density, wide, sides, ranks, counts):
    rows_x, rows_y, length = density.shape
    half = length // 2
    per_c = sum(counts)
    order = np.arange(half).reshape(wide, ranks, per_c).transpose(2, 1, 0).reshape(-1)
    angle = angles(np.arange(length), order, length)
    table = split_table(np.concatenate([np.cos(angle), -np.sin(angle)], axis=1))
    step = max(rows_x // 2, min(8, rows_x))

    def body(*refs):
        third_kernel(counts, *refs)

    return pl.pallas_call(
        body,
        grid=(rows_x // step,),
        in_specs=[
            whole(table.shape),
            pl.BlockSpec((step, rows_y, length), lambda i: (i, 0, 0)),
        ],
        out_specs=[
            whole((wide, sides, ranks, count, rows_x, 2 * rows_y)) for count in counts
        ],
        out_shape=[
            pltpu.VMEM((wide, sides, ranks, count, rows_x, 2 * rows_y), jnp.float32)
            for count in counts
        ],
        compiler_params=params(1),
        cost_estimate=cost(density.size * length, 12 * density.size),
    )(in_hbm(table), in_hbm(density))


PAIR = 2


def turn(angle):
    cosine, sine = np.cos(angle), np.sin(angle)
    return np.block([[cosine, -sine], [sine, cosine]])


def hand_on(sources, targets):
    @pl.when(pl.program_id(0) == 0)
    def _():
        for source, target in zip(sources, targets):
            target[...] = source[...]


def spectrum_kernel(slab, groups, first_c, filled, side_ref, start_ref, *refs):
    tables, in_ref, outs = refs[:5], refs[5], refs[6 + filled :]
    a_ref, b_ref, second_ref, first_ref, back_ref = tables
    hand_on(tables, outs[groups:])
    outs = outs[:groups]
    wide, narrow, _, rows_x, lanes = in_ref.shape
    length = wide * rows_x
    half = length // 2
    quarter = half // 2
    devices, tiles, message, tile = outs[0].shape
    count = slab // groups
    sign_back = 1.0 - 2.0 * side_ref[0].astype(jnp.float32)

    def column(c, n):
        return in_ref[:, n, c].reshape(length, lanes)

    def columns(numbers):
        return jnp.concatenate(
            [
                jnp.concatenate([column(c, n) for n in numbers], axis=1)
                for c in range(PAIR)
            ],
            axis=0,
        )

    low, high = columns(range(narrow // 2)), columns(range(narrow // 2, narrow))
    planes = [
        product(split(low + high), pair(second_ref.at[0])),
        product(split(low - high), pair(second_ref.at[1])),
    ]

    def stacked(sign):
        return jnp.concatenate(
            [
                jnp.concatenate(
                    [
                        plane[c * length : c * length + half, part * half : (part + 1) * half]
                        + sign
                        * plane[c * length + half : (c + 1) * length, part * half : (part + 1) * half]
                        for c in range(PAIR)
                        for plane in planes
                    ],
                    axis=1,
                )
                for part in range(2)
            ],
            axis=0,
        )

    squared_b, scale_b = b_ref[0], b_ref[1]
    field = []
    for parity, sign in ((0, 1.0), (1, -1.0)):
        value = product(pair(first_ref.at[parity]), split(stacked(sign)))
        smooth = []
        for c in range(PAIR):
            spot_c = start_ref[0] + (first_c + pl.program_id(0) * PAIR + c)
            wave_c = jnp.full_like(squared_b, spot_c.astype(jnp.float32)) * (2.0 * math.pi / length)
            scale_c = jnp.exp(-0.5 * wave_c * wave_c) * (1.0 / float(length) ** 3)
            squared = a_ref[1, parity] + (squared_b + wave_c * wave_c)
            inverse = scale_c / jnp.where(squared > 0, squared, 1.0)
            smooth.append(jnp.where(squared > 0, inverse * scale_b, 0.0) * a_ref[2, parity])
        smooth = jnp.concatenate(smooth, axis=1)
        field.append(value * jnp.concatenate([smooth, smooth], axis=0))
    upper = lax.broadcasted_iota(jnp.int32, (devices, message, tile), 1) < count
    for number in range(3):
        folded = jnp.concatenate(
            [
                field[parity][part * half : part * half + quarter]
                + sign_back * field[parity][part * half + quarter : (part + 1) * half]
                for part in range(2)
                for parity in range(2)
            ],
            axis=0,
        )
        values = [
            product(
                pair(back_ref.at[0, c % back_ref.shape[1]]),
                split(folded[:, c * length : (c + 1) * length]),
            )
            for c in range(PAIR)
        ]
        for spot in range(tiles // 3):
            parity, part = divmod(spot, 2)
            at = number * (tiles // 3) + spot
            here = [
                value[part * half : (part + 1) * half, parity * tile : (parity + 1) * tile]
                for value in values
            ]
            if groups == 2:
                even, odd = [value.reshape(devices, message, tile) for value in here]
                outs[0][:, at] = jnp.where(upper, even, odd)
                outs[1][:, at] = jnp.where(upper, odd, even)
            else:
                flat = outs[0].reshape(devices * tiles * message, tile)
                for c in range(PAIR):
                    for x in range(slab):
                        start = at * message + c * count + x
                        flat[pl.ds(start, devices, stride=tiles * message), :] = here[c][
                            x * devices : (x + 1) * devices
                        ]
        if number < 2:
            for parity in range(2):
                wave_a = a_ref[0, parity]
                field[parity] = field[parity] * jnp.concatenate([wave_a, wave_a], axis=0)


def halves(length):
    return np.arange(length).reshape(length // 2, 2).T


def spectrum_pass(received, side, start_c, devices, groups, steps, first_step, filled, carried):
    wide, narrow, per_c, rows_x, lanes = received.shape
    length = wide * rows_x
    rows_y = lanes // 2
    half = length // 2
    near = np.arange(half)
    split_index = halves(length)
    slab = half // devices
    second, first, back = [], [], []
    if groups == 2:
        orders = [
            near.reshape(devices, 2, slab // 2)[:, ::step].reshape(-1) for step in (1, -1)
        ]
    else:
        orders = [near.reshape(devices, slab).T.reshape(-1)]
    for parity, index in enumerate(split_index):
        table = turn(-angles(index, near, length)).reshape(2, half, 2, narrow // 2, rows_y)
        second.append(split_table(table.transpose(3, 2, 4, 0, 1).reshape(length, length)))
        first.append(split_table(turn(-angles(index, near, length))))
        columns = split_index[:, : half // 2].reshape(-1)
        back.append(
            [split_table(turn(angles(2 * order + parity, columns, length))) for order in orders]
        )
    tables = [np.stack(second), np.stack(first), np.stack([np.stack(each) for each in back])]
    wave = signed_wave(split_index, length)
    scale = np.where(split_index == half, 0.0, np.exp(-0.5 * wave**2))
    a_table = np.stack([wave, wave**2, scale]).astype(np.float32)[..., None]
    b_table = np.stack([wave**2, scale]).astype(np.float32).reshape(2, 1, length)
    message = PAIR * slab // groups
    spaces = [pltpu.VMEM, pltpu.HBM][:groups]
    out_shape = (devices, 3 * 2 * length // TILE, steps * message, TILE)
    block = out_shape[:2] + (message, TILE)

    def body(*refs):
        spectrum_kernel(slab, groups, first_step * PAIR, len(filled), *refs)

    def fixed(shape):
        return pl.BlockSpec(shape, lambda *_: (0,) * len(shape))

    tables = [a_table, b_table, *tables]
    table_specs = [fixed(table.shape) for table in tables[:4]]
    carry = [pltpu.VMEM(table.shape, table.dtype) for table in tables[:4]]
    carry.append(pltpu.VMEM((1,) + tables[4].shape[1:], tables[4].dtype))
    if carried:
        tables, last_spec = [keep(table, pltpu.VMEM) for table in carried], fixed(carry[4].shape)
    else:
        tables = [in_hbm(table) for table in tables]
        last_spec = pl.BlockSpec(carry[4].shape, lambda i, s, _: (s[0], 0, 0, 0, 0))
    if first_step + per_c // PAIR == steps:
        carry = []
    result = pl.pallas_call(
        body,
        grid_spec=pltpu.PrefetchScalarGridSpec(
            num_scalar_prefetch=2,
            grid=(per_c // PAIR,),
            in_specs=[
                *table_specs,
                last_spec,
                pl.BlockSpec((wide, narrow, PAIR, rows_x, lanes), lambda i, *_: (0, 0, i, 0, 0)),
                *[pl.BlockSpec(memory_space=pl.ANY)] * len(filled),
            ],
            out_specs=[pl.BlockSpec(block, lambda i, *_: (0, 0, first_step + i, 0))] * groups
            + [fixed(each.shape) for each in carry],
        ),
        out_shape=[space(out_shape, jnp.float32) for space in spaces] + carry,
        input_output_aliases={8 + spot: spot for spot in range(len(filled))},
        compiler_params=params(1),
        cost_estimate=cost(per_c * 7 * length**3, 20 * per_c * length**2 * 2),
    )(
        side,
        start_c,
        *tables,
        received,
        *[keep(each, space) for each, space in zip(filled, spaces)],
    )
    return result[:groups], result[groups:]


def shear_kernel(
    per_c,
    group,
    joined,
    own_first,
    _,
    row_ref,
    lane_ref,
    second_ref,
    third_ref,
    ahead_ref,
    last_ref,
    in_ref,
    *refs,
):
    outs, shear_ref = refs[:-1], refs[-1]
    if not own_first:
        outs = outs[-1:]
    step = pl.program_id(0)
    length = shear_ref.shape[0]
    half = length // 2
    devices, tiles, message, tile = in_ref.shape
    count = message // per_c
    flat = in_ref.reshape(devices * tiles * message, tile)

    @pl.when(step == 0)
    def _():
        shear_ref[...] = jnp.zeros_like(shear_ref)

    field = jnp.concatenate(
        [
            jnp.concatenate(
                [
                    flat[pl.ds((source * tiles + spot) * message + x, per_c, stride=count), :]
                    for x in range(count)
                    for source in range(devices)
                ],
                axis=0,
            )
            for spot in range(tiles)
        ],
        axis=1,
    )
    field = field * row_ref[0] * lane_ref[0]
    even = product(split(field[:, :length]), pair(second_ref.at[0]))
    odd = product(split(field[:, length:]), pair(second_ref.at[1]))
    near, far = even + odd, even - odd
    field = jnp.concatenate(
        [
            jnp.concatenate(
                [
                    value[x * half : (x + 1) * half, part * half : (part + 1) * half]
                    for x in range(count)
                    for value in (near, far)
                ],
                axis=1,
            )
            for part in range(2)
        ],
        axis=0,
    )
    field = product(pair(third_ref), split(field))
    shear_ref[...] += field * field

    @pl.when(step == 5)
    def _():
        ahead = jnp.concatenate(
            [shear_ref[:, x * length : (x + 1) * length] for x in range(count)], axis=0
        )
        ahead = product(split(ahead), pair(ahead_ref))
        ahead = jnp.concatenate(
            [
                jnp.concatenate(
                    [
                        ahead[x * length : (x + 1) * length, part * length : (part + 1) * length]
                        for x in range(count)
                    ],
                    axis=1,
                )
                for part in range(2)
            ],
            axis=0,
        )
        value = product(pair(last_ref.at[0]), split(ahead))
        wide, ranks, message_out, _ = outs[0].shape
        narrow = 2 * ranks if own_first else ranks
        rows_b = length // wide
        slots = tile // rows_b
        rows = 2 * length // slots
        run = rows // (2 * narrow * joined)
        flats = [ref.reshape(wide * ranks * message_out, tile) for ref in outs]
        lane = lax.broadcasted_iota(jnp.int32, (rows, tile), 1) // rows_b
        for x in range(count):
            for w in range(wide):
                block, place = divmod(w, slots)
                lanes = slice(x * length + block * tile, x * length + (block + 1) * tile)
                moved = None
                for slot in range(slots):
                    piece = value[slot * rows : (slot + 1) * rows, lanes]
                    if slot != place:
                        piece = pltpu.roll(piece, (slot - place) * rows_b % tile, 1)
                    moved = piece if moved is None else jnp.where(lane == slot, piece, moved)
                for n in range(narrow):
                    for part in range(2):
                        for join in range(joined):
                            start = ((n * 2 + part) * joined + join) * run
                            piece = moved[start : start + run]
                            at = (w * ranks + n % ranks) * message_out
                            if own_first:
                                flat = flats[n // ranks * 2 + part]
                                at += (join ^ group) * count + x
                                flat[pl.ds(at, run, stride=2 * count), :] = piece
                            elif joined == 2:
                                at += part * 2 * count + (join ^ group) * count + x
                                flats[0][pl.ds(at, run, stride=4 * count), :] = piece
                            else:
                                at += (x * 2 + part) * run
                                flats[0][pl.ds(at, run), :] = piece


def shear_pass(received, side, wide, narrow, per_c, group, joined, after):
    devices, tiles, message, tile = received.shape
    count = message // per_c
    length = tiles * tile // 6
    half = length // 2
    index = np.arange(length)
    angle = angles(index, index, length)
    cosine, sine = np.cos(angle), np.sin(angle)
    split_index = halves(length)
    second = np.stack(
        [split_table(turn(angles(np.arange(half), b, length)).T) for b in split_index]
    )
    row_c = np.arange(half) ^ group
    weight = np.where(row_c == 0, 1.0, 2.0)
    angle = angles(index, row_c, length)
    third = np.concatenate([weight * np.cos(angle), -weight * np.sin(angle)], axis=1)
    ahead = np.concatenate([cosine, -sine], axis=1)
    slots = TILE * wide // length
    order = index.reshape(narrow, -1, joined, slots).transpose(3, 0, 2, 1)
    angle = angles(order.reshape(-1), index, length)
    last = np.stack(
        [
            np.concatenate([np.cos(angle), np.sin(angle)], axis=1),
            np.concatenate([-np.sin(angle), np.cos(angle)], axis=1),
        ]
    )
    last = last.reshape(2, slots, narrow, -1, 2 * length).transpose(1, 2, 0, 3, 4)
    own_first = joined == 2 and group == 0
    last = np.stack(
        [
            split_table(np.roll(last, -own, axis=1).reshape(2 * length, 2 * length))
            for own in ((0, narrow // 2) if own_first else (0,))
        ]
    )
    wave = signed_wave(index, length)
    wave_rows = np.tile(wave[row_c], count)
    wave_lanes = np.stack([wave[split_index]] * 2, axis=1).reshape(-1)
    twice = math.sqrt(2.0)
    one_row, one_lane = np.ones_like(wave_rows), np.ones_like(wave_lanes)
    row_factor = np.stack(
        [one_row, twice * one_row, twice * wave_rows, one_row, twice * wave_rows, wave_rows**2]
    ).astype(np.float32)[:, :, None]
    lane_factor = np.stack(
        [one_lane, wave_lanes, one_lane, wave_lanes**2, wave_lanes, one_lane]
    ).astype(np.float32)[:, None, :]
    tables = [second, split_table(third), split_table(ahead)]
    rows_out = count * 2 * length // (narrow * slots)
    if own_first:
        out_shapes = [(wide, narrow // 2, rows_out // 2, TILE)] * 4
    else:
        out_shapes = [(wide, narrow, rows_out, TILE)]

    def body(*refs):
        shear_kernel(per_c, group, joined, own_first, *refs)

    def which(i, _):
        return (0, 2 - (i >= 1).astype(jnp.int32) - (i >= 3).astype(jnp.int32), 0, 0)

    def own_table(i, s):
        return (s[0] if own_first else 0, 0, 0, 0)

    return pl.pallas_call(
        body,
        grid_spec=pltpu.PrefetchScalarGridSpec(
            num_scalar_prefetch=1,
            grid=(6,),
            in_specs=[
                pl.BlockSpec((1, count * half, 1), lambda i, _: (i, 0, 0)),
                pl.BlockSpec((1, 1, 2 * length), lambda i, _: (i, 0, 0)),
                *[whole(table.shape) for table in tables],
                pl.BlockSpec((1,) + last.shape[1:], own_table),
                pl.BlockSpec((devices, tiles // 3, message, tile), which),
                *[pl.BlockSpec(memory_space=pl.ANY)] * len(after),
            ],
            out_specs=[whole(out_shape) for out_shape in out_shapes],
            scratch_shapes=[pltpu.VMEM((length, count * length), jnp.float32)],
        ),
        out_shape=[pltpu.HBM(out_shape, jnp.float32) for out_shape in out_shapes],
        compiler_params=params(1),
        cost_estimate=cost(count * 18 * length**3, 4 * received.size + 4 * 2**20),
    )(
        side,
        *[in_hbm(value) for value in (row_factor, lane_factor, *tables, last)],
        received,
        *[in_hbm(each) for each in after],
    )


def first_kernel(count, rows_b, joined, own_ref, anchor_ref, table_ref, *refs):
    ins, (real_ref, imag_ref) = refs[:-2], refs[-2:]
    wide, sides, ranks, rows, lanes = ins[-1].shape
    length = real_ref.shape[2]
    half = length // 2
    slots = lanes // rows_b
    steps = real_ref.shape[0] // (slots * joined)
    spot_row = lax.broadcasted_iota(jnp.int32, (lanes, half), 0)
    spot_a = lax.broadcasted_iota(jnp.int32, (lanes, half), 1)
    is_anchor = (anchor_ref[0] == 1) & (pl.program_id(0) == 0)
    start = pl.program_id(0) * steps
    anchor = (spot_row == 0) & (spot_a == 0) & is_anchor
    upper = lax.broadcasted_iota(jnp.int32, (wide * ranks, joined * count, lanes), 1) < count

    def gathered(side, step, part):
        if joined == 2:
            at = (start + step) * 2 * count
            near = pl.ds(pl.multiple_of(at, 2 * count), 2 * count)
            far = pl.ds(pl.multiple_of(2 * at + part * 2 * count, 2 * count), 2 * count)
            arrived = own_ref[0] ^ side
            own, other = [
                value.reshape(wide * ranks, 2 * count, lanes)
                for value in (ins[part][:, :, arrived, near], ins[2][:, side, :, far])
            ]
            both = [jnp.where(upper, own, other), jnp.where(upper, other, own)]
            return [value.reshape(half, lanes).T for value in both]
        flat = ins[0].reshape(wide * sides * ranks * rows, lanes)
        run = rows // count
        value = jnp.concatenate(
            [
                flat[
                    pl.ds((w * sides + side) * ranks * rows + part * steps + step, ranks * count, stride=run),
                    :,
                ]
                for w in range(wide)
            ],
            axis=0,
        )
        return [value.T]

    lefts = []
    for side in range(sides):
        tiles = [[gathered(side, step, part) for part in range(2)] for step in range(steps)]
        lefts.append(
            [
                jnp.concatenate(
                    [jnp.concatenate([part[join] for part in parts], axis=1) for parts in tiles], axis=0
                )
                for join in range(joined)
            ]
        )
    for join in range(joined):
        sums = [
            product(split(lefts[side][join]), pair(table_ref.at[join, side])) for side in range(sides)
        ]
        even, odd = sums
        for far, value in enumerate((even + odd, even - odd)):
            for step in range(steps):
                at = (step * joined + join) * slots
                columns = slice(far * half, (far + 1) * half)
                for part, ref in enumerate((real_ref, imag_ref)):
                    here = value[step * lanes : (step + 1) * lanes, part * half : (part + 1) * half]
                    if at == 0 and far == 0:
                        here = jnp.where(anchor, 0.0, here)
                    ref[at : at + slots, :, columns] = here.reshape(slots, rows_b, half)


def first_table(length, devices, joined, count, sides):
    scale = 1.0 / float(length) ** 1.5
    index = np.arange(length).reshape(devices, joined, count, sides)
    tables = []
    for join in range(joined):
        order = index[:, :: 1 - 2 * join].transpose(3, 0, 1, 2).reshape(sides, -1)
        tables.append(
            [split_table(scale * turn(-angles(np.arange(length // 2), x, length)).T) for x in order]
        )
    return np.stack([np.stack(each) for each in tables])


def first_pass(parts, table, side, is_anchor, length, wide, sides, count):
    devices, rows, lanes = parts[-1].shape
    joined = min(2, len(parts))
    ranks = devices // wide // sides
    rows_b = length // wide
    slots = lanes // rows_b
    total = rows // (2 * joined * count) if joined == 2 else rows // (2 * count)
    grid = 4 if joined == 2 and total % 4 == 0 else 1
    parts = [part.reshape(wide, ranks, 2, rows // 2, lanes) for part in parts[:-1]] + [
        parts[-1].reshape(wide, sides, ranks, rows, lanes)
    ]

    def body(*refs):
        first_kernel(count, rows_b, joined, *refs)

    rows_c = total * joined * slots
    out_shape = jax.ShapeDtypeStruct((rows_c, rows_b, length), jnp.float32)
    return pl.pallas_call(
        body,
        grid=(grid,),
        in_specs=[
            pl.BlockSpec(memory_space=pltpu.SMEM),
            pl.BlockSpec(memory_space=pltpu.SMEM),
            whole(table.shape),
            *[whole(part.shape) for part in parts],
        ],
        out_specs=[pl.BlockSpec((rows_c // grid, rows_b, length), lambda i: (i, 0, 0))] * 2,
        out_shape=[out_shape] * 2,
        compiler_params=params(1),
        cost_estimate=cost(rows_c * 2 * rows_b * length * length, 16 * rows_c * rows_b * length),
    )(side, is_anchor, in_hbm(table), *[keep(part, pltpu.VMEM) for part in parts])


def transpose(value, members=None):
    return lax.all_to_all(
        value, AXES, split_axis=0, concat_axis=0, tiled=True, axis_index_groups=members
    )


def solution(mesh):
    wide, narrow = mesh.shape["wide"], mesh.shape["narrow"]
    sides = 2
    ranks = narrow // sides
    devices = wide * ranks
    members = [
        [w * narrow + side * ranks + rank for w in range(wide) for rank in range(ranks)]
        for side in range(sides)
    ]

    def per_device(density):
        rows_x, rows_y, length = density.shape
        half = length // 2
        per_c = half // devices
        slab = half // devices
        steps = per_c // PAIR
        counts = [per_c - PAIR, PAIR] if steps > 1 else [per_c]
        groups = 2 if slab > 2 else 1
        spot_wide, spot_narrow = lax.axis_index("wide"), lax.axis_index("narrow")
        side = (spot_narrow // ranks).astype(jnp.int32).reshape(1)
        rank = spot_wide * ranks + spot_narrow % ranks
        start_c = (rank * per_c).astype(jnp.int32).reshape(1)
        chunks, carried, start = [], [], 0
        for planes, count in zip(third_pass(density, wide, sides, ranks, counts), counts):
            planes = transpose(planes.reshape(wide * narrow, count, rows_x, 2 * rows_y))
            planes = planes.reshape(wide, narrow, count, rows_x, 2 * rows_y)
            planes = keep(planes, pltpu.VMEM if start else pltpu.HBM)
            chunks, carried = spectrum_pass(
                planes, side, start_c, devices, groups, steps, start // PAIR, chunks, carried
            )
            start += count
        is_anchor = ((spot_wide == 0) & (spot_narrow == 0)).astype(jnp.int32).reshape(1)
        across = [(n, (n + ranks) % narrow) for n in range(narrow)]
        parts, after = [], []
        table = first_table(length, devices, groups, slab // groups, sides)
        for group, chunk in enumerate(chunks):
            received = keep(transpose(chunk, members), pltpu.VMEM if group else pltpu.HBM)
            result = shear_pass(received, side, wide, narrow, per_c, group, groups, after)
            result = [part.reshape((-1,) + part.shape[2:]) for part in result]
            if len(result) == 1:
                parts.append(transpose(result[0]))
                continue
            for own, other in zip(result[:2], result[2:]):
                after = [lax.ppermute(other, "narrow", across)]
                both = jnp.concatenate([own[:, None], after[0][:, None]], axis=1)
                parts.append(transpose(both, members))
        return tuple(first_pass(parts, table, side, is_anchor, length, wide, sides, slab // groups))

    return jax.shard_map(
        per_device,
        mesh=mesh,
        in_specs=(P("wide", "narrow", None),),
        out_specs=(P("narrow", "wide", None), P("narrow", "wide", None)),
        check_vma=False,
    )
```

```python
import math

import jax
import jax.numpy as jnp
import ml_dtypes
import numpy as np
from jax import lax
from jax.experimental import pallas as pl
from jax.experimental.pallas import tpu as pltpu
from jax.sharding import PartitionSpec as P

AXES = ("wide", "narrow")
TILE = 128
LIMIT = 16 * 1024 * 1024


def angles(rows, columns, length):
    return (2.0 * math.pi / length) * (np.outer(rows, columns) % length)


def split_table(table):
    table = np.asarray(table, np.float64)
    high = table.astype(ml_dtypes.bfloat16)
    low = (table - high.astype(np.float64)).astype(ml_dtypes.bfloat16)
    return np.stack([high, low])


def split(value):
    high = value.astype(jnp.bfloat16)
    low = (value - high.astype(jnp.float32)).astype(jnp.bfloat16)
    return high, low


def product(left, right, contract=((1,), (0,))):
    (left_axis,), (right_axis,) = contract
    left = jnp.concatenate([left[0], left[0], left[1]], axis=left_axis)
    right = jnp.concatenate([right[0], right[1], right[0]], axis=right_axis)
    return lax.dot_general(
        left, right, (contract, ((), ())), preferred_element_type=jnp.float32
    )


def product_wide(left, right):
    width = right[0].shape[1]
    high = jnp.dot(
        left[0], jnp.concatenate(right, axis=1), preferred_element_type=jnp.float32
    )
    low = jnp.dot(left[1], right[0], preferred_element_type=jnp.float32)
    return high[:, :width] + (high[:, width:] + low)


def pair(ref):
    return ref[0], ref[1]


def signed_wave(index, length):
    index = np.asarray(index)
    return np.where(index < length // 2, index, index - length) * (2.0 * math.pi / length)


def params(steps, limit=LIMIT):
    return pltpu.CompilerParams(
        vmem_limit_bytes=limit, dimension_semantics=("arbitrary",) * steps
    )


def whole(shape):
    return pl.BlockSpec(shape, lambda *_: (0,) * len(shape))


def keep(value, space):
    return pltpu.with_memory_space_constraint(jnp.asarray(value), space)


def in_hbm(value):
    return keep(value, pltpu.HBM)


def cost(macs, moved):
    return pl.CostEstimate(flops=6 * macs, bytes_accessed=moved, transcendentals=0)


def third_kernel(counts, table_ref, density_ref, *outs):
    step_x, rows_y, length = density_ref.shape
    wide, sides, ranks, _, rows_x, _ = outs[0].shape
    half = length // 2
    flats = [ref.reshape(math.prod(ref.shape[:5]), 2 * rows_y) for ref in outs]
    table = pair(table_ref)
    group = 4
    start_x = pl.program_id(0) * step_x
    for first in range(0, step_x, group):
        block = density_ref[first : first + group].reshape(group * rows_y, length)
        result = product_wide(split(block), table)
        for inner in range(group):
            rows = slice(inner * rows_y, (inner + 1) * rows_y)
            value = jnp.concatenate([result[rows, :half], result[rows, half:]], axis=0).T
            start = 0
            for flat, count in zip(flats, counts):
                for c in range(count):
                    for rank in range(ranks):
                        at = (rank * count + c) * rows_x + first + inner + start_x
                        stride = sides * ranks * count * rows_x
                        flat[pl.ds(at, wide, stride=stride), :] = value[start : start + wide]
                        start += wide
    for ref in outs:
        rows = pl.ds(pl.multiple_of(start_x, step_x), step_x)
        for side in range(1, sides):
            ref[:, side, :, :, rows] = ref[:, 0, :, :, rows]


def third_pass(density, wide, sides, ranks, counts):
    rows_x, rows_y, length = density.shape
    half = length // 2
    per_c = sum(counts)
    order = np.arange(half).reshape(wide, ranks, per_c).transpose(2, 1, 0).reshape(-1)
    angle = angles(np.arange(length), order, length)
    table = split_table(np.concatenate([np.cos(angle), -np.sin(angle)], axis=1))
    step = max(rows_x // 2, min(8, rows_x))

    def body(*refs):
        third_kernel(counts, *refs)

    return pl.pallas_call(
        body,
        grid=(rows_x // step,),
        in_specs=[
            whole(table.shape),
            pl.BlockSpec((step, rows_y, length), lambda i: (i, 0, 0)),
        ],
        out_specs=[
            whole((wide, sides, ranks, count, rows_x, 2 * rows_y)) for count in counts
        ],
        out_shape=[
            pltpu.VMEM((wide, sides, ranks, count, rows_x, 2 * rows_y), jnp.float32)
            for count in counts
        ],
        compiler_params=params(1),
        cost_estimate=cost(density.size * length, 12 * density.size),
    )(in_hbm(table), in_hbm(density))


PAIR = 2


def turn(angle):
    cosine, sine = np.cos(angle), np.sin(angle)
    return np.block([[cosine, -sine], [sine, cosine]])


def hand_on(sources, targets):
    @pl.when(pl.program_id(0) == 0)
    def _():
        for source, target in zip(sources, targets):
            target[...] = source[...]


def spectrum_kernel(slab, groups, first_c, filled, side_ref, start_ref, *refs):
    tables, in_ref, outs = refs[:5], refs[5], refs[6 + filled :]
    a_ref, b_ref, second_ref, first_ref, back_ref = tables
    hand_on(tables, outs[groups:])
    outs = outs[:groups]
    wide, narrow, _, rows_x, lanes = in_ref.shape
    length = wide * rows_x
    half = length // 2
    quarter = half // 2
    devices, tiles, message, tile = outs[0].shape
    count = slab // groups
    sign_back = 1.0 - 2.0 * side_ref[0].astype(jnp.float32)

    def column(c, n):
        return in_ref[:, n, c].reshape(length, lanes)

    def columns(numbers):
        return jnp.concatenate(
            [
                jnp.concatenate([column(c, n) for n in numbers], axis=1)
                for c in range(PAIR)
            ],
            axis=0,
        )

    low, high = columns(range(narrow // 2)), columns(range(narrow // 2, narrow))
    planes = [
        product(split(low + high), pair(second_ref.at[0])),
        product(split(low - high), pair(second_ref.at[1])),
    ]

    def stacked(sign):
        return jnp.concatenate(
            [
                jnp.concatenate(
                    [
                        plane[c * length : c * length + half, part * half : (part + 1) * half]
                        + sign
                        * plane[c * length + half : (c + 1) * length, part * half : (part + 1) * half]
                        for c in range(PAIR)
                        for plane in planes
                    ],
                    axis=1,
                )
                for part in range(2)
            ],
            axis=0,
        )

    squared_b, scale_b = b_ref[0], b_ref[1]
    field = []
    for parity, sign in ((0, 1.0), (1, -1.0)):
        value = product(pair(first_ref.at[parity]), split(stacked(sign)))
        smooth = []
        for c in range(PAIR):
            spot_c = start_ref[0] + (first_c + pl.program_id(0) * PAIR + c)
            wave_c = jnp.full_like(squared_b, spot_c.astype(jnp.float32)) * (2.0 * math.pi / length)
            scale_c = jnp.exp(-0.5 * wave_c * wave_c) * (1.0 / float(length) ** 3)
            squared = a_ref[1, parity] + (squared_b + wave_c * wave_c)
            inverse = scale_c / jnp.where(squared > 0, squared, 1.0)
            smooth.append(jnp.where(squared > 0, inverse * scale_b, 0.0) * a_ref[2, parity])
        smooth = jnp.concatenate(smooth, axis=1)
        field.append(value * jnp.concatenate([smooth, smooth], axis=0))
    upper = lax.broadcasted_iota(jnp.int32, (devices, message, tile), 1) < count
    for number in range(3):
        folded = jnp.concatenate(
            [
                field[parity][part * half : part * half + quarter]
                + sign_back * field[parity][part * half + quarter : (part + 1) * half]
                for part in range(2)
                for parity in range(2)
            ],
            axis=0,
        )
        values = [
            product(
                pair(back_ref.at[0, c % back_ref.shape[1]]),
                split(folded[:, c * length : (c + 1) * length]),
            )
            for c in range(PAIR)
        ]
        for spot in range(tiles // 3):
            parity, part = divmod(spot, 2)
            at = number * (tiles // 3) + spot
            here = [
                value[part * half : (part + 1) * half, parity * tile : (parity + 1) * tile]
                for value in values
            ]
            if groups == 2:
                even, odd = [value.reshape(devices, message, tile) for value in here]
                outs[0][:, at] = jnp.where(upper, even, odd)
                outs[1][:, at] = jnp.where(upper, odd, even)
            else:
                flat = outs[0].reshape(devices * tiles * message, tile)
                for c in range(PAIR):
                    for x in range(slab):
                        start = at * message + c * count + x
                        flat[pl.ds(start, devices, stride=tiles * message), :] = here[c][
                            x * devices : (x + 1) * devices
                        ]
        if number < 2:
            for parity in range(2):
                wave_a = a_ref[0, parity]
                field[parity] = field[parity] * jnp.concatenate([wave_a, wave_a], axis=0)


def halves(length):
    return np.arange(length).reshape(length // 2, 2).T


def spectrum_pass(received, side, start_c, devices, groups, steps, first_step, filled, carried):
    wide, narrow, per_c, rows_x, lanes = received.shape
    length = wide * rows_x
    rows_y = lanes // 2
    half = length // 2
    near = np.arange(half)
    split_index = halves(length)
    slab = half // devices
    second, first, back = [], [], []
    if groups == 2:
        orders = [
            near.reshape(devices, 2, slab // 2)[:, ::step].reshape(-1) for step in (1, -1)
        ]
    else:
        orders = [near.reshape(devices, slab).T.reshape(-1)]
    for parity, index in enumerate(split_index):
        table = turn(-angles(index, near, length)).reshape(2, half, 2, narrow // 2, rows_y)
        second.append(split_table(table.transpose(3, 2, 4, 0, 1).reshape(length, length)))
        first.append(split_table(turn(-angles(index, near, length))))
        columns = split_index[:, : half // 2].reshape(-1)
        back.append(
            [split_table(turn(angles(2 * order + parity, columns, length))) for order in orders]
        )
    tables = [np.stack(second), np.stack(first), np.stack([np.stack(each) for each in back])]
    wave = signed_wave(split_index, length)
    scale = np.where(split_index == half, 0.0, np.exp(-0.5 * wave**2))
    a_table = np.stack([wave, wave**2, scale]).astype(np.float32)[..., None]
    b_table = np.stack([wave**2, scale]).astype(np.float32).reshape(2, 1, length)
    message = PAIR * slab // groups
    spaces = [pltpu.VMEM, pltpu.HBM][:groups]
    out_shape = (devices, 3 * 2 * length // TILE, steps * message, TILE)
    block = out_shape[:2] + (message, TILE)

    def body(*refs):
        spectrum_kernel(slab, groups, first_step * PAIR, len(filled), *refs)

    def fixed(shape):
        return pl.BlockSpec(shape, lambda *_: (0,) * len(shape))

    tables = [a_table, b_table, *tables]
    table_specs = [fixed(table.shape) for table in tables[:4]]
    carry = [pltpu.VMEM(table.shape, table.dtype) for table in tables[:4]]
    carry.append(pltpu.VMEM((1,) + tables[4].shape[1:], tables[4].dtype))
    if carried:
        tables, last_spec = [keep(table, pltpu.VMEM) for table in carried], fixed(carry[4].shape)
    else:
        tables = [in_hbm(table) for table in tables]
        last_spec = pl.BlockSpec(carry[4].shape, lambda i, s, _: (s[0], 0, 0, 0, 0))
    if first_step + per_c // PAIR == steps:
        carry = []
    result = pl.pallas_call(
        body,
        grid_spec=pltpu.PrefetchScalarGridSpec(
            num_scalar_prefetch=2,
            grid=(per_c // PAIR,),
            in_specs=[
                *table_specs,
                last_spec,
                pl.BlockSpec((wide, narrow, PAIR, rows_x, lanes), lambda i, *_: (0, 0, i, 0, 0)),
                *[pl.BlockSpec(memory_space=pl.ANY)] * len(filled),
            ],
            out_specs=[pl.BlockSpec(block, lambda i, *_: (0, 0, first_step + i, 0))] * groups
            + [fixed(each.shape) for each in carry],
        ),
        out_shape=[space(out_shape, jnp.float32) for space in spaces] + carry,
        input_output_aliases={8 + spot: spot for spot in range(len(filled))},
        compiler_params=params(1),
        cost_estimate=cost(per_c * 7 * length**3, 20 * per_c * length**2 * 2),
    )(
        side,
        start_c,
        *tables,
        received,
        *[keep(each, space) for each, space in zip(filled, spaces)],
    )
    return result[:groups], result[groups:]


def shear_kernel(
    per_c, group, joined, row_ref, lane_ref, second_ref, third_ref, ahead_ref, last_ref, in_ref, *refs
):
    shear_ref = refs[-1]
    out_ref, carry_refs = refs[len(refs) // 2 - 1], refs[: len(refs) // 2 - 1]
    hand_on(carry_refs, refs[len(refs) // 2 : -1])
    step = pl.program_id(0)
    length = shear_ref.shape[0]
    half = length // 2
    devices, tiles, message, tile = in_ref.shape
    count = message // per_c
    flat = in_ref.reshape(devices * tiles * message, tile)

    @pl.when(step == 0)
    def _():
        shear_ref[...] = jnp.zeros_like(shear_ref)

    field = jnp.concatenate(
        [
            jnp.concatenate(
                [
                    flat[pl.ds((source * tiles + spot) * message + x, per_c, stride=count), :]
                    for x in range(count)
                    for source in range(devices)
                ],
                axis=0,
            )
            for spot in range(tiles)
        ],
        axis=1,
    )
    field = field * row_ref[0] * lane_ref[0]
    even = product(split(field[:, :length]), pair(second_ref.at[0]))
    odd = product(split(field[:, length:]), pair(second_ref.at[1]))
    near, far = even + odd, even - odd
    field = jnp.concatenate(
        [
            jnp.concatenate(
                [
                    value[x * half : (x + 1) * half, part * half : (part + 1) * half]
                    for x in range(count)
                    for value in (near, far)
                ],
                axis=1,
            )
            for part in range(2)
        ],
        axis=0,
    )
    field = product(pair(third_ref), split(field))
    shear_ref[...] += field * field

    @pl.when(step == 5)
    def _():
        ahead = jnp.concatenate(
            [shear_ref[:, x * length : (x + 1) * length] for x in range(count)], axis=0
        )
        ahead = product(split(ahead), pair(ahead_ref))
        ahead = jnp.concatenate(
            [
                jnp.concatenate(
                    [
                        ahead[x * length : (x + 1) * length, part * length : (part + 1) * length]
                        for x in range(count)
                    ],
                    axis=1,
                )
                for part in range(2)
            ],
            axis=0,
        )
        value = product(pair(last_ref), split(ahead))
        wide, narrow, message_out, _ = out_ref.shape
        rows_b = length // wide
        slots = tile // rows_b
        rows = 2 * length // slots
        run = rows // (2 * narrow * joined)
        out = out_ref.reshape(wide * narrow * message_out, tile)
        lane = lax.broadcasted_iota(jnp.int32, (rows, tile), 1) // rows_b
        for x in range(count):
            for w in range(wide):
                block, place = divmod(w, slots)
                lanes = slice(x * length + block * tile, x * length + (block + 1) * tile)
                moved = None
                for slot in range(slots):
                    piece = value[slot * rows : (slot + 1) * rows, lanes]
                    if slot != place:
                        piece = pltpu.roll(piece, (slot - place) * rows_b % tile, 1)
                    moved = piece if moved is None else jnp.where(lane == slot, piece, moved)
                for n in range(narrow):
                    for part in range(2):
                        for join in range(joined):
                            start = ((n * 2 + part) * joined + join) * run
                            piece = moved[start : start + run]
                            at = (w * narrow + n) * message_out
                            if joined == 2:
                                at += part * 2 * count + (join ^ group) * count + x
                                out[pl.ds(at, run, stride=4 * count), :] = piece
                            else:
                                at += (x * 2 + part) * run
                                out[pl.ds(at, run), :] = piece


def shear_pass(received, wide, narrow, per_c, group, joined, carry):
    devices, tiles, message, tile = received.shape
    count = message // per_c
    length = tiles * tile // 6
    half = length // 2
    index = np.arange(length)
    angle = angles(index, index, length)
    cosine, sine = np.cos(angle), np.sin(angle)
    split_index = halves(length)
    second = np.stack(
        [split_table(turn(angles(np.arange(half), b, length)).T) for b in split_index]
    )
    row_c = np.arange(half) ^ group
    weight = np.where(row_c == 0, 1.0, 2.0)
    angle = angles(index, row_c, length)
    third = np.concatenate([weight * np.cos(angle), -weight * np.sin(angle)], axis=1)
    ahead = np.concatenate([cosine, -sine], axis=1)
    slots = TILE * wide // length
    order = index.reshape(narrow, -1, joined, slots).transpose(3, 0, 2, 1)
    angle = angles(order.reshape(-1), index, length)
    last = np.stack(
        [
            np.concatenate([np.cos(angle), np.sin(angle)], axis=1),
            np.concatenate([-np.sin(angle), np.cos(angle)], axis=1),
        ]
    )
    last = last.reshape(2, slots, narrow, -1, 2 * length).transpose(1, 2, 0, 3, 4)
    last = last.reshape(2 * length, 2 * length)
    wave = signed_wave(index, length)
    wave_rows = np.tile(wave[row_c], count)
    wave_lanes = np.stack([wave[split_index]] * 2, axis=1).reshape(-1)
    twice = math.sqrt(2.0)
    one_row, one_lane = np.ones_like(wave_rows), np.ones_like(wave_lanes)
    row_factor = np.stack(
        [one_row, twice * one_row, twice * wave_rows, one_row, twice * wave_rows, wave_rows**2]
    ).astype(np.float32)[:, :, None]
    lane_factor = np.stack(
        [one_lane, wave_lanes, one_lane, wave_lanes**2, wave_lanes, one_lane]
    ).astype(np.float32)[:, None, :]
    tables = [second] + [split_table(table) for table in (third, ahead, last)]
    out_shape = (wide, narrow, count * 2 * length // (narrow * slots), TILE)

    def body(*refs):
        shear_kernel(per_c, group, joined, *refs)

    def which(i):
        return (0, 2 - (i >= 1).astype(jnp.int32) - (i >= 3).astype(jnp.int32), 0, 0)

    return pl.pallas_call(
        body,
        grid=(6,),
        in_specs=[
            pl.BlockSpec((1, count * half, 1), lambda i: (i, 0, 0)),
            pl.BlockSpec((1, 1, 2 * length), lambda i: (i, 0, 0)),
            *[whole(table.shape) for table in tables],
            pl.BlockSpec((devices, tiles // 3, message, tile), which),
            *[whole(each.shape) for each in carry],
        ],
        out_specs=[whole(out_shape)] + [whole(each.shape) for each in carry],
        out_shape=[pltpu.HBM(out_shape, jnp.float32)]
        + [pltpu.VMEM(each.shape, each.dtype) for each in carry],
        scratch_shapes=[pltpu.VMEM((length, count * length), jnp.float32)],
        compiler_params=params(1, 60 * 1024 * 1024),
        cost_estimate=cost(count * 18 * length**3, 4 * received.size + 4 * 2**20),
    )(
        *[in_hbm(value) for value in (row_factor, lane_factor, *tables)],
        received,
        *[in_hbm(each) for each in carry],
    )


def first_kernel(count, rows_b, anchor_ref, table_ref, *refs):
    ins, (real_ref, imag_ref) = refs[:-2], refs[-2:]
    wide, sides, ranks, rows, lanes = ins[0].shape
    length = real_ref.shape[2]
    half = length // 2
    slots = lanes // rows_b
    joined = len(ins)
    steps = real_ref.shape[0] // (slots * joined)
    spot_row = lax.broadcasted_iota(jnp.int32, (lanes, half), 0)
    spot_a = lax.broadcasted_iota(jnp.int32, (lanes, half), 1)
    is_anchor = (anchor_ref[0] == 1) & (pl.program_id(0) == 0)
    start = pl.program_id(0) * steps
    anchor = (spot_row == 0) & (spot_a == 0) & is_anchor
    upper = lax.broadcasted_iota(jnp.int32, (wide * ranks, joined * count, lanes), 1) < count

    def gathered(side, step, part):
        if joined == 2:
            at = ((start + step) * 2 + part) * 2 * count
            at = pl.ds(pl.multiple_of(at, 2 * count), 2 * count)
            own, other = [
                ref[:, side, :, at].reshape(wide * ranks, 2 * count, lanes) for ref in ins
            ]
            both = [jnp.where(upper, own, other), jnp.where(upper, other, own)]
            return [value.reshape(half, lanes).T for value in both]
        flat = ins[0].reshape(wide * sides * ranks * rows, lanes)
        run = rows // count
        value = jnp.concatenate(
            [
                flat[
                    pl.ds((w * sides + side) * ranks * rows + part * steps + step, ranks * count, stride=run),
                    :,
                ]
                for w in range(wide)
            ],
            axis=0,
        )
        return [value.T]

    lefts = []
    for side in range(sides):
        tiles = [[gathered(side, step, part) for part in range(2)] for step in range(steps)]
        lefts.append(
            [
                jnp.concatenate(
                    [jnp.concatenate([part[join] for part in parts], axis=1) for parts in tiles], axis=0
                )
                for join in range(joined)
            ]
        )
    for join in range(joined):
        sums = [
            product(split(lefts[side][join]), pair(table_ref.at[join, side])) for side in range(sides)
        ]
        even, odd = sums
        for far, value in enumerate((even + odd, even - odd)):
            for step in range(steps):
                at = (step * joined + join) * slots
                columns = slice(far * half, (far + 1) * half)
                for part, ref in enumerate((real_ref, imag_ref)):
                    here = value[step * lanes : (step + 1) * lanes, part * half : (part + 1) * half]
                    if at == 0 and far == 0:
                        here = jnp.where(anchor, 0.0, here)
                    ref[at : at + slots, :, columns] = here.reshape(slots, rows_b, half)


def first_table(length, devices, joined, count, sides):
    scale = 1.0 / float(length) ** 1.5
    index = np.arange(length).reshape(devices, joined, count, sides)
    tables = []
    for join in range(joined):
        order = index[:, :: 1 - 2 * join].transpose(3, 0, 1, 2).reshape(sides, -1)
        tables.append(
            [split_table(scale * turn(-angles(np.arange(length // 2), x, length)).T) for x in order]
        )
    return np.stack([np.stack(each) for each in tables])


def first_pass(parts, table, is_anchor, length, wide, sides, count):
    devices, rows, lanes = parts[0].shape
    joined = len(parts)
    ranks = devices // wide // sides
    rows_b = length // wide
    slots = lanes // rows_b
    total = rows // (2 * joined * count) if joined == 2 else rows // (2 * count)
    grid = total if joined == 2 else 1
    parts = [part.reshape(wide, sides, ranks, rows, lanes) for part in parts]

    def body(*refs):
        first_kernel(count, rows_b, *refs)

    rows_c = total * joined * slots
    out_shape = jax.ShapeDtypeStruct((rows_c, rows_b, length), jnp.float32)
    return pl.pallas_call(
        body,
        grid=(grid,),
        in_specs=[
            pl.BlockSpec(memory_space=pltpu.SMEM),
            whole(table.shape),
            *[whole((wide, sides, ranks, rows, lanes))] * joined,
        ],
        out_specs=[pl.BlockSpec((rows_c // grid, rows_b, length), lambda i: (i, 0, 0))] * 2,
        out_shape=[out_shape] * 2,
        compiler_params=params(1),
        cost_estimate=cost(rows_c * 2 * rows_b * length * length, 16 * rows_c * rows_b * length),
    )(is_anchor, in_hbm(table), *[keep(part, pltpu.VMEM) for part in parts])


def transpose(value, members=None):
    return lax.all_to_all(
        value, AXES, split_axis=0, concat_axis=0, tiled=True, axis_index_groups=members
    )


def solution(mesh):
    wide, narrow = mesh.shape["wide"], mesh.shape["narrow"]
    sides = 2
    ranks = narrow // sides
    devices = wide * ranks
    members = [
        [w * narrow + side * ranks + rank for w in range(wide) for rank in range(ranks)]
        for side in range(sides)
    ]

    def per_device(density):
        rows_x, rows_y, length = density.shape
        half = length // 2
        per_c = half // devices
        slab = half // devices
        steps = per_c // PAIR
        counts = [per_c - PAIR, PAIR] if steps > 1 else [per_c]
        groups = 2 if slab > 2 else 1
        spot_wide, spot_narrow = lax.axis_index("wide"), lax.axis_index("narrow")
        side = (spot_narrow // ranks).astype(jnp.int32).reshape(1)
        rank = spot_wide * ranks + spot_narrow % ranks
        start_c = (rank * per_c).astype(jnp.int32).reshape(1)
        chunks, carried, start = [], [], 0
        for planes, count in zip(third_pass(density, wide, sides, ranks, counts), counts):
            planes = transpose(planes.reshape(wide * narrow, count, rows_x, 2 * rows_y))
            planes = planes.reshape(wide, narrow, count, rows_x, 2 * rows_y)
            planes = keep(planes, pltpu.VMEM if start else pltpu.HBM)
            chunks, carried = spectrum_pass(
                planes, side, start_c, devices, groups, steps, start // PAIR, chunks, carried
            )
            start += count
        is_anchor = ((spot_wide == 0) & (spot_narrow == 0)).astype(jnp.int32).reshape(1)
        parts = []
        table = first_table(length, devices, groups, slab // groups, sides)
        for group, chunk in enumerate(chunks):
            received = in_hbm(transpose(chunk, members))
            (part,) = shear_pass(received, wide, narrow, per_c, group, groups, [])
            parts.append(transpose(part.reshape((wide * narrow,) + part.shape[2:])))
        return tuple(first_pass(parts, table, is_anchor, length, wide, sides, slab // groups))

    return jax.shard_map(
        per_device,
        mesh=mesh,
        in_specs=(P("wide", "narrow", None),),
        out_specs=(P("narrow", "wide", None), P("narrow", "wide", None)),
        check_vma=False,
    )
```

```python
import math

import jax
import jax.numpy as jnp
import ml_dtypes
import numpy as np
from jax import lax
from jax.experimental import pallas as pl
from jax.experimental.pallas import tpu as pltpu
from jax.sharding import PartitionSpec as P

AXES = ("wide", "narrow")
TILE = 128
LIMIT = 16 * 1024 * 1024


def angles(rows, columns, length):
    return (2.0 * math.pi / length) * (np.outer(rows, columns) % length)


def split_table(table):
    table = np.asarray(table, np.float64)
    high = table.astype(ml_dtypes.bfloat16)
    low = (table - high.astype(np.float64)).astype(ml_dtypes.bfloat16)
    return np.stack([high, low])


def split(value):
    high = value.astype(jnp.bfloat16)
    low = (value - high.astype(jnp.float32)).astype(jnp.bfloat16)
    return high, low


def product(left, right, contract=((1,), (0,))):
    (left_axis,), (right_axis,) = contract
    left = jnp.concatenate([left[0], left[0], left[1]], axis=left_axis)
    right = jnp.concatenate([right[0], right[1], right[0]], axis=right_axis)
    return lax.dot_general(
        left, right, (contract, ((), ())), preferred_element_type=jnp.float32
    )


def pair(ref):
    return ref[0], ref[1]


def signed_wave(index, length):
    index = np.asarray(index)
    return np.where(index < length // 2, index, index - length) * (2.0 * math.pi / length)


def params(steps):
    return pltpu.CompilerParams(
        vmem_limit_bytes=LIMIT, dimension_semantics=("arbitrary",) * steps
    )


def whole(shape):
    return pl.BlockSpec(shape, lambda *_: (0,) * len(shape))


def keep(value, space):
    return pltpu.with_memory_space_constraint(jnp.asarray(value), space)


def in_hbm(value):
    return keep(value, pltpu.HBM)


def cost(macs, moved):
    return pl.CostEstimate(flops=6 * macs, bytes_accessed=moved, transcendentals=0)


def third_kernel(counts, table_ref, density_ref, *outs):
    step_x, rows_y, length = density_ref.shape
    wide, sides, ranks, _, rows_x, _ = outs[0].shape
    half = length // 2
    flats = [ref.reshape(math.prod(ref.shape[:5]), 2 * rows_y) for ref in outs]
    table = pair(table_ref)
    group = step_x
    start_x = pl.program_id(0) * step_x
    for first in range(0, step_x, group):
        block = density_ref[first : first + group].reshape(group * rows_y, length)
        result = product(split(block), table)
        for inner in range(group):
            rows = slice(inner * rows_y, (inner + 1) * rows_y)
            value = jnp.concatenate([result[rows, :half], result[rows, half:]], axis=0).T
            start = 0
            for flat, count in zip(flats, counts):
                for c in range(count):
                    for rank in range(ranks):
                        at = (rank * count + c) * rows_x + first + inner + start_x
                        stride = sides * ranks * count * rows_x
                        flat[pl.ds(at, wide, stride=stride), :] = value[start : start + wide]
                        start += wide
    for ref in outs:
        rows = pl.ds(pl.multiple_of(start_x, step_x), step_x)
        for side in range(1, sides):
            ref[:, side, :, :, rows] = ref[:, 0, :, :, rows]


def third_pass(density, wide, sides, ranks, counts):
    rows_x, rows_y, length = density.shape
    half = length // 2
    per_c = sum(counts)
    order = np.arange(half).reshape(wide, ranks, per_c).transpose(2, 1, 0).reshape(-1)
    angle = angles(np.arange(length), order, length)
    table = split_table(np.concatenate([np.cos(angle), -np.sin(angle)], axis=1))
    step = max(rows_x // 2, min(8, rows_x))

    def body(*refs):
        third_kernel(counts, *refs)

    return pl.pallas_call(
        body,
        grid=(rows_x // step,),
        in_specs=[
            whole(table.shape),
            pl.BlockSpec((step, rows_y, length), lambda i: (i, 0, 0)),
        ],
        out_specs=[
            whole((wide, sides, ranks, count, rows_x, 2 * rows_y)) for count in counts
        ],
        out_shape=[
            pltpu.VMEM((wide, sides, ranks, count, rows_x, 2 * rows_y), jnp.float32)
            for count in counts
        ],
        compiler_params=params(1),
        cost_estimate=cost(density.size * length, 12 * density.size),
    )(in_hbm(table), in_hbm(density))


PAIR = 2


def turn(angle):
    cosine, sine = np.cos(angle), np.sin(angle)
    return np.block([[cosine, -sine], [sine, cosine]])


def hand_on(sources, targets):
    @pl.when(pl.program_id(0) == 0)
    def _():
        for source, target in zip(sources, targets):
            target[...] = source[...]


def spectrum_kernel(slab, groups, first_c, filled, side_ref, start_ref, *refs):
    tables, in_ref, outs = refs[:5], refs[5], refs[6 + filled :]
    a_ref, b_ref, second_ref, first_ref, back_ref = tables
    hand_on(tables, outs[groups:])
    outs = outs[:groups]
    wide, narrow, _, rows_x, lanes = in_ref.shape
    length = wide * rows_x
    half = length // 2
    quarter = half // 2
    devices, tiles, message, tile = outs[0].shape
    count = slab // groups
    sign_back = 1.0 - 2.0 * side_ref[0].astype(jnp.float32)

    def column(c, n):
        return in_ref[:, n, c].reshape(length, lanes)

    def columns(numbers):
        return jnp.concatenate(
            [
                jnp.concatenate([column(c, n) for n in numbers], axis=1)
                for c in range(PAIR)
            ],
            axis=0,
        )

    low, high = columns(range(narrow // 2)), columns(range(narrow // 2, narrow))
    planes = [
        product(split(low + high), pair(second_ref.at[0])),
        product(split(low - high), pair(second_ref.at[1])),
    ]

    def stacked(sign):
        return jnp.concatenate(
            [
                jnp.concatenate(
                    [
                        plane[c * length : c * length + half, part * half : (part + 1) * half]
                        + sign
                        * plane[c * length + half : (c + 1) * length, part * half : (part + 1) * half]
                        for c in range(PAIR)
                        for plane in planes
                    ],
                    axis=1,
                )
                for part in range(2)
            ],
            axis=0,
        )

    squared_b, scale_b = b_ref[0], b_ref[1]
    field = []
    for parity, sign in ((0, 1.0), (1, -1.0)):
        value = product(pair(first_ref.at[parity]), split(stacked(sign)))
        smooth = []
        for c in range(PAIR):
            spot_c = start_ref[0] + (first_c + pl.program_id(0) * PAIR + c)
            wave_c = jnp.full_like(squared_b, spot_c.astype(jnp.float32)) * (2.0 * math.pi / length)
            scale_c = jnp.exp(-0.5 * wave_c * wave_c) * (1.0 / float(length) ** 3)
            squared = a_ref[1, parity] + (squared_b + wave_c * wave_c)
            inverse = scale_c / jnp.where(squared > 0, squared, 1.0)
            smooth.append(jnp.where(squared > 0, inverse * scale_b, 0.0) * a_ref[2, parity])
        smooth = jnp.concatenate(smooth, axis=1)
        field.append(value * jnp.concatenate([smooth, smooth], axis=0))
    upper = lax.broadcasted_iota(jnp.int32, (devices, message, tile), 1) < count
    for number in range(3):
        folded = jnp.concatenate(
            [
                field[parity][part * half : part * half + quarter]
                + sign_back * field[parity][part * half + quarter : (part + 1) * half]
                for part in range(2)
                for parity in range(2)
            ],
            axis=0,
        )
        values = [
            product(
                pair(back_ref.at[0, c % back_ref.shape[1]]),
                split(folded[:, c * length : (c + 1) * length]),
            )
            for c in range(PAIR)
        ]
        for spot in range(tiles // 3):
            parity, part = divmod(spot, 2)
            at = number * (tiles // 3) + spot
            here = [
                value[part * half : (part + 1) * half, parity * tile : (parity + 1) * tile]
                for value in values
            ]
            if groups == 2:
                even, odd = [value.reshape(devices, message, tile) for value in here]
                outs[0][:, at] = jnp.where(upper, even, odd)
                outs[1][:, at] = jnp.where(upper, odd, even)
            else:
                flat = outs[0].reshape(devices * tiles * message, tile)
                for c in range(PAIR):
                    for x in range(slab):
                        start = at * message + c * count + x
                        flat[pl.ds(start, devices, stride=tiles * message), :] = here[c][
                            x * devices : (x + 1) * devices
                        ]
        if number < 2:
            for parity in range(2):
                wave_a = a_ref[0, parity]
                field[parity] = field[parity] * jnp.concatenate([wave_a, wave_a], axis=0)


def halves(length):
    return np.arange(length).reshape(length // 2, 2).T


def spectrum_pass(received, side, start_c, devices, groups, steps, first_step, filled, carried):
    wide, narrow, per_c, rows_x, lanes = received.shape
    length = wide * rows_x
    rows_y = lanes // 2
    half = length // 2
    near = np.arange(half)
    split_index = halves(length)
    slab = half // devices
    second, first, back = [], [], []
    if groups == 2:
        orders = [
            near.reshape(devices, 2, slab // 2)[:, ::step].reshape(-1) for step in (1, -1)
        ]
    else:
        orders = [near.reshape(devices, slab).T.reshape(-1)]
    for parity, index in enumerate(split_index):
        table = turn(-angles(index, near, length)).reshape(2, half, 2, narrow // 2, rows_y)
        second.append(split_table(table.transpose(3, 2, 4, 0, 1).reshape(length, length)))
        first.append(split_table(turn(-angles(index, near, length))))
        columns = split_index[:, : half // 2].reshape(-1)
        back.append(
            [split_table(turn(angles(2 * order + parity, columns, length))) for order in orders]
        )
    tables = [np.stack(second), np.stack(first), np.stack([np.stack(each) for each in back])]
    wave = signed_wave(split_index, length)
    scale = np.where(split_index == half, 0.0, np.exp(-0.5 * wave**2))
    a_table = np.stack([wave, wave**2, scale]).astype(np.float32)[..., None]
    b_table = np.stack([wave**2, scale]).astype(np.float32).reshape(2, 1, length)
    message = PAIR * slab // groups
    spaces = [pltpu.HBM] * groups
    out_shape = (devices, 3 * 2 * length // TILE, steps * message, TILE)
    block = out_shape[:2] + (message, TILE)

    def body(*refs):
        spectrum_kernel(slab, groups, first_step * PAIR, len(filled), *refs)

    def fixed(shape):
        return pl.BlockSpec(shape, lambda *_: (0,) * len(shape))

    tables = [a_table, b_table, *tables]
    table_specs = [fixed(table.shape) for table in tables[:4]]
    carry = [pltpu.VMEM(table.shape, table.dtype) for table in tables[:4]]
    carry.append(pltpu.VMEM((1,) + tables[4].shape[1:], tables[4].dtype))
    if carried:
        tables, last_spec = [keep(table, pltpu.VMEM) for table in carried], fixed(carry[4].shape)
    else:
        tables = [in_hbm(table) for table in tables]
        last_spec = pl.BlockSpec(carry[4].shape, lambda i, s, _: (s[0], 0, 0, 0, 0))
    if first_step + per_c // PAIR == steps:
        carry = []
    result = pl.pallas_call(
        body,
        grid_spec=pltpu.PrefetchScalarGridSpec(
            num_scalar_prefetch=2,
            grid=(per_c // PAIR,),
            in_specs=[
                *table_specs,
                last_spec,
                pl.BlockSpec((wide, narrow, PAIR, rows_x, lanes), lambda i, *_: (0, 0, i, 0, 0)),
                *[pl.BlockSpec(memory_space=pl.ANY)] * len(filled),
            ],
            out_specs=[pl.BlockSpec(block, lambda i, *_: (0, 0, first_step + i, 0))] * groups
            + [fixed(each.shape) for each in carry],
        ),
        out_shape=[space(out_shape, jnp.float32) for space in spaces] + carry,
        input_output_aliases={8 + spot: spot for spot in range(len(filled))},
        compiler_params=params(1),
        cost_estimate=cost(per_c * 7 * length**3, 20 * per_c * length**2 * 2),
    )(
        side,
        start_c,
        *tables,
        received,
        *[keep(each, space) for each, space in zip(filled, spaces)],
    )
    return result[:groups], result[groups:]


def shear_kernel(
    per_c, group, joined, row_ref, lane_ref, second_ref, third_ref, ahead_ref, last_ref, in_ref, *refs
):
    out_ref, shear_ref = refs
    step = pl.program_id(0)
    length = shear_ref.shape[0]
    half = length // 2
    devices, tiles, message, tile = in_ref.shape
    count = message // per_c
    flat = in_ref.reshape(devices * tiles * message, tile)

    @pl.when(step == 0)
    def _():
        shear_ref[...] = jnp.zeros_like(shear_ref)

    field = jnp.concatenate(
        [
            jnp.concatenate(
                [
                    flat[pl.ds((source * tiles + spot) * message + x, per_c, stride=count), :]
                    for x in range(count)
                    for source in range(devices)
                ],
                axis=0,
            )
            for spot in range(tiles)
        ],
        axis=1,
    )
    field = field * row_ref[0] * lane_ref[0]
    even = product(split(field[:, :length]), pair(second_ref.at[0]))
    odd = product(split(field[:, length:]), pair(second_ref.at[1]))
    near, far = even + odd, even - odd
    field = jnp.concatenate(
        [
            jnp.concatenate(
                [
                    value[x * half : (x + 1) * half, part * half : (part + 1) * half]
                    for x in range(count)
                    for value in (near, far)
                ],
                axis=1,
            )
            for part in range(2)
        ],
        axis=0,
    )
    field = product(pair(third_ref), split(field))
    shear_ref[...] += field * field

    @pl.when(step == 5)
    def _():
        ahead = jnp.concatenate(
            [shear_ref[:, x * length : (x + 1) * length] for x in range(count)], axis=0
        )
        ahead = product(split(ahead), pair(ahead_ref))
        ahead = jnp.concatenate(
            [
                jnp.concatenate(
                    [
                        ahead[x * length : (x + 1) * length, part * length : (part + 1) * length]
                        for x in range(count)
                    ],
                    axis=1,
                )
                for part in range(2)
            ],
            axis=0,
        )
        value = product(pair(last_ref), split(ahead))
        wide, narrow, message_out, _ = out_ref.shape
        rows_b = length // wide
        slots = tile // rows_b
        rows = 2 * length // slots
        run = rows // (2 * narrow * joined)
        out = out_ref.reshape(wide * narrow * message_out, tile)
        lane = lax.broadcasted_iota(jnp.int32, (rows, tile), 1) // rows_b
        for x in range(count):
            for w in range(wide):
                block, place = divmod(w, slots)
                lanes = slice(x * length + block * tile, x * length + (block + 1) * tile)
                moved = None
                for slot in range(slots):
                    piece = value[slot * rows : (slot + 1) * rows, lanes]
                    if slot != place:
                        piece = pltpu.roll(piece, (slot - place) * rows_b % tile, 1)
                    moved = piece if moved is None else jnp.where(lane == slot, piece, moved)
                for n in range(narrow):
                    for part in range(2):
                        for join in range(joined):
                            start = ((n * 2 + part) * joined + join) * run
                            piece = moved[start : start + run]
                            at = (w * narrow + n) * message_out
                            if joined == 2:
                                at += part * 2 * count + (join ^ group) * count + x
                                out[pl.ds(at, run, stride=4 * count), :] = piece
                            else:
                                at += (x * 2 + part) * run
                                out[pl.ds(at, run), :] = piece


def shear_pass(received, wide, narrow, per_c, group, joined):
    devices, tiles, message, tile = received.shape
    count = message // per_c
    length = tiles * tile // 6
    half = length // 2
    index = np.arange(length)
    angle = angles(index, index, length)
    cosine, sine = np.cos(angle), np.sin(angle)
    split_index = halves(length)
    second = np.stack(
        [split_table(turn(angles(np.arange(half), b, length)).T) for b in split_index]
    )
    row_c = np.arange(half) ^ group
    weight = np.where(row_c == 0, 1.0, 2.0)
    angle = angles(index, row_c, length)
    third = np.concatenate([weight * np.cos(angle), -weight * np.sin(angle)], axis=1)
    ahead = np.concatenate([cosine, -sine], axis=1)
    slots = TILE * wide // length
    order = index.reshape(narrow, -1, joined, slots).transpose(3, 0, 2, 1)
    angle = angles(order.reshape(-1), index, length)
    last = np.stack(
        [
            np.concatenate([np.cos(angle), np.sin(angle)], axis=1),
            np.concatenate([-np.sin(angle), np.cos(angle)], axis=1),
        ]
    )
    last = last.reshape(2, slots, narrow, -1, 2 * length).transpose(1, 2, 0, 3, 4)
    last = last.reshape(2 * length, 2 * length)
    wave = signed_wave(index, length)
    wave_rows = np.tile(wave[row_c], count)
    wave_lanes = np.stack([wave[split_index]] * 2, axis=1).reshape(-1)
    twice = math.sqrt(2.0)
    one_row, one_lane = np.ones_like(wave_rows), np.ones_like(wave_lanes)
    row_factor = np.stack(
        [one_row, twice * one_row, twice * wave_rows, one_row, twice * wave_rows, wave_rows**2]
    ).astype(np.float32)[:, :, None]
    lane_factor = np.stack(
        [one_lane, wave_lanes, one_lane, wave_lanes**2, wave_lanes, one_lane]
    ).astype(np.float32)[:, None, :]
    tables = [second] + [split_table(table) for table in (third, ahead, last)]
    out_shape = (wide, narrow, count * 2 * length // (narrow * slots), TILE)

    def body(*refs):
        shear_kernel(per_c, group, joined, *refs)

    def which(i):
        return (0, 2 - (i >= 1).astype(jnp.int32) - (i >= 3).astype(jnp.int32), 0, 0)

    return pl.pallas_call(
        body,
        grid=(6,),
        in_specs=[
            pl.BlockSpec((1, count * half, 1), lambda i: (i, 0, 0)),
            pl.BlockSpec((1, 1, 2 * length), lambda i: (i, 0, 0)),
            *[whole(table.shape) for table in tables],
            pl.BlockSpec((devices, tiles // 3, message, tile), which),
        ],
        out_specs=[whole(out_shape)],
        out_shape=[pltpu.HBM(out_shape, jnp.float32)],
        scratch_shapes=[pltpu.VMEM((length, count * length), jnp.float32)],
        compiler_params=params(1),
        cost_estimate=cost(count * 18 * length**3, 4 * received.size + 4 * 2**20),
    )(
        *[in_hbm(value) for value in (row_factor, lane_factor, *tables)],
        received,
    )


def first_kernel(count, rows_b, anchor_ref, table_ref, *refs):
    ins, (real_ref, imag_ref) = refs[:-2], refs[-2:]
    wide, sides, ranks, rows, lanes = ins[0].shape
    length = real_ref.shape[2]
    half = length // 2
    slots = lanes // rows_b
    joined = len(ins)
    steps = real_ref.shape[0] // (slots * joined)
    spot_row = lax.broadcasted_iota(jnp.int32, (lanes, half), 0)
    spot_a = lax.broadcasted_iota(jnp.int32, (lanes, half), 1)
    is_anchor = (anchor_ref[0] == 1) & (pl.program_id(0) == 0)
    start = pl.program_id(0) * steps
    anchor = (spot_row == 0) & (spot_a == 0) & is_anchor
    upper = lax.broadcasted_iota(jnp.int32, (wide * ranks, joined * count, lanes), 1) < count

    def gathered(side, step, part):
        if joined == 2:
            at = ((start + step) * 2 + part) * 2 * count
            at = pl.ds(pl.multiple_of(at, 2 * count), 2 * count)
            own, other = [
                ref[:, side, :, at].reshape(wide * ranks, 2 * count, lanes) for ref in ins
            ]
            both = jnp.where(upper, own, other), pltpu.roll(jnp.where(upper, other, own), count, 1)
            return [value.reshape(half, lanes).T for value in both]
        flat = ins[0].reshape(wide * sides * ranks * rows, lanes)
        run = rows // count
        value = jnp.concatenate(
            [
                flat[
                    pl.ds((w * sides + side) * ranks * rows + part * steps + step, ranks * count, stride=run),
                    :,
                ]
                for w in range(wide)
            ],
            axis=0,
        )
        return [value.T]

    sums = []
    for side in range(sides):
        tiles = [[gathered(side, step, part) for part in range(2)] for step in range(steps)]
        left = jnp.concatenate(
            [
                jnp.concatenate([part[join] for part in parts], axis=1)
                for parts in tiles
                for join in range(joined)
            ],
            axis=0,
        )
        sums.append(product(split(left), pair(table_ref.at[side])))
    even, odd = sums
    for far, value in enumerate((even + odd, even - odd)):
        columns = slice(far * half, (far + 1) * half)
        for at in range(steps * joined):
            for part, ref in enumerate((real_ref, imag_ref)):
                here = value[at * lanes : (at + 1) * lanes, part * half : (part + 1) * half]
                if at == 0 and far == 0:
                    here = jnp.where(anchor, 0.0, here)
                ref[at * slots : (at + 1) * slots, :, columns] = here.reshape(slots, rows_b, half)


def first_table(length, devices, sides):
    scale = 1.0 / float(length) ** 1.5
    order = np.arange(length).reshape(devices, -1, sides).transpose(2, 0, 1).reshape(sides, -1)
    return np.stack(
        [split_table(scale * turn(-angles(np.arange(length // 2), x, length)).T) for x in order]
    )


def first_pass(parts, table, is_anchor, length, wide, sides, count):
    devices, rows, lanes = parts[0].shape
    joined = len(parts)
    ranks = devices // wide // sides
    rows_b = length // wide
    slots = lanes // rows_b
    total = rows // (2 * joined * count) if joined == 2 else rows // (2 * count)
    grid = 4 if joined == 2 and total % 4 == 0 else 1
    parts = [part.reshape(wide, sides, ranks, rows, lanes) for part in parts]

    def body(*refs):
        first_kernel(count, rows_b, *refs)

    rows_c = total * joined * slots
    out_shape = jax.ShapeDtypeStruct((rows_c, rows_b, length), jnp.float32)
    return pl.pallas_call(
        body,
        grid=(grid,),
        in_specs=[
            pl.BlockSpec(memory_space=pltpu.SMEM),
            whole(table.shape),
            *[whole((wide, sides, ranks, rows, lanes))] * joined,
        ],
        out_specs=[pl.BlockSpec((rows_c // grid, rows_b, length), lambda i: (i, 0, 0))] * 2,
        out_shape=[out_shape] * 2,
        compiler_params=params(1),
        cost_estimate=cost(rows_c * 2 * rows_b * length * length, 16 * rows_c * rows_b * length),
    )(is_anchor, in_hbm(table), *[keep(part, pltpu.VMEM) for part in parts])


def transpose(value, members=None):
    return lax.all_to_all(
        value, AXES, split_axis=0, concat_axis=0, tiled=True, axis_index_groups=members
    )


def solution(mesh):
    wide, narrow = mesh.shape["wide"], mesh.shape["narrow"]
    sides = 2
    ranks = narrow // sides
    devices = wide * ranks
    members = [
        [w * narrow + side * ranks + rank for w in range(wide) for rank in range(ranks)]
        for side in range(sides)
    ]

    def per_device(density):
        rows_x, rows_y, length = density.shape
        half = length // 2
        per_c = half // devices
        slab = half // devices
        steps = per_c // PAIR
        counts = [per_c - PAIR, PAIR] if steps > 1 else [per_c]
        groups = 2 if slab > 2 else 1
        spot_wide, spot_narrow = lax.axis_index("wide"), lax.axis_index("narrow")
        side = (spot_narrow // ranks).astype(jnp.int32).reshape(1)
        rank = spot_wide * ranks + spot_narrow % ranks
        start_c = (rank * per_c).astype(jnp.int32).reshape(1)
        chunks, carried, start = [], [], 0
        for planes, count in zip(third_pass(density, wide, sides, ranks, counts), counts):
            planes = transpose(planes.reshape(wide * narrow, count, rows_x, 2 * rows_y))
            planes = planes.reshape(wide, narrow, count, rows_x, 2 * rows_y)
            planes = keep(planes, pltpu.VMEM if start else pltpu.HBM)
            chunks, carried = spectrum_pass(
                planes, side, start_c, devices, groups, steps, start // PAIR, chunks, carried
            )
            start += count
        is_anchor = ((spot_wide == 0) & (spot_narrow == 0)).astype(jnp.int32).reshape(1)
        parts = []
        table = first_table(length, devices, sides)
        for group, chunk in enumerate(chunks):
            received = keep(transpose(chunk, members), pltpu.VMEM if group else pltpu.HBM)
            (part,) = shear_pass(received, wide, narrow, per_c, group, groups)
            parts.append(transpose(part.reshape((wide * narrow,) + part.shape[2:])))
        return tuple(first_pass(parts, table, is_anchor, length, wide, sides, slab // groups))

    return jax.shard_map(
        per_device,
        mesh=mesh,
        in_specs=(P("wide", "narrow", None),),
        out_specs=(P("narrow", "wide", None), P("narrow", "wide", None)),
        check_vma=False,
    )
```

```python
import math

import jax
import jax.numpy as jnp
import ml_dtypes
import numpy as np
from jax import lax
from jax.experimental import pallas as pl
from jax.experimental.pallas import tpu as pltpu
from jax.sharding import PartitionSpec as P

AXES = ("wide", "narrow")
TILE = 128
LIMIT = 16 * 1024 * 1024


def angles(rows, columns, length):
    return (2.0 * math.pi / length) * (np.outer(rows, columns) % length)


def split_table(table):
    table = np.asarray(table, np.float64)
    high = table.astype(ml_dtypes.bfloat16)
    low = (table - high.astype(np.float64)).astype(ml_dtypes.bfloat16)
    return np.stack([high, low])


def split(value):
    high = value.astype(jnp.bfloat16)
    low = (value - high.astype(jnp.float32)).astype(jnp.bfloat16)
    return high, low


def product(left, right, contract=((1,), (0,))):
    (left_axis,), (right_axis,) = contract
    left = jnp.concatenate([left[0], left[0], left[1]], axis=left_axis)
    right = jnp.concatenate([right[0], right[1], right[0]], axis=right_axis)
    return lax.dot_general(
        left, right, (contract, ((), ())), preferred_element_type=jnp.float32
    )


def pair(ref):
    return ref[0], ref[1]


def signed_wave(index, length):
    index = np.asarray(index)
    return np.where(index < length // 2, index, index - length) * (2.0 * math.pi / length)


def params(steps):
    return pltpu.CompilerParams(
        vmem_limit_bytes=LIMIT, dimension_semantics=("arbitrary",) * steps
    )


def whole(shape):
    return pl.BlockSpec(shape, lambda *_: (0,) * len(shape))


def keep(value, space):
    return pltpu.with_memory_space_constraint(jnp.asarray(value), space)


def in_hbm(value):
    return keep(value, pltpu.HBM)


def cost(macs, moved):
    return pl.CostEstimate(flops=6 * macs, bytes_accessed=moved, transcendentals=0)


def third_kernel(counts, table_ref, density_ref, *outs):
    step_x, rows_y, length = density_ref.shape
    wide, sides, ranks, _, rows_x, _ = outs[0].shape
    half = length // 2
    flats = [ref.reshape(math.prod(ref.shape[:5]), 2 * rows_y) for ref in outs]
    table = pair(table_ref)
    group = step_x
    start_x = pl.program_id(0) * step_x
    for first in range(0, step_x, group):
        block = density_ref[first : first + group].reshape(group * rows_y, length)
        result = product(split(block), table)
        for inner in range(group):
            rows = slice(inner * rows_y, (inner + 1) * rows_y)
            value = jnp.concatenate([result[rows, :half], result[rows, half:]], axis=0).T
            start = 0
            for flat, count in zip(flats, counts):
                for c in range(count):
                    for rank in range(ranks):
                        at = (rank * count + c) * rows_x + first + inner + start_x
                        stride = sides * ranks * count * rows_x
                        flat[pl.ds(at, wide, stride=stride), :] = value[start : start + wide]
                        start += wide
    for ref in outs:
        rows = pl.ds(pl.multiple_of(start_x, step_x), step_x)
        for side in range(1, sides):
            ref[:, side, :, :, rows] = ref[:, 0, :, :, rows]


def third_pass(density, wide, sides, ranks, counts):
    rows_x, rows_y, length = density.shape
    half = length // 2
    per_c = sum(counts)
    order = np.arange(half).reshape(wide, ranks, per_c).transpose(2, 1, 0).reshape(-1)
    angle = angles(np.arange(length), order, length)
    table = split_table(np.concatenate([np.cos(angle), -np.sin(angle)], axis=1))
    step = max(rows_x // 2, min(8, rows_x))

    def body(*refs):
        third_kernel(counts, *refs)

    return pl.pallas_call(
        body,
        grid=(rows_x // step,),
        in_specs=[
            whole(table.shape),
            pl.BlockSpec((step, rows_y, length), lambda i: (i, 0, 0)),
        ],
        out_specs=[
            whole((wide, sides, ranks, count, rows_x, 2 * rows_y)) for count in counts
        ],
        out_shape=[
            pltpu.VMEM((wide, sides, ranks, count, rows_x, 2 * rows_y), jnp.float32)
            for count in counts
        ],
        compiler_params=params(1),
        cost_estimate=cost(density.size * length, 12 * density.size),
    )(in_hbm(table), in_hbm(density))


PAIR = 2


def turn(angle):
    cosine, sine = np.cos(angle), np.sin(angle)
    return np.block([[cosine, -sine], [sine, cosine]])


def hand_on(sources, targets):
    @pl.when(pl.program_id(0) == 0)
    def _():
        for source, target in zip(sources, targets):
            target[...] = source[...]


def spectrum_kernel(slab, groups, first_c, filled, side_ref, start_ref, *refs):
    tables, in_ref, outs = refs[:5], refs[5], refs[6 + filled :]
    a_ref, b_ref, second_ref, first_ref, back_ref = tables
    hand_on(tables, outs[groups:])
    outs = outs[:groups]
    wide, narrow, _, rows_x, lanes = in_ref.shape
    length = wide * rows_x
    half = length // 2
    quarter = half // 2
    devices, tiles, message, tile = outs[0].shape
    count = slab // groups
    sign_back = 1.0 - 2.0 * side_ref[0].astype(jnp.float32)

    def column(c, n):
        return in_ref[:, n, c].reshape(length, lanes)

    def columns(numbers):
        return jnp.concatenate(
            [
                jnp.concatenate([column(c, n) for n in numbers], axis=1)
                for c in range(PAIR)
            ],
            axis=0,
        )

    low, high = columns(range(narrow // 2)), columns(range(narrow // 2, narrow))
    planes = [
        product(split(low + high), pair(second_ref.at[0])),
        product(split(low - high), pair(second_ref.at[1])),
    ]

    def stacked(sign):
        return jnp.concatenate(
            [
                jnp.concatenate(
                    [
                        plane[c * length : c * length + half, part * half : (part + 1) * half]
                        + sign
                        * plane[c * length + half : (c + 1) * length, part * half : (part + 1) * half]
                        for c in range(PAIR)
                        for plane in planes
                    ],
                    axis=1,
                )
                for part in range(2)
            ],
            axis=0,
        )

    squared_b, scale_b = b_ref[0], b_ref[1]
    field = []
    for parity, sign in ((0, 1.0), (1, -1.0)):
        value = product(pair(first_ref.at[parity]), split(stacked(sign)))
        smooth = []
        for c in range(PAIR):
            spot_c = start_ref[0] + (first_c + pl.program_id(0) * PAIR + c)
            wave_c = jnp.full_like(squared_b, spot_c.astype(jnp.float32)) * (2.0 * math.pi / length)
            scale_c = jnp.exp(-0.5 * wave_c * wave_c) * (1.0 / float(length) ** 3)
            squared = a_ref[1, parity] + (squared_b + wave_c * wave_c)
            inverse = scale_c / jnp.where(squared > 0, squared, 1.0)
            smooth.append(jnp.where(squared > 0, inverse * scale_b, 0.0) * a_ref[2, parity])
        smooth = jnp.concatenate(smooth, axis=1)
        field.append(value * jnp.concatenate([smooth, smooth], axis=0))
    upper = lax.broadcasted_iota(jnp.int32, (devices, message, tile), 1) < count
    for number in range(3):
        folded = jnp.concatenate(
            [
                field[parity][part * half : part * half + quarter]
                + sign_back * field[parity][part * half + quarter : (part + 1) * half]
                for part in range(2)
                for parity in range(2)
            ],
            axis=0,
        )
        values = [
            product(
                pair(back_ref.at[0, c % back_ref.shape[1]]),
                split(folded[:, c * length : (c + 1) * length]),
            )
            for c in range(PAIR)
        ]
        for spot in range(tiles // 3):
            parity, part = divmod(spot, 2)
            at = number * (tiles // 3) + spot
            here = [
                value[part * half : (part + 1) * half, parity * tile : (parity + 1) * tile]
                for value in values
            ]
            if groups == 2:
                even, odd = [value.reshape(devices, message, tile) for value in here]
                outs[0][:, at] = jnp.where(upper, even, odd)
                outs[1][:, at] = jnp.where(upper, odd, even)
            else:
                flat = outs[0].reshape(devices * tiles * message, tile)
                for c in range(PAIR):
                    for x in range(slab):
                        start = at * message + c * count + x
                        flat[pl.ds(start, devices, stride=tiles * message), :] = here[c][
                            x * devices : (x + 1) * devices
                        ]
        if number < 2:
            for parity in range(2):
                wave_a = a_ref[0, parity]
                field[parity] = field[parity] * jnp.concatenate([wave_a, wave_a], axis=0)


def halves(length):
    return np.arange(length).reshape(length // 2, 2).T


def spectrum_pass(received, side, start_c, devices, groups, steps, first_step, filled, carried):
    wide, narrow, per_c, rows_x, lanes = received.shape
    length = wide * rows_x
    rows_y = lanes // 2
    half = length // 2
    near = np.arange(half)
    split_index = halves(length)
    slab = half // devices
    second, first, back = [], [], []
    if groups == 2:
        orders = [
            near.reshape(devices, 2, slab // 2)[:, ::step].reshape(-1) for step in (1, -1)
        ]
    else:
        orders = [near.reshape(devices, slab).T.reshape(-1)]
    for parity, index in enumerate(split_index):
        table = turn(-angles(index, near, length)).reshape(2, half, 2, narrow // 2, rows_y)
        second.append(split_table(table.transpose(3, 2, 4, 0, 1).reshape(length, length)))
        first.append(split_table(turn(-angles(index, near, length))))
        columns = split_index[:, : half // 2].reshape(-1)
        back.append(
            [split_table(turn(angles(2 * order + parity, columns, length))) for order in orders]
        )
    tables = [np.stack(second), np.stack(first), np.stack([np.stack(each) for each in back])]
    wave = signed_wave(split_index, length)
    scale = np.where(split_index == half, 0.0, np.exp(-0.5 * wave**2))
    a_table = np.stack([wave, wave**2, scale]).astype(np.float32)[..., None]
    b_table = np.stack([wave**2, scale]).astype(np.float32).reshape(2, 1, length)
    message = PAIR * slab // groups
    spaces = [pltpu.HBM] * groups
    out_shape = (devices, 3 * 2 * length // TILE, steps * message, TILE)
    block = out_shape[:2] + (message, TILE)

    def body(*refs):
        spectrum_kernel(slab, groups, first_step * PAIR, len(filled), *refs)

    def fixed(shape):
        return pl.BlockSpec(shape, lambda *_: (0,) * len(shape))

    tables = [a_table, b_table, *tables]
    table_specs = [fixed(table.shape) for table in tables[:4]]
    carry = [pltpu.VMEM(table.shape, table.dtype) for table in tables[:4]]
    carry.append(pltpu.VMEM((1,) + tables[4].shape[1:], tables[4].dtype))
    if carried:
        tables, last_spec = [keep(table, pltpu.VMEM) for table in carried], fixed(carry[4].shape)
    else:
        tables = [in_hbm(table) for table in tables]
        last_spec = pl.BlockSpec(carry[4].shape, lambda i, s, _: (s[0], 0, 0, 0, 0))
    if first_step + per_c // PAIR == steps:
        carry = []
    result = pl.pallas_call(
        body,
        grid_spec=pltpu.PrefetchScalarGridSpec(
            num_scalar_prefetch=2,
            grid=(per_c // PAIR,),
            in_specs=[
                *table_specs,
                last_spec,
                pl.BlockSpec((wide, narrow, PAIR, rows_x, lanes), lambda i, *_: (0, 0, i, 0, 0)),
                *[pl.BlockSpec(memory_space=pl.ANY)] * len(filled),
            ],
            out_specs=[pl.BlockSpec(block, lambda i, *_: (0, 0, first_step + i, 0))] * groups
            + [fixed(each.shape) for each in carry],
        ),
        out_shape=[space(out_shape, jnp.float32) for space in spaces] + carry,
        input_output_aliases={8 + spot: spot for spot in range(len(filled))},
        compiler_params=params(1),
        cost_estimate=cost(per_c * 7 * length**3, 20 * per_c * length**2 * 2),
    )(
        side,
        start_c,
        *tables,
        received,
        *[keep(each, space) for each, space in zip(filled, spaces)],
    )
    return result[:groups], result[groups:]


def shear_kernel(
    per_c, group, joined, row_ref, lane_ref, second_ref, third_ref, ahead_ref, last_ref, in_ref, *refs
):
    out_ref, shear_ref = refs
    step = pl.program_id(0)
    length = shear_ref.shape[0]
    half = length // 2
    devices, tiles, message, tile = in_ref.shape
    count = message // per_c
    flat = in_ref.reshape(devices * tiles * message, tile)

    @pl.when(step == 0)
    def _():
        shear_ref[...] = jnp.zeros_like(shear_ref)

    field = jnp.concatenate(
        [
            jnp.concatenate(
                [
                    flat[pl.ds((source * tiles + spot) * message + x, per_c, stride=count), :]
                    for x in range(count)
                    for source in range(devices)
                ],
                axis=0,
            )
            for spot in range(tiles)
        ],
        axis=1,
    )
    field = field * row_ref[0] * lane_ref[0]
    even = product(split(field[:, :length]), pair(second_ref.at[0]))
    odd = product(split(field[:, length:]), pair(second_ref.at[1]))
    near, far = even + odd, even - odd
    field = jnp.concatenate(
        [
            jnp.concatenate(
                [
                    value[x * half : (x + 1) * half, part * half : (part + 1) * half]
                    for x in range(count)
                    for value in (near, far)
                ],
                axis=1,
            )
            for part in range(2)
        ],
        axis=0,
    )
    field = product(pair(third_ref), split(field))
    shear_ref[...] += field * field

    @pl.when(step == 5)
    def _():
        ahead = jnp.concatenate(
            [shear_ref[:, x * length : (x + 1) * length] for x in range(count)], axis=0
        )
        ahead = product(split(ahead), pair(ahead_ref))
        ahead = jnp.concatenate(
            [
                jnp.concatenate(
                    [
                        ahead[x * length : (x + 1) * length, part * length : (part + 1) * length]
                        for x in range(count)
                    ],
                    axis=1,
                )
                for part in range(2)
            ],
            axis=0,
        )
        value = product(pair(last_ref), split(ahead))
        wide, narrow, message_out, _ = out_ref.shape
        rows_b = length // wide
        slots = tile // rows_b
        rows = 2 * length // slots
        run = rows // (2 * narrow * joined)
        out = out_ref.reshape(wide * narrow * message_out, tile)
        lane = lax.broadcasted_iota(jnp.int32, (rows, tile), 1) // rows_b
        for x in range(count):
            for w in range(wide):
                block, place = divmod(w, slots)
                lanes = slice(x * length + block * tile, x * length + (block + 1) * tile)
                moved = None
                for slot in range(slots):
                    piece = value[slot * rows : (slot + 1) * rows, lanes]
                    if slot != place:
                        piece = pltpu.roll(piece, (slot - place) * rows_b % tile, 1)
                    moved = piece if moved is None else jnp.where(lane == slot, piece, moved)
                for n in range(narrow):
                    for part in range(2):
                        for join in range(joined):
                            start = ((n * 2 + part) * joined + join) * run
                            piece = moved[start : start + run]
                            at = (w * narrow + n) * message_out
                            if joined == 2:
                                at += part * 2 * count + (join ^ group) * count + x
                                out[pl.ds(at, run, stride=4 * count), :] = piece
                            else:
                                at += (x * 2 + part) * run
                                out[pl.ds(at, run), :] = piece


def shear_pass(received, wide, narrow, per_c, group, joined):
    devices, tiles, message, tile = received.shape
    count = message // per_c
    length = tiles * tile // 6
    half = length // 2
    index = np.arange(length)
    angle = angles(index, index, length)
    cosine, sine = np.cos(angle), np.sin(angle)
    split_index = halves(length)
    second = np.stack(
        [split_table(turn(angles(np.arange(half), b, length)).T) for b in split_index]
    )
    row_c = np.arange(half) ^ group
    weight = np.where(row_c == 0, 1.0, 2.0)
    angle = angles(index, row_c, length)
    third = np.concatenate([weight * np.cos(angle), -weight * np.sin(angle)], axis=1)
    ahead = np.concatenate([cosine, -sine], axis=1)
    slots = TILE * wide // length
    order = index.reshape(narrow, -1, joined, slots).transpose(3, 0, 2, 1)
    angle = angles(order.reshape(-1), index, length)
    last = np.stack(
        [
            np.concatenate([np.cos(angle), np.sin(angle)], axis=1),
            np.concatenate([-np.sin(angle), np.cos(angle)], axis=1),
        ]
    )
    last = last.reshape(2, slots, narrow, -1, 2 * length).transpose(1, 2, 0, 3, 4)
    last = last.reshape(2 * length, 2 * length)
    wave = signed_wave(index, length)
    wave_rows = np.tile(wave[row_c], count)
    wave_lanes = np.stack([wave[split_index]] * 2, axis=1).reshape(-1)
    twice = math.sqrt(2.0)
    one_row, one_lane = np.ones_like(wave_rows), np.ones_like(wave_lanes)
    row_factor = np.stack(
        [one_row, twice * one_row, twice * wave_rows, one_row, twice * wave_rows, wave_rows**2]
    ).astype(np.float32)[:, :, None]
    lane_factor = np.stack(
        [one_lane, wave_lanes, one_lane, wave_lanes**2, wave_lanes, one_lane]
    ).astype(np.float32)[:, None, :]
    tables = [second] + [split_table(table) for table in (third, ahead, last)]
    out_shape = (wide, narrow, count * 2 * length // (narrow * slots), TILE)

    def body(*refs):
        shear_kernel(per_c, group, joined, *refs)

    def which(i):
        return (0, 2 - (i >= 1).astype(jnp.int32) - (i >= 3).astype(jnp.int32), 0, 0)

    return pl.pallas_call(
        body,
        grid=(6,),
        in_specs=[
            pl.BlockSpec((1, count * half, 1), lambda i: (i, 0, 0)),
            pl.BlockSpec((1, 1, 2 * length), lambda i: (i, 0, 0)),
            *[whole(table.shape) for table in tables],
            pl.BlockSpec((devices, tiles // 3, message, tile), which),
        ],
        out_specs=[whole(out_shape)],
        out_shape=[pltpu.HBM(out_shape, jnp.float32)],
        scratch_shapes=[pltpu.VMEM((length, count * length), jnp.float32)],
        compiler_params=params(1),
        cost_estimate=cost(count * 18 * length**3, 4 * received.size + 4 * 2**20),
    )(
        *[in_hbm(value) for value in (row_factor, lane_factor, *tables)],
        received,
    )


def first_kernel(count, rows_b, joined, pieces, anchor_ref, table_in, *refs):
    ins, (real_out, imag_out) = list(refs[:joined]), refs[joined : joined + 2]
    table_ref, real_ref, imag_ref, first_ref, in_sems, out_sems = refs[joined + 2 :]
    wide, sides, ranks, rows, lanes = ins[-1].shape
    rows_c, _, length = real_ref.shape
    half = length // 2
    slots = lanes // rows_b
    steps = rows_c // (slots * joined) // pieces
    table_copy = pltpu.make_async_copy(table_in, table_ref, in_sems.at[pieces])
    table_copy.start()
    in_copies = []
    if joined == 2:
        for piece in range(pieces):
            at = pl.ds(piece * (rows // pieces), rows // pieces)
            copy = pltpu.make_async_copy(
                ins[0].at[:, :, :, at], first_ref.at[:, :, :, at], in_sems.at[piece]
            )
            copy.start()
            in_copies.append(copy)
        ins[0] = first_ref
    table_copy.wait()
    spot_row = lax.broadcasted_iota(jnp.int32, (lanes, half), 0)
    spot_a = lax.broadcasted_iota(jnp.int32, (lanes, half), 1)
    anchor = (spot_row == 0) & (spot_a == 0) & (anchor_ref[0] == 1)
    upper = lax.broadcasted_iota(jnp.int32, (wide * ranks, joined * count, lanes), 1) < count

    def gathered(side, step, part):
        if joined == 2:
            at = pl.ds((step * 2 + part) * 2 * count, 2 * count)
            own, other = [
                ref[:, side, :, at].reshape(wide * ranks, 2 * count, lanes) for ref in ins
            ]
            both = jnp.where(upper, own, other), pltpu.roll(jnp.where(upper, other, own), count, 1)
            return [value.reshape(half, lanes).T for value in both]
        flat = ins[0].reshape(wide * sides * ranks * rows, lanes)
        run = rows // count
        value = jnp.concatenate(
            [
                flat[
                    pl.ds((w * sides + side) * ranks * rows + part * steps + step, ranks * count, stride=run),
                    :,
                ]
                for w in range(wide)
            ],
            axis=0,
        )
        return [value.T]

    out_copies = []
    for piece in range(pieces):
        if in_copies:
            in_copies[piece].wait()
        sums = []
        for side in range(sides):
            tiles = [
                [gathered(side, piece * steps + step, part) for part in range(2)] for step in range(steps)
            ]
            left = jnp.concatenate(
                [
                    jnp.concatenate([part[join] for part in parts], axis=1)
                    for parts in tiles
                    for join in range(joined)
                ],
                axis=0,
            )
            sums.append(product(split(left), pair(table_ref.at[side])))
        even, odd = sums
        first = piece * steps * joined * slots
        for far, value in enumerate((even + odd, even - odd)):
            columns = slice(far * half, (far + 1) * half)
            for at in range(steps * joined):
                for part, ref in enumerate((real_ref, imag_ref)):
                    here = value[at * lanes : (at + 1) * lanes, part * half : (part + 1) * half]
                    if first + at == 0 and far == 0:
                        here = jnp.where(anchor, 0.0, here)
                    spots = slice(first + at * slots, first + (at + 1) * slots)
                    ref[spots, :, columns] = here.reshape(slots, rows_b, half)
        at = pl.ds(first, steps * joined * slots)
        for part, (ref, out) in enumerate(((real_ref, real_out), (imag_ref, imag_out))):
            copy = pltpu.make_async_copy(ref.at[at], out.at[at], out_sems.at[2 * piece + part])
            copy.start()
            out_copies.append(copy)
    for copy in out_copies:
        copy.wait()


def first_table(length, devices, sides):
    scale = 1.0 / float(length) ** 1.5
    order = np.arange(length).reshape(devices, -1, sides).transpose(2, 0, 1).reshape(sides, -1)
    return np.stack(
        [split_table(scale * turn(-angles(np.arange(length // 2), x, length)).T) for x in order]
    )


def first_pass(parts, table, is_anchor, length, wide, sides, count):
    devices, rows, lanes = parts[0].shape
    joined = len(parts)
    ranks = devices // wide // sides
    rows_b = length // wide
    slots = lanes // rows_b
    total = rows // (2 * joined * count)
    pieces = 4 if joined == 2 and total % 4 == 0 else 1
    parts = [part.reshape(wide, sides, ranks, rows, lanes) for part in parts]

    def body(*refs):
        first_kernel(count, rows_b, joined, pieces, *refs)

    rows_c = total * joined * slots
    out_shape = (rows_c, rows_b, length)
    first_shape = parts[0].shape if joined == 2 else (8, TILE)
    anywhere = pl.BlockSpec(memory_space=pl.ANY)
    return pl.pallas_call(
        body,
        grid=(1,),
        in_specs=[
            pl.BlockSpec(memory_space=pltpu.SMEM),
            anywhere,
            *[anywhere] * (joined - 1),
            whole(parts[-1].shape),
        ],
        out_specs=[anywhere] * 2,
        out_shape=[pltpu.HBM(out_shape, jnp.float32)] * 2,
        scratch_shapes=[
            pltpu.VMEM(table.shape, table.dtype),
            pltpu.VMEM(out_shape, jnp.float32),
            pltpu.VMEM(out_shape, jnp.float32),
            pltpu.VMEM(first_shape, jnp.float32),
            pltpu.SemaphoreType.DMA((pieces + 1,)),
            pltpu.SemaphoreType.DMA((2 * pieces,)),
        ],
        compiler_params=params(1),
        cost_estimate=cost(rows_c * 2 * rows_b * length * length, 16 * rows_c * rows_b * length),
    )(
        is_anchor,
        in_hbm(table),
        *[in_hbm(part) for part in parts[:-1]],
        keep(parts[-1], pltpu.VMEM),
    )


def transpose(value, members=None):
    return lax.all_to_all(
        value, AXES, split_axis=0, concat_axis=0, tiled=True, axis_index_groups=members
    )


def solution(mesh):
    wide, narrow = mesh.shape["wide"], mesh.shape["narrow"]
    sides = 2
    ranks = narrow // sides
    devices = wide * ranks
    members = [
        [w * narrow + side * ranks + rank for w in range(wide) for rank in range(ranks)]
        for side in range(sides)
    ]

    def per_device(density):
        rows_x, rows_y, length = density.shape
        half = length // 2
        per_c = half // devices
        slab = half // devices
        steps = per_c // PAIR
        counts = [per_c - PAIR, PAIR] if steps > 1 else [per_c]
        groups = 2 if slab > 2 else 1
        spot_wide, spot_narrow = lax.axis_index("wide"), lax.axis_index("narrow")
        side = (spot_narrow // ranks).astype(jnp.int32).reshape(1)
        rank = spot_wide * ranks + spot_narrow % ranks
        start_c = (rank * per_c).astype(jnp.int32).reshape(1)
        chunks, carried, start = [], [], 0
        for planes, count in zip(third_pass(density, wide, sides, ranks, counts), counts):
            planes = transpose(planes.reshape(wide * narrow, count, rows_x, 2 * rows_y))
            planes = planes.reshape(wide, narrow, count, rows_x, 2 * rows_y)
            planes = keep(planes, pltpu.VMEM if start else pltpu.HBM)
            chunks, carried = spectrum_pass(
                planes, side, start_c, devices, groups, steps, start // PAIR, chunks, carried
            )
            start += count
        is_anchor = ((spot_wide == 0) & (spot_narrow == 0)).astype(jnp.int32).reshape(1)
        parts = []
        table = first_table(length, devices, sides)
        for group, chunk in enumerate(chunks):
            received = keep(transpose(chunk, members), pltpu.VMEM if group else pltpu.HBM)
            (part,) = shear_pass(received, wide, narrow, per_c, group, groups)
            parts.append(transpose(part.reshape((wide * narrow,) + part.shape[2:])))
        return tuple(first_pass(parts, table, is_anchor, length, wide, sides, slab // groups))

    return jax.shard_map(
        per_device,
        mesh=mesh,
        in_specs=(P("wide", "narrow", None),),
        out_specs=(P("narrow", "wide", None), P("narrow", "wide", None)),
        check_vma=False,
    )
```

```python
import math

import jax
import jax.numpy as jnp
import ml_dtypes
import numpy as np
from jax import lax
from jax.experimental import pallas as pl
from jax.experimental.pallas import tpu as pltpu
from jax.sharding import PartitionSpec as P

AXES = ("wide", "narrow")
TILE = 128
LIMIT = 16 * 1024 * 1024


def angles(rows, columns, length):
    return (2.0 * math.pi / length) * (np.outer(rows, columns) % length)


def split_table(table):
    table = np.asarray(table, np.float64)
    high = table.astype(ml_dtypes.bfloat16)
    low = (table - high.astype(np.float64)).astype(ml_dtypes.bfloat16)
    return np.stack([high, low])


def split(value):
    high = value.astype(jnp.bfloat16)
    low = (value - high.astype(jnp.float32)).astype(jnp.bfloat16)
    return high, low


def product(left, right, contract=((1,), (0,))):
    (left_axis,), (right_axis,) = contract
    left = jnp.concatenate([left[0], left[0], left[1]], axis=left_axis)
    right = jnp.concatenate([right[0], right[1], right[0]], axis=right_axis)
    return lax.dot_general(
        left, right, (contract, ((), ())), preferred_element_type=jnp.float32
    )


def pair(ref):
    return ref[0], ref[1]


def signed_wave(index, length):
    index = np.asarray(index)
    return np.where(index < length // 2, index, index - length) * (2.0 * math.pi / length)


def params(steps):
    return pltpu.CompilerParams(
        vmem_limit_bytes=LIMIT, dimension_semantics=("arbitrary",) * steps
    )


def whole(shape):
    return pl.BlockSpec(shape, lambda *_: (0,) * len(shape))


def keep(value, space):
    return pltpu.with_memory_space_constraint(jnp.asarray(value), space)


def in_hbm(value):
    return keep(value, pltpu.HBM)


def cost(macs, moved):
    return pl.CostEstimate(flops=6 * macs, bytes_accessed=moved, transcendentals=0)


def third_kernel(counts, pieces, table_in, density_in, *refs):
    outs, (table_ref, density_ref, second_ref, in_sems, out_sems) = refs[:-5], refs[-5:]
    rows_x, rows_y, length = density_ref.shape
    wide, sides, ranks = outs[0].shape[:3]
    step_x = rows_x // pieces
    half = length // 2
    table_copy = pltpu.make_async_copy(table_in, table_ref, in_sems.at[pieces])
    table_copy.start()
    in_copies = []
    for piece in range(pieces):
        at = pl.ds(piece * step_x, step_x)
        copy = pltpu.make_async_copy(density_in.at[at], density_ref.at[at], in_sems.at[piece])
        copy.start()
        in_copies.append(copy)
    table_copy.wait()
    table = pair(table_ref)
    targets = [outs[0], second_ref][: len(counts)]
    flats = [ref.reshape(math.prod(ref.shape[:5]), 2 * rows_y) for ref in targets]
    out_copies = []
    for piece in range(pieces):
        in_copies[piece].wait()
        first = piece * step_x
        block = density_ref[first : first + step_x].reshape(step_x * rows_y, length)
        result = product(split(block), table)
        for inner in range(step_x):
            rows = slice(inner * rows_y, (inner + 1) * rows_y)
            value = jnp.concatenate([result[rows, :half], result[rows, half:]], axis=0).T
            start = 0
            for flat, count in zip(flats, counts):
                for c in range(count):
                    for rank in range(ranks):
                        at = (rank * count + c) * rows_x + first + inner
                        stride = sides * ranks * count * rows_x
                        flat[pl.ds(at, wide, stride=stride), :] = value[start : start + wide]
                        start += wide
        rows = pl.ds(first, step_x)
        for ref in targets[::-1]:
            for side in range(1, sides):
                ref[:, side, :, :, rows] = ref[:, 0, :, :, rows]
            if ref is second_ref:
                copy = pltpu.make_async_copy(
                    ref.at[:, :, :, :, rows], outs[1].at[:, :, :, :, rows], out_sems.at[piece]
                )
                copy.start()
                out_copies.append(copy)
    for copy in out_copies:
        copy.wait()


def third_pass(density, wide, sides, ranks, counts):
    rows_x, rows_y, length = density.shape
    half = length // 2
    per_c = sum(counts)
    order = np.arange(half).reshape(wide, ranks, per_c).transpose(2, 1, 0).reshape(-1)
    angle = angles(np.arange(length), order, length)
    table = split_table(np.concatenate([np.cos(angle), -np.sin(angle)], axis=1))
    pieces = max(1, rows_x // 8)
    shapes = [(wide, sides, ranks, count, rows_x, 2 * rows_y) for count in counts]
    anywhere = pl.BlockSpec(memory_space=pl.ANY)

    def body(*refs):
        third_kernel(counts, pieces, *refs)

    return pl.pallas_call(
        body,
        grid=(1,),
        in_specs=[anywhere] * 2,
        out_specs=[whole(shapes[0])] + [anywhere] * (len(counts) - 1),
        out_shape=[
            (pltpu.HBM if spot else pltpu.VMEM)(shape, jnp.float32)
            for spot, shape in enumerate(shapes)
        ],
        scratch_shapes=[
            pltpu.VMEM(table.shape, table.dtype),
            pltpu.VMEM(density.shape, jnp.float32),
            pltpu.VMEM(shapes[1] if len(counts) == 2 else (8, TILE), jnp.float32),
            pltpu.SemaphoreType.DMA((pieces + 1,)),
            pltpu.SemaphoreType.DMA((pieces,)),
        ],
        compiler_params=params(1),
        cost_estimate=cost(density.size * length, 12 * density.size),
    )(in_hbm(table), in_hbm(density))


PAIR = 2


def turn(angle):
    cosine, sine = np.cos(angle), np.sin(angle)
    return np.block([[cosine, -sine], [sine, cosine]])


def hand_on(sources, targets):
    @pl.when(pl.program_id(0) == 0)
    def _():
        for source, target in zip(sources, targets):
            target[...] = source[...]


def spectrum_kernel(slab, groups, first_c, filled, side_ref, start_ref, *refs):
    tables, in_ref, outs = refs[:5], refs[5], refs[6 + filled :]
    a_ref, b_ref, second_ref, first_ref, back_ref = tables
    hand_on(tables, outs[groups:])
    outs = outs[:groups]
    wide, narrow, _, rows_x, lanes = in_ref.shape
    length = wide * rows_x
    half = length // 2
    quarter = half // 2
    devices, tiles, message, tile = outs[0].shape
    count = slab // groups
    sign_back = 1.0 - 2.0 * side_ref[0].astype(jnp.float32)

    def column(c, n):
        return in_ref[:, n, c].reshape(length, lanes)

    def columns(numbers):
        return jnp.concatenate(
            [
                jnp.concatenate([column(c, n) for n in numbers], axis=1)
                for c in range(PAIR)
            ],
            axis=0,
        )

    low, high = columns(range(narrow // 2)), columns(range(narrow // 2, narrow))
    planes = [
        product(split(low + high), pair(second_ref.at[0])),
        product(split(low - high), pair(second_ref.at[1])),
    ]

    def stacked(sign):
        return jnp.concatenate(
            [
                jnp.concatenate(
                    [
                        plane[c * length : c * length + half, part * half : (part + 1) * half]
                        + sign
                        * plane[c * length + half : (c + 1) * length, part * half : (part + 1) * half]
                        for c in range(PAIR)
                        for plane in planes
                    ],
                    axis=1,
                )
                for part in range(2)
            ],
            axis=0,
        )

    squared_b, scale_b = b_ref[0], b_ref[1]
    field = []
    for parity, sign in ((0, 1.0), (1, -1.0)):
        value = product(pair(first_ref.at[parity]), split(stacked(sign)))
        smooth = []
        for c in range(PAIR):
            spot_c = start_ref[0] + (first_c + pl.program_id(0) * PAIR + c)
            wave_c = jnp.full_like(squared_b, spot_c.astype(jnp.float32)) * (2.0 * math.pi / length)
            scale_c = jnp.exp(-0.5 * wave_c * wave_c) * (1.0 / float(length) ** 3)
            squared = a_ref[1, parity] + (squared_b + wave_c * wave_c)
            inverse = scale_c / jnp.where(squared > 0, squared, 1.0)
            smooth.append(jnp.where(squared > 0, inverse * scale_b, 0.0) * a_ref[2, parity])
        smooth = jnp.concatenate(smooth, axis=1)
        field.append(value * jnp.concatenate([smooth, smooth], axis=0))
    upper = lax.broadcasted_iota(jnp.int32, (devices, message, tile), 1) < count
    for number in range(3):
        folded = jnp.concatenate(
            [
                field[parity][part * half : part * half + quarter]
                + sign_back * field[parity][part * half + quarter : (part + 1) * half]
                for part in range(2)
                for parity in range(2)
            ],
            axis=0,
        )
        values = [
            product(
                pair(back_ref.at[0, c % back_ref.shape[1]]),
                split(folded[:, c * length : (c + 1) * length]),
            )
            for c in range(PAIR)
        ]
        for spot in range(tiles // 3):
            parity, part = divmod(spot, 2)
            at = number * (tiles // 3) + spot
            here = [
                value[part * half : (part + 1) * half, parity * tile : (parity + 1) * tile]
                for value in values
            ]
            if groups == 2:
                even, odd = [value.reshape(devices, message, tile) for value in here]
                outs[0][:, at] = jnp.where(upper, even, odd)
                outs[1][:, at] = jnp.where(upper, odd, even)
            else:
                flat = outs[0].reshape(devices * tiles * message, tile)
                for c in range(PAIR):
                    for x in range(slab):
                        start = at * message + c * count + x
                        flat[pl.ds(start, devices, stride=tiles * message), :] = here[c][
                            x * devices : (x + 1) * devices
                        ]
        if number < 2:
            for parity in range(2):
                wave_a = a_ref[0, parity]
                field[parity] = field[parity] * jnp.concatenate([wave_a, wave_a], axis=0)


def halves(length):
    return np.arange(length).reshape(length // 2, 2).T


def spectrum_pass(received, side, start_c, devices, groups, steps, first_step, filled, carried):
    wide, narrow, per_c, rows_x, lanes = received.shape
    length = wide * rows_x
    rows_y = lanes // 2
    half = length // 2
    near = np.arange(half)
    split_index = halves(length)
    slab = half // devices
    second, first, back = [], [], []
    if groups == 2:
        orders = [
            near.reshape(devices, 2, slab // 2)[:, ::step].reshape(-1) for step in (1, -1)
        ]
    else:
        orders = [near.reshape(devices, slab).T.reshape(-1)]
    for parity, index in enumerate(split_index):
        table = turn(-angles(index, near, length)).reshape(2, half, 2, narrow // 2, rows_y)
        second.append(split_table(table.transpose(3, 2, 4, 0, 1).reshape(length, length)))
        first.append(split_table(turn(-angles(index, near, length))))
        columns = split_index[:, : half // 2].reshape(-1)
        back.append(
            [split_table(turn(angles(2 * order + parity, columns, length))) for order in orders]
        )
    tables = [np.stack(second), np.stack(first), np.stack([np.stack(each) for each in back])]
    wave = signed_wave(split_index, length)
    scale = np.where(split_index == half, 0.0, np.exp(-0.5 * wave**2))
    a_table = np.stack([wave, wave**2, scale]).astype(np.float32)[..., None]
    b_table = np.stack([wave**2, scale]).astype(np.float32).reshape(2, 1, length)
    message = PAIR * slab // groups
    spaces = [pltpu.HBM] * groups
    out_shape = (devices, 3 * 2 * length // TILE, steps * message, TILE)
    block = out_shape[:2] + (message, TILE)

    def body(*refs):
        spectrum_kernel(slab, groups, first_step * PAIR, len(filled), *refs)

    def fixed(shape):
        return pl.BlockSpec(shape, lambda *_: (0,) * len(shape))

    tables = [a_table, b_table, *tables]
    table_specs = [fixed(table.shape) for table in tables[:4]]
    carry = [pltpu.VMEM(table.shape, table.dtype) for table in tables[:4]]
    carry.append(pltpu.VMEM((1,) + tables[4].shape[1:], tables[4].dtype))
    if carried:
        tables, last_spec = [keep(table, pltpu.VMEM) for table in carried], fixed(carry[4].shape)
    else:
        tables = [in_hbm(table) for table in tables]
        last_spec = pl.BlockSpec(carry[4].shape, lambda i, s, _: (s[0], 0, 0, 0, 0))
    if first_step + per_c // PAIR == steps:
        carry = []
    result = pl.pallas_call(
        body,
        grid_spec=pltpu.PrefetchScalarGridSpec(
            num_scalar_prefetch=2,
            grid=(per_c // PAIR,),
            in_specs=[
                *table_specs,
                last_spec,
                pl.BlockSpec((wide, narrow, PAIR, rows_x, lanes), lambda i, *_: (0, 0, i, 0, 0)),
                *[pl.BlockSpec(memory_space=pl.ANY)] * len(filled),
            ],
            out_specs=[pl.BlockSpec(block, lambda i, *_: (0, 0, first_step + i, 0))] * groups
            + [fixed(each.shape) for each in carry],
        ),
        out_shape=[space(out_shape, jnp.float32) for space in spaces] + carry,
        input_output_aliases={8 + spot: spot for spot in range(len(filled))},
        compiler_params=params(1),
        cost_estimate=cost(per_c * 7 * length**3, 20 * per_c * length**2 * 2),
    )(
        side,
        start_c,
        *tables,
        received,
        *[keep(each, space) for each, space in zip(filled, spaces)],
    )
    return result[:groups], result[groups:]


def shear_kernel(
    per_c, group, joined, row_ref, lane_ref, second_ref, third_ref, ahead_ref, last_ref, in_ref, *refs
):
    out_ref, shear_ref = refs
    step = pl.program_id(0)
    length = shear_ref.shape[0]
    half = length // 2
    devices, tiles, message, tile = in_ref.shape
    count = message // per_c
    flat = in_ref.reshape(devices * tiles * message, tile)

    @pl.when(step == 0)
    def _():
        shear_ref[...] = jnp.zeros_like(shear_ref)

    field = jnp.concatenate(
        [
            jnp.concatenate(
                [
                    flat[pl.ds((source * tiles + spot) * message + x, per_c, stride=count), :]
                    for x in range(count)
                    for source in range(devices)
                ],
                axis=0,
            )
            for spot in range(tiles)
        ],
        axis=1,
    )
    field = field * row_ref[0] * lane_ref[0]
    even = product(split(field[:, :length]), pair(second_ref.at[0]))
    odd = product(split(field[:, length:]), pair(second_ref.at[1]))
    near, far = even + odd, even - odd
    field = jnp.concatenate(
        [
            jnp.concatenate(
                [
                    value[x * half : (x + 1) * half, part * half : (part + 1) * half]
                    for x in range(count)
                    for value in (near, far)
                ],
                axis=1,
            )
            for part in range(2)
        ],
        axis=0,
    )
    field = product(pair(third_ref), split(field))
    shear_ref[...] += field * field

    @pl.when(step == 5)
    def _():
        ahead = jnp.concatenate(
            [shear_ref[:, x * length : (x + 1) * length] for x in range(count)], axis=0
        )
        ahead = product(split(ahead), pair(ahead_ref))
        ahead = jnp.concatenate(
            [
                jnp.concatenate(
                    [
                        ahead[x * length : (x + 1) * length, part * length : (part + 1) * length]
                        for x in range(count)
                    ],
                    axis=1,
                )
                for part in range(2)
            ],
            axis=0,
        )
        value = product(pair(last_ref), split(ahead))
        wide, narrow, message_out, _ = out_ref.shape
        rows_b = length // wide
        slots = tile // rows_b
        rows = 2 * length // slots
        run = rows // (2 * narrow * joined)
        out = out_ref.reshape(wide * narrow * message_out, tile)
        lane = lax.broadcasted_iota(jnp.int32, (rows, tile), 1) // rows_b
        for x in range(count):
            for w in range(wide):
                block, place = divmod(w, slots)
                lanes = slice(x * length + block * tile, x * length + (block + 1) * tile)
                moved = None
                for slot in range(slots):
                    piece = value[slot * rows : (slot + 1) * rows, lanes]
                    if slot != place:
                        piece = pltpu.roll(piece, (slot - place) * rows_b % tile, 1)
                    moved = piece if moved is None else jnp.where(lane == slot, piece, moved)
                for n in range(narrow):
                    for part in range(2):
                        for join in range(joined):
                            start = ((n * 2 + part) * joined + join) * run
                            piece = moved[start : start + run]
                            at = (w * narrow + n) * message_out
                            if joined == 2:
                                at += part * 2 * count + (join ^ group) * count + x
                                out[pl.ds(at, run, stride=4 * count), :] = piece
                            else:
                                at += (x * 2 + part) * run
                                out[pl.ds(at, run), :] = piece


def shear_pass(received, wide, narrow, per_c, group, joined):
    devices, tiles, message, tile = received.shape
    count = message // per_c
    length = tiles * tile // 6
    half = length // 2
    index = np.arange(length)
    angle = angles(index, index, length)
    cosine, sine = np.cos(angle), np.sin(angle)
    split_index = halves(length)
    second = np.stack(
        [split_table(turn(angles(np.arange(half), b, length)).T) for b in split_index]
    )
    row_c = np.arange(half) ^ group
    weight = np.where(row_c == 0, 1.0, 2.0)
    angle = angles(index, row_c, length)
    third = np.concatenate([weight * np.cos(angle), -weight * np.sin(angle)], axis=1)
    ahead = np.concatenate([cosine, -sine], axis=1)
    slots = TILE * wide // length
    order = index.reshape(narrow, -1, joined, slots).transpose(3, 0, 2, 1)
    angle = angles(order.reshape(-1), index, length)
    last = np.stack(
        [
            np.concatenate([np.cos(angle), np.sin(angle)], axis=1),
            np.concatenate([-np.sin(angle), np.cos(angle)], axis=1),
        ]
    )
    last = last.reshape(2, slots, narrow, -1, 2 * length).transpose(1, 2, 0, 3, 4)
    last = last.reshape(2 * length, 2 * length)
    wave = signed_wave(index, length)
    wave_rows = np.tile(wave[row_c], count)
    wave_lanes = np.stack([wave[split_index]] * 2, axis=1).reshape(-1)
    twice = math.sqrt(2.0)
    one_row, one_lane = np.ones_like(wave_rows), np.ones_like(wave_lanes)
    row_factor = np.stack(
        [one_row, twice * one_row, twice * wave_rows, one_row, twice * wave_rows, wave_rows**2]
    ).astype(np.float32)[:, :, None]
    lane_factor = np.stack(
        [one_lane, wave_lanes, one_lane, wave_lanes**2, wave_lanes, one_lane]
    ).astype(np.float32)[:, None, :]
    tables = [second] + [split_table(table) for table in (third, ahead, last)]
    out_shape = (wide, narrow, count * 2 * length // (narrow * slots), TILE)

    def body(*refs):
        shear_kernel(per_c, group, joined, *refs)

    def which(i):
        return (0, 2 - (i >= 1).astype(jnp.int32) - (i >= 3).astype(jnp.int32), 0, 0)

    return pl.pallas_call(
        body,
        grid=(6,),
        in_specs=[
            pl.BlockSpec((1, count * half, 1), lambda i: (i, 0, 0)),
            pl.BlockSpec((1, 1, 2 * length), lambda i: (i, 0, 0)),
            *[whole(table.shape) for table in tables],
            pl.BlockSpec((devices, tiles // 3, message, tile), which),
        ],
        out_specs=[whole(out_shape)],
        out_shape=[pltpu.HBM(out_shape, jnp.float32)],
        scratch_shapes=[pltpu.VMEM((length, count * length), jnp.float32)],
        compiler_params=params(1),
        cost_estimate=cost(count * 18 * length**3, 4 * received.size + 4 * 2**20),
    )(
        *[in_hbm(value) for value in (row_factor, lane_factor, *tables)],
        received,
    )


def first_kernel(count, rows_b, joined, pieces, anchor_ref, table_in, *refs):
    ins, (real_out, imag_out) = list(refs[:joined]), refs[joined : joined + 2]
    table_ref, real_ref, imag_ref, first_ref, in_sems, out_sems = refs[joined + 2 :]
    wide, sides, ranks, rows, lanes = ins[-1].shape
    rows_c, _, length = real_ref.shape
    half = length // 2
    slots = lanes // rows_b
    steps = rows_c // (slots * joined) // pieces
    table_copies = []
    for join in range(joined):
        copy = pltpu.make_async_copy(
            table_in.at[join], table_ref.at[join], in_sems.at[pieces + join]
        )
        copy.start()
        table_copies.append(copy)
    in_copies = []
    if joined == 2:
        for piece in range(pieces):
            at = pl.ds(piece * (rows // pieces), rows // pieces)
            copy = pltpu.make_async_copy(
                ins[0].at[:, :, :, at], first_ref.at[:, :, :, at], in_sems.at[piece]
            )
            copy.start()
            in_copies.append(copy)
        ins[0] = first_ref
    for copy in table_copies:
        copy.wait()
    spot_row = lax.broadcasted_iota(jnp.int32, (lanes, half), 0)
    spot_a = lax.broadcasted_iota(jnp.int32, (lanes, half), 1)
    anchor = (spot_row == 0) & (spot_a == 0) & (anchor_ref[0] == 1)
    upper = lax.broadcasted_iota(jnp.int32, (wide * ranks, joined * count, lanes), 1) < count

    def gathered(side, step, part):
        if joined == 2:
            at = pl.ds((step * 2 + part) * 2 * count, 2 * count)
            own, other = [
                ref[:, side, :, at].reshape(wide * ranks, 2 * count, lanes) for ref in ins
            ]
            both = jnp.where(upper, own, other), jnp.where(upper, other, own)
            return [value.reshape(half, lanes).T for value in both]
        flat = ins[0].reshape(wide * sides * ranks * rows, lanes)
        run = rows // count
        value = jnp.concatenate(
            [
                flat[
                    pl.ds((w * sides + side) * ranks * rows + part * steps + step, ranks * count, stride=run),
                    :,
                ]
                for w in range(wide)
            ],
            axis=0,
        )
        return [value.T]

    out_copies = []
    for piece in range(pieces):
        if in_copies:
            in_copies[piece].wait()
        tiles = [
            [
                [gathered(side, piece * steps + step, part) for part in range(2)]
                for step in range(steps)
            ]
            for side in range(sides)
        ]
        first = piece * steps * joined * slots
        for join in range(joined):
            sums = []
            for side in range(sides):
                left = jnp.concatenate(
                    [
                        jnp.concatenate([part[join] for part in parts], axis=1)
                        for parts in tiles[side]
                    ],
                    axis=0,
                )
                sums.append(product(split(left), pair(table_ref.at[join, side])))
            even, odd = sums
            for far, value in enumerate((even + odd, even - odd)):
                columns = slice(far * half, (far + 1) * half)
                for step in range(steps):
                    for part, ref in enumerate((real_ref, imag_ref)):
                        here = value[step * lanes : (step + 1) * lanes, part * half : (part + 1) * half]
                        at = first + (step * joined + join) * slots
                        if at == 0 and far == 0:
                            here = jnp.where(anchor, 0.0, here)
                        ref[at : at + slots, :, columns] = here.reshape(slots, rows_b, half)
        at = pl.ds(first, steps * joined * slots)
        for part, (ref, out) in enumerate(((real_ref, real_out), (imag_ref, imag_out))):
            copy = pltpu.make_async_copy(ref.at[at], out.at[at], out_sems.at[2 * piece + part])
            copy.start()
            out_copies.append(copy)
    for copy in out_copies:
        copy.wait()


def first_table(length, devices, joined, count, sides):
    scale = 1.0 / float(length) ** 1.5
    index = np.arange(length).reshape(devices, joined, count, sides)
    tables = []
    for join in range(joined):
        order = index[:, :: 1 - 2 * join].transpose(3, 0, 1, 2).reshape(sides, -1)
        tables.append(
            [split_table(scale * turn(-angles(np.arange(length // 2), x, length)).T) for x in order]
        )
    return np.stack([np.stack(each) for each in tables])


def first_pass(parts, table, is_anchor, length, wide, sides, count):
    devices, rows, lanes = parts[0].shape
    joined = len(parts)
    ranks = devices // wide // sides
    rows_b = length // wide
    slots = lanes // rows_b
    total = rows // (2 * joined * count)
    pieces = 4 if joined == 2 and total % 4 == 0 else 1
    parts = [part.reshape(wide, sides, ranks, rows, lanes) for part in parts]

    def body(*refs):
        first_kernel(count, rows_b, joined, pieces, *refs)

    rows_c = total * joined * slots
    out_shape = (rows_c, rows_b, length)
    first_shape = parts[0].shape if joined == 2 else (8, TILE)
    anywhere = pl.BlockSpec(memory_space=pl.ANY)
    return pl.pallas_call(
        body,
        grid=(1,),
        in_specs=[
            pl.BlockSpec(memory_space=pltpu.SMEM),
            anywhere,
            *[anywhere] * (joined - 1),
            whole(parts[-1].shape),
        ],
        out_specs=[anywhere] * 2,
        out_shape=[pltpu.HBM(out_shape, jnp.float32)] * 2,
        scratch_shapes=[
            pltpu.VMEM(table.shape, table.dtype),
            pltpu.VMEM(out_shape, jnp.float32),
            pltpu.VMEM(out_shape, jnp.float32),
            pltpu.VMEM(first_shape, jnp.float32),
            pltpu.SemaphoreType.DMA((pieces + joined,)),
            pltpu.SemaphoreType.DMA((2 * pieces,)),
        ],
        compiler_params=params(1),
        cost_estimate=cost(rows_c * 2 * rows_b * length * length, 16 * rows_c * rows_b * length),
    )(
        is_anchor,
        in_hbm(table),
        *[in_hbm(part) for part in parts[:-1]],
        keep(parts[-1], pltpu.VMEM),
    )


def transpose(value, members=None):
    return lax.all_to_all(
        value, AXES, split_axis=0, concat_axis=0, tiled=True, axis_index_groups=members
    )


def solution(mesh):
    wide, narrow = mesh.shape["wide"], mesh.shape["narrow"]
    sides = 2
    ranks = narrow // sides
    devices = wide * ranks
    members = [
        [w * narrow + side * ranks + rank for w in range(wide) for rank in range(ranks)]
        for side in range(sides)
    ]

    def per_device(density):
        rows_x, rows_y, length = density.shape
        half = length // 2
        per_c = half // devices
        slab = half // devices
        steps = per_c // PAIR
        counts = [per_c - PAIR, PAIR] if steps > 1 else [per_c]
        groups = 2 if slab > 2 else 1
        spot_wide, spot_narrow = lax.axis_index("wide"), lax.axis_index("narrow")
        side = (spot_narrow // ranks).astype(jnp.int32).reshape(1)
        rank = spot_wide * ranks + spot_narrow % ranks
        start_c = (rank * per_c).astype(jnp.int32).reshape(1)
        chunks, carried, start = [], [], 0
        for planes, count in zip(third_pass(density, wide, sides, ranks, counts), counts):
            planes = transpose(planes.reshape(wide * narrow, count, rows_x, 2 * rows_y))
            planes = planes.reshape(wide, narrow, count, rows_x, 2 * rows_y)
            planes = keep(planes, pltpu.VMEM if start else pltpu.HBM)
            chunks, carried = spectrum_pass(
                planes, side, start_c, devices, groups, steps, start // PAIR, chunks, carried
            )
            start += count
        is_anchor = ((spot_wide == 0) & (spot_narrow == 0)).astype(jnp.int32).reshape(1)
        parts = []
        table = first_table(length, devices, groups, slab // groups, sides)
        for group, chunk in enumerate(chunks):
            received = keep(transpose(chunk, members), pltpu.VMEM if group else pltpu.HBM)
            (part,) = shear_pass(received, wide, narrow, per_c, group, groups)
            parts.append(transpose(part.reshape((wide * narrow,) + part.shape[2:])))
        return tuple(first_pass(parts, table, is_anchor, length, wide, sides, slab // groups))

    return jax.shard_map(
        per_device,
        mesh=mesh,
        in_specs=(P("wide", "narrow", None),),
        out_specs=(P("narrow", "wide", None), P("narrow", "wide", None)),
        check_vma=False,
    )
```

```python
import math

import jax
import jax.numpy as jnp
import ml_dtypes
import numpy as np
from jax import lax
from jax.experimental import pallas as pl
from jax.experimental.pallas import tpu as pltpu
from jax.sharding import PartitionSpec as P

AXES = ("narrow", "wide")
TILE = 128
LIMIT = 16 * 1024 * 1024


def angles(rows, columns, length):
    return (2.0 * math.pi / length) * (np.outer(rows, columns) % length)


def split_table(table):
    table = np.asarray(table, np.float64)
    high = table.astype(ml_dtypes.bfloat16)
    low = (table - high.astype(np.float64)).astype(ml_dtypes.bfloat16)
    return np.stack([high, low])


def split(value):
    high = value.astype(jnp.bfloat16)
    low = (value - high.astype(jnp.float32)).astype(jnp.bfloat16)
    return high, low


def product(left, right, contract=((1,), (0,))):
    (left_axis,), (right_axis,) = contract
    left = jnp.concatenate([left[0], left[0], left[1]], axis=left_axis)
    right = jnp.concatenate([right[0], right[1], right[0]], axis=right_axis)
    return lax.dot_general(
        left, right, (contract, ((), ())), preferred_element_type=jnp.float32
    )


def pair(ref):
    return ref[0], ref[1]


def signed_wave(index, length):
    index = np.asarray(index)
    return np.where(index < length // 2, index, index - length) * (2.0 * math.pi / length)


def params(steps):
    return pltpu.CompilerParams(
        vmem_limit_bytes=LIMIT, dimension_semantics=("arbitrary",) * steps
    )


def whole(shape):
    return pl.BlockSpec(shape, lambda *_: (0,) * len(shape))


def keep(value, space):
    return pltpu.with_memory_space_constraint(jnp.asarray(value), space)


def in_hbm(value):
    return keep(value, pltpu.HBM)


def cost(macs, moved):
    return pl.CostEstimate(flops=6 * macs, bytes_accessed=moved, transcendentals=0)


def third_kernel(counts, table_ref, density_ref, *outs):
    step_x, rows_y, length = density_ref.shape
    sides, ranks, wide, _, rows_x, _ = outs[0].shape
    half = length // 2
    flats = [ref.reshape(math.prod(ref.shape[:5]), 2 * rows_y) for ref in outs]
    table = pair(table_ref)
    group = 4
    start_x = pl.program_id(0) * step_x
    for first in range(0, step_x, group):
        block = density_ref[first : first + group].reshape(group * rows_y, length)
        result = product(split(block), table)
        for inner in range(group):
            rows = slice(inner * rows_y, (inner + 1) * rows_y)
            value = jnp.concatenate([result[rows, :half], result[rows, half:]], axis=0).T
            start = 0
            for flat, count in zip(flats, counts):
                for c in range(count):
                    for rank in range(ranks):
                        at = (rank * wide * count + c) * rows_x + first + inner + start_x
                        stride = count * rows_x
                        flat[pl.ds(at, wide, stride=stride), :] = value[start : start + wide]
                        start += wide
    for ref in outs:
        rows = pl.ds(pl.multiple_of(start_x, step_x), step_x)
        for side in range(1, sides):
            ref[side, :, :, :, rows] = ref[0, :, :, :, rows]


def third_pass(density, wide, sides, ranks, counts):
    rows_x, rows_y, length = density.shape
    half = length // 2
    per_c = sum(counts)
    order = np.arange(half).reshape(wide, ranks, per_c).transpose(2, 1, 0).reshape(-1)
    angle = angles(np.arange(length), order, length)
    table = split_table(np.concatenate([np.cos(angle), -np.sin(angle)], axis=1))
    step = max(rows_x // 2, min(8, rows_x))

    def body(*refs):
        third_kernel(counts, *refs)

    return pl.pallas_call(
        body,
        grid=(rows_x // step,),
        in_specs=[
            whole(table.shape),
            pl.BlockSpec((step, rows_y, length), lambda i: (i, 0, 0)),
        ],
        out_specs=[
            whole((sides, ranks, wide, count, rows_x, 2 * rows_y)) for count in counts
        ],
        out_shape=[
            pltpu.VMEM((sides, ranks, wide, count, rows_x, 2 * rows_y), jnp.float32)
            for count in counts
        ],
        compiler_params=params(1),
        cost_estimate=cost(density.size * length, 12 * density.size),
    )(in_hbm(table), in_hbm(density))


PAIR = 2


def turn(angle):
    cosine, sine = np.cos(angle), np.sin(angle)
    return np.block([[cosine, -sine], [sine, cosine]])


def hand_on(sources, targets):
    @pl.when(pl.program_id(0) == 0)
    def _():
        for source, target in zip(sources, targets):
            target[...] = source[...]


def spectrum_kernel(slab, groups, first_c, filled, side_ref, start_ref, *refs):
    tables, in_ref, outs = refs[:5], refs[5], refs[6 + filled :]
    a_ref, b_ref, second_ref, first_ref, back_ref = tables
    hand_on(tables, outs[groups:])
    outs = outs[:groups]
    narrow, wide, _, rows_x, lanes = in_ref.shape
    length = wide * rows_x
    half = length // 2
    quarter = half // 2
    devices, tiles, message, tile = outs[0].shape
    count = slab // groups
    sign_back = 1.0 - 2.0 * side_ref[0].astype(jnp.float32)

    def column(c, n):
        return in_ref[n, :, c].reshape(length, lanes)

    def columns(numbers):
        return jnp.concatenate(
            [
                jnp.concatenate([column(c, n) for n in numbers], axis=1)
                for c in range(PAIR)
            ],
            axis=0,
        )

    low, high = columns(range(narrow // 2)), columns(range(narrow // 2, narrow))
    planes = [
        product(split(low + high), pair(second_ref.at[0])),
        product(split(low - high), pair(second_ref.at[1])),
    ]

    def stacked(sign):
        return jnp.concatenate(
            [
                jnp.concatenate(
                    [
                        plane[c * length : c * length + half, part * half : (part + 1) * half]
                        + sign
                        * plane[c * length + half : (c + 1) * length, part * half : (part + 1) * half]
                        for c in range(PAIR)
                        for plane in planes
                    ],
                    axis=1,
                )
                for part in range(2)
            ],
            axis=0,
        )

    squared_b, scale_b = b_ref[0], b_ref[1]
    field = []
    for parity, sign in ((0, 1.0), (1, -1.0)):
        value = product(pair(first_ref.at[parity]), split(stacked(sign)))
        smooth = []
        for c in range(PAIR):
            spot_c = start_ref[0] + (first_c + pl.program_id(0) * PAIR + c)
            wave_c = jnp.full_like(squared_b, spot_c.astype(jnp.float32)) * (2.0 * math.pi / length)
            scale_c = jnp.exp(-0.5 * wave_c * wave_c) * (1.0 / float(length) ** 3)
            squared = a_ref[1, parity] + (squared_b + wave_c * wave_c)
            inverse = scale_c / jnp.where(squared > 0, squared, 1.0)
            smooth.append(jnp.where(squared > 0, inverse * scale_b, 0.0) * a_ref[2, parity])
        smooth = jnp.concatenate(smooth, axis=1)
        field.append(value * jnp.concatenate([smooth, smooth], axis=0))
    upper = lax.broadcasted_iota(jnp.int32, (devices, message, tile), 1) < count
    for number in range(3):
        folded = jnp.concatenate(
            [
                field[parity][part * half : part * half + quarter]
                + sign_back * field[parity][part * half + quarter : (part + 1) * half]
                for part in range(2)
                for parity in range(2)
            ],
            axis=0,
        )
        values = [
            product(
                pair(back_ref.at[0, c % back_ref.shape[1]]),
                split(folded[:, c * length : (c + 1) * length]),
            )
            for c in range(PAIR)
        ]
        for spot in range(tiles // 3):
            parity, part = divmod(spot, 2)
            at = number * (tiles // 3) + spot
            here = [
                value[part * half : (part + 1) * half, parity * tile : (parity + 1) * tile]
                for value in values
            ]
            if groups == 2:
                even, odd = [value.reshape(devices, message, tile) for value in here]
                outs[0][:, at] = jnp.where(upper, even, odd)
                outs[1][:, at] = jnp.where(upper, odd, even)
            else:
                flat = outs[0].reshape(devices * tiles * message, tile)
                for c in range(PAIR):
                    for x in range(slab):
                        start = at * message + c * count + x
                        flat[pl.ds(start, devices, stride=tiles * message), :] = here[c][
                            x * devices : (x + 1) * devices
                        ]
        if number < 2:
            for parity in range(2):
                wave_a = a_ref[0, parity]
                field[parity] = field[parity] * jnp.concatenate([wave_a, wave_a], axis=0)


def halves(length):
    return np.arange(length).reshape(length // 2, 2).T


def spectrum_pass(received, side, start_c, devices, groups, steps, first_step, filled, carried):
    narrow, wide, per_c, rows_x, lanes = received.shape
    length = wide * rows_x
    rows_y = lanes // 2
    half = length // 2
    near = np.arange(half)
    split_index = halves(length)
    slab = half // devices
    second, first, back = [], [], []
    if groups == 2:
        orders = [
            near.reshape(devices, 2, slab // 2)[:, ::step].reshape(-1) for step in (1, -1)
        ]
    else:
        orders = [near.reshape(devices, slab).T.reshape(-1)]
    for parity, index in enumerate(split_index):
        table = turn(-angles(index, near, length)).reshape(2, half, 2, narrow // 2, rows_y)
        second.append(split_table(table.transpose(3, 2, 4, 0, 1).reshape(length, length)))
        first.append(split_table(turn(-angles(index, near, length))))
        columns = split_index[:, : half // 2].reshape(-1)
        back.append(
            [split_table(turn(angles(2 * order + parity, columns, length))) for order in orders]
        )
    tables = [np.stack(second), np.stack(first), np.stack([np.stack(each) for each in back])]
    wave = signed_wave(split_index, length)
    scale = np.where(split_index == half, 0.0, np.exp(-0.5 * wave**2))
    a_table = np.stack([wave, wave**2, scale]).astype(np.float32)[..., None]
    b_table = np.stack([wave**2, scale]).astype(np.float32).reshape(2, 1, length)
    message = PAIR * slab // groups
    spaces = [pltpu.VMEM, pltpu.HBM][:groups]
    out_shape = (devices, 3 * 2 * length // TILE, steps * message, TILE)
    block = out_shape[:2] + (message, TILE)

    def body(*refs):
        spectrum_kernel(slab, groups, first_step * PAIR, len(filled), *refs)

    def fixed(shape):
        return pl.BlockSpec(shape, lambda *_: (0,) * len(shape))

    tables = [a_table, b_table, *tables]
    table_specs = [fixed(table.shape) for table in tables[:4]]
    carry = [pltpu.VMEM(table.shape, table.dtype) for table in tables[:4]]
    carry.append(pltpu.VMEM((1,) + tables[4].shape[1:], tables[4].dtype))
    if carried:
        tables, last_spec = [keep(table, pltpu.VMEM) for table in carried], fixed(carry[4].shape)
    else:
        tables = [in_hbm(table) for table in tables]
        last_spec = pl.BlockSpec(carry[4].shape, lambda i, s, _: (s[0], 0, 0, 0, 0))
    if first_step + per_c // PAIR == steps:
        carry = []
    result = pl.pallas_call(
        body,
        grid_spec=pltpu.PrefetchScalarGridSpec(
            num_scalar_prefetch=2,
            grid=(per_c // PAIR,),
            in_specs=[
                *table_specs,
                last_spec,
                pl.BlockSpec((narrow, wide, PAIR, rows_x, lanes), lambda i, *_: (0, 0, i, 0, 0)),
                *[pl.BlockSpec(memory_space=pl.ANY)] * len(filled),
            ],
            out_specs=[pl.BlockSpec(block, lambda i, *_: (0, 0, first_step + i, 0))] * groups
            + [fixed(each.shape) for each in carry],
        ),
        out_shape=[space(out_shape, jnp.float32) for space in spaces] + carry,
        input_output_aliases={8 + spot: spot for spot in range(len(filled))},
        compiler_params=params(1),
        cost_estimate=cost(per_c * 7 * length**3, 20 * per_c * length**2 * 2),
    )(
        side,
        start_c,
        *tables,
        received,
        *[keep(each, space) for each, space in zip(filled, spaces)],
    )
    return result[:groups], result[groups:]


def shear_kernel(
    per_c, group, joined, row_ref, lane_ref, second_ref, third_ref, ahead_ref, last_ref, in_ref, *refs
):
    shear_ref = refs[-1]
    out_ref, carry_refs = refs[len(refs) // 2 - 1], refs[: len(refs) // 2 - 1]
    hand_on(carry_refs, refs[len(refs) // 2 : -1])
    step = pl.program_id(0)
    length = shear_ref.shape[0]
    half = length // 2
    devices, tiles, message, tile = in_ref.shape
    count = message // per_c
    flat = in_ref.reshape(devices * tiles * message, tile)

    @pl.when(step == 0)
    def _():
        shear_ref[...] = jnp.zeros_like(shear_ref)

    field = jnp.concatenate(
        [
            jnp.concatenate(
                [
                    flat[pl.ds((source * tiles + spot) * message + x, per_c, stride=count), :]
                    for x in range(count)
                    for source in range(devices)
                ],
                axis=0,
            )
            for spot in range(tiles)
        ],
        axis=1,
    )
    field = field * row_ref[0] * lane_ref[0]
    even = product(split(field[:, :length]), pair(second_ref.at[0]))
    odd = product(split(field[:, length:]), pair(second_ref.at[1]))
    near, far = even + odd, even - odd
    field = jnp.concatenate(
        [
            jnp.concatenate(
                [
                    value[x * half : (x + 1) * half, part * half : (part + 1) * half]
                    for x in range(count)
                    for value in (near, far)
                ],
                axis=1,
            )
            for part in range(2)
        ],
        axis=0,
    )
    field = product(pair(third_ref), split(field))
    shear_ref[...] += field * field

    @pl.when(step == 5)
    def _():
        ahead = jnp.concatenate(
            [shear_ref[:, x * length : (x + 1) * length] for x in range(count)], axis=0
        )
        ahead = product(split(ahead), pair(ahead_ref))
        ahead = jnp.concatenate(
            [
                jnp.concatenate(
                    [
                        ahead[x * length : (x + 1) * length, part * length : (part + 1) * length]
                        for x in range(count)
                    ],
                    axis=1,
                )
                for part in range(2)
            ],
            axis=0,
        )
        value = product(pair(last_ref), split(ahead))
        narrow, wide, message_out, _ = out_ref.shape
        rows_b = length // wide
        slots = tile // rows_b
        rows = 2 * length // slots
        run = rows // (2 * narrow * joined)
        out = out_ref.reshape(wide * narrow * message_out, tile)
        lane = lax.broadcasted_iota(jnp.int32, (rows, tile), 1) // rows_b
        for x in range(count):
            for w in range(wide):
                block, place = divmod(w, slots)
                lanes = slice(x * length + block * tile, x * length + (block + 1) * tile)
                moved = None
                for slot in range(slots):
                    piece = value[slot * rows : (slot + 1) * rows, lanes]
                    if slot != place:
                        piece = pltpu.roll(piece, (slot - place) * rows_b % tile, 1)
                    moved = piece if moved is None else jnp.where(lane == slot, piece, moved)
                for n in range(narrow):
                    for part in range(2):
                        for join in range(joined):
                            start = ((n * 2 + part) * joined + join) * run
                            piece = moved[start : start + run]
                            at = (n * wide + w) * message_out
                            if joined == 2:
                                at += part * 2 * count + (join ^ group) * count + x
                                out[pl.ds(at, run, stride=4 * count), :] = piece
                            else:
                                at += (x * 2 + part) * run
                                out[pl.ds(at, run), :] = piece


def shear_pass(received, wide, narrow, per_c, group, joined, carry):
    devices, tiles, message, tile = received.shape
    count = message // per_c
    length = tiles * tile // 6
    half = length // 2
    index = np.arange(length)
    angle = angles(index, index, length)
    cosine, sine = np.cos(angle), np.sin(angle)
    split_index = halves(length)
    second = np.stack(
        [split_table(turn(angles(np.arange(half), b, length)).T) for b in split_index]
    )
    row_c = np.arange(half) ^ group
    weight = np.where(row_c == 0, 1.0, 2.0)
    angle = angles(index, row_c, length)
    third = np.concatenate([weight * np.cos(angle), -weight * np.sin(angle)], axis=1)
    ahead = np.concatenate([cosine, -sine], axis=1)
    slots = TILE * wide // length
    order = index.reshape(narrow, -1, joined, slots).transpose(3, 0, 2, 1)
    angle = angles(order.reshape(-1), index, length)
    last = np.stack(
        [
            np.concatenate([np.cos(angle), np.sin(angle)], axis=1),
            np.concatenate([-np.sin(angle), np.cos(angle)], axis=1),
        ]
    )
    last = last.reshape(2, slots, narrow, -1, 2 * length).transpose(1, 2, 0, 3, 4)
    last = last.reshape(2 * length, 2 * length)
    wave = signed_wave(index, length)
    wave_rows = np.tile(wave[row_c], count)
    wave_lanes = np.stack([wave[split_index]] * 2, axis=1).reshape(-1)
    twice = math.sqrt(2.0)
    one_row, one_lane = np.ones_like(wave_rows), np.ones_like(wave_lanes)
    row_factor = np.stack(
        [one_row, twice * one_row, twice * wave_rows, one_row, twice * wave_rows, wave_rows**2]
    ).astype(np.float32)[:, :, None]
    lane_factor = np.stack(
        [one_lane, wave_lanes, one_lane, wave_lanes**2, wave_lanes, one_lane]
    ).astype(np.float32)[:, None, :]
    tables = [second] + [split_table(table) for table in (third, ahead, last)]
    out_shape = (narrow, wide, count * 2 * length // (narrow * slots), TILE)

    def body(*refs):
        shear_kernel(per_c, group, joined, *refs)

    def which(i):
        return (0, 2 - (i >= 1).astype(jnp.int32) - (i >= 3).astype(jnp.int32), 0, 0)

    return pl.pallas_call(
        body,
        grid=(6,),
        in_specs=[
            pl.BlockSpec((1, count * half, 1), lambda i: (i, 0, 0)),
            pl.BlockSpec((1, 1, 2 * length), lambda i: (i, 0, 0)),
            *[whole(table.shape) for table in tables],
            pl.BlockSpec((devices, tiles // 3, message, tile), which),
            *[whole(each.shape) for each in carry],
        ],
        out_specs=[whole(out_shape)] + [whole(each.shape) for each in carry],
        out_shape=[pltpu.HBM(out_shape, jnp.float32)]
        + [pltpu.VMEM(each.shape, each.dtype) for each in carry],
        scratch_shapes=[pltpu.VMEM((length, count * length), jnp.float32)],
        compiler_params=params(1),
        cost_estimate=cost(count * 18 * length**3, 4 * received.size + 4 * 2**20),
    )(
        *[in_hbm(value) for value in (row_factor, lane_factor, *tables)],
        received,
        *[in_hbm(each) for each in carry],
    )


def first_kernel(count, rows_b, anchor_ref, table_ref, *refs):
    ins, (real_ref, imag_ref) = refs[:-2], refs[-2:]
    sides, ranks, wide, rows, lanes = ins[0].shape
    length = real_ref.shape[2]
    half = length // 2
    slots = lanes // rows_b
    joined = len(ins)
    steps = real_ref.shape[0] // (slots * joined)
    spot_row = lax.broadcasted_iota(jnp.int32, (lanes, half), 0)
    spot_a = lax.broadcasted_iota(jnp.int32, (lanes, half), 1)
    is_anchor = (anchor_ref[0] == 1) & (pl.program_id(0) == 0)
    start = pl.program_id(0) * steps
    anchor = (spot_row == 0) & (spot_a == 0) & is_anchor
    upper = lax.broadcasted_iota(jnp.int32, (wide * ranks, joined * count, lanes), 1) < count

    def gathered(side, step, part):
        if joined == 2:
            at = ((start + step) * 2 + part) * 2 * count
            at = pl.ds(pl.multiple_of(at, 2 * count), 2 * count)
            own, other = [
                ref[side, :, :, at].reshape(wide * ranks, 2 * count, lanes) for ref in ins
            ]
            both = [jnp.where(upper, own, other), jnp.where(upper, other, own)]
            return [value.reshape(half, lanes).T for value in both]
        flat = ins[0].reshape(wide * sides * ranks * rows, lanes)
        run = rows // count
        start_row = side * ranks * wide * rows + part * steps + step
        value = flat[pl.ds(start_row, ranks * wide * count, stride=run), :]
        return [value.T]

    lefts = []
    for side in range(sides):
        tiles = [[gathered(side, step, part) for part in range(2)] for step in range(steps)]
        lefts.append(
            [
                jnp.concatenate(
                    [jnp.concatenate([part[join] for part in parts], axis=1) for parts in tiles], axis=0
                )
                for join in range(joined)
            ]
        )
    for join in range(joined):
        sums = [
            product(split(lefts[side][join]), pair(table_ref.at[join, side])) for side in range(sides)
        ]
        even, odd = sums
        for far, value in enumerate((even + odd, even - odd)):
            for step in range(steps):
                at = (step * joined + join) * slots
                columns = slice(far * half, (far + 1) * half)
                for part, ref in enumerate((real_ref, imag_ref)):
                    here = value[step * lanes : (step + 1) * lanes, part * half : (part + 1) * half]
                    if at == 0 and far == 0:
                        here = jnp.where(anchor, 0.0, here)
                    ref[at : at + slots, :, columns] = here.reshape(slots, rows_b, half)


def first_table(length, wide, ranks, joined, count, sides):
    scale = 1.0 / float(length) ** 1.5
    index = np.arange(length).reshape(wide, ranks, joined, count, sides)
    index = index.swapaxes(0, 1).reshape(wide * ranks, joined, count, sides)
    tables = []
    for join in range(joined):
        order = index[:, :: 1 - 2 * join].transpose(3, 0, 1, 2).reshape(sides, -1)
        tables.append(
            [split_table(scale * turn(-angles(np.arange(length // 2), x, length)).T) for x in order]
        )
    return np.stack([np.stack(each) for each in tables])


def first_pass(parts, table, is_anchor, length, wide, sides, count):
    devices, rows, lanes = parts[0].shape
    joined = len(parts)
    ranks = devices // wide // sides
    rows_b = length // wide
    slots = lanes // rows_b
    total = rows // (2 * joined * count) if joined == 2 else rows // (2 * count)
    grid = 4 if joined == 2 and total % 4 == 0 else 1
    parts = [part.reshape(sides, ranks, wide, rows, lanes) for part in parts]

    def body(*refs):
        first_kernel(count, rows_b, *refs)

    rows_c = total * joined * slots
    out_shape = jax.ShapeDtypeStruct((rows_c, rows_b, length), jnp.float32)
    return pl.pallas_call(
        body,
        grid=(grid,),
        in_specs=[
            pl.BlockSpec(memory_space=pltpu.SMEM),
            whole(table.shape),
            *[whole((sides, ranks, wide, rows, lanes))] * joined,
        ],
        out_specs=[pl.BlockSpec((rows_c // grid, rows_b, length), lambda i: (i, 0, 0))] * 2,
        out_shape=[out_shape] * 2,
        compiler_params=params(1),
        cost_estimate=cost(rows_c * 2 * rows_b * length * length, 16 * rows_c * rows_b * length),
    )(is_anchor, keep(table, pltpu.VMEM), *[keep(part, pltpu.VMEM) for part in parts])


def transpose(value, members=None):
    return lax.all_to_all(
        value, AXES, split_axis=0, concat_axis=0, tiled=True, axis_index_groups=members
    )


def solution(mesh):
    wide, narrow = mesh.shape["wide"], mesh.shape["narrow"]
    sides = 2
    ranks = narrow // sides
    devices = wide * ranks
    members = [
        [(side * ranks + rank) * wide + w for w in range(wide) for rank in range(ranks)]
        for side in range(sides)
    ]

    def per_device(density):
        rows_x, rows_y, length = density.shape
        half = length // 2
        per_c = half // devices
        slab = half // devices
        steps = per_c // PAIR
        counts = [per_c - PAIR, PAIR] if steps > 1 else [per_c]
        groups = 2 if slab > 2 else 1
        spot_wide, spot_narrow = lax.axis_index("wide"), lax.axis_index("narrow")
        side = (spot_narrow // ranks).astype(jnp.int32).reshape(1)
        rank = spot_wide * ranks + spot_narrow % ranks
        start_c = (rank * per_c).astype(jnp.int32).reshape(1)
        chunks, carried, start = [], [], 0
        for planes, count in zip(third_pass(density, wide, sides, ranks, counts), counts):
            planes = transpose(planes.reshape(wide * narrow, count, rows_x, 2 * rows_y))
            planes = planes.reshape(narrow, wide, count, rows_x, 2 * rows_y)
            planes = keep(planes, pltpu.VMEM if start else pltpu.HBM)
            chunks, carried = spectrum_pass(
                planes, side, start_c, devices, groups, steps, start // PAIR, chunks, carried
            )
            start += count
        is_anchor = ((spot_wide == 0) & (spot_narrow == 0)).astype(jnp.int32).reshape(1)
        parts = []
        table = first_table(length, wide, ranks, groups, slab // groups, sides)
        for group, chunk in enumerate(chunks):
            carry = [table] if group == groups - 1 else []
            received = keep(transpose(chunk, members), pltpu.VMEM if group else pltpu.HBM)
            part, *carry = shear_pass(received, wide, narrow, per_c, group, groups, carry)
            parts.append(transpose(part.reshape((wide * narrow,) + part.shape[2:])))
        return tuple(first_pass(parts, *carry, is_anchor, length, wide, sides, slab // groups))

    return jax.shard_map(
        per_device,
        mesh=mesh,
        in_specs=(P("wide", "narrow", None),),
        out_specs=(P("narrow", "wide", None), P("narrow", "wide", None)),
        check_vma=False,
    )
```

```python
import math

import jax
import jax.numpy as jnp
import ml_dtypes
import numpy as np
from jax import lax
from jax.experimental import pallas as pl
from jax.experimental.pallas import tpu as pltpu
from jax.sharding import PartitionSpec as P

AXES = ("wide", "narrow")
TILE = 128
LIMIT = 16 * 1024 * 1024


def angles(rows, columns, length):
    return (2.0 * math.pi / length) * (np.outer(rows, columns) % length)


def split_table(table):
    table = np.asarray(table, np.float64)
    high = table.astype(ml_dtypes.bfloat16)
    low = (table - high.astype(np.float64)).astype(ml_dtypes.bfloat16)
    return np.stack([high, low])


def split(value):
    high = value.astype(jnp.bfloat16)
    low = (value - high.astype(jnp.float32)).astype(jnp.bfloat16)
    return high, low


def product(left, right, contract=((1,), (0,))):
    (left_axis,), (right_axis,) = contract
    left = jnp.concatenate([left[0], left[0], left[1]], axis=left_axis)
    right = jnp.concatenate([right[0], right[1], right[0]], axis=right_axis)
    return lax.dot_general(
        left, right, (contract, ((), ())), preferred_element_type=jnp.float32
    )


def pair(ref):
    return ref[0], ref[1]


def signed_wave(index, length):
    index = np.asarray(index)
    return np.where(index < length // 2, index, index - length) * (2.0 * math.pi / length)


def params(steps):
    return pltpu.CompilerParams(
        vmem_limit_bytes=LIMIT, dimension_semantics=("arbitrary",) * steps
    )


def whole(shape):
    return pl.BlockSpec(shape, lambda *_: (0,) * len(shape))


def keep(value, space):
    return pltpu.with_memory_space_constraint(jnp.asarray(value), space)


def in_hbm(value):
    return keep(value, pltpu.HBM)


def cost(macs, moved):
    return pl.CostEstimate(flops=6 * macs, bytes_accessed=moved, transcendentals=0)


def third_kernel(counts, table_ref, density_ref, *outs):
    step_x, rows_y, length = density_ref.shape
    wide, sides, ranks, _, rows_x, _ = outs[0].shape
    half = length // 2
    flats = [ref.reshape(math.prod(ref.shape[:5]), 2 * rows_y) for ref in outs]
    table = pair(table_ref)
    group = 4
    start_x = pl.program_id(0) * step_x
    for first in range(0, step_x, group):
        block = density_ref[first : first + group].reshape(group * rows_y, length)
        result = product(split(block), table)
        for inner in range(group):
            rows = slice(inner * rows_y, (inner + 1) * rows_y)
            value = jnp.concatenate([result[rows, :half], result[rows, half:]], axis=0).T
            start = 0
            for flat, count in zip(flats, counts):
                for c in range(count):
                    for rank in range(ranks):
                        at = (rank * count + c) * rows_x + first + inner + start_x
                        stride = sides * ranks * count * rows_x
                        flat[pl.ds(at, wide, stride=stride), :] = value[start : start + wide]
                        start += wide
    for ref in outs:
        rows = pl.ds(pl.multiple_of(start_x, step_x), step_x)
        for side in range(1, sides):
            ref[:, side, :, :, rows] = ref[:, 0, :, :, rows]


def third_pass(density, wide, sides, ranks, counts):
    rows_x, rows_y, length = density.shape
    half = length // 2
    per_c = sum(counts)
    order = np.arange(half).reshape(wide, ranks, per_c).transpose(2, 1, 0).reshape(-1)
    angle = angles(np.arange(length), order, length)
    table = split_table(np.concatenate([np.cos(angle), -np.sin(angle)], axis=1))
    step = max(rows_x // 2, min(8, rows_x))

    def body(*refs):
        third_kernel(counts, *refs)

    return pl.pallas_call(
        body,
        grid=(rows_x // step,),
        in_specs=[
            whole(table.shape),
            pl.BlockSpec((step, rows_y, length), lambda i: (i, 0, 0)),
        ],
        out_specs=[
            whole((wide, sides, ranks, count, rows_x, 2 * rows_y)) for count in counts
        ],
        out_shape=[
            pltpu.VMEM((wide, sides, ranks, count, rows_x, 2 * rows_y), jnp.float32)
            for count in counts
        ],
        compiler_params=params(1),
        cost_estimate=cost(density.size * length, 12 * density.size),
    )(in_hbm(table), in_hbm(density))


PAIR = 2


def turn(angle):
    cosine, sine = np.cos(angle), np.sin(angle)
    return np.block([[cosine, -sine], [sine, cosine]])


def hand_on(sources, targets):
    @pl.when(pl.program_id(0) == 0)
    def _():
        for source, target in zip(sources, targets):
            target[...] = source[...]


def spectrum_kernel(slab, groups, first_c, filled, side_ref, start_ref, *refs):
    tables, in_ref, outs = refs[:5], refs[5], refs[6 + filled :]
    a_ref, b_ref, second_ref, first_ref, back_ref = tables
    hand_on(tables, outs[groups:])
    outs = outs[:groups]
    wide, narrow, _, rows_x, lanes = in_ref.shape
    length = wide * rows_x
    half = length // 2
    quarter = half // 2
    devices, tiles, message, tile = outs[0].shape
    count = slab // groups
    sign_back = 1.0 - 2.0 * side_ref[0].astype(jnp.float32)

    def column(c, n):
        return in_ref[:, n, c].reshape(length, lanes)

    def columns(numbers):
        return jnp.concatenate(
            [
                jnp.concatenate([column(c, n) for n in numbers], axis=1)
                for c in range(PAIR)
            ],
            axis=0,
        )

    low, high = columns(range(narrow // 2)), columns(range(narrow // 2, narrow))
    planes = [
        product(split(low + high), pair(second_ref.at[0])),
        product(split(low - high), pair(second_ref.at[1])),
    ]

    def stacked(sign):
        return jnp.concatenate(
            [
                jnp.concatenate(
                    [
                        plane[c * length : c * length + half, part * half : (part + 1) * half]
                        + sign
                        * plane[c * length + half : (c + 1) * length, part * half : (part + 1) * half]
                        for c in range(PAIR)
                        for plane in planes
                    ],
                    axis=1,
                )
                for part in range(2)
            ],
            axis=0,
        )

    squared_b, scale_b = b_ref[0], b_ref[1]
    field = []
    for parity, sign in ((0, 1.0), (1, -1.0)):
        value = product(pair(first_ref.at[parity]), split(stacked(sign)))
        smooth = []
        for c in range(PAIR):
            spot_c = start_ref[0] + (first_c + pl.program_id(0) * PAIR + c)
            wave_c = jnp.full_like(squared_b, spot_c.astype(jnp.float32)) * (2.0 * math.pi / length)
            scale_c = jnp.exp(-0.5 * wave_c * wave_c) * (1.0 / float(length) ** 3)
            squared = a_ref[1, parity] + (squared_b + wave_c * wave_c)
            inverse = scale_c / jnp.where(squared > 0, squared, 1.0)
            smooth.append(jnp.where(squared > 0, inverse * scale_b, 0.0) * a_ref[2, parity])
        smooth = jnp.concatenate(smooth, axis=1)
        field.append(value * jnp.concatenate([smooth, smooth], axis=0))
    upper = lax.broadcasted_iota(jnp.int32, (devices, message, tile), 1) < count
    for number in range(3):
        folded = jnp.concatenate(
            [
                field[parity][part * half : part * half + quarter]
                + sign_back * field[parity][part * half + quarter : (part + 1) * half]
                for part in range(2)
                for parity in range(2)
            ],
            axis=0,
        )
        values = [
            product(
                pair(back_ref.at[0, c % back_ref.shape[1]]),
                split(folded[:, c * length : (c + 1) * length]),
            )
            for c in range(PAIR)
        ]
        for spot in range(tiles // 3):
            parity, part = divmod(spot, 2)
            at = number * (tiles // 3) + spot
            here = [
                value[part * half : (part + 1) * half, parity * tile : (parity + 1) * tile]
                for value in values
            ]
            if groups == 2:
                even, odd = [value.reshape(devices, message, tile) for value in here]
                outs[0][:, at] = jnp.where(upper, even, odd)
                outs[1][:, at] = jnp.where(upper, odd, even)
            else:
                flat = outs[0].reshape(devices * tiles * message, tile)
                for c in range(PAIR):
                    for x in range(slab):
                        start = at * message + c * count + x
                        flat[pl.ds(start, devices, stride=tiles * message), :] = here[c][
                            x * devices : (x + 1) * devices
                        ]
        if number < 2:
            for parity in range(2):
                wave_a = a_ref[0, parity]
                field[parity] = field[parity] * jnp.concatenate([wave_a, wave_a], axis=0)


def halves(length):
    return np.arange(length).reshape(length // 2, 2).T


def spectrum_pass(received, side, start_c, devices, groups, steps, first_step, filled, carried):
    wide, narrow, per_c, rows_x, lanes = received.shape
    length = wide * rows_x
    rows_y = lanes // 2
    half = length // 2
    near = np.arange(half)
    split_index = halves(length)
    slab = half // devices
    second, first, back = [], [], []
    if groups == 2:
        orders = [
            near.reshape(devices, 2, slab // 2)[:, ::step].reshape(-1) for step in (1, -1)
        ]
    else:
        orders = [near.reshape(devices, slab).T.reshape(-1)]
    for parity, index in enumerate(split_index):
        table = turn(-angles(index, near, length)).reshape(2, half, 2, narrow // 2, rows_y)
        second.append(split_table(table.transpose(3, 2, 4, 0, 1).reshape(length, length)))
        first.append(split_table(turn(-angles(index, near, length))))
        columns = split_index[:, : half // 2].reshape(-1)
        back.append(
            [split_table(turn(angles(2 * order + parity, columns, length))) for order in orders]
        )
    tables = [np.stack(second), np.stack(first), np.stack([np.stack(each) for each in back])]
    wave = signed_wave(split_index, length)
    scale = np.where(split_index == half, 0.0, np.exp(-0.5 * wave**2))
    a_table = np.stack([wave, wave**2, scale]).astype(np.float32)[..., None]
    b_table = np.stack([wave**2, scale]).astype(np.float32).reshape(2, 1, length)
    message = PAIR * slab // groups
    spaces = [pltpu.VMEM, pltpu.HBM][:groups]
    out_shape = (devices, 3 * 2 * length // TILE, steps * message, TILE)
    block = out_shape[:2] + (message, TILE)

    def body(*refs):
        spectrum_kernel(slab, groups, first_step * PAIR, len(filled), *refs)

    def fixed(shape):
        return pl.BlockSpec(shape, lambda *_: (0,) * len(shape))

    tables = [a_table, b_table, *tables]
    table_specs = [fixed(table.shape) for table in tables[:4]]
    carry = [pltpu.VMEM(table.shape, table.dtype) for table in tables[:4]]
    carry.append(pltpu.VMEM((1,) + tables[4].shape[1:], tables[4].dtype))
    if carried:
        tables, last_spec = [keep(table, pltpu.VMEM) for table in carried], fixed(carry[4].shape)
    else:
        tables = [in_hbm(table) for table in tables]
        last_spec = pl.BlockSpec(carry[4].shape, lambda i, s, _: (s[0], 0, 0, 0, 0))
    if first_step + per_c // PAIR == steps:
        carry = []
    result = pl.pallas_call(
        body,
        grid_spec=pltpu.PrefetchScalarGridSpec(
            num_scalar_prefetch=2,
            grid=(per_c // PAIR,),
            in_specs=[
                *table_specs,
                last_spec,
                pl.BlockSpec((wide, narrow, PAIR, rows_x, lanes), lambda i, *_: (0, 0, i, 0, 0)),
                *[pl.BlockSpec(memory_space=pl.ANY)] * len(filled),
            ],
            out_specs=[pl.BlockSpec(block, lambda i, *_: (0, 0, first_step + i, 0))] * groups
            + [fixed(each.shape) for each in carry],
        ),
        out_shape=[space(out_shape, jnp.float32) for space in spaces] + carry,
        input_output_aliases={8 + spot: spot for spot in range(len(filled))},
        compiler_params=params(1),
        cost_estimate=cost(per_c * 7 * length**3, 20 * per_c * length**2 * 2),
    )(
        side,
        start_c,
        *tables,
        received,
        *[keep(each, space) for each, space in zip(filled, spaces)],
    )
    return result[:groups], result[groups:]


def shear_kernel(
    per_c, group, joined, row_ref, lane_ref, second_ref, third_ref, ahead_ref, last_ref, in_ref, *refs
):
    shear_ref = refs[-1]
    out_ref, carry_refs = refs[len(refs) // 2 - 1], refs[: len(refs) // 2 - 1]
    hand_on(carry_refs, refs[len(refs) // 2 : -1])
    step = pl.program_id(0)
    length = shear_ref.shape[0]
    half = length // 2
    devices, tiles, message, tile = in_ref.shape
    count = message // per_c
    flat = in_ref.reshape(devices * tiles * message, tile)

    @pl.when(step == 0)
    def _():
        shear_ref[...] = jnp.zeros_like(shear_ref)

    field = jnp.concatenate(
        [
            jnp.concatenate(
                [
                    flat[pl.ds((source * tiles + spot) * message + x, per_c, stride=count), :]
                    for x in range(count)
                    for source in range(devices)
                ],
                axis=0,
            )
            for spot in range(tiles)
        ],
        axis=1,
    )
    field = field * row_ref[0] * lane_ref[0]
    even = product(split(field[:, :length]), pair(second_ref.at[0]))
    odd = product(split(field[:, length:]), pair(second_ref.at[1]))
    near, far = even + odd, even - odd
    field = jnp.concatenate(
        [
            jnp.concatenate(
                [
                    value[x * half : (x + 1) * half, part * half : (part + 1) * half]
                    for x in range(count)
                    for value in (near, far)
                ],
                axis=1,
            )
            for part in range(2)
        ],
        axis=0,
    )
    field = product(pair(third_ref), split(field))
    shear_ref[...] += field * field

    @pl.when(step == 5)
    def _():
        ahead = jnp.concatenate(
            [shear_ref[:, x * length : (x + 1) * length] for x in range(count)], axis=0
        )
        ahead = product(split(ahead), pair(ahead_ref))
        ahead = jnp.concatenate(
            [
                jnp.concatenate(
                    [
                        ahead[x * length : (x + 1) * length, part * length : (part + 1) * length]
                        for x in range(count)
                    ],
                    axis=1,
                )
                for part in range(2)
            ],
            axis=0,
        )
        value = product(pair(last_ref), split(ahead))
        wide, narrow, message_out, _ = out_ref.shape
        rows_b = length // wide
        slots = tile // rows_b
        rows = 2 * length // slots
        run = rows // (2 * narrow * joined)
        out = out_ref.reshape(wide * narrow * message_out, tile)
        lane = lax.broadcasted_iota(jnp.int32, (rows, tile), 1) // rows_b
        for x in range(count):
            for w in range(wide):
                block, place = divmod(w, slots)
                lanes = slice(x * length + block * tile, x * length + (block + 1) * tile)
                moved = None
                for slot in range(slots):
                    piece = value[slot * rows : (slot + 1) * rows, lanes]
                    if slot != place:
                        piece = pltpu.roll(piece, (slot - place) * rows_b % tile, 1)
                    moved = piece if moved is None else jnp.where(lane == slot, piece, moved)
                for n in range(narrow):
                    for part in range(2):
                        for join in range(joined):
                            start = ((n * 2 + part) * joined + join) * run
                            piece = moved[start : start + run]
                            at = (w * narrow + n) * message_out
                            if joined == 2:
                                at += part * 2 * count + (join ^ group) * count + x
                                out[pl.ds(at, run, stride=4 * count), :] = piece
                            else:
                                at += (x * 2 + part) * run
                                out[pl.ds(at, run), :] = piece


def shear_pass(received, wide, narrow, per_c, group, joined, carry):
    devices, tiles, message, tile = received.shape
    count = message // per_c
    length = tiles * tile // 6
    half = length // 2
    index = np.arange(length)
    angle = angles(index, index, length)
    cosine, sine = np.cos(angle), np.sin(angle)
    split_index = halves(length)
    second = np.stack(
        [split_table(turn(angles(np.arange(half), b, length)).T) for b in split_index]
    )
    row_c = np.arange(half) ^ group
    weight = np.where(row_c == 0, 1.0, 2.0)
    angle = angles(index, row_c, length)
    third = np.concatenate([weight * np.cos(angle), -weight * np.sin(angle)], axis=1)
    ahead = np.concatenate([cosine, -sine], axis=1)
    slots = TILE * wide // length
    order = index.reshape(narrow, -1, joined, slots).transpose(3, 0, 2, 1)
    angle = angles(order.reshape(-1), index, length)
    last = np.stack(
        [
            np.concatenate([np.cos(angle), np.sin(angle)], axis=1),
            np.concatenate([-np.sin(angle), np.cos(angle)], axis=1),
        ]
    )
    last = last.reshape(2, slots, narrow, -1, 2 * length).transpose(1, 2, 0, 3, 4)
    last = last.reshape(2 * length, 2 * length)
    wave = signed_wave(index, length)
    wave_rows = np.tile(wave[row_c], count)
    wave_lanes = np.stack([wave[split_index]] * 2, axis=1).reshape(-1)
    twice = math.sqrt(2.0)
    one_row, one_lane = np.ones_like(wave_rows), np.ones_like(wave_lanes)
    row_factor = np.stack(
        [one_row, twice * one_row, twice * wave_rows, one_row, twice * wave_rows, wave_rows**2]
    ).astype(np.float32)[:, :, None]
    lane_factor = np.stack(
        [one_lane, wave_lanes, one_lane, wave_lanes**2, wave_lanes, one_lane]
    ).astype(np.float32)[:, None, :]
    tables = [second] + [split_table(table) for table in (third, ahead, last)]
    out_shape = (wide, narrow, count * 2 * length // (narrow * slots), TILE)

    def body(*refs):
        shear_kernel(per_c, group, joined, *refs)

    def which(i):
        return (0, 2 - (i >= 1).astype(jnp.int32) - (i >= 3).astype(jnp.int32), 0, 0)

    return pl.pallas_call(
        body,
        grid=(6,),
        in_specs=[
            pl.BlockSpec((1, count * half, 1), lambda i: (i, 0, 0)),
            pl.BlockSpec((1, 1, 2 * length), lambda i: (i, 0, 0)),
            *[whole(table.shape) for table in tables],
            pl.BlockSpec((devices, tiles // 3, message, tile), which),
            *[whole(each.shape) for each in carry],
        ],
        out_specs=[whole(out_shape)] + [whole(each.shape) for each in carry],
        out_shape=[pltpu.HBM(out_shape, jnp.float32)]
        + [pltpu.VMEM(each.shape, each.dtype) for each in carry],
        scratch_shapes=[pltpu.VMEM((length, count * length), jnp.float32)],
        compiler_params=params(1),
        cost_estimate=cost(count * 18 * length**3, 4 * received.size + 4 * 2**20),
    )(
        *[in_hbm(value) for value in (row_factor, lane_factor, *tables)],
        received,
        *[in_hbm(each) for each in carry],
    )


def first_kernel(count, rows_b, joined, pieces, anchor_ref, table_ref, *refs):
    ins, (real_out, imag_out) = list(refs[:joined]), refs[joined : joined + 2]
    real_ref, imag_ref, first_ref, in_sems, out_sems = refs[joined + 2 :]
    wide, sides, ranks, rows, lanes = ins[-1].shape
    rows_c, _, length = real_ref.shape
    half = length // 2
    slots = lanes // rows_b
    steps = rows_c // (slots * joined) // pieces
    in_copies = []
    if joined == 2:
        for piece in range(pieces):
            at = pl.ds(piece * (rows // pieces), rows // pieces)
            copy = pltpu.make_async_copy(
                ins[0].at[:, :, :, at], first_ref.at[:, :, :, at], in_sems.at[piece]
            )
            copy.start()
            in_copies.append(copy)
        ins[0] = first_ref
    spot_row = lax.broadcasted_iota(jnp.int32, (lanes, half), 0)
    spot_a = lax.broadcasted_iota(jnp.int32, (lanes, half), 1)
    anchor = (spot_row == 0) & (spot_a == 0) & (anchor_ref[0] == 1)
    upper = lax.broadcasted_iota(jnp.int32, (wide * ranks, joined * count, lanes), 1) < count

    def gathered(side, step, part):
        if joined == 2:
            at = pl.ds((step * 2 + part) * 2 * count, 2 * count)
            own, other = [
                ref[:, side, :, at].reshape(wide * ranks, 2 * count, lanes) for ref in ins
            ]
            both = jnp.where(upper, own, other), jnp.where(upper, other, own)
            return [value.reshape(half, lanes).T for value in both]
        flat = ins[0].reshape(wide * sides * ranks * rows, lanes)
        run = rows // count
        value = jnp.concatenate(
            [
                flat[
                    pl.ds((w * sides + side) * ranks * rows + part * steps + step, ranks * count, stride=run),
                    :,
                ]
                for w in range(wide)
            ],
            axis=0,
        )
        return [value.T]

    out_copies = []
    for piece in range(pieces):
        if in_copies:
            in_copies[piece].wait()
        tiles = [
            [
                [gathered(side, piece * steps + step, part) for part in range(2)]
                for step in range(steps)
            ]
            for side in range(sides)
        ]
        first = piece * steps * joined * slots
        for join in range(joined):
            sums = []
            for side in range(sides):
                left = jnp.concatenate(
                    [
                        jnp.concatenate([part[join] for part in parts], axis=1)
                        for parts in tiles[side]
                    ],
                    axis=0,
                )
                sums.append(product(split(left), pair(table_ref.at[join, side])))
            even, odd = sums
            for far, value in enumerate((even + odd, even - odd)):
                columns = slice(far * half, (far + 1) * half)
                for step in range(steps):
                    for part, ref in enumerate((real_ref, imag_ref)):
                        here = value[step * lanes : (step + 1) * lanes, part * half : (part + 1) * half]
                        at = first + (step * joined + join) * slots
                        if at == 0 and far == 0:
                            here = jnp.where(anchor, 0.0, here)
                        ref[at : at + slots, :, columns] = here.reshape(slots, rows_b, half)
        at = pl.ds(first, steps * joined * slots)
        for part, (ref, out) in enumerate(((real_ref, real_out), (imag_ref, imag_out))):
            copy = pltpu.make_async_copy(ref.at[at], out.at[at], out_sems.at[2 * piece + part])
            copy.start()
            out_copies.append(copy)
    for copy in out_copies:
        copy.wait()


def first_table(length, devices, joined, count, sides):
    scale = 1.0 / float(length) ** 1.5
    index = np.arange(length).reshape(devices, joined, count, sides)
    tables = []
    for join in range(joined):
        order = index[:, :: 1 - 2 * join].transpose(3, 0, 1, 2).reshape(sides, -1)
        tables.append(
            [split_table(scale * turn(-angles(np.arange(length // 2), x, length)).T) for x in order]
        )
    return np.stack([np.stack(each) for each in tables])


def first_pass(parts, table, is_anchor, length, wide, sides, count):
    devices, rows, lanes = parts[0].shape
    joined = len(parts)
    ranks = devices // wide // sides
    rows_b = length // wide
    slots = lanes // rows_b
    total = rows // (2 * joined * count)
    pieces = 4 if joined == 2 and total % 4 == 0 else 1
    parts = [part.reshape(wide, sides, ranks, rows, lanes) for part in parts]

    def body(*refs):
        first_kernel(count, rows_b, joined, pieces, *refs)

    rows_c = total * joined * slots
    out_shape = (rows_c, rows_b, length)
    first_shape = parts[0].shape if joined == 2 else (8, TILE)
    anywhere = pl.BlockSpec(memory_space=pl.ANY)
    return pl.pallas_call(
        body,
        grid=(1,),
        in_specs=[
            pl.BlockSpec(memory_space=pltpu.SMEM),
            whole(table.shape),
            *[anywhere] * (joined - 1),
            whole(parts[-1].shape),
        ],
        out_specs=[anywhere] * 2,
        out_shape=[pltpu.HBM(out_shape, jnp.float32)] * 2,
        scratch_shapes=[
            pltpu.VMEM(out_shape, jnp.float32),
            pltpu.VMEM(out_shape, jnp.float32),
            pltpu.VMEM(first_shape, jnp.float32),
            pltpu.SemaphoreType.DMA((pieces,)),
            pltpu.SemaphoreType.DMA((2 * pieces,)),
        ],
        compiler_params=params(1),
        cost_estimate=cost(rows_c * 2 * rows_b * length * length, 16 * rows_c * rows_b * length),
    )(
        is_anchor,
        keep(table, pltpu.VMEM),
        *[in_hbm(part) for part in parts[:-1]],
        keep(parts[-1], pltpu.VMEM),
    )


def transpose(value, members=None):
    return lax.all_to_all(
        value, AXES, split_axis=0, concat_axis=0, tiled=True, axis_index_groups=members
    )


def solution(mesh):
    wide, narrow = mesh.shape["wide"], mesh.shape["narrow"]
    sides = 2
    ranks = narrow // sides
    devices = wide * ranks
    members = [
        [w * narrow + side * ranks + rank for w in range(wide) for rank in range(ranks)]
        for side in range(sides)
    ]

    def per_device(density):
        rows_x, rows_y, length = density.shape
        half = length // 2
        per_c = half // devices
        slab = half // devices
        steps = per_c // PAIR
        counts = [per_c - PAIR, PAIR] if steps > 1 else [per_c]
        groups = 2 if slab > 2 else 1
        spot_wide, spot_narrow = lax.axis_index("wide"), lax.axis_index("narrow")
        side = (spot_narrow // ranks).astype(jnp.int32).reshape(1)
        rank = spot_wide * ranks + spot_narrow % ranks
        start_c = (rank * per_c).astype(jnp.int32).reshape(1)
        chunks, carried, start = [], [], 0
        for planes, count in zip(third_pass(density, wide, sides, ranks, counts), counts):
            planes = transpose(planes.reshape(wide * narrow, count, rows_x, 2 * rows_y))
            planes = planes.reshape(wide, narrow, count, rows_x, 2 * rows_y)
            planes = keep(planes, pltpu.VMEM if start else pltpu.HBM)
            chunks, carried = spectrum_pass(
                planes, side, start_c, devices, groups, steps, start // PAIR, chunks, carried
            )
            start += count
        is_anchor = ((spot_wide == 0) & (spot_narrow == 0)).astype(jnp.int32).reshape(1)
        parts = []
        table = first_table(length, devices, groups, slab // groups, sides)
        for group, chunk in enumerate(chunks):
            carry = [table] if group == groups - 1 else []
            received = keep(transpose(chunk, members), pltpu.VMEM if group else pltpu.HBM)
            part, *carry = shear_pass(received, wide, narrow, per_c, group, groups, carry)
            parts.append(transpose(part.reshape((wide * narrow,) + part.shape[2:])))
        return tuple(first_pass(parts, *carry, is_anchor, length, wide, sides, slab // groups))

    return jax.shard_map(
        per_device,
        mesh=mesh,
        in_specs=(P("wide", "narrow", None),),
        out_specs=(P("narrow", "wide", None), P("narrow", "wide", None)),
        check_vma=False,
    )
```
